32 devices in a mesh: group: 2 (over x), gx: 16 (over z, y, core).
Axes of the slice: x: 2, y: 2, z: 4, core: 2. Of those that a mesh axis runs over, the one named last changes fastest.
Arguments:
- initial: float32 [4, 64, 64, 256], P('group', 'gx'), parts along dimension 0, may hold values from -1.25 to 1.25
- observed: float32 [4, 64, 64, 256], P('group', 'gx'), parts along dimension 0, may hold values from -6 to 6
- mobility: float32 [128, 64, 256], P(('group', 'gx')), parts along dimension 0, may hold values from 0.25 to 2
Outputs:
- mobility_sensitivity: float32 [128, 64, 256], P(('group', 'gx')), parts along dimension 0
- misfit: float32 [2], P('group'), parts along dimension 0
The draws below stay inside these ranges and needn't reach their ends.
There are 2 independent parts, one for each index of `group`. The reference program is written for one: setup_inputs(seed, part) draws one part's arguments, and reference() takes and returns one part's arrays. A program takes and returns all parts, laid end to end along the dimension named above; each array names one. Nothing has to cross between parts.
All inputs are finite; a program needn't handle non-finite values.
Results may differ from the reference program's by a relative error of at most 0.00002.
Values sent between devices are 32-bit elements; how exact they have to be, the bound alone decides.
No kernel may reach another device: no remote copies, remote signals or barrier semaphores. Data moves between devices by JAX's collectives and lax.ppermute only.
A program may use at most 64 MiB of HBM per device.

```python
import math
import jax
import jax.numpy as jnp

NY = 64
NZ = 256
RUNS = 2
NX = 64


def draw_observed(key, part):
    key = jax.random.fold_in(key, 7)
    place = jnp.arange(NX, dtype=jnp.float32).reshape(1, NX, 1, 1) / NX
    spread = 0.3 + 1.2 * place
    noise = jax.random.normal(key, (RUNS, NX, NY, NZ), jnp.float32)
    values = spread * noise
    return jnp.clip(values, -6.0, 6.0).astype(jnp.float32)


def levels(stream_key, dims, pieces, smallest, largest):
    factor_of = 1.0
    for axis_at, parts in pieces:
        heights = jax.random.uniform(jax.random.fold_in(jax.random.fold_in(stream_key, 6), axis_at), (parts,), jnp.float32, smallest / len(pieces), largest / len(pieces))
        factor_of = factor_of * jnp.repeat(jnp.exp(heights), dims[axis_at] // parts).reshape((-1,) + (1,) * (len(dims) - 1 - axis_at))
    return factor_of


def centred(rng, dims, deviation, limit, split=(), held_as=jnp.bfloat16):
    factor_of = levels(rng, dims, split, -0.22, 0.18) if split else 1.0
    entries = jax.random.normal(rng, dims, jnp.float32) * deviation * factor_of
    return jnp.minimum(jnp.maximum(entries, -limit), limit).astype(held_as)


def setup_inputs(seed: int = 0, part: int = 0) -> dict:
    arg_keys = jax.random.split(jax.random.key(seed), 4)
    part_splits = jax.random.split(jax.random.fold_in(arg_keys[3], part), 4)
    initial = centred(part_splits[0], (RUNS, NX, NY, NZ), 0.5, 1.25, ((1, 16),), jnp.float32)
    observed = draw_observed(jax.random.fold_in(jax.random.fold_in(arg_keys[3], part), 71), part)
    mobility = jnp.clip(jnp.exp(math.log(2.0) - 2.0794415 * jax.random.uniform(part_splits[2], (NX, NY, NZ), jnp.float32) ** levels(part_splits[2], (NX, NY, NZ), ((0, 16),), -0.2, 0.2)), 0.25, 2.0)
    return dict(initial=initial, observed=observed, mobility=mobility)


stiffness = 0.5
time_step = 0.005


def laplace(field):
    inner = field[:, 1:-1]
    beside_all = field[:, 2:] + field[:, :-2]
    beside_all = beside_all + jnp.roll(inner, 1, 2) + jnp.roll(inner, -1, 2)
    beside_all = beside_all + jnp.roll(inner, 1, 3) + jnp.roll(inner, -1, 3)
    return beside_all - 6.0 * inner


def potential(conc):
    inner = conc[:, 1:-1]
    return inner * inner * inner - inner - stiffness * laplace(conc)


def transport(mob, field):
    m_mid = mob[:, 1:-1]
    f_mid = field[:, 1:-1]
    total = (mob[:, 2:] + m_mid) * (field[:, 2:] - f_mid)
    total = total + (mob[:, :-2] + m_mid) * (field[:, :-2] - f_mid)
    for axis_num in (2, 3):
        for offset in (1, -1):
            total = total + (jnp.roll(m_mid, offset, axis_num) + m_mid) * (jnp.roll(f_mid, offset, axis_num) - f_mid)
    return 0.5 * total


def sensitivity(adjoint, chem):
    a_mid = adjoint[:, 1:-1]
    c_mid = chem[:, 1:-1]
    total = (adjoint[:, 2:] - a_mid) * (chem[:, 2:] - c_mid)
    total = total + (adjoint[:, :-2] - a_mid) * (chem[:, :-2] - c_mid)
    for axis_num in (2, 3):
        for offset in (1, -1):
            total = total + (jnp.roll(a_mid, offset, axis_num) - a_mid) * (jnp.roll(c_mid, offset, axis_num) - c_mid)
    return -0.5 * jnp.sum(total, axis=0)


def wrapped(field, width):
    return jnp.concatenate([field[:, -width:], field, field[:, :width]], axis=1)


def reference(initial, observed, mobility):
    mob = wrapped(mobility[None], 2)
    chem0 = potential(wrapped(initial, 2))
    state1 = initial + time_step * transport(mob[:, 1:-1], chem0)
    chem1 = potential(wrapped(state1, 2))
    state2 = state1 + time_step * transport(mob[:, 1:-1], chem1)
    miss = state2 - observed
    misfit = (0.5 / RUNS) * jnp.sum(miss * miss)
    adjoint2 = wrapped(miss / RUNS, 2)
    flow = transport(mob, adjoint2)
    adjoint1 = adjoint2[:, 2:-2] + time_step * ((3.0 * state1 * state1 - 1.0) * flow[:, 1:-1] - stiffness * laplace(flow))
    result = sensitivity(adjoint2[:, 1:-1], chem1) + sensitivity(wrapped(adjoint1, 1), chem0)
    return result, misfit.reshape(1)
```

```python
import functools

import jax
import jax.numpy as jnp
from jax import lax
from jax.experimental import pallas as pl
from jax.experimental.pallas import tpu as pltpu
from jax.sharding import PartitionSpec as P

stiffness = 0.5
time_step = 0.005
VMEM = pl.BlockSpec(memory_space=pltpu.VMEM)


def before(field, axis):
    return pltpu.roll(field, 1, axis)


def after(field, axis):
    return pltpu.roll(field, field.shape[axis] - 1, axis)


def in_plane(field):
    return before(field, 0) + after(field, 0) + (before(field, 1) + after(field, 1))


def planes(count, body):
    lax.fori_loop(0, count, lambda at, carry: (body(at), carry)[1], 0)


def copy_planes(pieces, target):
    start = 0
    for piece in pieces:
        target[start : start + piece.shape[0]] = piece[...]
        start += piece.shape[0]


def transport(mx, my, mz, m_at, field, at, want_steps=False):
    mid = field[at]
    step_y = after(mid, 0) - mid
    step_z = after(mid, 1) - mid
    flux_y = my[m_at] * step_y
    flux_z = mz[m_at] * step_z
    total = mx[m_at + 1] * (field[at + 1] - mid) - mx[m_at] * (mid - field[at - 1])
    total = total + (flux_y - before(flux_y, 0)) + (flux_z - before(flux_z, 1))
    return (total, step_y, step_z) if want_steps else total


def mobility_kernel(low, own, high, mx, my, mz, mob):
    copy_planes((low, own, high), mob)

    def faces(at):
        mx[at] = 0.5 * (mob[at] + mob[at + 1])

    planes(mx.shape[0], faces)

    def sides(at):
        mid = mob[at + 1]
        my[at] = 0.5 * (mid + after(mid, 0))
        mz[at] = 0.5 * (mid + after(mid, 1))

    planes(my.shape[0], sides)


def forward_kernel(
    runs, low, own, high, observed, mx, my, mz, miss_in, sum_y_in, sum_z_in,
    adjoint2, first, last, state1, chem0, chem1, step_y0, step_z0, miss_sum, sum_y, sum_z,
    conc, wide0, wide1,
):
    n = own.shape[0]
    copy_planes((low, own, high), conc)

    def potential(field, at):
        mid = field[at]
        beside = field[at - 1] + field[at + 1] + in_plane(mid)
        return mid * (mid * mid + (6.0 * stiffness - 1.0)) - stiffness * beside

    def potential0(at):
        wide0[at] = potential(conc, at + 1)

    planes(n + 6, potential0)

    def step0(at):
        wide1[at] = conc[at + 2] + time_step * transport(mx, my, mz, at, wide0, at + 1)

    planes(n + 4, step0)

    def potential1(at):
        state1[at] = wide1[at + 1]
        chem0[at] = wide0[at + 2]
        chem1[at] = potential(wide1, at + 1)

    planes(n + 2, potential1)
    miss_sum[...] = miss_in[...]

    def step1(at):
        flow, step_y1, step_z1 = transport(mx, my, mz, at + 2, chem1, at + 1, True)
        miss = state1[at + 1] + time_step * flow - observed[at]
        squares = miss * miss
        rows, columns = miss_sum.shape
        part = jnp.zeros((rows, columns), jnp.float32)
        for row in range(0, squares.shape[0], rows):
            for column in range(0, squares.shape[1], columns):
                part = part + squares[row : row + rows, column : column + columns]
        miss_sum[...] += part
        adj = miss * (1.0 / runs)
        adjoint2[at] = adj
        sum_y[at] = sum_y_in[at] + (after(adj, 0) - adj) * step_y1
        sum_z[at] = sum_z_in[at] + (after(adj, 1) - adj) * step_z1
        mid = chem0[at + 1]
        step_y0[at] = after(mid, 0) - mid
        step_z0[at] = after(mid, 1) - mid

    planes(n, step1)
    first[...] = adjoint2[: first.shape[0]]
    last[...] = adjoint2[n - last.shape[0] :]


def backward_kernel(
    final, low, own, high, mx, my, mz, state1, chem0, chem1, step_y0, step_z0, sum_y_in, sum_z_in,
    *rest,
):
    if final:
        sum_x_in, result, adj2, flow, adj1, sum_y, sum_z, sum_x = rest
    else:
        sum_x_in, sum_y, sum_z, sum_x, adj2, flow, adj1 = rest
    n = own.shape[0]
    copy_planes((low, own, high), adj2)

    def flows(at):
        flow[at] = transport(mx, my, mz, at, adj2, at + 1)

    planes(n + 4, flows)

    def adjoint(at):
        mid = flow[at + 1]
        beside = flow[at] + flow[at + 2] + in_plane(mid)
        conc = state1[at]
        slope = 3.0 * conc * conc + (6.0 * stiffness - 1.0)
        adj1[at] = adj2[at + 2] + time_step * (slope * mid - stiffness * beside)

    planes(n + 2, adjoint)

    def products(at):
        mid = adj1[at + 1]
        total_y = sum_y_in[at] + (after(mid, 0) - mid) * step_y0[at]
        total_z = sum_z_in[at] + (after(mid, 1) - mid) * step_z0[at]
        total_x = sum_x_in[at]
        for side in (0, 2):
            total_x = total_x + (adj1[at + side] - mid) * (chem0[at + side] - chem0[at + 1])
            total_x = total_x + (adj2[at + 2 + side] - adj2[at + 3]) * (
                chem1[at + side] - chem1[at + 1]
            )
        if final:
            total = total_x + (total_y + before(total_y, 0)) + (total_z + before(total_z, 1))
            result[at] = -0.5 * total
        else:
            sum_y[at] = total_y
            sum_z[at] = total_z
            sum_x[at] = total_x

    planes(n, products)


def call(kernel, outs, scratch, args, flops):
    moved = sum(a.size * 4 for a in args) + sum(4 * functools.reduce(lambda a, b: a * b, o) for o in outs)
    return pl.pallas_call(
        kernel,
        out_shape=tuple(jax.ShapeDtypeStruct(o, jnp.float32) for o in outs),
        in_specs=[VMEM] * len(args),
        out_specs=tuple([VMEM] * len(outs)),
        scratch_shapes=[pltpu.VMEM(s, jnp.float32) for s in scratch],
        compiler_params=pltpu.CompilerParams(vmem_limit_bytes=24 * 1024 * 1024),
        cost_estimate=pl.CostEstimate(flops=flops, bytes_accessed=moved, transcendentals=0),
    )(*args)


def sum_over(value, axis):
    count = lax.axis_size(axis)
    if count & (count - 1):
        return lax.psum(value, axis)
    hop = 1
    while hop < count:
        value = value + lax.ppermute(value, axis, [(i, i ^ hop) for i in range(count)])
        hop *= 2
    return value


def on_device(initial, observed, mobility):
    runs, n, ny, nz = initial.shape
    count = lax.axis_size("gx")
    forward = [(i, (i + 1) % count) for i in range(count)]
    backward = [(i, (i - 1) % count) for i in range(count)]

    def beside(first, last):
        return lax.ppermute(last, "gx", forward), lax.ppermute(first, "gx", backward)

    def size(count):
        return (count, ny, nz)

    cell = ny * nz
    low, high = beside(mobility[:3], mobility[n - 3 :])
    initial_sides = [beside(initial[r, :4], initial[r, n - 4 :]) for r in range(runs)]
    mx, my, mz = call(
        mobility_kernel,
        (size(n + 5), size(n + 4), size(n + 4)),
        (size(n + 6),),
        (low, mobility, high),
        30 * (n + 4) * cell,
    )
    sum_y = sum_z = sum_x = jnp.zeros(size(n), jnp.float32)
    miss_sum = jnp.zeros((8, 128), jnp.float32)
    kept = []
    for r in range(runs):
        low, high = initial_sides[r]
        (adj, first, last, state1, chem0, chem1, step_y0, step_z0, miss_sum, sum_y, sum_z) = call(
            functools.partial(forward_kernel, runs),
            (size(n), size(3), size(3), size(n + 2), size(n + 2), size(n + 2), size(n), size(n), (8, 128), size(n), size(n)),
            (size(n + 8), size(n + 6), size(n + 4)),
            (low, initial[r], high, observed[r], mx, my, mz, miss_sum, sum_y, sum_z),
            200 * (n + 4) * cell,
        )
        kept.append((adj, beside(first, last), state1, chem0, chem1, step_y0, step_z0))
    misfit = sum_over(0.5 / runs * jnp.sum(miss_sum), "gx")
    for r in range(runs):
        adj, (low, high), state1, chem0, chem1, step_y0, step_z0 = kept[r]
        args = (low, adj, high, mx, my, mz, state1, chem0, chem1, step_y0, step_z0, sum_y, sum_z, sum_x)
        scratch = (size(n + 6), size(n + 4), size(n + 2))
        final = r == runs - 1
        outs = (size(n),) if final else (size(n),) * 3
        if final:
            scratch = scratch + (size(n),) * 3
        out = call(functools.partial(backward_kernel, final), outs, scratch, args, 150 * (n + 4) * cell)
        if final:
            (result,) = out
        else:
            sum_y, sum_z, sum_x = out
    return (result, jnp.reshape(misfit, (1,)))


def solution(mesh):
    placed = (
        P("group", "gx", None, None),
        P("group", "gx", None, None),
        P(("group", "gx"), None, None),
    )
    return jax.shard_map(
        on_device,
        mesh=mesh,
        in_specs=placed,
        out_specs=(P(("group", "gx"), None, None), P("group")),
        check_vma=False,
    )
```

```python
import functools
import math

import jax
import jax.numpy as jnp
from jax import lax
from jax.experimental import pallas as pl
from jax.experimental.pallas import tpu as pltpu
from jax.sharding import PartitionSpec as P

stiffness = 0.5
time_step = 0.005
VMEM = pl.BlockSpec(memory_space=pltpu.VMEM)
LANES = 128
PAD = 8
CHUNK = 16


def chunks(ny):
    return range(0, ny, CHUNK)


def plain(ref, lead, row):
    return [
        ref[(*lead, pl.ds(row, CHUNK), pl.ds(at, LANES))] for at in range(0, ref.shape[-1], LANES)
    ]


def put_plain(ref, lead, row, value):
    for block, part in enumerate(value):
        ref[(*lead, pl.ds(row, CHUNK), pl.ds(block * LANES, LANES))] = part


def flat(ref, lead, row):
    return [ref[(*lead, block, pl.ds(row, CHUNK))] for block in range(ref.shape[-3])]


def put_flat(ref, lead, row, value):
    for block, part in enumerate(value):
        ref[(*lead, block, pl.ds(row, CHUNK))] = part


def padded(ref, lead, row, shift=0):
    return [ref[(*lead, block, pl.ds(PAD + row + shift, CHUNK))] for block in range(ref.shape[-3])]


def put_padded(ref, lead, row, value):
    ny = ref.shape[-2] - 2 * PAD
    for block, part in enumerate(value):
        ref[(*lead, block, pl.ds(PAD + row, CHUNK))] = part
        if row == 0:
            ref[(*lead, block, pl.ds(PAD + ny, 1))] = part[:1]
        if row + CHUNK == ny:
            ref[(*lead, block, pl.ds(PAD - 1, 1))] = part[CHUNK - 1 :]


def lane():
    return lax.broadcasted_iota(jnp.int32, (CHUNK, LANES), 1)


def after_z(value):
    turned = [pltpu.roll(part, LANES - 1, 1) for part in value]
    turned.append(turned[0])
    edge = lane() == LANES - 1
    return [jnp.where(edge, turned[at + 1], turned[at]) for at in range(len(value))]


def before_z(value):
    turned = [pltpu.roll(part, 1, 1) for part in value]
    edge = lane() == 0
    return [jnp.where(edge, turned[at - 1], turned[at]) for at in range(len(value))]


def each(function, *values):
    return [function(*parts) for parts in zip(*values)]


def beside(low, high, up, down, mid):
    return each(
        lambda a, b, c, d, e, f: (a + b) + (c + d) + (e + f),
        low, high, up, down, after_z(mid), before_z(mid),
    )


def potential(low, mid, high, up, down):
    return each(
        lambda c, total: c * (c * c + (6.0 * stiffness - 1.0)) - stiffness * total,
        mid, beside(low, high, up, down, mid),
    )


def flow_in_plane(faces, row, at, mid, up, down):
    _, my, mz, mz_low, m_all = faces
    return each(
        lambda a, b, c, d, e, u, v, w, x, y: (a * u + b * v) + (c * w + d * x) - e * y,
        padded(my, (at,), row), padded(my, (at,), row, -1), flat(mz, (at,), row),
        flat(mz_low, (at,), row), flat(m_all, (at,), row), up, down, after_z(mid), before_z(mid), mid,
    )


def add_product(total, a, b):
    return each(lambda t, x, y: t + x * y, total, a, b)


def sub(a, b):
    return each(lambda x, y: x - y, a, b)


def chem_kernel(low, own, high, chem0, conc):
    runs, n, ny, _ = own.shape

    def source(at):
        if at < 0:
            return low, at + low.shape[1]
        return (own, at) if at < n else (high, at - n)

    def one_run(run, carry):
        for row in chunks(ny):
            for at in range(-4, n + 4):
                ref, place = source(at)
                put_padded(conc, (at + 4,), row, plain(ref, (run, place), row))
        for row in chunks(ny):
            mids = [padded(conc, (at,), row) for at in range(n + 8)]
            for at in range(1, n + 7):
                value = potential(
                    mids[at - 1], mids[at], mids[at + 1],
                    padded(conc, (at,), row, 1), padded(conc, (at,), row, -1),
                )
                put_padded(chem0, (run, at - 1), row, value)
        return carry

    lax.fori_loop(0, runs, one_run, 0)


def forward_kernel(
    m_low, m_own, m_high, low, own, high, observed, chem0,
    mx, my, mz, mz_low, m_all, state1, chem1, adjoint2, first, last, miss_sum,
    mob, total,
):
    runs, n, ny, _ = own.shape
    pieces = [(m_low, at) for at in range(3)] + [(m_own, at) for at in range(n)] + [(m_high, at) for at in range(3)]
    for row in chunks(ny):
        for at, (ref, place) in enumerate(pieces):
            put_padded(mob, (at,), row, plain(ref, (place,), row))
    mean = lambda a, b: 0.5 * (a + b)
    for row in chunks(ny):
        face = None
        for at in range(n + 5):
            mid = padded(mob, (at,), row)
            face_low, face = face, each(mean, mid, padded(mob, (at + 1,), row))
            put_flat(mx, (at,), row, face)
            if at == 0:
                continue
            side_y = each(mean, mid, padded(mob, (at,), row, 1))
            side_y_low = each(mean, mid, padded(mob, (at,), row, -1))
            side_z = each(mean, mid, after_z(mid))
            side_z_low = each(mean, mid, before_z(mid))
            put_padded(my, (at - 1,), row, side_y)
            put_flat(mz, (at - 1,), row, side_z)
            put_flat(mz_low, (at - 1,), row, side_z_low)
            put_flat(m_all, (at - 1,), row, each(
                lambda a, b, c, d, e, f: (a + b) + (c + d) + (e + f),
                face, face_low, side_y, side_y_low, side_z, side_z_low,
            ))
    faces = (mx, my, mz, mz_low, m_all)
    total[...] = jnp.zeros_like(total)

    def source(at):
        if at < 0:
            return low, at + low.shape[1]
        return (own, at) if at < n else (high, at - n)

    def one_run(run, carry):
        for row in chunks(ny):
            mids = [padded(chem0, (run, at), row) for at in range(n + 6)]
            for at in range(n + 4):
                flow = flow_in_plane(
                    faces, row, at, mids[at + 1],
                    padded(chem0, (run, at + 1), row, 1), padded(chem0, (run, at + 1), row, -1),
                )
                flow = add_product(flow, flat(mx, (at,), row), mids[at])
                flow = add_product(flow, flat(mx, (at + 1,), row), mids[at + 2])
                ref, place = source(at - 2)
                value = each(lambda a, b: a + time_step * b, plain(ref, (run, place), row), flow)
                put_padded(state1, (run, at), row, value)
        for row in chunks(ny):
            mids = [padded(state1, (run, at), row) for at in range(n + 4)]
            for at in range(1, n + 3):
                value = potential(
                    mids[at - 1], mids[at], mids[at + 1],
                    padded(state1, (run, at), row, 1), padded(state1, (run, at), row, -1),
                )
                put_padded(chem1, (run, at - 1), row, value)
        squares = None
        for row in chunks(ny):
            mids = [padded(chem1, (run, at), row) for at in range(n + 2)]
            for at in range(n):
                flow = flow_in_plane(
                    faces, row, at + 2, mids[at + 1],
                    padded(chem1, (run, at + 1), row, 1), padded(chem1, (run, at + 1), row, -1),
                )
                flow = add_product(flow, flat(mx, (at + 2,), row), mids[at])
                flow = add_product(flow, flat(mx, (at + 3,), row), mids[at + 2])
                miss = each(
                    lambda a, b, c: a + time_step * b - c,
                    padded(state1, (run, at + 2), row), flow, plain(observed, (run, at), row),
                )
                for part in miss:
                    square = part * part
                    squares = square if squares is None else squares + square
                value = each(lambda a: a * (1.0 / runs), miss)
                put_padded(adjoint2, (run, at), row, value)
                if at < 3:
                    put_plain(first, (run, at), row, value)
                if at >= n - 3:
                    put_plain(last, (run, at - (n - 3)), row, value)
        total[...] += squares
        return carry

    lax.fori_loop(0, runs, one_run, 0)
    miss_sum[...] = (0.5 / runs) * jnp.sum(total[...], axis=0, keepdims=True)


def middle_kernel(
    mx, my, mz, mz_low, m_all, state1, chem0, chem1, adjoint2,
    flow_own, weight, step_z0, sum_x, sum_y, sum_z,
):
    runs, n = adjoint2.shape[:2]
    ny = flow_own.shape[-2] - 2 * PAD
    faces = (mx, my, mz, mz_low, m_all)
    sum_x[...] = jnp.zeros_like(sum_x)
    sum_y[...] = jnp.zeros_like(sum_y)
    sum_z[...] = jnp.zeros_like(sum_z)

    def one_run(run, carry):
        for row in chunks(ny):
            mids = [padded(adjoint2, (run, at), row) for at in range(n)]
            chems = [padded(chem1, (run, at + 1), row) for at in range(n)]
            for at in range(n):
                up = padded(adjoint2, (run, at), row, 1)
                flow = flow_in_plane(faces, row, at + 2, mids[at], up, padded(adjoint2, (run, at), row, -1))
                if at > 0:
                    flow = add_product(flow, flat(mx, (at + 2,), row), mids[at - 1])
                if at < n - 1:
                    flow = add_product(flow, flat(mx, (at + 3,), row), mids[at + 1])
                    face = add_product(
                        flat(sum_x, (at + 1,), row), sub(mids[at + 1], mids[at]), sub(chems[at + 1], chems[at])
                    )
                    put_flat(sum_x, (at + 1,), row, face)
                put_padded(flow_own, (run, at), row, flow)
                put_flat(sum_y, (at,), row, add_product(
                    flat(sum_y, (at,), row), sub(up, mids[at]),
                    sub(padded(chem1, (run, at + 1), row, 1), chems[at]),
                ))
                put_flat(sum_z, (at,), row, add_product(
                    flat(sum_z, (at,), row), sub(after_z(mids[at]), mids[at]),
                    sub(after_z(chems[at]), chems[at]),
                ))
                mid = padded(chem0, (run, at + 3), row)
                put_flat(step_z0, (run, at), row, sub(after_z(mid), mid))
            for at in range(n + 2):
                value = each(
                    lambda c: time_step * (3.0 * c * c + (6.0 * stiffness - 1.0)),
                    padded(state1, (run, at + 1), row),
                )
                put_flat(weight, (run, at), row, value)
        return carry

    lax.fori_loop(0, runs, one_run, 0)


def backward_kernel(
    low, high, mx, my, mz, mz_low, m_all, chem0, chem1, adjoint2, flow_own, weight, step_z0,
    sum_x_in, sum_y_in, sum_z_in, result, wide, flow_rim, adjoint1, sum_x, sum_y, sum_z,
):
    runs, n = adjoint2.shape[:2]
    ny = flow_own.shape[-2] - 2 * PAD
    faces = (mx, my, mz, mz_low, m_all)
    sum_x[...] = sum_x_in[...]
    sum_z[...] = sum_z_in[...]
    for row in chunks(ny):
        for at in range(n):
            put_padded(sum_y, (at,), row, flat(sum_y_in, (at,), row))

    def adj2(run, at):
        if at < 0:
            return wide, (at + 3,)
        return (adjoint2, (run, at)) if at < n else (wide, (at - n + 3,))

    def flow(run, at):
        if at <= 0:
            return flow_rim, (at + 2,)
        return (flow_own, (run, at)) if at < n - 1 else (flow_rim, (at - (n - 1) + 3,))

    def one_run(run, carry):
        for row in chunks(ny):
            for at in range(3):
                put_padded(wide, (at,), row, plain(low, (run, at), row))
                put_padded(wide, (at + 3,), row, plain(high, (run, at), row))
        for row in chunks(ny):
            mids = {at: padded(*adj2(run, at), row) for at in range(-3, n + 3)}
            for at in (-2, -1, n, n + 1):
                ref, lead = adj2(run, at)
                value = flow_in_plane(
                    faces, row, at + 2, mids[at], padded(ref, lead, row, 1), padded(ref, lead, row, -1)
                )
                value = add_product(value, flat(mx, (at + 2,), row), mids[at - 1])
                value = add_product(value, flat(mx, (at + 3,), row), mids[at + 1])
                put_padded(*flow(run, at), row, value)
            for at, side, face in ((0, -1, 2), (n - 1, n, n + 2)):
                value = add_product(
                    padded(flow_own, (run, at), row), flat(mx, (face,), row), mids[side]
                )
                put_padded(*flow(run, at), row, value)
        for row in chunks(ny):
            mids = {at: padded(*flow(run, at), row) for at in range(-2, n + 2)}
            for at in range(-1, n + 1):
                ref, lead = flow(run, at)
                total = beside(
                    mids[at - 1], mids[at + 1], padded(ref, lead, row, 1), padded(ref, lead, row, -1), mids[at]
                )
                value = each(
                    lambda a, w, f, t: a + w * f - (time_step * stiffness) * t,
                    padded(*adj2(run, at), row), flat(weight, (run, at + 1), row), mids[at], total,
                )
                put_padded(adjoint1, (at + 1,), row, value)
        for row in chunks(ny):
            mids = [padded(adjoint1, (at,), row) for at in range(n + 2)]
            chems = [padded(chem0, (run, at + 2), row) for at in range(n + 2)]
            for at in range(n + 1):
                face = add_product(
                    flat(sum_x, (at,), row), sub(mids[at + 1], mids[at]), sub(chems[at + 1], chems[at])
                )
                if at in (0, n):
                    face = add_product(
                        face, sub(padded(*adj2(run, at), row), padded(*adj2(run, at - 1), row)),
                        sub(padded(chem1, (run, at + 1), row), padded(chem1, (run, at), row)),
                    )
                put_flat(sum_x, (at,), row, face)
            for at in range(n):
                mid = mids[at + 1]
                put_padded(sum_y, (at,), row, add_product(
                    padded(sum_y, (at,), row), sub(padded(adjoint1, (at + 1,), row, 1), mid),
                    sub(padded(chem0, (run, at + 3), row, 1), chems[at + 1]),
                ))
                put_flat(sum_z, (at,), row, add_product(
                    flat(sum_z, (at,), row), sub(after_z(mid), mid), flat(step_z0, (run, at), row)
                ))
        return carry

    lax.fori_loop(0, runs, one_run, 0)
    for row in chunks(ny):
        for at in range(n):
            sides = flat(sum_z, (at,), row)
            value = each(
                lambda a, b, c, d, e, f: -0.5 * ((a + b) + (c + d) + (e + f)),
                flat(sum_x, (at,), row), flat(sum_x, (at + 1,), row),
                padded(sum_y, (at,), row), padded(sum_y, (at,), row, -1), sides, before_z(sides),
            )
            put_plain(result, (at,), row, value)


def misfit_kernel(parts, misfit):
    misfit[0] = jnp.sum(parts[...])


def call(kernel, outs, scratch, args, flops, out_space=None):
    moved = 4 * (sum(a.size for a in args) + sum(math.prod(o) for o in outs))
    return pl.pallas_call(
        kernel,
        out_shape=tuple(jax.ShapeDtypeStruct(o, jnp.float32) for o in outs),
        in_specs=[VMEM] * len(args),
        out_specs=tuple([out_space or VMEM] * len(outs)),
        scratch_shapes=[pltpu.VMEM(s, jnp.float32) for s in scratch],
        compiler_params=pltpu.CompilerParams(vmem_limit_bytes=16 * 1024 * 1024),
        cost_estimate=pl.CostEstimate(flops=flops, bytes_accessed=moved, transcendentals=0),
    )(*args)


def on_device(initial, observed, mobility):
    runs, n, ny, nz = initial.shape
    blocks = nz // LANES
    count = lax.axis_size("gx")
    forward = [(i, (i + 1) % count) for i in range(count)]
    backward = [(i, (i - 1) % count) for i in range(count)]
    cell = ny * nz

    def neighbours(first, last):
        return lax.ppermute(last, "gx", forward), lax.ppermute(first, "gx", backward)

    def lies(*lead):
        return (*lead, blocks, ny, LANES)

    def lies_padded(*lead):
        return (*lead, blocks, ny + 2 * PAD, LANES)

    low, high = neighbours(initial[:, :4], initial[:, n - 4 :])
    m_low, m_high = neighbours(mobility[:3], mobility[n - 3 :])
    (chem0,) = call(
        chem_kernel, (lies_padded(runs, n + 6),), (lies_padded(n + 8),), (low, initial, high),
        20 * runs * (n + 6) * cell,
    )
    *faces, state1, chem1, adjoint2, first, last, miss_sum = call(
        forward_kernel,
        (
            lies(n + 5), lies_padded(n + 4), lies(n + 4), lies(n + 4), lies(n + 4),
            lies_padded(runs, n + 4), lies_padded(runs, n + 2), lies_padded(runs, n),
            (runs, 3, ny, nz), (runs, 3, ny, nz), (1, LANES),
        ),
        (lies_padded(n + 6), (CHUNK, LANES)),
        (m_low, mobility, m_high, low, initial, high, observed, chem0),
        60 * runs * (n + 4) * cell,
    )
    low, high = neighbours(first, last)
    parts = lax.all_gather(miss_sum, "gx")
    flow_own, weight, step_z0, sum_x, sum_y, sum_z = call(
        middle_kernel,
        (
            lies_padded(runs, n), lies(runs, n + 2), lies(runs, n),
            lies(n + 1), lies(n), lies(n),
        ),
        (),
        (*faces, state1, chem0, chem1, adjoint2),
        40 * runs * n * cell,
    )
    (result,) = call(
        backward_kernel,
        ((n, ny, nz),),
        (
            lies_padded(6), lies_padded(6), lies_padded(n + 2),
            lies(n + 1), lies_padded(n), lies(n),
        ),
        (low, high, *faces, chem0, chem1, adjoint2, flow_own, weight, step_z0, sum_x, sum_y, sum_z),
        40 * runs * (n + 2) * cell,
    )
    (misfit,) = call(
        misfit_kernel, ((1,),), (), (parts,), parts.size, pl.BlockSpec(memory_space=pltpu.SMEM)
    )
    return (result, misfit)


def solution(mesh):
    placed = (
        P("group", "gx", None, None),
        P("group", "gx", None, None),
        P(("group", "gx"), None, None),
    )
    return jax.shard_map(
        on_device,
        mesh=mesh,
        in_specs=placed,
        out_specs=(P(("group", "gx"), None, None), P("group")),
        check_vma=False,
    )
```

```python
import functools
import math

import jax
import jax.numpy as jnp
from jax import lax
from jax.experimental import pallas as pl
from jax.experimental.pallas import tpu as pltpu
from jax.sharding import PartitionSpec as P

stiffness = 0.5
time_step = 0.005
VMEM = pl.BlockSpec(memory_space=pltpu.VMEM)
SMEM = pl.BlockSpec(memory_space=pltpu.SMEM)
LANES = 128
PAD = 8
CHUNK = 16


def chunks(ny):
    return range(0, ny, CHUNK)


def plain(ref, lead, row):
    return [
        ref[(*lead, pl.ds(row, CHUNK), pl.ds(at, LANES))] for at in range(0, ref.shape[-1], LANES)
    ]


def put_plain(ref, lead, row, value):
    for block, part in enumerate(value):
        ref[(*lead, pl.ds(row, CHUNK), pl.ds(block * LANES, LANES))] = part


def flat(ref, lead, row):
    return [ref[(*lead, block, pl.ds(row, CHUNK))] for block in range(ref.shape[-3])]


def put_flat(ref, lead, row, value):
    for block, part in enumerate(value):
        ref[(*lead, block, pl.ds(row, CHUNK))] = part


def padded(ref, lead, row, shift=0):
    return [ref[(*lead, block, pl.ds(PAD + row + shift, CHUNK))] for block in range(ref.shape[-3])]


def put_padded(ref, lead, row, value):
    ny = ref.shape[-2] - 2 * PAD
    for block, part in enumerate(value):
        ref[(*lead, block, pl.ds(PAD + row, CHUNK))] = part
        if row == 0:
            ref[(*lead, block, pl.ds(PAD + ny, 1))] = part[:1]
        if row + CHUNK == ny:
            ref[(*lead, block, pl.ds(PAD - 1, 1))] = part[CHUNK - 1 :]


def lane():
    return lax.broadcasted_iota(jnp.int32, (CHUNK, LANES), 1)


def after_z(value):
    turned = [pltpu.roll(part, LANES - 1, 1) for part in value]
    turned.append(turned[0])
    edge = lane() == LANES - 1
    return [jnp.where(edge, turned[at + 1], turned[at]) for at in range(len(value))]


def before_z(value):
    turned = [pltpu.roll(part, 1, 1) for part in value]
    edge = lane() == 0
    return [jnp.where(edge, turned[at - 1], turned[at]) for at in range(len(value))]


def each(function, *values):
    return [function(*parts) for parts in zip(*values)]


def beside(low, high, up, down, mid):
    return each(
        lambda a, b, c, d, e, f: (a + b) + (c + d) + (e + f),
        low, high, up, down, after_z(mid), before_z(mid),
    )


def potential(low, mid, high, up, down):
    return each(
        lambda c, total: c * (c * c + (6.0 * stiffness - 1.0)) - stiffness * total,
        mid, beside(low, high, up, down, mid),
    )


def flow_in_plane(faces, row, at, mid, up, down):
    _, my, mz, mz_low, m_all = faces
    return each(
        lambda a, b, c, d, e, u, v, w, x, y: (a * u + b * v) + (c * w + d * x) - e * y,
        padded(my, (at,), row), padded(my, (at,), row, -1), flat(mz, (at,), row),
        flat(mz_low, (at,), row), flat(m_all, (at,), row), up, down, after_z(mid), before_z(mid), mid,
    )


def add_product(total, a, b):
    return each(lambda t, x, y: t + x * y, total, a, b)


def sub(a, b):
    return each(lambda x, y: x - y, a, b)


def own_kernel(initial, mobility, conc, mob, first, last):
    runs, n, ny, _ = initial.shape

    def one_run(run, carry):
        for row in chunks(ny):
            for at in range(n):
                put_padded(conc, (run, at), row, plain(initial, (run, at), row))
        return carry

    lax.fori_loop(0, runs, one_run, 0)
    for row in chunks(ny):
        for at in range(n):
            put_padded(mob, (at,), row, plain(mobility, (at,), row))
    first[...] = mobility[:3]
    last[...] = mobility[n - 3 :]


def chem_kernel(low, own, high, chem0, rim):
    runs, n = own.shape[:2]
    ny = low.shape[2]

    def conc(run, at):
        if at < 0:
            return rim, (at + 4,)
        return (own, (run, at)) if at < n else (rim, (at - n + 4,))

    def one_run(run, carry):
        for row in chunks(ny):
            for at in range(4):
                put_padded(rim, (at,), row, plain(low, (run, at), row))
                put_padded(rim, (at + 4,), row, plain(high, (run, at), row))
        for row in chunks(ny):
            mids = {at: padded(*conc(run, at), row) for at in range(-4, n + 4)}
            for at in range(-3, n + 3):
                ref, lead = conc(run, at)
                value = potential(
                    mids[at - 1], mids[at], mids[at + 1], padded(ref, lead, row, 1), padded(ref, lead, row, -1)
                )
                put_padded(chem0, (run, at + 3), row, value)
        return carry

    lax.fori_loop(0, runs, one_run, 0)


def forward_kernel(
    m_low, m_own, m_high, low, own, high, observed, chem0,
    mx, my, mz, mz_low, m_all, state1, chem1, adjoint2, first, last, miss_sum,
    rim, total,
):
    runs, n, ny, _ = observed.shape
    for row in chunks(ny):
        for at in range(3):
            put_padded(rim, (at,), row, plain(m_low, (at,), row))
            put_padded(rim, (at + 3,), row, plain(m_high, (at,), row))

    def mob(at):
        if at < 3:
            return rim, (at,)
        return (m_own, (at - 3,)) if at < n + 3 else (rim, (at - n,))

    mean = lambda a, b: 0.5 * (a + b)
    for row in chunks(ny):
        face = None
        for at in range(n + 5):
            mid = padded(*mob(at), row)
            face_low, face = face, each(mean, mid, padded(*mob(at + 1), row))
            put_flat(mx, (at,), row, face)
            if at == 0:
                continue
            side_y = each(mean, mid, padded(*mob(at), row, 1))
            side_y_low = each(mean, mid, padded(*mob(at), row, -1))
            side_z = each(mean, mid, after_z(mid))
            side_z_low = each(mean, mid, before_z(mid))
            put_padded(my, (at - 1,), row, side_y)
            put_flat(mz, (at - 1,), row, side_z)
            put_flat(mz_low, (at - 1,), row, side_z_low)
            put_flat(m_all, (at - 1,), row, each(
                lambda a, b, c, d, e, f: (a + b) + (c + d) + (e + f),
                face, face_low, side_y, side_y_low, side_z, side_z_low,
            ))
    faces = (mx, my, mz, mz_low, m_all)
    total[...] = jnp.zeros_like(total)

    def conc(run, at, row):
        if 0 <= at < n:
            return padded(own, (run, at), row)
        return plain(low, (run, at + 4), row) if at < 0 else plain(high, (run, at - n), row)

    def one_run(run, carry):
        for row in chunks(ny):
            mids = [padded(chem0, (run, at), row) for at in range(n + 6)]
            for at in range(n + 4):
                flow = flow_in_plane(
                    faces, row, at, mids[at + 1],
                    padded(chem0, (run, at + 1), row, 1), padded(chem0, (run, at + 1), row, -1),
                )
                flow = add_product(flow, flat(mx, (at,), row), mids[at])
                flow = add_product(flow, flat(mx, (at + 1,), row), mids[at + 2])
                value = each(lambda a, b: a + time_step * b, conc(run, at - 2, row), flow)
                put_padded(state1, (run, at), row, value)
        for row in chunks(ny):
            mids = [padded(state1, (run, at), row) for at in range(n + 4)]
            for at in range(1, n + 3):
                value = potential(
                    mids[at - 1], mids[at], mids[at + 1],
                    padded(state1, (run, at), row, 1), padded(state1, (run, at), row, -1),
                )
                put_padded(chem1, (run, at - 1), row, value)
        squares = None
        for row in chunks(ny):
            mids = [padded(chem1, (run, at), row) for at in range(n + 2)]
            for at in range(n):
                flow = flow_in_plane(
                    faces, row, at + 2, mids[at + 1],
                    padded(chem1, (run, at + 1), row, 1), padded(chem1, (run, at + 1), row, -1),
                )
                flow = add_product(flow, flat(mx, (at + 2,), row), mids[at])
                flow = add_product(flow, flat(mx, (at + 3,), row), mids[at + 2])
                miss = each(
                    lambda a, b, c: a + time_step * b - c,
                    padded(state1, (run, at + 2), row), flow, plain(observed, (run, at), row),
                )
                for part in miss:
                    square = part * part
                    squares = square if squares is None else squares + square
                value = each(lambda a: a * (1.0 / runs), miss)
                put_padded(adjoint2, (run, at), row, value)
                if at < 3:
                    put_plain(first, (run, at), row, value)
                if at >= n - 3:
                    put_plain(last, (run, at - (n - 3)), row, value)
        total[...] += squares
        return carry

    lax.fori_loop(0, runs, one_run, 0)
    miss_sum[...] = (0.5 / runs) * jnp.sum(total[...], axis=0, keepdims=True)


def middle_kernel(
    mx, my, mz, mz_low, m_all, state1, chem0, chem1, adjoint2, miss_sum,
    shares, flow_own, weight, step_z0, sum_x, sum_y, sum_z,
):
    runs, n = adjoint2.shape[:2]
    ny = flow_own.shape[-2] - 2 * PAD
    faces = (mx, my, mz, mz_low, m_all)
    shares[...] = jnp.broadcast_to(miss_sum[...][None], shares.shape)
    sum_x[...] = jnp.zeros_like(sum_x)
    sum_y[...] = jnp.zeros_like(sum_y)
    sum_z[...] = jnp.zeros_like(sum_z)

    def one_run(run, carry):
        for row in chunks(ny):
            mids = [padded(adjoint2, (run, at), row) for at in range(n)]
            chems = [padded(chem1, (run, at + 1), row) for at in range(n)]
            for at in range(n):
                up = padded(adjoint2, (run, at), row, 1)
                flow = flow_in_plane(faces, row, at + 2, mids[at], up, padded(adjoint2, (run, at), row, -1))
                if at > 0:
                    flow = add_product(flow, flat(mx, (at + 2,), row), mids[at - 1])
                if at < n - 1:
                    flow = add_product(flow, flat(mx, (at + 3,), row), mids[at + 1])
                    face = add_product(
                        flat(sum_x, (at + 1,), row), sub(mids[at + 1], mids[at]), sub(chems[at + 1], chems[at])
                    )
                    put_flat(sum_x, (at + 1,), row, face)
                put_padded(flow_own, (run, at), row, flow)
                put_flat(sum_y, (at,), row, add_product(
                    flat(sum_y, (at,), row), sub(up, mids[at]),
                    sub(padded(chem1, (run, at + 1), row, 1), chems[at]),
                ))
                put_flat(sum_z, (at,), row, add_product(
                    flat(sum_z, (at,), row), sub(after_z(mids[at]), mids[at]),
                    sub(after_z(chems[at]), chems[at]),
                ))
                mid = padded(chem0, (run, at + 3), row)
                put_flat(step_z0, (run, at), row, sub(after_z(mid), mid))
            for at in range(n + 2):
                value = each(
                    lambda c: time_step * (3.0 * c * c + (6.0 * stiffness - 1.0)),
                    padded(state1, (run, at + 1), row),
                )
                put_flat(weight, (run, at), row, value)
        return carry

    lax.fori_loop(0, runs, one_run, 0)


def backward_kernel(
    low, high, mx, my, mz, mz_low, m_all, chem0, chem1, adjoint2, flow_own, weight, step_z0,
    sum_x_in, sum_y_in, sum_z_in, shares, result, misfit, wide, flow_rim, adjoint1, sum_x, sum_y, sum_z,
):
    runs, n = adjoint2.shape[:2]
    ny = flow_own.shape[-2] - 2 * PAD
    faces = (mx, my, mz, mz_low, m_all)
    misfit[0] = jnp.sum(shares[...])
    sum_x[...] = sum_x_in[...]
    sum_z[...] = sum_z_in[...]
    for row in chunks(ny):
        for at in range(n):
            put_padded(sum_y, (at,), row, flat(sum_y_in, (at,), row))

    def adj2(run, at):
        if at < 0:
            return wide, (at + 3,)
        return (adjoint2, (run, at)) if at < n else (wide, (at - n + 3,))

    def flow(run, at):
        if at <= 0:
            return flow_rim, (at + 2,)
        return (flow_own, (run, at)) if at < n - 1 else (flow_rim, (at - (n - 1) + 3,))

    def one_run(run, carry):
        for row in chunks(ny):
            for at in range(3):
                put_padded(wide, (at,), row, plain(low, (run, at), row))
                put_padded(wide, (at + 3,), row, plain(high, (run, at), row))
        for row in chunks(ny):
            mids = {at: padded(*adj2(run, at), row) for at in range(-3, n + 3)}
            for at in (-2, -1, n, n + 1):
                ref, lead = adj2(run, at)
                value = flow_in_plane(
                    faces, row, at + 2, mids[at], padded(ref, lead, row, 1), padded(ref, lead, row, -1)
                )
                value = add_product(value, flat(mx, (at + 2,), row), mids[at - 1])
                value = add_product(value, flat(mx, (at + 3,), row), mids[at + 1])
                put_padded(*flow(run, at), row, value)
            for at, side, face in ((0, -1, 2), (n - 1, n, n + 2)):
                value = add_product(
                    padded(flow_own, (run, at), row), flat(mx, (face,), row), mids[side]
                )
                put_padded(*flow(run, at), row, value)
        for row in chunks(ny):
            mids = {at: padded(*flow(run, at), row) for at in range(-2, n + 2)}
            for at in range(-1, n + 1):
                ref, lead = flow(run, at)
                total = beside(
                    mids[at - 1], mids[at + 1], padded(ref, lead, row, 1), padded(ref, lead, row, -1), mids[at]
                )
                value = each(
                    lambda a, w, f, t: a + w * f - (time_step * stiffness) * t,
                    padded(*adj2(run, at), row), flat(weight, (run, at + 1), row), mids[at], total,
                )
                put_padded(adjoint1, (at + 1,), row, value)
        for row in chunks(ny):
            mids = [padded(adjoint1, (at,), row) for at in range(n + 2)]
            chems = [padded(chem0, (run, at + 2), row) for at in range(n + 2)]
            for at in range(n + 1):
                face = add_product(
                    flat(sum_x, (at,), row), sub(mids[at + 1], mids[at]), sub(chems[at + 1], chems[at])
                )
                if at in (0, n):
                    face = add_product(
                        face, sub(padded(*adj2(run, at), row), padded(*adj2(run, at - 1), row)),
                        sub(padded(chem1, (run, at + 1), row), padded(chem1, (run, at), row)),
                    )
                put_flat(sum_x, (at,), row, face)
            for at in range(n):
                mid = mids[at + 1]
                put_padded(sum_y, (at,), row, add_product(
                    padded(sum_y, (at,), row), sub(padded(adjoint1, (at + 1,), row, 1), mid),
                    sub(padded(chem0, (run, at + 3), row, 1), chems[at + 1]),
                ))
                put_flat(sum_z, (at,), row, add_product(
                    flat(sum_z, (at,), row), sub(after_z(mid), mid), flat(step_z0, (run, at), row)
                ))
        return carry

    lax.fori_loop(0, runs, one_run, 0)
    for row in chunks(ny):
        for at in range(n):
            sides = flat(sum_z, (at,), row)
            value = each(
                lambda a, b, c, d, e, f: -0.5 * ((a + b) + (c + d) + (e + f)),
                flat(sum_x, (at,), row), flat(sum_x, (at + 1,), row),
                padded(sum_y, (at,), row), padded(sum_y, (at,), row, -1), sides, before_z(sides),
            )
            put_plain(result, (at,), row, value)


def call(kernel, outs, scratch, args, flops, scalar=None):
    moved = 4 * (sum(a.size for a in args) + sum(math.prod(o) for o in outs))
    return pl.pallas_call(
        kernel,
        out_shape=tuple(jax.ShapeDtypeStruct(o, jnp.float32) for o in outs),
        in_specs=[VMEM] * len(args),
        out_specs=tuple(SMEM if at == scalar else VMEM for at in range(len(outs))),
        scratch_shapes=[pltpu.VMEM(s, jnp.float32) for s in scratch],
        compiler_params=pltpu.CompilerParams(vmem_limit_bytes=16 * 1024 * 1024),
        cost_estimate=pl.CostEstimate(flops=flops, bytes_accessed=moved, transcendentals=0),
    )(*args)


def on_device(initial, observed, mobility):
    runs, n, ny, nz = initial.shape
    blocks = nz // LANES
    count = lax.axis_size("gx")
    forward = [(i, (i + 1) % count) for i in range(count)]
    backward = [(i, (i - 1) % count) for i in range(count)]
    cell = ny * nz

    def neighbours(first, last):
        return lax.ppermute(last, "gx", forward), lax.ppermute(first, "gx", backward)

    def lies(*lead):
        return (*lead, blocks, ny, LANES)

    def lies_padded(*lead):
        return (*lead, blocks, ny + 2 * PAD, LANES)

    low, high = neighbours(initial[:, :4], initial[:, n - 4 :])
    conc, mob, first, last = call(
        own_kernel,
        (lies_padded(runs, n), lies_padded(n), (3, ny, nz), (3, ny, nz)),
        (),
        (initial, mobility),
        runs * n * cell,
    )
    m_low, m_high = neighbours(first, last)
    (chem0,) = call(
        chem_kernel, (lies_padded(runs, n + 6),), (lies_padded(8),), (low, conc, high),
        20 * runs * (n + 6) * cell,
    )
    *faces, state1, chem1, adjoint2, first, last, miss_sum = call(
        forward_kernel,
        (
            lies(n + 5), lies_padded(n + 4), lies(n + 4), lies(n + 4), lies(n + 4),
            lies_padded(runs, n + 4), lies_padded(runs, n + 2), lies_padded(runs, n),
            (runs, 3, ny, nz), (runs, 3, ny, nz), (1, LANES),
        ),
        (lies_padded(6), (CHUNK, LANES)),
        (m_low, mob, m_high, low, conc, high, observed, chem0),
        60 * runs * (n + 4) * cell,
    )
    low, high = neighbours(first, last)
    shares, flow_own, weight, step_z0, sum_x, sum_y, sum_z = call(
        middle_kernel,
        (
            (count, 1, LANES), lies_padded(runs, n), lies(runs, n + 2), lies(runs, n),
            lies(n + 1), lies(n), lies(n),
        ),
        (),
        (*faces, state1, chem0, chem1, adjoint2, miss_sum),
        40 * runs * n * cell,
    )
    shares = lax.all_to_all(shares, "gx", 0, 0)
    return call(
        backward_kernel,
        ((n, ny, nz), (1,)),
        (
            lies_padded(6), lies_padded(6), lies_padded(n + 2),
            lies(n + 1), lies_padded(n), lies(n),
        ),
        (
            low, high, *faces, chem0, chem1, adjoint2, flow_own, weight, step_z0,
            sum_x, sum_y, sum_z, shares,
        ),
        40 * runs * (n + 2) * cell,
        scalar=1,
    )


def solution(mesh):
    placed = (
        P("group", "gx", None, None),
        P("group", "gx", None, None),
        P(("group", "gx"), None, None),
    )
    return jax.shard_map(
        on_device,
        mesh=mesh,
        in_specs=placed,
        out_specs=(P(("group", "gx"), None, None), P("group")),
        check_vma=False,
    )
```

```python
import functools
import math

import jax
import jax.numpy as jnp
from jax import lax
from jax.experimental import pallas as pl
from jax.experimental.pallas import tpu as pltpu
from jax.sharding import PartitionSpec as P

stiffness = 0.5
time_step = 0.005
VMEM = pl.BlockSpec(memory_space=pltpu.VMEM)
LANES = 128
PAD = 8
CHUNK = 16


def chunks(ny):
    return range(0, ny, CHUNK)


def plain(ref, lead, row):
    return [
        ref[(*lead, pl.ds(row, CHUNK), pl.ds(at, LANES))] for at in range(0, ref.shape[-1], LANES)
    ]


def put_plain(ref, lead, row, value):
    for block, part in enumerate(value):
        ref[(*lead, pl.ds(row, CHUNK), pl.ds(block * LANES, LANES))] = part


def flat(ref, lead, row):
    return [ref[(*lead, block, pl.ds(row, CHUNK))] for block in range(ref.shape[-3])]


def put_flat(ref, lead, row, value):
    for block, part in enumerate(value):
        ref[(*lead, block, pl.ds(row, CHUNK))] = part


def padded(ref, lead, row, shift=0):
    return [ref[(*lead, block, pl.ds(PAD + row + shift, CHUNK))] for block in range(ref.shape[-3])]


def put_padded(ref, lead, row, value):
    ny = ref.shape[-2] - 2 * PAD
    for block, part in enumerate(value):
        ref[(*lead, block, pl.ds(PAD + row, CHUNK))] = part
        if row == 0:
            ref[(*lead, block, pl.ds(PAD + ny, 1))] = part[:1]
        if row + CHUNK == ny:
            ref[(*lead, block, pl.ds(PAD - 1, 1))] = part[CHUNK - 1 :]


def lane():
    return lax.broadcasted_iota(jnp.int32, (CHUNK, LANES), 1)


def after_z(value):
    turned = [pltpu.roll(part, LANES - 1, 1) for part in value]
    turned.append(turned[0])
    edge = lane() == LANES - 1
    return [jnp.where(edge, turned[at + 1], turned[at]) for at in range(len(value))]


def before_z(value):
    turned = [pltpu.roll(part, 1, 1) for part in value]
    edge = lane() == 0
    return [jnp.where(edge, turned[at - 1], turned[at]) for at in range(len(value))]


def each(function, *values):
    return [function(*parts) for parts in zip(*values)]


def beside(low, high, up, down, mid):
    return each(
        lambda a, b, c, d, e, f: (a + b) + (c + d) + (e + f),
        low, high, up, down, after_z(mid), before_z(mid),
    )


def potential(low, mid, high, up, down):
    return each(
        lambda c, total: c * (c * c + (6.0 * stiffness - 1.0)) - stiffness * total,
        mid, beside(low, high, up, down, mid),
    )


def flow_in_plane(faces, row, at, mid, up, down):
    _, my, mz, mz_low, m_all = faces
    return each(
        lambda a, b, c, d, e, u, v, w, x, y: (a * u + b * v) + (c * w + d * x) - e * y,
        padded(my, (at,), row), padded(my, (at,), row, -1), flat(mz, (at,), row),
        flat(mz_low, (at,), row), flat(m_all, (at,), row), up, down, after_z(mid), before_z(mid), mid,
    )


def add_product(total, a, b):
    return each(lambda t, x, y: t + x * y, total, a, b)


def sub(a, b):
    return each(lambda x, y: x - y, a, b)


def own_kernel(initial, mobility, conc, mob, *runs_out):
    runs, n, ny, _ = initial.shape

    def one_run(run, carry):
        for row in chunks(ny):
            for at in range(n):
                put_padded(conc, (run, at), row, plain(initial, (run, at), row))
        return carry

    lax.fori_loop(0, runs, one_run, 0)
    for row in chunks(ny):
        for at in range(n):
            put_padded(mob, (at,), row, plain(mobility, (at,), row))
    for run, out in enumerate(runs_out):
        out[...] = initial[run]


def faces_kernel(m_low, m_own, m_high, mx, my, mz, mz_low, m_all, rim):
    n = m_own.shape[0]
    ny = m_low.shape[1]
    for row in chunks(ny):
        for at in range(3):
            put_padded(rim, (at,), row, plain(m_low, (at + 1,), row))
            put_padded(rim, (at + 3,), row, plain(m_high, (at,), row))

    def mob(at):
        if at < 3:
            return rim, (at,)
        return (m_own, (at - 3,)) if at < n + 3 else (rim, (at - n,))

    mean = lambda a, b: 0.5 * (a + b)
    for row in chunks(ny):
        face = None
        for at in range(n + 5):
            mid = padded(*mob(at), row)
            face_low, face = face, each(mean, mid, padded(*mob(at + 1), row))
            put_flat(mx, (at,), row, face)
            if at == 0:
                continue
            side_y = each(mean, mid, padded(*mob(at), row, 1))
            side_y_low = each(mean, mid, padded(*mob(at), row, -1))
            side_z = each(mean, mid, after_z(mid))
            side_z_low = each(mean, mid, before_z(mid))
            put_padded(my, (at - 1,), row, side_y)
            put_flat(mz, (at - 1,), row, side_z)
            put_flat(mz_low, (at - 1,), row, side_z_low)
            put_flat(m_all, (at - 1,), row, each(
                lambda a, b, c, d, e, f: (a + b) + (c + d) + (e + f),
                face, face_low, side_y, side_y_low, side_z, side_z_low,
            ))


def forward_kernel(
    run, low, own, high, observed, mx, my, mz, mz_low, m_all, miss_in,
    chem0, state1, chem1, adjoint2, first, last, miss_sum, rim,
):
    runs, n, ny, _ = observed.shape
    faces = (mx, my, mz, mz_low, m_all)

    def conc(at):
        if at < 0:
            return rim, (at + 4,)
        return (own, (run, at)) if at < n else (rim, (at - n + 4,))

    for row in chunks(ny):
        for at in range(4):
            put_padded(rim, (at,), row, plain(low, (at,), row))
            put_padded(rim, (at + 4,), row, plain(high, (at,), row))
    for row in chunks(ny):
        mids = {at: padded(*conc(at), row) for at in range(-4, n + 4)}
        for at in range(-3, n + 3):
            ref, lead = conc(at)
            value = potential(
                mids[at - 1], mids[at], mids[at + 1], padded(ref, lead, row, 1), padded(ref, lead, row, -1)
            )
            put_padded(chem0, (at + 3,), row, value)
    for row in chunks(ny):
        mids = [padded(chem0, (at,), row) for at in range(n + 6)]
        for at in range(n + 4):
            flow = flow_in_plane(
                faces, row, at, mids[at + 1],
                padded(chem0, (at + 1,), row, 1), padded(chem0, (at + 1,), row, -1),
            )
            flow = add_product(flow, flat(mx, (at,), row), mids[at])
            flow = add_product(flow, flat(mx, (at + 1,), row), mids[at + 2])
            value = each(lambda a, b: a + time_step * b, padded(*conc(at - 2), row), flow)
            put_padded(state1, (at,), row, value)
    for row in chunks(ny):
        mids = [padded(state1, (at,), row) for at in range(n + 4)]
        for at in range(1, n + 3):
            value = potential(
                mids[at - 1], mids[at], mids[at + 1],
                padded(state1, (at,), row, 1), padded(state1, (at,), row, -1),
            )
            put_padded(chem1, (at - 1,), row, value)
    squares = None
    for row in chunks(ny):
        mids = [padded(chem1, (at,), row) for at in range(n + 2)]
        for at in range(n):
            flow = flow_in_plane(
                faces, row, at + 2, mids[at + 1],
                padded(chem1, (at + 1,), row, 1), padded(chem1, (at + 1,), row, -1),
            )
            flow = add_product(flow, flat(mx, (at + 2,), row), mids[at])
            flow = add_product(flow, flat(mx, (at + 3,), row), mids[at + 2])
            miss = each(
                lambda a, b, c: a + time_step * b - c,
                padded(state1, (at + 2,), row), flow, plain(observed, (run, at), row),
            )
            for part in miss:
                square = part * part
                squares = square if squares is None else squares + square
            value = each(lambda a: a * (1.0 / runs), miss)
            put_padded(adjoint2, (at,), row, value)
            if at < 3:
                put_plain(first, (at,), row, value)
            if at >= n - 3:
                put_plain(last, (at - (n - 3),), row, value)
    total = jnp.sum(squares, axis=0, keepdims=True)
    total = (0.5 / runs) * jnp.sum(total, axis=1, keepdims=True)
    miss_sum[...] = miss_in[...] + jnp.broadcast_to(total, miss_sum.shape)


def middle_kernel(
    run, mx, my, mz, mz_low, m_all, state1, chem0, chem1, adjoint2, share_in, sum_x_in, sum_y_in, sum_z_in,
    share, flow_own, weight, step_z0, sum_x, sum_y, sum_z,
):
    n = adjoint2.shape[0]
    ny = flow_own.shape[-2] - 2 * PAD
    faces = (mx, my, mz, mz_low, m_all)
    share[...] = share_in[...]

    def plus(sum_in, lead, row, a, b):
        if run == 0:
            return each(lambda x, y: x * y, a, b)
        return add_product(flat(sum_in, lead, row), a, b)

    for row in chunks(ny):
        mids = [padded(adjoint2, (at,), row) for at in range(n)]
        chems = [padded(chem1, (at + 1,), row) for at in range(n)]
        for at in range(n):
            up = padded(adjoint2, (at,), row, 1)
            flow = flow_in_plane(faces, row, at + 2, mids[at], up, padded(adjoint2, (at,), row, -1))
            if at > 0:
                flow = add_product(flow, flat(mx, (at + 2,), row), mids[at - 1])
            if at < n - 1:
                flow = add_product(flow, flat(mx, (at + 3,), row), mids[at + 1])
                face = plus(sum_x_in, (at + 1,), row, sub(mids[at + 1], mids[at]), sub(chems[at + 1], chems[at]))
                put_flat(sum_x, (at + 1,), row, face)
            put_padded(flow_own, (at,), row, flow)
            put_flat(sum_y, (at,), row, plus(
                sum_y_in, (at,), row, sub(up, mids[at]), sub(padded(chem1, (at + 1,), row, 1), chems[at])
            ))
            put_flat(sum_z, (at,), row, plus(
                sum_z_in, (at,), row, sub(after_z(mids[at]), mids[at]), sub(after_z(chems[at]), chems[at])
            ))
            mid = padded(chem0, (at + 3,), row)
            put_flat(step_z0, (at,), row, sub(after_z(mid), mid))
        for at in range(n + 2):
            value = each(
                lambda c: time_step * (3.0 * c * c + (6.0 * stiffness - 1.0)),
                padded(state1, (at + 1,), row),
            )
            put_flat(weight, (at,), row, value)
        for at in (0, n):
            chem = padded(chem1, (at,), row)
            put_flat(sum_x, (at,), row, each(jnp.zeros_like, chem) if run == 0 else flat(sum_x_in, (at,), row))


def backward_kernel(
    final, low, high, mx, my, mz, mz_low, m_all, chem0, chem1, adjoint2, flow_own, weight, step_z0,
    sum_x_in, sum_y_in, sum_z_in, *rest,
):
    n = adjoint2.shape[0]
    ny = flow_own.shape[-2] - 2 * PAD
    faces = (mx, my, mz, mz_low, m_all)
    if final:
        result, wide, flow_rim, adjoint1, sum_x, sum_y, sum_z = rest
    else:
        sum_x, sum_y, sum_z, wide, flow_rim, adjoint1 = rest

    def adj2(at):
        if at < 0:
            return wide, (at + 3,)
        return (adjoint2, (at,)) if at < n else (wide, (at - n + 3,))

    def flow(at):
        if at <= 0:
            return flow_rim, (at + 2,)
        return (flow_own, (at,)) if at < n - 1 else (flow_rim, (at - (n - 1) + 3,))

    for row in chunks(ny):
        for at in range(3):
            put_padded(wide, (at,), row, plain(low, (at,), row))
            put_padded(wide, (at + 3,), row, plain(high, (at,), row))
    for row in chunks(ny):
        mids = {at: padded(*adj2(at), row) for at in range(-3, n + 3)}
        for at in (-2, -1, n, n + 1):
            ref, lead = adj2(at)
            value = flow_in_plane(
                faces, row, at + 2, mids[at], padded(ref, lead, row, 1), padded(ref, lead, row, -1)
            )
            value = add_product(value, flat(mx, (at + 2,), row), mids[at - 1])
            value = add_product(value, flat(mx, (at + 3,), row), mids[at + 1])
            put_padded(*flow(at), row, value)
        for at, side, face in ((0, -1, 2), (n - 1, n, n + 2)):
            value = add_product(padded(flow_own, (at,), row), flat(mx, (face,), row), mids[side])
            put_padded(*flow(at), row, value)
    for row in chunks(ny):
        mids = {at: padded(*flow(at), row) for at in range(-2, n + 2)}
        for at in range(-1, n + 1):
            ref, lead = flow(at)
            total = beside(
                mids[at - 1], mids[at + 1], padded(ref, lead, row, 1), padded(ref, lead, row, -1), mids[at]
            )
            value = each(
                lambda a, w, f, t: a + w * f - (time_step * stiffness) * t,
                padded(*adj2(at), row), flat(weight, (at + 1,), row), mids[at], total,
            )
            put_padded(adjoint1, (at + 1,), row, value)
    for row in chunks(ny):
        mids = [padded(adjoint1, (at,), row) for at in range(n + 2)]
        chems = [padded(chem0, (at + 2,), row) for at in range(n + 2)]
        for at in range(n + 1):
            face = add_product(
                flat(sum_x_in, (at,), row), sub(mids[at + 1], mids[at]), sub(chems[at + 1], chems[at])
            )
            if at in (0, n):
                face = add_product(
                    face, sub(padded(*adj2(at), row), padded(*adj2(at - 1), row)),
                    sub(padded(chem1, (at + 1,), row), padded(chem1, (at,), row)),
                )
            put_flat(sum_x, (at,), row, face)
        for at in range(n):
            mid = mids[at + 1]
            total = add_product(
                flat(sum_y_in, (at,), row), sub(padded(adjoint1, (at + 1,), row, 1), mid),
                sub(padded(chem0, (at + 3,), row, 1), chems[at + 1]),
            )
            (put_padded if final else put_flat)(sum_y, (at,), row, total)
            put_flat(sum_z, (at,), row, add_product(
                flat(sum_z_in, (at,), row), sub(after_z(mid), mid), flat(step_z0, (at,), row)
            ))
    if not final:
        return
    for row in chunks(ny):
        for at in range(n):
            sides = flat(sum_z, (at,), row)
            value = each(
                lambda a, b, c, d, e, f: -0.5 * ((a + b) + (c + d) + (e + f)),
                flat(sum_x, (at,), row), flat(sum_x, (at + 1,), row),
                padded(sum_y, (at,), row), padded(sum_y, (at,), row, -1), sides, before_z(sides),
            )
            put_plain(result, (at,), row, value)


def call(kernel, outs, scratch, args, flops):
    moved = 4 * (sum(a.size for a in args) + sum(math.prod(o) for o in outs))
    return pl.pallas_call(
        kernel,
        out_shape=tuple(jax.ShapeDtypeStruct(o, jnp.float32) for o in outs),
        in_specs=[VMEM] * len(args),
        out_specs=tuple([VMEM] * len(outs)),
        scratch_shapes=[pltpu.VMEM(s, jnp.float32) for s in scratch],
        compiler_params=pltpu.CompilerParams(vmem_limit_bytes=16 * 1024 * 1024),
        cost_estimate=pl.CostEstimate(flops=flops, bytes_accessed=moved, transcendentals=0),
    )(*args)


def sum_over(value, axis, order):
    count = lax.axis_size(axis)
    if count & (count - 1):
        return lax.psum(value, axis)
    hops = [1 << bit for bit in range(count.bit_length() - 1)]
    hops = [hop for hop in order if hop in hops] + [hop for hop in hops if hop not in order]
    for hop in hops:
        value = value + lax.ppermute(value, axis, [(i, i ^ hop) for i in range(count)])
    return value


def on_device(initial, observed, mobility):
    runs, n, ny, nz = initial.shape
    blocks = nz // LANES
    count = lax.axis_size("gx")
    forward = [(i, (i + 1) % count) for i in range(count)]
    backward = [(i, (i - 1) % count) for i in range(count)]
    cell = ny * nz

    def neighbours(first, last):
        return lax.ppermute(last, "gx", forward), lax.ppermute(first, "gx", backward)

    def lies(*lead):
        return (*lead, blocks, ny, LANES)

    def lies_padded(*lead):
        return (*lead, blocks, ny + 2 * PAD, LANES)

    m_low, m_high = neighbours(mobility[:4], mobility[n - 4 :])
    conc, mob, *initials = call(
        own_kernel,
        (lies_padded(runs, n), lies_padded(n), *[(n, ny, nz)] * runs),
        (),
        (initial, mobility),
        runs * n * cell,
    )
    sides = [neighbours(part[:4], part[n - 4 :]) for part in initials]
    faces = call(
        faces_kernel,
        (lies(n + 5), lies_padded(n + 4), lies(n + 4), lies(n + 4), lies(n + 4)),
        (lies_padded(6),),
        (m_low, mob, m_high),
        15 * (n + 4) * cell,
    )
    share = jnp.zeros((1, LANES), jnp.float32)
    kept = []
    for run, (low, high) in enumerate(sides):
        chem0, state1, chem1, adjoint2, first, last, share = call(
            functools.partial(forward_kernel, run),
            (
                lies_padded(n + 6), lies_padded(n + 4), lies_padded(n + 2), lies_padded(n),
                (3, ny, nz), (3, ny, nz), (1, LANES),
            ),
            (lies_padded(8),),
            (low, conc, high, observed, *faces, share),
            80 * (n + 4) * cell,
        )
        kept.append((chem0, state1, chem1, adjoint2, neighbours(first, last)))
    sums = (jnp.zeros(lies(n + 1), jnp.float32), jnp.zeros(lies(n), jnp.float32), jnp.zeros(lies(n), jnp.float32))
    ready = []
    for run, (chem0, state1, chem1, adjoint2, (low, high)) in enumerate(kept):
        share, flow_own, weight, step_z0, *sums = call(
            functools.partial(middle_kernel, run),
            (
                (1, LANES), lies_padded(n), lies(n + 2), lies(n),
                lies(n + 1), lies(n), lies(n),
            ),
            (),
            (*faces, state1, chem0, chem1, adjoint2, share, *sums),
            40 * n * cell,
        )
        ready.append((low, high, *faces, chem0, chem1, adjoint2, flow_own, weight, step_z0))
    misfit = sum_over(share, "gx", (1, 4, 8, 2))
    for run, args in enumerate(ready):
        final = run == runs - 1
        scratch = (lies_padded(6), lies_padded(6), lies_padded(n + 2))
        if final:
            outs, scratch = ((n, ny, nz),), (*scratch, lies(n + 1), lies_padded(n), lies(n))
        else:
            outs = (lies(n + 1), lies(n), lies(n))
        sums = call(
            functools.partial(backward_kernel, final), outs, scratch, (*args, *sums), 40 * (n + 2) * cell
        )
    return (sums[0], misfit[0, :1])


def solution(mesh):
    placed = (
        P("group", "gx", None, None),
        P("group", "gx", None, None),
        P(("group", "gx"), None, None),
    )
    return jax.shard_map(
        on_device,
        mesh=mesh,
        in_specs=placed,
        out_specs=(P(("group", "gx"), None, None), P("group")),
        check_vma=False,
    )
```

```python
import functools
import math

import jax
import jax.numpy as jnp
from jax import lax
from jax.experimental import pallas as pl
from jax.experimental.pallas import tpu as pltpu
from jax.sharding import PartitionSpec as P

stiffness = 0.5
time_step = 0.005
VMEM = pl.BlockSpec(memory_space=pltpu.VMEM)
SMEM = pl.BlockSpec(memory_space=pltpu.SMEM)
LANES = 128
PAD = 8
CHUNK = 16


def chunks(ny):
    return range(0, ny, CHUNK)


def plain(ref, lead, row):
    return [
        ref[(*lead, pl.ds(row, CHUNK), pl.ds(at, LANES))] for at in range(0, ref.shape[-1], LANES)
    ]


def put_plain(ref, lead, row, value):
    for block, part in enumerate(value):
        ref[(*lead, pl.ds(row, CHUNK), pl.ds(block * LANES, LANES))] = part


def flat(ref, lead, row):
    return [ref[(*lead, block, pl.ds(row, CHUNK))] for block in range(ref.shape[-3])]


def put_flat(ref, lead, row, value):
    for block, part in enumerate(value):
        ref[(*lead, block, pl.ds(row, CHUNK))] = part


def padded(ref, lead, row, shift=0):
    return [ref[(*lead, block, pl.ds(PAD + row + shift, CHUNK))] for block in range(ref.shape[-3])]


def put_padded(ref, lead, row, value):
    ny = ref.shape[-2] - 2 * PAD
    for block, part in enumerate(value):
        ref[(*lead, block, pl.ds(PAD + row, CHUNK))] = part
        if row == 0:
            ref[(*lead, block, pl.ds(PAD + ny, 1))] = part[:1]
        if row + CHUNK == ny:
            ref[(*lead, block, pl.ds(PAD - 1, 1))] = part[CHUNK - 1 :]


def lane():
    return lax.broadcasted_iota(jnp.int32, (CHUNK, LANES), 1)


def after_z(value):
    turned = [pltpu.roll(part, LANES - 1, 1) for part in value]
    turned.append(turned[0])
    edge = lane() == LANES - 1
    return [jnp.where(edge, turned[at + 1], turned[at]) for at in range(len(value))]


def before_z(value):
    turned = [pltpu.roll(part, 1, 1) for part in value]
    edge = lane() == 0
    return [jnp.where(edge, turned[at - 1], turned[at]) for at in range(len(value))]


def side():
    return lax.rem(lax.axis_index("gx"), 2)


def place(count):
    at = side() * count
    return at, count - at


def each(function, *values):
    return [function(*parts) for parts in zip(*values)]


def beside(low, high, up, down, mid):
    return each(
        lambda a, b, c, d, e, f: (a + b) + (c + d) + (e + f),
        low, high, up, down, after_z(mid), before_z(mid),
    )


def potential(low, mid, high, up, down):
    return each(
        lambda c, total: c * (c * c + (6.0 * stiffness - 1.0)) - stiffness * total,
        mid, beside(low, high, up, down, mid),
    )


def flow_in_plane(faces, row, at, mid, up, down):
    _, my, mz, mz_low, m_all = faces
    return each(
        lambda a, b, c, d, e, u, v, w, x, y: (a * u + b * v) + (c * w + d * x) - e * y,
        padded(my, (at,), row), padded(my, (at,), row, -1), flat(mz, (at,), row),
        flat(mz_low, (at,), row), flat(m_all, (at,), row), up, down, after_z(mid), before_z(mid), mid,
    )


def add_product(total, a, b):
    return each(lambda t, x, y: t + x * y, total, a, b)


def sub(a, b):
    return each(lambda x, y: x - y, a, b)


def own_kernel(initial, mobility, conc, mob, to_chip, to_core):
    runs, n, ny, _ = initial.shape

    def one_run(run, carry):
        for row in chunks(ny):
            for at in range(n):
                put_padded(conc, (run, at), row, plain(initial, (run, at), row))
        return carry

    lax.fori_loop(0, runs, one_run, 0)
    for row in chunks(ny):
        for at in range(n):
            put_padded(mob, (at,), row, plain(mobility, (at,), row))
    at_chip, at_core = place(n - 3)
    to_chip[...] = mobility[pl.ds(at_chip, 3)]
    to_core[...] = mobility[pl.ds(at_core, 3)]


def chem_kernel(of_chip, of_core, own, chem0, rim):
    runs, n = own.shape[:2]
    ny = of_chip.shape[2]
    at_chip, at_core = place(4)

    def conc(run, at):
        if at < 0:
            return rim, (run, at + 4)
        return (own, (run, at)) if at < n else (rim, (run, at - n + 4))

    def one_run(run, carry):
        for row in chunks(ny):
            for at in range(4):
                put_padded(rim, (run, at_chip + at), row, plain(of_chip, (run, at), row))
                put_padded(rim, (run, at_core + at), row, plain(of_core, (run, at), row))
        for row in chunks(ny):
            mids = {at: padded(*conc(run, at), row) for at in range(-4, n + 4)}
            for at in range(-3, n + 3):
                ref, lead = conc(run, at)
                value = potential(
                    mids[at - 1], mids[at], mids[at + 1], padded(ref, lead, row, 1), padded(ref, lead, row, -1)
                )
                put_padded(chem0, (run, at + 3), row, value)
        return carry

    lax.fori_loop(0, runs, one_run, 0)


def forward_kernel(
    m_chip, m_core, m_own, own, conc_rim, observed, chem0,
    mx, my, mz, mz_low, m_all, state1, chem1, adjoint2, to_chip, to_core, miss_sum,
    rim, total,
):
    runs, n, ny, _ = observed.shape
    at_chip, at_core = place(3)
    for row in chunks(ny):
        for at in range(3):
            put_padded(rim, (at_chip + at,), row, plain(m_chip, (at,), row))
            put_padded(rim, (at_core + at,), row, plain(m_core, (at,), row))

    def mob(at):
        if at < 3:
            return rim, (at,)
        return (m_own, (at - 3,)) if at < n + 3 else (rim, (at - n,))

    mean = lambda a, b: 0.5 * (a + b)
    for row in chunks(ny):
        face = None
        for at in range(n + 5):
            mid = padded(*mob(at), row)
            face_low, face = face, each(mean, mid, padded(*mob(at + 1), row))
            put_flat(mx, (at,), row, face)
            if at == 0:
                continue
            side_y = each(mean, mid, padded(*mob(at), row, 1))
            side_y_low = each(mean, mid, padded(*mob(at), row, -1))
            side_z = each(mean, mid, after_z(mid))
            side_z_low = each(mean, mid, before_z(mid))
            put_padded(my, (at - 1,), row, side_y)
            put_flat(mz, (at - 1,), row, side_z)
            put_flat(mz_low, (at - 1,), row, side_z_low)
            put_flat(m_all, (at - 1,), row, each(
                lambda a, b, c, d, e, f: (a + b) + (c + d) + (e + f),
                face, face_low, side_y, side_y_low, side_z, side_z_low,
            ))
    faces = (mx, my, mz, mz_low, m_all)
    total[...] = jnp.zeros_like(total)

    def conc(run, at, row):
        if 0 <= at < n:
            return padded(own, (run, at), row)
        return padded(conc_rim, (run, at + 4 if at < 0 else at - n + 4), row)

    def one_run(run, carry):
        for row in chunks(ny):
            mids = [padded(chem0, (run, at), row) for at in range(n + 6)]
            for at in range(n + 4):
                flow = flow_in_plane(
                    faces, row, at, mids[at + 1],
                    padded(chem0, (run, at + 1), row, 1), padded(chem0, (run, at + 1), row, -1),
                )
                flow = add_product(flow, flat(mx, (at,), row), mids[at])
                flow = add_product(flow, flat(mx, (at + 1,), row), mids[at + 2])
                value = each(lambda a, b: a + time_step * b, conc(run, at - 2, row), flow)
                put_padded(state1, (run, at), row, value)
        for row in chunks(ny):
            mids = [padded(state1, (run, at), row) for at in range(n + 4)]
            for at in range(1, n + 3):
                value = potential(
                    mids[at - 1], mids[at], mids[at + 1],
                    padded(state1, (run, at), row, 1), padded(state1, (run, at), row, -1),
                )
                put_padded(chem1, (run, at - 1), row, value)
        squares = None
        for row in chunks(ny):
            mids = [padded(chem1, (run, at), row) for at in range(n + 2)]
            for at in range(n):
                flow = flow_in_plane(
                    faces, row, at + 2, mids[at + 1],
                    padded(chem1, (run, at + 1), row, 1), padded(chem1, (run, at + 1), row, -1),
                )
                flow = add_product(flow, flat(mx, (at + 2,), row), mids[at])
                flow = add_product(flow, flat(mx, (at + 3,), row), mids[at + 2])
                miss = each(
                    lambda a, b, c: a + time_step * b - c,
                    padded(state1, (run, at + 2), row), flow, plain(observed, (run, at), row),
                )
                for part in miss:
                    square = part * part
                    squares = square if squares is None else squares + square
                value = each(lambda a: a * (1.0 / runs), miss)
                put_padded(adjoint2, (run, at), row, value)
        at_chip, at_core = place(n - 3)
        for row in chunks(ny):
            for at in range(3):
                put_flat(to_chip, (run, at), row, padded(adjoint2, (run, at_chip + at), row))
                put_flat(to_core, (run, at), row, padded(adjoint2, (run, at_core + at), row))
        total[...] += squares
        return carry

    lax.fori_loop(0, runs, one_run, 0)
    miss_sum[...] = (0.5 / runs) * jnp.sum(total[...], axis=0, keepdims=True)


def middle_kernel(
    mx, my, mz, mz_low, m_all, state1, chem0, chem1, adjoint2, miss_sum,
    shares, flow_own, weight, step_z0, sum_x, sum_y, sum_z,
):
    runs, n = adjoint2.shape[:2]
    ny = flow_own.shape[-2] - 2 * PAD
    faces = (mx, my, mz, mz_low, m_all)
    shares[...] = jnp.broadcast_to(miss_sum[...][None], shares.shape)
    sum_x[...] = jnp.zeros_like(sum_x)
    sum_y[...] = jnp.zeros_like(sum_y)
    sum_z[...] = jnp.zeros_like(sum_z)

    def one_run(run, carry):
        for row in chunks(ny):
            mids = [padded(adjoint2, (run, at), row) for at in range(n)]
            chems = [padded(chem1, (run, at + 1), row) for at in range(n)]
            for at in range(n):
                up = padded(adjoint2, (run, at), row, 1)
                flow = flow_in_plane(faces, row, at + 2, mids[at], up, padded(adjoint2, (run, at), row, -1))
                if at > 0:
                    flow = add_product(flow, flat(mx, (at + 2,), row), mids[at - 1])
                if at < n - 1:
                    flow = add_product(flow, flat(mx, (at + 3,), row), mids[at + 1])
                    face = add_product(
                        flat(sum_x, (at + 1,), row), sub(mids[at + 1], mids[at]), sub(chems[at + 1], chems[at])
                    )
                    put_flat(sum_x, (at + 1,), row, face)
                put_padded(flow_own, (run, at), row, flow)
                put_flat(sum_y, (at,), row, add_product(
                    flat(sum_y, (at,), row), sub(up, mids[at]),
                    sub(padded(chem1, (run, at + 1), row, 1), chems[at]),
                ))
                put_flat(sum_z, (at,), row, add_product(
                    flat(sum_z, (at,), row), sub(after_z(mids[at]), mids[at]),
                    sub(after_z(chems[at]), chems[at]),
                ))
                mid = padded(chem0, (run, at + 3), row)
                put_flat(step_z0, (run, at), row, sub(after_z(mid), mid))
            for at in range(n + 2):
                value = each(
                    lambda c: time_step * (3.0 * c * c + (6.0 * stiffness - 1.0)),
                    padded(state1, (run, at + 1), row),
                )
                put_flat(weight, (run, at), row, value)
        return carry

    lax.fori_loop(0, runs, one_run, 0)


def backward_kernel(
    of_chip, of_core, mx, my, mz, mz_low, m_all, chem0, chem1, adjoint2, flow_own, weight, step_z0,
    sum_x_in, sum_y_in, sum_z_in, shares, result, misfit, wide, flow_rim, adjoint1, sum_x, sum_y, sum_z,
):
    runs, n = adjoint2.shape[:2]
    ny = flow_own.shape[-2] - 2 * PAD
    faces = (mx, my, mz, mz_low, m_all)
    misfit[0] = jnp.sum(shares[...])
    sum_x[...] = sum_x_in[...]
    sum_z[...] = sum_z_in[...]
    for row in chunks(ny):
        for at in range(n):
            put_padded(sum_y, (at,), row, flat(sum_y_in, (at,), row))

    def adj2(run, at):
        if at < 0:
            return wide, (at + 3,)
        return (adjoint2, (run, at)) if at < n else (wide, (at - n + 3,))

    def flow(run, at):
        if at <= 0:
            return flow_rim, (at + 2,)
        return (flow_own, (run, at)) if at < n - 1 else (flow_rim, (at - (n - 1) + 3,))

    at_chip, at_core = place(3)

    def one_run(run, carry):
        for row in chunks(ny):
            for at in range(3):
                put_padded(wide, (at_chip + at,), row, flat(of_chip, (run, at), row))
                put_padded(wide, (at_core + at,), row, flat(of_core, (run, at), row))
        for row in chunks(ny):
            mids = {at: padded(*adj2(run, at), row) for at in range(-3, n + 3)}
            for at in (-2, -1, n, n + 1):
                ref, lead = adj2(run, at)
                value = flow_in_plane(
                    faces, row, at + 2, mids[at], padded(ref, lead, row, 1), padded(ref, lead, row, -1)
                )
                value = add_product(value, flat(mx, (at + 2,), row), mids[at - 1])
                value = add_product(value, flat(mx, (at + 3,), row), mids[at + 1])
                put_padded(*flow(run, at), row, value)
            for at, side, face in ((0, -1, 2), (n - 1, n, n + 2)):
                value = add_product(
                    padded(flow_own, (run, at), row), flat(mx, (face,), row), mids[side]
                )
                put_padded(*flow(run, at), row, value)
        for row in chunks(ny):
            mids = {at: padded(*flow(run, at), row) for at in range(-2, n + 2)}
            for at in range(-1, n + 1):
                ref, lead = flow(run, at)
                total = beside(
                    mids[at - 1], mids[at + 1], padded(ref, lead, row, 1), padded(ref, lead, row, -1), mids[at]
                )
                value = each(
                    lambda a, w, f, t: a + w * f - (time_step * stiffness) * t,
                    padded(*adj2(run, at), row), flat(weight, (run, at + 1), row), mids[at], total,
                )
                put_padded(adjoint1, (at + 1,), row, value)
        for row in chunks(ny):
            mids = [padded(adjoint1, (at,), row) for at in range(n + 2)]
            chems = [padded(chem0, (run, at + 2), row) for at in range(n + 2)]
            for at in range(n + 1):
                face = add_product(
                    flat(sum_x, (at,), row), sub(mids[at + 1], mids[at]), sub(chems[at + 1], chems[at])
                )
                if at in (0, n):
                    face = add_product(
                        face, sub(padded(*adj2(run, at), row), padded(*adj2(run, at - 1), row)),
                        sub(padded(chem1, (run, at + 1), row), padded(chem1, (run, at), row)),
                    )
                put_flat(sum_x, (at,), row, face)
            for at in range(n):
                mid = mids[at + 1]
                put_padded(sum_y, (at,), row, add_product(
                    padded(sum_y, (at,), row), sub(padded(adjoint1, (at + 1,), row, 1), mid),
                    sub(padded(chem0, (run, at + 3), row, 1), chems[at + 1]),
                ))
                put_flat(sum_z, (at,), row, add_product(
                    flat(sum_z, (at,), row), sub(after_z(mid), mid), flat(step_z0, (run, at), row)
                ))
        return carry

    lax.fori_loop(0, runs, one_run, 0)
    for row in chunks(ny):
        for at in range(n):
            sides = flat(sum_z, (at,), row)
            value = each(
                lambda a, b, c, d, e, f: -0.5 * ((a + b) + (c + d) + (e + f)),
                flat(sum_x, (at,), row), flat(sum_x, (at + 1,), row),
                padded(sum_y, (at,), row), padded(sum_y, (at,), row, -1), sides, before_z(sides),
            )
            put_plain(result, (at,), row, value)


def call(kernel, outs, scratch, args, flops, scalar=None):
    moved = 4 * (sum(a.size for a in args) + sum(math.prod(o) for o in outs))
    return pl.pallas_call(
        kernel,
        out_shape=tuple(jax.ShapeDtypeStruct(o, jnp.float32) for o in outs),
        in_specs=[VMEM] * len(args),
        out_specs=tuple(SMEM if at == scalar else VMEM for at in range(len(outs))),
        scratch_shapes=[pltpu.VMEM(s, jnp.float32) for s in scratch],
        compiler_params=pltpu.CompilerParams(vmem_limit_bytes=16 * 1024 * 1024),
        cost_estimate=pl.CostEstimate(flops=flops, bytes_accessed=moved, transcendentals=0),
    )(*args)


def on_device(initial, observed, mobility):
    runs, n, ny, nz = initial.shape
    blocks = nz // LANES
    count = lax.axis_size("gx")
    over_chips = [(i, (i - 1 + 2 * (i % 2)) % count) for i in range(count)]
    over_cores = [(i, i ^ 1) for i in range(count)]
    cell = ny * nz

    def neighbours(to_chip, to_core):
        return lax.ppermute(to_chip, "gx", over_chips), lax.ppermute(to_core, "gx", over_cores)

    def lies(*lead):
        return (*lead, blocks, ny, LANES)

    def lies_padded(*lead):
        return (*lead, blocks, ny + 2 * PAD, LANES)

    if n == 4:
        near = (initial, initial)
    else:
        near = [lax.dynamic_slice_in_dim(initial, at, 4, 1) for at in place(n - 4)]
    of_chip, of_core = neighbours(*near)
    conc, mob, to_chip, to_core = call(
        own_kernel,
        (lies_padded(runs, n), lies_padded(n), (3, ny, nz), (3, ny, nz)),
        (),
        (initial, mobility),
        runs * n * cell,
    )
    m_chip, m_core = neighbours(to_chip, to_core)
    chem0, conc_rim = call(
        chem_kernel, (lies_padded(runs, n + 6), lies_padded(runs, 8)), (), (of_chip, of_core, conc),
        20 * runs * (n + 6) * cell,
    )
    *faces, state1, chem1, adjoint2, to_chip, to_core, miss_sum = call(
        forward_kernel,
        (
            lies(n + 5), lies_padded(n + 4), lies(n + 4), lies(n + 4), lies(n + 4),
            lies_padded(runs, n + 4), lies_padded(runs, n + 2), lies_padded(runs, n),
            lies(runs, 3), lies(runs, 3), (1, LANES),
        ),
        (lies_padded(6), (CHUNK, LANES)),
        (m_chip, m_core, mob, conc, conc_rim, observed, chem0),
        60 * runs * (n + 4) * cell,
    )
    of_chip, of_core = neighbours(to_chip, to_core)
    shares, flow_own, weight, step_z0, sum_x, sum_y, sum_z = call(
        middle_kernel,
        (
            (count, 1, LANES), lies_padded(runs, n), lies(runs, n + 2), lies(runs, n),
            lies(n + 1), lies(n), lies(n),
        ),
        (),
        (*faces, state1, chem0, chem1, adjoint2, miss_sum),
        40 * runs * n * cell,
    )
    shares = lax.all_to_all(shares, "gx", 0, 0)
    return call(
        backward_kernel,
        ((n, ny, nz), (1,)),
        (
            lies_padded(6), lies_padded(6), lies_padded(n + 2),
            lies(n + 1), lies_padded(n), lies(n),
        ),
        (
            of_chip, of_core, *faces, chem0, chem1, adjoint2, flow_own, weight, step_z0,
            sum_x, sum_y, sum_z, shares,
        ),
        40 * runs * (n + 2) * cell,
        scalar=1,
    )


def solution(mesh):
    placed = (
        P("group", "gx", None, None),
        P("group", "gx", None, None),
        P(("group", "gx"), None, None),
    )
    return jax.shard_map(
        on_device,
        mesh=mesh,
        in_specs=placed,
        out_specs=(P(("group", "gx"), None, None), P("group")),
        check_vma=False,
    )
```

```python
import functools
import math

import jax
import jax.numpy as jnp
from jax import lax
from jax.experimental import pallas as pl
from jax.experimental.pallas import tpu as pltpu
from jax.sharding import PartitionSpec as P

stiffness = 0.5
time_step = 0.005
VMEM = pl.BlockSpec(memory_space=pltpu.VMEM)
SMEM = pl.BlockSpec(memory_space=pltpu.SMEM)
LANES = 128
PAD = 8
CHUNK = 16


def chunks(ny):
    return range(0, ny, CHUNK)


def plain(ref, lead, row):
    return [
        ref[(*lead, pl.ds(row, CHUNK), pl.ds(at, LANES))] for at in range(0, ref.shape[-1], LANES)
    ]


def put_plain(ref, lead, row, value):
    for block, part in enumerate(value):
        ref[(*lead, pl.ds(row, CHUNK), pl.ds(block * LANES, LANES))] = part


def flat(ref, lead, row):
    return [ref[(*lead, block, pl.ds(row, CHUNK))] for block in range(ref.shape[-3])]


def put_flat(ref, lead, row, value):
    for block, part in enumerate(value):
        ref[(*lead, block, pl.ds(row, CHUNK))] = part


def padded(ref, lead, row, shift=0):
    return [ref[(*lead, block, pl.ds(PAD + row + shift, CHUNK))] for block in range(ref.shape[-3])]


def put_padded(ref, lead, row, value):
    ny = ref.shape[-2] - 2 * PAD
    for block, part in enumerate(value):
        ref[(*lead, block, pl.ds(PAD + row, CHUNK))] = part
        if row == 0:
            ref[(*lead, block, pl.ds(PAD + ny, 1))] = part[:1]
        if row + CHUNK == ny:
            ref[(*lead, block, pl.ds(PAD - 1, 1))] = part[CHUNK - 1 :]


def lane():
    return lax.broadcasted_iota(jnp.int32, (CHUNK, LANES), 1)


def after_z(value):
    turned = [pltpu.roll(part, LANES - 1, 1) for part in value]
    turned.append(turned[0])
    edge = lane() == LANES - 1
    return [jnp.where(edge, turned[at + 1], turned[at]) for at in range(len(value))]


def before_z(value):
    turned = [pltpu.roll(part, 1, 1) for part in value]
    edge = lane() == 0
    return [jnp.where(edge, turned[at - 1], turned[at]) for at in range(len(value))]


def side():
    return lax.rem(lax.axis_index("gx"), 2)


def place(count):
    at = side() * count
    return at, count - at


def each(function, *values):
    return [function(*parts) for parts in zip(*values)]


def beside(low, high, up, down, mid):
    return each(
        lambda a, b, c, d, e, f: (a + b) + (c + d) + (e + f),
        low, high, up, down, after_z(mid), before_z(mid),
    )


def potential(low, mid, high, up, down):
    return each(
        lambda c, total: c * (c * c + (6.0 * stiffness - 1.0)) - stiffness * total,
        mid, beside(low, high, up, down, mid),
    )


def flow_in_plane(faces, row, at, mid, up, down):
    _, my, mz, mz_low, m_all = faces
    return each(
        lambda a, b, c, d, e, u, v, w, x, y: (a * u + b * v) + (c * w + d * x) - e * y,
        padded(my, (at,), row), padded(my, (at,), row, -1), flat(mz, (at,), row),
        flat(mz_low, (at,), row), flat(m_all, (at,), row), up, down, after_z(mid), before_z(mid), mid,
    )


def add_product(total, a, b):
    return each(lambda t, x, y: t + x * y, total, a, b)


def sub(a, b):
    return each(lambda x, y: x - y, a, b)


def own_kernel(initial, mobility, conc, mob, to_chip, to_core):
    runs, n, ny, _ = initial.shape

    def one_run(run, carry):
        for row in chunks(ny):
            for at in range(n):
                put_padded(conc, (run, at), row, plain(initial, (run, at), row))
        return carry

    lax.fori_loop(0, runs, one_run, 0)
    for row in chunks(ny):
        for at in range(n):
            put_padded(mob, (at,), row, plain(mobility, (at,), row))
    at_chip, at_core = place(n - 3)
    to_chip[...] = mobility[pl.ds(at_chip, 3)]
    to_core[...] = mobility[pl.ds(at_core, 3)]


def chem_kernel(of_chip, of_core, own, chem0, rim):
    runs, n = own.shape[:2]
    ny = of_chip.shape[2]
    at_chip, at_core = place(4)

    def conc(run, at):
        if at < 0:
            return rim, (run, at + 4)
        return (own, (run, at)) if at < n else (rim, (run, at - n + 4))

    def one_run(run, carry):
        for row in chunks(ny):
            for at in range(4):
                put_padded(rim, (run, at_chip + at), row, plain(of_chip, (run, at), row))
                put_padded(rim, (run, at_core + at), row, plain(of_core, (run, at), row))
        for row in chunks(ny):
            mids = {at: padded(*conc(run, at), row) for at in range(-4, n + 4)}
            for at in range(-3, n + 3):
                ref, lead = conc(run, at)
                value = potential(
                    mids[at - 1], mids[at], mids[at + 1], padded(ref, lead, row, 1), padded(ref, lead, row, -1)
                )
                put_padded(chem0, (run, at + 3), row, value)
        return carry

    lax.fori_loop(0, runs, one_run, 0)


def forward_kernel(
    m_chip, m_core, m_own, own, conc_rim, observed, chem0,
    mx, my, mz, mz_low, m_all, state1, chem1, adjoint2, to_core, to_chip, miss_sum,
    rim, total,
):
    runs, n, ny, _ = observed.shape
    at_chip, at_core = place(3)
    for row in chunks(ny):
        for at in range(3):
            put_padded(rim, (at_chip + at,), row, plain(m_chip, (at,), row))
            put_padded(rim, (at_core + at,), row, plain(m_core, (at,), row))

    def mob(at):
        if at < 3:
            return rim, (at,)
        return (m_own, (at - 3,)) if at < n + 3 else (rim, (at - n,))

    mean = lambda a, b: 0.5 * (a + b)
    for row in chunks(ny):
        face = None
        for at in range(n + 5):
            mid = padded(*mob(at), row)
            face_low, face = face, each(mean, mid, padded(*mob(at + 1), row))
            put_flat(mx, (at,), row, face)
            if at == 0:
                continue
            side_y = each(mean, mid, padded(*mob(at), row, 1))
            side_y_low = each(mean, mid, padded(*mob(at), row, -1))
            side_z = each(mean, mid, after_z(mid))
            side_z_low = each(mean, mid, before_z(mid))
            put_padded(my, (at - 1,), row, side_y)
            put_flat(mz, (at - 1,), row, side_z)
            put_flat(mz_low, (at - 1,), row, side_z_low)
            put_flat(m_all, (at - 1,), row, each(
                lambda a, b, c, d, e, f: (a + b) + (c + d) + (e + f),
                face, face_low, side_y, side_y_low, side_z, side_z_low,
            ))
    faces = (mx, my, mz, mz_low, m_all)
    total[...] = jnp.zeros_like(total)

    def conc(run, at, row):
        if 0 <= at < n:
            return padded(own, (run, at), row)
        return padded(conc_rim, (run, at + 4 if at < 0 else at - n + 4), row)

    def one_run(run, carry):
        for row in chunks(ny):
            mids = [padded(chem0, (run, at), row) for at in range(n + 6)]
            for at in range(n + 4):
                flow = flow_in_plane(
                    faces, row, at, mids[at + 1],
                    padded(chem0, (run, at + 1), row, 1), padded(chem0, (run, at + 1), row, -1),
                )
                flow = add_product(flow, flat(mx, (at,), row), mids[at])
                flow = add_product(flow, flat(mx, (at + 1,), row), mids[at + 2])
                value = each(lambda a, b: a + time_step * b, conc(run, at - 2, row), flow)
                put_padded(state1, (run, at), row, value)
        for row in chunks(ny):
            mids = [padded(state1, (run, at), row) for at in range(n + 4)]
            for at in range(1, n + 3):
                value = potential(
                    mids[at - 1], mids[at], mids[at + 1],
                    padded(state1, (run, at), row, 1), padded(state1, (run, at), row, -1),
                )
                put_padded(chem1, (run, at - 1), row, value)
        squares = None
        for row in chunks(ny):
            mids = [padded(chem1, (run, at), row) for at in range(n + 2)]
            for at in range(n):
                flow = flow_in_plane(
                    faces, row, at + 2, mids[at + 1],
                    padded(chem1, (run, at + 1), row, 1), padded(chem1, (run, at + 1), row, -1),
                )
                flow = add_product(flow, flat(mx, (at + 2,), row), mids[at])
                flow = add_product(flow, flat(mx, (at + 3,), row), mids[at + 2])
                miss = each(
                    lambda a, b, c: a + time_step * b - c,
                    padded(state1, (run, at + 2), row), flow, plain(observed, (run, at), row),
                )
                for part in miss:
                    square = part * part
                    squares = square if squares is None else squares + square
                value = each(lambda a: a * (1.0 / runs), miss)
                put_padded(adjoint2, (run, at), row, value)
        at_chip, at_core = place(n - 3)
        for row in chunks(ny):
            for at in range(3):
                put_flat(to_chip, (run, at), row, padded(adjoint2, (run, at_chip + at), row))
                put_flat(to_core, (run, at), row, padded(adjoint2, (run, at_core + at), row))
        total[...] += squares
        return carry

    lax.fori_loop(0, runs, one_run, 0)
    miss_sum[...] = (0.5 / runs) * jnp.sum(total[...], axis=0, keepdims=True)


def middle_kernel(
    mx, my, mz, mz_low, m_all, state1, chem0, chem1, adjoint2, miss_sum,
    shares, flow_own, weight, step_z0, sum_x, sum_y, sum_z,
):
    runs, n = adjoint2.shape[:2]
    ny = flow_own.shape[-2] - 2 * PAD
    faces = (mx, my, mz, mz_low, m_all)
    shares[...] = jnp.broadcast_to(miss_sum[...][None], shares.shape)
    sum_x[...] = jnp.zeros_like(sum_x)
    sum_y[...] = jnp.zeros_like(sum_y)
    sum_z[...] = jnp.zeros_like(sum_z)

    def one_run(run, carry):
        for row in chunks(ny):
            mids = [padded(adjoint2, (run, at), row) for at in range(n)]
            chems = [padded(chem1, (run, at + 1), row) for at in range(n)]
            for at in range(n):
                up = padded(adjoint2, (run, at), row, 1)
                flow = flow_in_plane(faces, row, at + 2, mids[at], up, padded(adjoint2, (run, at), row, -1))
                if at > 0:
                    flow = add_product(flow, flat(mx, (at + 2,), row), mids[at - 1])
                if at < n - 1:
                    flow = add_product(flow, flat(mx, (at + 3,), row), mids[at + 1])
                    face = add_product(
                        flat(sum_x, (at + 1,), row), sub(mids[at + 1], mids[at]), sub(chems[at + 1], chems[at])
                    )
                    put_flat(sum_x, (at + 1,), row, face)
                put_padded(flow_own, (run, at), row, flow)
                put_flat(sum_y, (at,), row, add_product(
                    flat(sum_y, (at,), row), sub(up, mids[at]),
                    sub(padded(chem1, (run, at + 1), row, 1), chems[at]),
                ))
                put_flat(sum_z, (at,), row, add_product(
                    flat(sum_z, (at,), row), sub(after_z(mids[at]), mids[at]),
                    sub(after_z(chems[at]), chems[at]),
                ))
                mid = padded(chem0, (run, at + 3), row)
                put_flat(step_z0, (run, at), row, sub(after_z(mid), mid))
            for at in range(n + 2):
                value = each(
                    lambda c: time_step * (3.0 * c * c + (6.0 * stiffness - 1.0)),
                    padded(state1, (run, at + 1), row),
                )
                put_flat(weight, (run, at), row, value)
        return carry

    lax.fori_loop(0, runs, one_run, 0)


def backward_kernel(
    of_core, of_chip, mx, my, mz, mz_low, m_all, chem0, chem1, adjoint2, flow_own, weight, step_z0,
    sum_x_in, sum_y_in, sum_z_in, shares, result, misfit, wide, flow_rim, adjoint1, sum_x, sum_y, sum_z,
):
    runs, n = adjoint2.shape[:2]
    ny = flow_own.shape[-2] - 2 * PAD
    faces = (mx, my, mz, mz_low, m_all)
    misfit[0] = jnp.sum(shares[...])
    sum_x[...] = sum_x_in[...]
    sum_z[...] = sum_z_in[...]
    for row in chunks(ny):
        for at in range(n):
            put_padded(sum_y, (at,), row, flat(sum_y_in, (at,), row))

    def adj2(run, at):
        if at < 0:
            return wide, (at + 3,)
        return (adjoint2, (run, at)) if at < n else (wide, (at - n + 3,))

    def flow(run, at):
        if at <= 0:
            return flow_rim, (at + 2,)
        return (flow_own, (run, at)) if at < n - 1 else (flow_rim, (at - (n - 1) + 3,))

    at_chip, at_core = place(3)

    def one_run(run, carry):
        for row in chunks(ny):
            for at in range(3):
                put_padded(wide, (at_chip + at,), row, flat(of_chip, (run, at), row))
                put_padded(wide, (at_core + at,), row, flat(of_core, (run, at), row))
        for row in chunks(ny):
            mids = {at: padded(*adj2(run, at), row) for at in range(-3, n + 3)}
            for at in (-2, -1, n, n + 1):
                ref, lead = adj2(run, at)
                value = flow_in_plane(
                    faces, row, at + 2, mids[at], padded(ref, lead, row, 1), padded(ref, lead, row, -1)
                )
                value = add_product(value, flat(mx, (at + 2,), row), mids[at - 1])
                value = add_product(value, flat(mx, (at + 3,), row), mids[at + 1])
                put_padded(*flow(run, at), row, value)
            for at, side, face in ((0, -1, 2), (n - 1, n, n + 2)):
                value = add_product(
                    padded(flow_own, (run, at), row), flat(mx, (face,), row), mids[side]
                )
                put_padded(*flow(run, at), row, value)
        for row in chunks(ny):
            mids = {at: padded(*flow(run, at), row) for at in range(-2, n + 2)}
            for at in range(-1, n + 1):
                ref, lead = flow(run, at)
                total = beside(
                    mids[at - 1], mids[at + 1], padded(ref, lead, row, 1), padded(ref, lead, row, -1), mids[at]
                )
                value = each(
                    lambda a, w, f, t: a + w * f - (time_step * stiffness) * t,
                    padded(*adj2(run, at), row), flat(weight, (run, at + 1), row), mids[at], total,
                )
                put_padded(adjoint1, (at + 1,), row, value)
        for row in chunks(ny):
            mids = [padded(adjoint1, (at,), row) for at in range(n + 2)]
            chems = [padded(chem0, (run, at + 2), row) for at in range(n + 2)]
            for at in range(n + 1):
                face = add_product(
                    flat(sum_x, (at,), row), sub(mids[at + 1], mids[at]), sub(chems[at + 1], chems[at])
                )
                if at in (0, n):
                    face = add_product(
                        face, sub(padded(*adj2(run, at), row), padded(*adj2(run, at - 1), row)),
                        sub(padded(chem1, (run, at + 1), row), padded(chem1, (run, at), row)),
                    )
                put_flat(sum_x, (at,), row, face)
            for at in range(n):
                mid = mids[at + 1]
                put_padded(sum_y, (at,), row, add_product(
                    padded(sum_y, (at,), row), sub(padded(adjoint1, (at + 1,), row, 1), mid),
                    sub(padded(chem0, (run, at + 3), row, 1), chems[at + 1]),
                ))
                put_flat(sum_z, (at,), row, add_product(
                    flat(sum_z, (at,), row), sub(after_z(mid), mid), flat(step_z0, (run, at), row)
                ))
        return carry

    lax.fori_loop(0, runs, one_run, 0)
    for row in chunks(ny):
        for at in range(n):
            sides = flat(sum_z, (at,), row)
            value = each(
                lambda a, b, c, d, e, f: -0.5 * ((a + b) + (c + d) + (e + f)),
                flat(sum_x, (at,), row), flat(sum_x, (at + 1,), row),
                padded(sum_y, (at,), row), padded(sum_y, (at,), row, -1), sides, before_z(sides),
            )
            put_plain(result, (at,), row, value)


def call(kernel, outs, scratch, args, flops, scalar=None):
    moved = 4 * (sum(a.size for a in args) + sum(math.prod(o) for o in outs))
    return pl.pallas_call(
        kernel,
        out_shape=tuple(jax.ShapeDtypeStruct(o, jnp.float32) for o in outs),
        in_specs=[VMEM] * len(args),
        out_specs=tuple(SMEM if at == scalar else VMEM for at in range(len(outs))),
        scratch_shapes=[pltpu.VMEM(s, jnp.float32) for s in scratch],
        compiler_params=pltpu.CompilerParams(vmem_limit_bytes=16 * 1024 * 1024),
        cost_estimate=pl.CostEstimate(flops=flops, bytes_accessed=moved, transcendentals=0),
    )(*args)


def on_device(initial, observed, mobility):
    runs, n, ny, nz = initial.shape
    blocks = nz // LANES
    count = lax.axis_size("gx")
    over_chips = [(i, (i - 1 + 2 * (i % 2)) % count) for i in range(count)]
    over_cores = [(i, i ^ 1) for i in range(count)]
    cell = ny * nz

    def neighbours(to_chip, to_core):
        of_core = lax.ppermute(to_core, "gx", over_cores)
        return lax.ppermute(to_chip, "gx", over_chips), of_core

    def lies(*lead):
        return (*lead, blocks, ny, LANES)

    def lies_padded(*lead):
        return (*lead, blocks, ny + 2 * PAD, LANES)

    if n == 4:
        near = (initial, initial)
    else:
        near = [lax.dynamic_slice_in_dim(initial, at, 4, 1) for at in place(n - 4)]
    of_chip, of_core = neighbours(*near)
    conc, mob, to_chip, to_core = call(
        own_kernel,
        (lies_padded(runs, n), lies_padded(n), (3, ny, nz), (3, ny, nz)),
        (),
        (initial, mobility),
        runs * n * cell,
    )
    m_chip, m_core = neighbours(to_chip, to_core)
    chem0, conc_rim = call(
        chem_kernel, (lies_padded(runs, n + 6), lies_padded(runs, 8)), (), (of_chip, of_core, conc),
        20 * runs * (n + 6) * cell,
    )
    *faces, state1, chem1, adjoint2, to_core, to_chip, miss_sum = call(
        forward_kernel,
        (
            lies(n + 5), lies_padded(n + 4), lies(n + 4), lies(n + 4), lies(n + 4),
            lies_padded(runs, n + 4), lies_padded(runs, n + 2), lies_padded(runs, n),
            lies(runs, 3), lies(runs, 3), (1, LANES),
        ),
        (lies_padded(6), (CHUNK, LANES)),
        (m_chip, m_core, mob, conc, conc_rim, observed, chem0),
        60 * runs * (n + 4) * cell,
    )
    of_chip, of_core = neighbours(to_chip, to_core)
    shares, flow_own, weight, step_z0, sum_x, sum_y, sum_z = call(
        middle_kernel,
        (
            (count, 1, LANES), lies_padded(runs, n), lies(runs, n + 2), lies(runs, n),
            lies(n + 1), lies(n), lies(n),
        ),
        (),
        (*faces, state1, chem0, chem1, adjoint2, miss_sum),
        40 * runs * n * cell,
    )
    shares = lax.all_to_all(shares, "gx", 0, 0)
    return call(
        backward_kernel,
        ((n, ny, nz), (1,)),
        (
            lies_padded(6), lies_padded(6), lies_padded(n + 2),
            lies(n + 1), lies_padded(n), lies(n),
        ),
        (
            of_core, of_chip, *faces, chem0, chem1, adjoint2, flow_own, weight, step_z0,
            sum_x, sum_y, sum_z, shares,
        ),
        40 * runs * (n + 2) * cell,
        scalar=1,
    )


def solution(mesh):
    placed = (
        P("group", "gx", None, None),
        P("group", "gx", None, None),
        P(("group", "gx"), None, None),
    )
    return jax.shard_map(
        on_device,
        mesh=mesh,
        in_specs=placed,
        out_specs=(P(("group", "gx"), None, None), P("group")),
        check_vma=False,
    )
```

```python
import functools
import math

import jax
import jax.numpy as jnp
from jax import lax
from jax.experimental import pallas as pl
from jax.experimental.pallas import tpu as pltpu
from jax.sharding import PartitionSpec as P

stiffness = 0.5
time_step = 0.005
VMEM = pl.BlockSpec(memory_space=pltpu.VMEM)
LANES = 128
ROWS = 8
PAD = ROWS
CHUNK = 16


def chunks(ny):
    return range(0, ny, CHUNK)


def plain(ref, lead, row):
    return [
        ref[(*lead, pl.ds(row, CHUNK), pl.ds(at, LANES))] for at in range(0, ref.shape[-1], LANES)
    ]


def put_plain(ref, lead, row, value):
    for block, part in enumerate(value):
        ref[(*lead, pl.ds(row, CHUNK), pl.ds(block * LANES, LANES))] = part


def flat(ref, lead, row):
    return [ref[(*lead, block, pl.ds(row, CHUNK))] for block in range(ref.shape[-3])]


def put_flat(ref, lead, row, value):
    for block, part in enumerate(value):
        ref[(*lead, block, pl.ds(row, CHUNK))] = part


def padded(ref, lead, row, shift=0):
    return [ref[(*lead, block, pl.ds(PAD + row + shift, CHUNK))] for block in range(ref.shape[-3])]


def put_padded(ref, lead, row, value):
    ny = ref.shape[-2] - 2 * PAD
    for block, part in enumerate(value):
        ref[(*lead, block, pl.ds(PAD + row, CHUNK))] = part
        if row == 0:
            ref[(*lead, block, pl.ds(PAD + ny, 1))] = part[:1]
        if row + CHUNK == ny:
            ref[(*lead, block, pl.ds(PAD - 1, 1))] = part[CHUNK - 1 :]


def lane():
    return lax.broadcasted_iota(jnp.int32, (CHUNK, LANES), 1)


def after_z(value):
    turned = [pltpu.roll(part, LANES - 1, 1) for part in value]
    turned.append(turned[0])
    edge = lane() == LANES - 1
    return [jnp.where(edge, turned[at + 1], turned[at]) for at in range(len(value))]


def before_z(value):
    turned = [pltpu.roll(part, 1, 1) for part in value]
    edge = lane() == 0
    return [jnp.where(edge, turned[at - 1], turned[at]) for at in range(len(value))]


def side():
    return lax.rem(lax.axis_index("gx"), 2)


def either(first, second):
    return first + side() * (second - first)


class Line:
    def __init__(self, *parts):
        self.parts = parts

    def __call__(self, at, *lead):
        for ref, first, last in self.parts:
            if first <= at <= last:
                return ref, (*lead, at - first)
        raise IndexError(at)


def each(function, *values):
    return [function(*parts) for parts in zip(*values)]


def beside(low, high, up, down, mid):
    return each(
        lambda a, b, c, d, e, f: (a + b) + (c + d) + (e + f),
        low, high, up, down, after_z(mid), before_z(mid),
    )


def potential(low, mid, high, up, down):
    return each(
        lambda c, total: c * (c * c + (6.0 * stiffness - 1.0)) - stiffness * total,
        mid, beside(low, high, up, down, mid),
    )


class Faces:
    def __init__(self, n, refs):
        mx_a, my_a, mz_a, mz_low_a, all_a, *late = refs
        two = lambda ref, first, last, at: ((ref, first, last), *(((late[at], last + 1, n + 1),) if late else ()))
        self.mx = Line(*two(mx_a, -3, n - 2, 0))
        self.my = Line(*two(my_a, -2, n - 1, 1))
        self.mz = Line(*two(mz_a, -2, n - 1, 2))
        self.mz_low = Line(*two(mz_low_a, -2, n - 1, 3))
        self.all = Line(*two(all_a, -2, n - 2, 4))

    def flow(self, row, at, mid, up, down, low=None, high=None):
        total = each(
            lambda a, b, c, d, e, u, v, w, x, y: (a * u + b * v) + (c * w + d * x) - e * y,
            padded(*self.my(at), row), padded(*self.my(at), row, -1), flat(*self.mz(at), row),
            flat(*self.mz_low(at), row), flat(*self.all(at), row), up, down, after_z(mid), before_z(mid), mid,
        )
        if low is not None:
            total = add_product(total, flat(*self.mx(at - 1), row), low)
        if high is not None:
            total = add_product(total, flat(*self.mx(at), row), high)
        return total


def add_product(total, a, b):
    return each(lambda t, x, y: t + x * y, total, a, b)


def sub(a, b):
    return each(lambda x, y: x - y, a, b)


def own_kernel(initial, mobility, conc, mob, to_chip, to_core):
    runs, n, ny, _ = initial.shape
    place = [either(n - 1 - at, at) for at in range(n)]

    def one_run(run, carry):
        for row in chunks(ny):
            for at in range(n):
                put_padded(conc, (run, at), row, plain(initial, (run, place[at]), row))
        return carry

    lax.fori_loop(0, runs, one_run, 0)
    for row in chunks(ny):
        for at in range(n):
            value = plain(mobility, (place[at],), row)
            put_padded(mob, (at,), row, value)
            if at < 3:
                put_flat(to_core, (at,), row, value)
            if at >= n - 3:
                put_flat(to_chip, (n - 1 - at,), row, value)


def mean(a, b):
    return 0.5 * (a + b)


def put_faces(row, mob, places, my, mz, mz_low):
    for at in places:
        mid = padded(*mob(at), row)
        put_padded(*my(at), row, each(mean, mid, padded(*mob(at), row, 1)))
        put_flat(*mz(at), row, each(mean, mid, after_z(mid)))
        put_flat(*mz_low(at), row, each(mean, mid, before_z(mid)))


def put_all(row, faces, places):
    for at in places:
        put_flat(*faces.all(at), row, each(
            lambda a, b, c, d, e, f: (a + b) + (c + d) + (e + f),
            flat(*faces.mx(at - 1), row), flat(*faces.mx(at), row), padded(*faces.my(at), row),
            padded(*faces.my(at), row, -1), flat(*faces.mz(at), row), flat(*faces.mz_low(at), row),
        ))


def put_potential(row, field, run, places, target):
    mids = {at: padded(*field(at, run), row) for at in range(places[0] - 1, places[-1] + 2)}
    for at in places:
        value = potential(
            mids[at - 1], mids[at], mids[at + 1],
            padded(*field(at, run), row, 1), padded(*field(at, run), row, -1),
        )
        put_padded(*target(at, run), row, value)


def put_step(row, faces, chem, state, run, places, target):
    mids = {at: padded(*chem(at, run), row) for at in range(places[0] - 1, places[-1] + 2)}
    for at in places:
        flow = faces.flow(
            row, at, mids[at], padded(*chem(at, run), row, 1), padded(*chem(at, run), row, -1),
            mids[at - 1], mids[at + 1],
        )
        value = each(lambda a, b: a + time_step * b, padded(*state(at, run), row), flow)
        target(at, value)


def put_miss(row, runs, observed, place, run, at, value, adjoint2):
    miss = sub(value, plain(observed, (run, place[at]), row))
    adjoint = each(lambda a: a * (1.0 / runs), miss)
    put_padded(*adjoint2(at, run), row, adjoint)
    return adjoint, sum(part * part for part in miss)


def core_kernel(of_core, m_core, conc_own, mob_own, conc_core, chem0, mx, my, mz, mz_low, m_all, rim):
    runs, n = conc_own.shape[:2]
    ny = of_core.shape[2]
    mob = Line((rim, -3, -1), (mob_own, 0, n - 1))
    faces = Faces(n, (mx, my, mz, mz_low, m_all))
    for row in chunks(ny):
        for at in range(3):
            put_padded(rim, (2 - at,), row, flat(m_core, (at,), row))
    for row in chunks(ny):
        mids = [padded(*mob(at), row) for at in range(-3, n)]
        for at in range(n + 2):
            put_flat(mx, (at,), row, each(mean, mids[at], mids[at + 1]))
        put_faces(row, mob, range(-2, n), faces.my, faces.mz, faces.mz_low)
    for row in chunks(ny):
        put_all(row, faces, range(-2, n - 1))
    place = [either(at, 3 - at) for at in range(4)]
    conc = Line((conc_core, -4, -1), (conc_own, 0, n - 1))

    def one_run(run, carry):
        for row in chunks(ny):
            for at in range(4):
                put_padded(conc_core, (run, 3 - at), row, plain(of_core, (run, place[at]), row))
        for row in chunks(ny):
            put_potential(row, conc, run, range(-3, n - 1), Line((chem0, -3, n - 2)))
        return carry

    lax.fori_loop(0, runs, one_run, 0)


def chip_kernel(
    of_chip, conc_own, conc_core, chem0_a, observed, mx, my, mz, mz_low, m_all,
    conc_chip, chem0_b, state1_a, chem1_a, adjoint2_a, squares,
):
    runs, n = conc_own.shape[:2]
    ny = observed.shape[2]
    faces = Faces(n, (mx, my, mz, mz_low, m_all))
    message = [either(3 - at, at) for at in range(4)]
    place = [either(n - 1 - at, at) for at in range(n)]
    conc = Line((conc_core, -4, -1), (conc_own, 0, n - 1), (conc_chip, n, n + 3))
    chem0 = Line((chem0_a, -3, n - 2), (chem0_b, n - 1, n + 2))
    state1 = Line((state1_a, -2, n - 2))
    chem1 = Line((chem1_a, -1, n - 3))
    adjoint2 = Line((adjoint2_a, 0, n - 4))
    squares[...] = jnp.zeros_like(squares)

    def one_run(run, carry):
        for row in chunks(ny):
            for at in range(4):
                put_padded(conc_chip, (run, at), row, plain(of_chip, (run, message[at]), row))
        for row in chunks(ny):
            put_potential(row, conc, run, range(n - 1, n + 3), chem0)
        for row in chunks(ny):
            put_step(
                row, faces, chem0, conc, run, range(-2, n - 1),
                lambda at, value: put_padded(*state1(at, run), row, value),
            )
        for row in chunks(ny):
            put_potential(row, state1, run, range(-1, n - 2), chem1)
        for row in chunks(ny):

            def target(at, value):
                squares[...] += put_miss(row, runs, observed, place, run, at, value, adjoint2)[1]

            put_step(row, faces, chem1, state1, run, range(0, n - 3), target)
        return carry

    lax.fori_loop(0, runs, one_run, 0)


def forward_kernel(
    m_chip, mob_own, conc_own, conc_chip, chem0_a, chem0_b, state1_a, chem1_a, adjoint2_a, squares, observed,
    mx_a, my_a, mz_a, mz_low_a, all_a,
    mx_b, my_b, mz_b, mz_low_b, all_b, state1_b, chem1_b, adjoint2_b, to_core, to_chip, share, rim, total,
):
    runs, n = conc_own.shape[:2]
    ny = observed.shape[2]
    faces = Faces(n, (mx_a, my_a, mz_a, mz_low_a, all_a, mx_b, my_b, mz_b, mz_low_b, all_b))
    mob = Line((mob_own, 0, n - 1), (rim, n, n + 2))
    place = [either(n - 1 - at, at) for at in range(n)]
    conc = Line((conc_own, 0, n - 1), (conc_chip, n, n + 3))
    chem0 = Line((chem0_a, -3, n - 2), (chem0_b, n - 1, n + 2))
    state1 = Line((state1_a, -2, n - 2), (state1_b, n - 1, n + 1))
    chem1 = Line((chem1_a, -1, n - 3), (chem1_b, n - 2, n))
    adjoint2 = Line((adjoint2_a, 0, n - 4), (adjoint2_b, n - 3, n - 1))
    for row in chunks(ny):
        for at in range(3):
            put_padded(rim, (at,), row, flat(m_chip, (at,), row))
    for row in chunks(ny):
        mids = [padded(*mob(at), row) for at in range(n - 1, n + 3)]
        for at in range(3):
            put_flat(mx_b, (at,), row, each(mean, mids[at], mids[at + 1]))
        put_faces(row, mob, range(n, n + 2), faces.my, faces.mz, faces.mz_low)
    for row in chunks(ny):
        put_all(row, faces, range(n - 1, n + 2))
    total[...] = squares[...]

    def one_run(run, carry):
        for row in chunks(ny):
            put_step(
                row, faces, chem0, conc, run, range(n - 1, n + 2),
                lambda at, value: put_padded(*state1(at, run), row, value),
            )
        for row in chunks(ny):
            put_potential(row, state1, run, range(n - 2, n + 1), chem1)
        for row in chunks(ny):

            def target(at, value):
                adjoint, square = put_miss(row, runs, observed, place, run, at, value, adjoint2)
                total[...] += square
                put_flat(to_chip, (run, n - 1 - at), row, adjoint)
                if at < 3:
                    put_flat(to_core, (run, at), row, adjoint)

            put_step(row, faces, chem1, state1, run, range(n - 3, n), target)
            for at in range(min(3, n - 3)):
                put_flat(to_core, (run, at), row, padded(*adjoint2(at, run), row))
        return carry

    lax.fori_loop(0, runs, one_run, 0)
    columns = (0.5 / runs) * jnp.sum(total[...], axis=0, keepdims=True)
    mine = jnp.broadcast_to(jnp.sum(columns, axis=1, keepdims=True), share.shape)
    share[...] = mine
    to_core[0, 0, 0, ny:] = mine


def put_adjoint1(row, flow, adjoint2, run, places, weight, target):
    mids = {at: padded(*flow(at, run), row) for at in range(places[0] - 1, places[-1] + 2)}
    for at in places:
        total = beside(
            mids[at - 1], mids[at + 1], padded(*flow(at, run), row, 1), padded(*flow(at, run), row, -1), mids[at]
        )
        value = each(
            lambda a, w, f, t: a + w * f - (time_step * stiffness) * t,
            padded(*adjoint2(at, run), row), weight(at), mids[at], total,
        )
        put_padded(*target(at, run), row, value)


def slope(state):
    return each(lambda c: time_step * (3.0 * c * c + (6.0 * stiffness - 1.0)), state)


def step_x(field, run, at, row):
    return sub(padded(*field(at + 1, run), row), padded(*field(at, run), row))


def step_y(field, run, at, row):
    return sub(padded(*field(at, run), row, 1), padded(*field(at, run), row))


def step_z(field, run, at, row):
    mid = padded(*field(at, run), row)
    return sub(after_z(mid), mid)


def early_kernel(
    of_core, mx_a, my_a, mz_a, mz_low_a, all_a, mx_b, my_b, mz_b, mz_low_b, all_b,
    chem0_a, chem0_b, state1_a, state1_b, chem1_a, chem1_b, adjoint2_a, adjoint2_b,
    share_in, flow_a, flow_part, adjoint1_a, weight_b, step_z_b, part, sum_x_b, sum_y_b, sum_z_b, share,
    rim, sum_x, sum_y, sum_z,
):
    share[...] = share_in[...]
    runs = of_core.shape[0]
    n = part.shape[0] + 2
    ny = part.shape[-2]
    faces = Faces(n, (mx_a, my_a, mz_a, mz_low_a, all_a, mx_b, my_b, mz_b, mz_low_b, all_b))
    chem0 = Line((chem0_a, -3, n - 2), (chem0_b, n - 1, n + 2))
    state1 = Line((state1_a, -2, n - 2), (state1_b, n - 1, n + 1))
    chem1 = Line((chem1_a, -1, n - 3), (chem1_b, n - 2, n))
    adjoint2 = Line((rim, -3, -1), (adjoint2_a, 0, n - 4), (adjoint2_b, n - 3, n - 1))
    flow = Line((flow_a, -2, n - 2), (flow_part, n - 1, n - 1))
    adjoint1 = Line((adjoint1_a, -1, n - 3))
    for sums in (sum_x, sum_y, sum_z):
        sums[...] = jnp.zeros_like(sums)

    def one_run(run, carry):
        for row in chunks(ny):
            for at in range(3):
                put_padded(rim, (run, 2 - at), row, flat(of_core, (run, at), row))
        for row in chunks(ny):
            mids = {at: padded(*adjoint2(at, run), row) for at in range(-3, n)}
            for at in range(-2, n):
                value = faces.flow(
                    row, at, mids[at], padded(*adjoint2(at, run), row, 1), padded(*adjoint2(at, run), row, -1),
                    mids[at - 1], mids.get(at + 1),
                )
                put_padded(*flow(at, run), row, value)
        for row in chunks(ny):
            put_adjoint1(
                row, flow, adjoint2, run, range(-1, n - 2),
                lambda at: slope(padded(*state1(at, run), row)), adjoint1,
            )
            for at in range(n - 2, n + 1):
                put_flat(weight_b, (run, at - (n - 2)), row, slope(padded(*state1(at, run), row)))
        for row in chunks(ny):
            for at in range(-1, n - 1):
                total = add_product(
                    flat(sum_x, (at + 1,), row), step_x(adjoint2, run, at, row), step_x(chem1, run, at, row)
                )
                if at < n - 3:
                    total = add_product(total, step_x(adjoint1, run, at, row), step_x(chem0, run, at, row))
                put_flat(sum_x, (at + 1,), row, total)
            for at in range(n):
                total_y = add_product(
                    padded(sum_y, (at,), row), step_y(adjoint2, run, at, row), step_y(chem1, run, at, row)
                )
                total_z = add_product(
                    flat(sum_z, (at,), row), step_z(adjoint2, run, at, row), step_z(chem1, run, at, row)
                )
                slant = step_z(chem0, run, at, row)
                if at < n - 2:
                    total_y = add_product(total_y, step_y(adjoint1, run, at, row), step_y(chem0, run, at, row))
                    total_z = add_product(total_z, step_z(adjoint1, run, at, row), slant)
                else:
                    put_flat(step_z_b, (run, at - (n - 2)), row, slant)
                put_padded(sum_y, (at,), row, total_y)
                put_flat(sum_z, (at,), row, total_z)
        return carry

    lax.fori_loop(0, runs, one_run, 0)
    for row in chunks(ny):
        for at in range(n - 2):
            sides = flat(sum_z, (at,), row)
            value = each(
                lambda a, b, c, d, e: -0.5 * ((a + b) + (c + d) + e),
                padded(sum_y, (at,), row), padded(sum_y, (at,), row, -1), sides, before_z(sides),
                flat(sum_x, (at,), row),
            )
            if at < n - 3:
                value = each(lambda a, b: a - 0.5 * b, value, flat(sum_x, (at + 1,), row))
            put_flat(part, (at,), row, value)
        for at in range(2):
            put_flat(sum_x_b, (at,), row, flat(sum_x, (n - 2 + at,), row))
            put_flat(sum_y_b, (at,), row, padded(sum_y, (n - 2 + at,), row))
            put_flat(sum_z_b, (at,), row, flat(sum_z, (n - 2 + at,), row))


def late_kernel(
    of_chip, mx_a, my_a, mz_a, mz_low_a, all_a, mx_b, my_b, mz_b, mz_low_b, all_b,
    chem0_a, chem0_b, chem1_b, adjoint2_b, flow_a, flow_part, adjoint1_a, weight_b, step_z_b,
    part, sum_x_b, sum_y_b, sum_z_b, share_in, result, share, rim, flow_b, adjoint1_b, sum_x, sum_y, sum_z,
):
    share[...] = share_in[...]
    runs = of_chip.shape[0]
    n, ny, _ = result.shape
    faces = Faces(n, (mx_a, my_a, mz_a, mz_low_a, all_a, mx_b, my_b, mz_b, mz_low_b, all_b))
    place = [either(n - 1 - at, at) for at in range(n)]
    chem0 = Line((chem0_a, -3, n - 2), (chem0_b, n - 1, n + 2))
    chem1 = Line((chem1_b, n - 2, n))
    adjoint2 = Line((adjoint2_b, n - 3, n - 1), (rim, n, n + 2))
    flow = Line((flow_a, -2, n - 2), (flow_b, n - 1, n + 1))
    adjoint1 = Line((adjoint1_a, -1, n - 3), (adjoint1_b, n - 2, n))
    for row in chunks(ny):
        for at in range(2):
            put_flat(sum_x, (at,), row, flat(sum_x_b, (at,), row))
            put_padded(sum_y, (at,), row, flat(sum_y_b, (at,), row))
            put_flat(sum_z, (at,), row, flat(sum_z_b, (at,), row))
    sum_x[2] = jnp.zeros_like(sum_x[2])

    def one_run(run, carry):
        for row in chunks(ny):
            for at in range(3):
                put_padded(rim, (run, at), row, flat(of_chip, (run, at), row))
        for row in chunks(ny):
            mids = {at: padded(*adjoint2(at, run), row) for at in range(n - 1, n + 3)}
            value = add_product(padded(flow_part, (run, 0), row), flat(*faces.mx(n - 1), row), mids[n])
            put_padded(*flow(n - 1, run), row, value)
            for at in range(n, n + 2):
                value = faces.flow(
                    row, at, mids[at], padded(*adjoint2(at, run), row, 1), padded(*adjoint2(at, run), row, -1),
                    mids[at - 1], mids[at + 1],
                )
                put_padded(*flow(at, run), row, value)
        for row in chunks(ny):
            put_adjoint1(
                row, flow, adjoint2, run, range(n - 2, n + 1),
                lambda at: flat(weight_b, (run, at - (n - 2)), row), adjoint1,
            )
        for row in chunks(ny):
            for at in range(n - 3, n):
                total = add_product(
                    flat(sum_x, (at - (n - 3),), row), step_x(adjoint1, run, at, row), step_x(chem0, run, at, row)
                )
                if at == n - 1:
                    total = add_product(total, step_x(adjoint2, run, at, row), step_x(chem1, run, at, row))
                put_flat(sum_x, (at - (n - 3),), row, total)
            for at in range(n - 2, n):
                to = (at - (n - 2),)
                put_padded(sum_y, to, row, add_product(
                    padded(sum_y, to, row), step_y(adjoint1, run, at, row), step_y(chem0, run, at, row)
                ))
                put_flat(sum_z, to, row, add_product(
                    flat(sum_z, to, row), step_z(adjoint1, run, at, row), flat(step_z_b, (run, *to), row)
                ))
        return carry

    lax.fori_loop(0, runs, one_run, 0)
    for row in chunks(ny):
        for at in range(n - 2):
            value = flat(part, (at,), row)
            if at == n - 3:
                value = each(lambda a, b: a - 0.5 * b, value, flat(sum_x, (0,), row))
            put_plain(result, (place[at],), row, value)
        for at in range(2):
            sides = flat(sum_z, (at,), row)
            value = each(
                lambda a, b, c, d, e, f: -0.5 * ((a + b) + (c + d) + (e + f)),
                flat(sum_x, (at,), row), flat(sum_x, (at + 1,), row),
                padded(sum_y, (at,), row), padded(sum_y, (at,), row, -1), sides, before_z(sides),
            )
            put_plain(result, (place[n - 2 + at],), row, value)


def call(kernel, outs, scratch, args, flops):
    moved = 4 * (sum(a.size for a in args) + sum(math.prod(o) for o in outs))
    return pl.pallas_call(
        kernel,
        out_shape=tuple(jax.ShapeDtypeStruct(o, jnp.float32) for o in outs),
        in_specs=[VMEM] * len(args),
        out_specs=tuple([VMEM] * len(outs)),
        scratch_shapes=[pltpu.VMEM(s, jnp.float32) for s in scratch],
        compiler_params=pltpu.CompilerParams(vmem_limit_bytes=16 * 1024 * 1024),
        cost_estimate=pl.CostEstimate(flops=flops, bytes_accessed=moved, transcendentals=0),
    )(*args)


def on_device(initial, observed, mobility):
    runs, n, ny, nz = initial.shape
    blocks = nz // LANES
    count = lax.axis_size("gx")
    over_chips = [(i, (i - 1 + 2 * (i % 2)) % count) for i in range(count)]
    over_cores = [(i, i ^ 1) for i in range(count)]
    cell = ny * nz

    def neighbours(to_chip, to_core):
        of_core = lax.ppermute(to_core, "gx", over_cores)
        return lax.ppermute(to_chip, "gx", over_chips), of_core

    def lies(*lead):
        return (*lead, blocks, ny, LANES)

    def lies_padded(*lead):
        return (*lead, blocks, ny + 2 * PAD, LANES)

    if n == 4:
        near = (initial, initial)
    else:
        near = [lax.dynamic_slice_in_dim(initial, at, 4, 1) for at in (either(0, n - 4), either(n - 4, 0))]
    of_chip, of_core = neighbours(*near)
    conc, mob, to_chip, to_core = call(
        own_kernel, (lies_padded(runs, n), lies_padded(n), lies(3), lies(3)), (), (initial, mobility),
        runs * n * cell,
    )
    m_chip, m_core = neighbours(to_chip, to_core)
    conc_core, chem0_a, *faces_a = call(
        core_kernel,
        (
            lies_padded(runs, 4), lies_padded(runs, n + 2),
            lies(n + 2), lies_padded(n + 2), lies(n + 2), lies(n + 2), lies(n + 1),
        ),
        (lies_padded(3),),
        (of_core, m_core, conc, mob),
        20 * runs * (n + 2) * cell,
    )
    conc_chip, chem0_b, state1_a, chem1_a, adjoint2_a, squares = call(
        chip_kernel,
        (
            lies_padded(runs, 4), lies_padded(runs, 4), lies_padded(runs, n + 1),
            lies_padded(runs, n - 1), lies_padded(runs, n - 3), (CHUNK, LANES),
        ),
        (),
        (of_chip, conc, conc_core, chem0_a, observed, *faces_a),
        60 * runs * (n - 1) * cell,
    )
    *faces_b, state1_b, chem1_b, adjoint2_b, to_core, to_chip, share = call(
        forward_kernel,
        (
            lies(3), lies_padded(2), lies(2), lies(2), lies(3),
            lies_padded(runs, 3), lies_padded(runs, 3), lies_padded(runs, 3),
            (runs, 3, blocks, ny + ROWS, LANES), lies(runs, 3), (ROWS, LANES),
        ),
        (lies_padded(3), (CHUNK, LANES)),
        (m_chip, mob, conc, conc_chip, chem0_a, chem0_b, state1_a, chem1_a, adjoint2_a, squares, observed, *faces_a),
        60 * runs * 3 * cell,
    )
    faces = (*faces_a, *faces_b)
    of_chip, of_core = neighbours(to_chip, to_core)
    hops = []
    if count & (count - 1):
        share = lax.psum(share, "gx")
    else:
        share = share + of_core[0, 0, 0, ny:]
        hops = [1 << bit for bit in range(count.bit_length() - 1, 0, -1) if 1 << bit < count]

    def hop_of(value, hop):
        return lax.ppermute(value, "gx", [(i, i ^ hop) for i in range(count)])

    far = hop_of(share, hops[0]) if hops else None
    flow_a, flow_part, adjoint1_a, weight_b, step_z_b, part, *sums_b, share = call(
        early_kernel,
        (
            lies_padded(runs, n + 1), lies_padded(runs, 1), lies_padded(runs, n - 1), lies(runs, 3), lies(runs, 2),
            lies(n - 2), lies(2), lies(2), lies(2), (ROWS, LANES),
        ),
        (lies_padded(runs, 3), lies(n), lies_padded(n), lies(n)),
        (of_core, *faces, chem0_a, chem0_b, state1_a, state1_b, chem1_a, chem1_b, adjoint2_a, adjoint2_b, share),
        60 * runs * n * cell,
    )
    for hop in hops[1:]:
        share = share + far
        far = hop_of(share, hop)
    result, share = call(
        late_kernel,
        ((n, ny, nz), (ROWS, LANES)),
        (
            lies_padded(runs, 3), lies_padded(runs, 3), lies_padded(runs, 3),
            lies(3), lies_padded(2), lies(2),
        ),
        (
            of_chip, *faces, chem0_a, chem0_b, chem1_b, adjoint2_b, flow_a, flow_part, adjoint1_a,
            weight_b, step_z_b, part, *sums_b, share,
        ),
        60 * runs * 3 * cell,
    )
    if hops:
        share = share + far
    return (result, share[0, :1])


def solution(mesh):
    placed = (
        P("group", "gx", None, None),
        P("group", "gx", None, None),
        P(("group", "gx"), None, None),
    )
    return jax.shard_map(
        on_device,
        mesh=mesh,
        in_specs=placed,
        out_specs=(P(("group", "gx"), None, None), P("group")),
        check_vma=False,
    )
```

```python
import functools
import math

import jax
import jax.numpy as jnp
from jax import lax
from jax.experimental import pallas as pl
from jax.experimental.pallas import tpu as pltpu
from jax.sharding import PartitionSpec as P

stiffness = 0.5
time_step = 0.005
VMEM = pl.BlockSpec(memory_space=pltpu.VMEM)
LANES = 128
ROWS = 8
PAD = ROWS
CHUNK = 16


def chunks(ny):
    return range(0, ny, CHUNK)


def plain(ref, lead, row):
    return [
        ref[(*lead, pl.ds(row, CHUNK), pl.ds(at, LANES))] for at in range(0, ref.shape[-1], LANES)
    ]


def put_plain(ref, lead, row, value):
    for block, part in enumerate(value):
        ref[(*lead, pl.ds(row, CHUNK), pl.ds(block * LANES, LANES))] = part


def flat(ref, lead, row):
    return [ref[(*lead, block, pl.ds(row, CHUNK))] for block in range(ref.shape[-3])]


def put_flat(ref, lead, row, value):
    for block, part in enumerate(value):
        ref[(*lead, block, pl.ds(row, CHUNK))] = part


def padded(ref, lead, row, shift=0):
    return [ref[(*lead, block, pl.ds(PAD + row + shift, CHUNK))] for block in range(ref.shape[-3])]


def put_padded(ref, lead, row, value):
    ny = ref.shape[-2] - 2 * PAD
    for block, part in enumerate(value):
        ref[(*lead, block, pl.ds(PAD + row, CHUNK))] = part
        if row == 0:
            ref[(*lead, block, pl.ds(PAD + ny, 1))] = part[:1]
        if row + CHUNK == ny:
            ref[(*lead, block, pl.ds(PAD - 1, 1))] = part[CHUNK - 1 :]


def lane():
    return lax.broadcasted_iota(jnp.int32, (CHUNK, LANES), 1)


def after_z(value):
    turned = [pltpu.roll(part, LANES - 1, 1) for part in value]
    turned.append(turned[0])
    edge = lane() == LANES - 1
    return [jnp.where(edge, turned[at + 1], turned[at]) for at in range(len(value))]


def before_z(value):
    turned = [pltpu.roll(part, 1, 1) for part in value]
    edge = lane() == 0
    return [jnp.where(edge, turned[at - 1], turned[at]) for at in range(len(value))]


def side():
    return lax.rem(lax.axis_index("gx"), 2)


def either(first, second):
    return first + side() * (second - first)


class Line:
    def __init__(self, *parts):
        self.parts = parts

    def __call__(self, at, *lead):
        for ref, first, last in self.parts:
            if first <= at <= last:
                return ref, (*lead, at - first)
        raise IndexError(at)


def each(function, *values):
    return [function(*parts) for parts in zip(*values)]


def beside(low, high, up, down, mid):
    return each(
        lambda a, b, c, d, e, f: (a + b) + (c + d) + (e + f),
        low, high, up, down, after_z(mid), before_z(mid),
    )


def potential(low, mid, high, up, down):
    return each(
        lambda c, total: c * (c * c + (6.0 * stiffness - 1.0)) - stiffness * total,
        mid, beside(low, high, up, down, mid),
    )


class Faces:
    def __init__(self, n, refs):
        mx_a, my_a, mz_a, mz_low_a, all_a, *late = refs
        two = lambda ref, first, last, at: ((ref, first, last), *(((late[at], last + 1, n + 1),) if late else ()))
        self.mx = Line(*two(mx_a, -3, n - 2, 0))
        self.my = Line(*two(my_a, -2, n - 1, 1))
        self.mz = Line(*two(mz_a, -2, n - 1, 2))
        self.mz_low = Line(*two(mz_low_a, -2, n - 1, 3))
        self.all = Line(*two(all_a, -2, n - 2, 4))

    def flow(self, row, at, mid, up, down, low=None, high=None):
        total = each(
            lambda a, b, c, d, e, u, v, w, x, y: (a * u + b * v) + (c * w + d * x) - e * y,
            padded(*self.my(at), row), padded(*self.my(at), row, -1), flat(*self.mz(at), row),
            flat(*self.mz_low(at), row), flat(*self.all(at), row), up, down, after_z(mid), before_z(mid), mid,
        )
        if low is not None:
            total = add_product(total, flat(*self.mx(at - 1), row), low)
        if high is not None:
            total = add_product(total, flat(*self.mx(at), row), high)
        return total


def add_product(total, a, b):
    return each(lambda t, x, y: t + x * y, total, a, b)


def sub(a, b):
    return each(lambda x, y: x - y, a, b)


def own_kernel(initial, mobility, conc, mob, to_chip, to_core):
    runs, n, ny, _ = initial.shape
    place = [either(n - 1 - at, at) for at in range(n)]

    def one_run(run, carry):
        for row in chunks(ny):
            for at in range(n):
                put_padded(conc, (run, at), row, plain(initial, (run, place[at]), row))
        return carry

    lax.fori_loop(0, runs, one_run, 0)
    for row in chunks(ny):
        for at in range(n):
            value = plain(mobility, (place[at],), row)
            put_padded(mob, (at,), row, value)
            if at < 3:
                put_flat(to_core, (at,), row, value)
            if at >= n - 3:
                put_flat(to_chip, (n - 1 - at,), row, value)


def mean(a, b):
    return 0.5 * (a + b)


def put_faces(row, mob, places, my, mz, mz_low):
    for at in places:
        mid = padded(*mob(at), row)
        put_padded(*my(at), row, each(mean, mid, padded(*mob(at), row, 1)))
        put_flat(*mz(at), row, each(mean, mid, after_z(mid)))
        put_flat(*mz_low(at), row, each(mean, mid, before_z(mid)))


def put_all(row, faces, places):
    for at in places:
        put_flat(*faces.all(at), row, each(
            lambda a, b, c, d, e, f: (a + b) + (c + d) + (e + f),
            flat(*faces.mx(at - 1), row), flat(*faces.mx(at), row), padded(*faces.my(at), row),
            padded(*faces.my(at), row, -1), flat(*faces.mz(at), row), flat(*faces.mz_low(at), row),
        ))


def put_potential(row, field, run, places, target):
    mids = {at: padded(*field(at, run), row) for at in range(places[0] - 1, places[-1] + 2)}
    for at in places:
        value = potential(
            mids[at - 1], mids[at], mids[at + 1],
            padded(*field(at, run), row, 1), padded(*field(at, run), row, -1),
        )
        put_padded(*target(at, run), row, value)


def put_step(row, faces, chem, state, run, places, target):
    mids = {at: padded(*chem(at, run), row) for at in range(places[0] - 1, places[-1] + 2)}
    for at in places:
        flow = faces.flow(
            row, at, mids[at], padded(*chem(at, run), row, 1), padded(*chem(at, run), row, -1),
            mids[at - 1], mids[at + 1],
        )
        value = each(lambda a, b: a + time_step * b, padded(*state(at, run), row), flow)
        target(at, value)


def put_miss(row, runs, observed, place, run, at, value, adjoint2):
    miss = sub(value, plain(observed, (run, place[at]), row))
    adjoint = each(lambda a: a * (1.0 / runs), miss)
    put_padded(*adjoint2(at, run), row, adjoint)
    return adjoint, sum(part * part for part in miss)


def core_kernel(of_core, m_core, conc_own, mob_own, conc_core, chem0, mx, my, mz, mz_low, m_all, rim):
    runs, n = conc_own.shape[:2]
    ny = of_core.shape[2]
    mob = Line((rim, -3, -1), (mob_own, 0, n - 1))
    faces = Faces(n, (mx, my, mz, mz_low, m_all))
    for row in chunks(ny):
        for at in range(3):
            put_padded(rim, (2 - at,), row, flat(m_core, (at,), row))
    for row in chunks(ny):
        mids = [padded(*mob(at), row) for at in range(-3, n)]
        for at in range(n + 2):
            put_flat(mx, (at,), row, each(mean, mids[at], mids[at + 1]))
        put_faces(row, mob, range(-2, n), faces.my, faces.mz, faces.mz_low)
    for row in chunks(ny):
        put_all(row, faces, range(-2, n - 1))
    place = [either(at, 3 - at) for at in range(4)]
    conc = Line((conc_core, -4, -1), (conc_own, 0, n - 1))

    def one_run(run, carry):
        for row in chunks(ny):
            for at in range(4):
                put_padded(conc_core, (run, 3 - at), row, plain(of_core, (run, place[at]), row))
        for row in chunks(ny):
            put_potential(row, conc, run, range(-3, n - 1), Line((chem0, -3, n - 2)))
        return carry

    lax.fori_loop(0, runs, one_run, 0)


def chip_kernel(
    of_chip, conc_own, conc_core, chem0_a, observed, mx, my, mz, mz_low, m_all,
    conc_chip, chem0_b, state1_a, chem1_a, adjoint2_a, squares,
):
    runs, n = conc_own.shape[:2]
    ny = observed.shape[2]
    faces = Faces(n, (mx, my, mz, mz_low, m_all))
    message = [either(3 - at, at) for at in range(4)]
    place = [either(n - 1 - at, at) for at in range(n)]
    conc = Line((conc_core, -4, -1), (conc_own, 0, n - 1), (conc_chip, n, n + 3))
    chem0 = Line((chem0_a, -3, n - 2), (chem0_b, n - 1, n + 2))
    state1 = Line((state1_a, -2, n - 2))
    chem1 = Line((chem1_a, -1, n - 3))
    adjoint2 = Line((adjoint2_a, 0, n - 4))
    squares[...] = jnp.zeros_like(squares)

    def one_run(run, carry):
        for row in chunks(ny):
            for at in range(4):
                put_padded(conc_chip, (run, at), row, plain(of_chip, (run, message[at]), row))
        for row in chunks(ny):
            put_potential(row, conc, run, range(n - 1, n + 3), chem0)
        for row in chunks(ny):
            put_step(
                row, faces, chem0, conc, run, range(-2, n - 1),
                lambda at, value: put_padded(*state1(at, run), row, value),
            )
        for row in chunks(ny):
            put_potential(row, state1, run, range(-1, n - 2), chem1)
        for row in chunks(ny):

            def target(at, value):
                squares[...] += put_miss(row, runs, observed, place, run, at, value, adjoint2)[1]

            put_step(row, faces, chem1, state1, run, range(0, n - 3), target)
        return carry

    lax.fori_loop(0, runs, one_run, 0)


def forward_kernel(
    m_chip, mob_own, conc_own, conc_chip, chem0_a, chem0_b, state1_a, chem1_a, adjoint2_a, squares, observed,
    mx_a, my_a, mz_a, mz_low_a, all_a,
    mx_b, my_b, mz_b, mz_low_b, all_b, state1_b, chem1_b, adjoint2_b, to_core, to_chip, share, rim, total,
):
    runs, n = conc_own.shape[:2]
    ny = observed.shape[2]
    faces = Faces(n, (mx_a, my_a, mz_a, mz_low_a, all_a, mx_b, my_b, mz_b, mz_low_b, all_b))
    mob = Line((mob_own, 0, n - 1), (rim, n, n + 2))
    place = [either(n - 1 - at, at) for at in range(n)]
    conc = Line((conc_own, 0, n - 1), (conc_chip, n, n + 3))
    chem0 = Line((chem0_a, -3, n - 2), (chem0_b, n - 1, n + 2))
    state1 = Line((state1_a, -2, n - 2), (state1_b, n - 1, n + 1))
    chem1 = Line((chem1_a, -1, n - 3), (chem1_b, n - 2, n))
    adjoint2 = Line((adjoint2_a, 0, n - 4), (adjoint2_b, n - 3, n - 1))
    for row in chunks(ny):
        for at in range(3):
            put_padded(rim, (at,), row, flat(m_chip, (at,), row))
    for row in chunks(ny):
        mids = [padded(*mob(at), row) for at in range(n - 1, n + 3)]
        for at in range(3):
            put_flat(mx_b, (at,), row, each(mean, mids[at], mids[at + 1]))
        put_faces(row, mob, range(n, n + 2), faces.my, faces.mz, faces.mz_low)
    for row in chunks(ny):
        put_all(row, faces, range(n - 1, n + 2))
    total[...] = squares[...]

    def one_run(run, carry):
        for row in chunks(ny):
            put_step(
                row, faces, chem0, conc, run, range(n - 1, n + 2),
                lambda at, value: put_padded(*state1(at, run), row, value),
            )
        for row in chunks(ny):
            put_potential(row, state1, run, range(n - 2, n + 1), chem1)
        for row in chunks(ny):

            def target(at, value):
                adjoint, square = put_miss(row, runs, observed, place, run, at, value, adjoint2)
                total[...] += square
                put_flat(to_chip, (run, n - 1 - at), row, adjoint)
                if at < 3:
                    put_flat(to_core, (run, at), row, adjoint)

            put_step(row, faces, chem1, state1, run, range(n - 3, n), target)
            for at in range(min(3, n - 3)):
                put_flat(to_core, (run, at), row, padded(*adjoint2(at, run), row))
        return carry

    lax.fori_loop(0, runs, one_run, 0)
    columns = (0.5 / runs) * jnp.sum(total[...], axis=0, keepdims=True)
    mine = jnp.broadcast_to(jnp.sum(columns, axis=1, keepdims=True), share.shape)
    share[...] = mine


def put_adjoint1(row, flow, adjoint2, run, places, weight, target):
    mids = {at: padded(*flow(at, run), row) for at in range(places[0] - 1, places[-1] + 2)}
    for at in places:
        total = beside(
            mids[at - 1], mids[at + 1], padded(*flow(at, run), row, 1), padded(*flow(at, run), row, -1), mids[at]
        )
        value = each(
            lambda a, w, f, t: a + w * f - (time_step * stiffness) * t,
            padded(*adjoint2(at, run), row), weight(at), mids[at], total,
        )
        put_padded(*target(at, run), row, value)


def slope(state):
    return each(lambda c: time_step * (3.0 * c * c + (6.0 * stiffness - 1.0)), state)


def step_x(field, run, at, row):
    return sub(padded(*field(at + 1, run), row), padded(*field(at, run), row))


def step_y(field, run, at, row):
    return sub(padded(*field(at, run), row, 1), padded(*field(at, run), row))


def step_z(field, run, at, row):
    mid = padded(*field(at, run), row)
    return sub(after_z(mid), mid)


def early_kernel(
    of_core, mx_a, my_a, mz_a, mz_low_a, all_a, mx_b, my_b, mz_b, mz_low_b, all_b,
    chem0_a, chem0_b, state1_a, state1_b, chem1_a, chem1_b, adjoint2_a, adjoint2_b,
    flow_a, flow_part, adjoint1_a, weight_b, step_z_b, part, sum_x_b, sum_y_b, sum_z_b,
    rim, sum_x, sum_y, sum_z,
):
    runs = of_core.shape[0]
    n = part.shape[0] + 2
    ny = part.shape[-2]
    faces = Faces(n, (mx_a, my_a, mz_a, mz_low_a, all_a, mx_b, my_b, mz_b, mz_low_b, all_b))
    chem0 = Line((chem0_a, -3, n - 2), (chem0_b, n - 1, n + 2))
    state1 = Line((state1_a, -2, n - 2), (state1_b, n - 1, n + 1))
    chem1 = Line((chem1_a, -1, n - 3), (chem1_b, n - 2, n))
    adjoint2 = Line((rim, -3, -1), (adjoint2_a, 0, n - 4), (adjoint2_b, n - 3, n - 1))
    flow = Line((flow_a, -2, n - 2), (flow_part, n - 1, n - 1))
    adjoint1 = Line((adjoint1_a, -1, n - 3))
    for sums in (sum_x, sum_y, sum_z):
        sums[...] = jnp.zeros_like(sums)

    def one_run(run, carry):
        for row in chunks(ny):
            for at in range(3):
                put_padded(rim, (run, 2 - at), row, flat(of_core, (run, at), row))
        for row in chunks(ny):
            mids = {at: padded(*adjoint2(at, run), row) for at in range(-3, n)}
            for at in range(-2, n):
                value = faces.flow(
                    row, at, mids[at], padded(*adjoint2(at, run), row, 1), padded(*adjoint2(at, run), row, -1),
                    mids[at - 1], mids.get(at + 1),
                )
                put_padded(*flow(at, run), row, value)
        for row in chunks(ny):
            put_adjoint1(
                row, flow, adjoint2, run, range(-1, n - 2),
                lambda at: slope(padded(*state1(at, run), row)), adjoint1,
            )
            for at in range(n - 2, n + 1):
                put_flat(weight_b, (run, at - (n - 2)), row, slope(padded(*state1(at, run), row)))
        for row in chunks(ny):
            for at in range(-1, n - 1):
                total = add_product(
                    flat(sum_x, (at + 1,), row), step_x(adjoint2, run, at, row), step_x(chem1, run, at, row)
                )
                if at < n - 3:
                    total = add_product(total, step_x(adjoint1, run, at, row), step_x(chem0, run, at, row))
                put_flat(sum_x, (at + 1,), row, total)
            for at in range(n):
                total_y = add_product(
                    padded(sum_y, (at,), row), step_y(adjoint2, run, at, row), step_y(chem1, run, at, row)
                )
                total_z = add_product(
                    flat(sum_z, (at,), row), step_z(adjoint2, run, at, row), step_z(chem1, run, at, row)
                )
                slant = step_z(chem0, run, at, row)
                if at < n - 2:
                    total_y = add_product(total_y, step_y(adjoint1, run, at, row), step_y(chem0, run, at, row))
                    total_z = add_product(total_z, step_z(adjoint1, run, at, row), slant)
                else:
                    put_flat(step_z_b, (run, at - (n - 2)), row, slant)
                put_padded(sum_y, (at,), row, total_y)
                put_flat(sum_z, (at,), row, total_z)
        return carry

    lax.fori_loop(0, runs, one_run, 0)
    for row in chunks(ny):
        for at in range(n - 2):
            sides = flat(sum_z, (at,), row)
            value = each(
                lambda a, b, c, d, e: -0.5 * ((a + b) + (c + d) + e),
                padded(sum_y, (at,), row), padded(sum_y, (at,), row, -1), sides, before_z(sides),
                flat(sum_x, (at,), row),
            )
            if at < n - 3:
                value = each(lambda a, b: a - 0.5 * b, value, flat(sum_x, (at + 1,), row))
            put_flat(part, (at,), row, value)
        for at in range(2):
            put_flat(sum_x_b, (at,), row, flat(sum_x, (n - 2 + at,), row))
            put_flat(sum_y_b, (at,), row, padded(sum_y, (n - 2 + at,), row))
            put_flat(sum_z_b, (at,), row, flat(sum_z, (n - 2 + at,), row))


def late_kernel(
    of_chip, mx_a, my_a, mz_a, mz_low_a, all_a, mx_b, my_b, mz_b, mz_low_b, all_b,
    chem0_a, chem0_b, chem1_b, adjoint2_b, flow_a, flow_part, adjoint1_a, weight_b, step_z_b,
    part, sum_x_b, sum_y_b, sum_z_b, result, rim, flow_b, adjoint1_b, sum_x, sum_y, sum_z,
):
    runs = of_chip.shape[0]
    n, ny, _ = result.shape
    faces = Faces(n, (mx_a, my_a, mz_a, mz_low_a, all_a, mx_b, my_b, mz_b, mz_low_b, all_b))
    place = [either(n - 1 - at, at) for at in range(n)]
    chem0 = Line((chem0_a, -3, n - 2), (chem0_b, n - 1, n + 2))
    chem1 = Line((chem1_b, n - 2, n))
    adjoint2 = Line((adjoint2_b, n - 3, n - 1), (rim, n, n + 2))
    flow = Line((flow_a, -2, n - 2), (flow_b, n - 1, n + 1))
    adjoint1 = Line((adjoint1_a, -1, n - 3), (adjoint1_b, n - 2, n))
    for row in chunks(ny):
        for at in range(2):
            put_flat(sum_x, (at,), row, flat(sum_x_b, (at,), row))
            put_padded(sum_y, (at,), row, flat(sum_y_b, (at,), row))
            put_flat(sum_z, (at,), row, flat(sum_z_b, (at,), row))
    sum_x[2] = jnp.zeros_like(sum_x[2])

    def one_run(run, carry):
        for row in chunks(ny):
            for at in range(3):
                put_padded(rim, (run, at), row, flat(of_chip, (run, at), row))
        for row in chunks(ny):
            mids = {at: padded(*adjoint2(at, run), row) for at in range(n - 1, n + 3)}
            value = add_product(padded(flow_part, (run, 0), row), flat(*faces.mx(n - 1), row), mids[n])
            put_padded(*flow(n - 1, run), row, value)
            for at in range(n, n + 2):
                value = faces.flow(
                    row, at, mids[at], padded(*adjoint2(at, run), row, 1), padded(*adjoint2(at, run), row, -1),
                    mids[at - 1], mids[at + 1],
                )
                put_padded(*flow(at, run), row, value)
        for row in chunks(ny):
            put_adjoint1(
                row, flow, adjoint2, run, range(n - 2, n + 1),
                lambda at: flat(weight_b, (run, at - (n - 2)), row), adjoint1,
            )
        for row in chunks(ny):
            for at in range(n - 3, n):
                total = add_product(
                    flat(sum_x, (at - (n - 3),), row), step_x(adjoint1, run, at, row), step_x(chem0, run, at, row)
                )
                if at == n - 1:
                    total = add_product(total, step_x(adjoint2, run, at, row), step_x(chem1, run, at, row))
                put_flat(sum_x, (at - (n - 3),), row, total)
            for at in range(n - 2, n):
                to = (at - (n - 2),)
                put_padded(sum_y, to, row, add_product(
                    padded(sum_y, to, row), step_y(adjoint1, run, at, row), step_y(chem0, run, at, row)
                ))
                put_flat(sum_z, to, row, add_product(
                    flat(sum_z, to, row), step_z(adjoint1, run, at, row), flat(step_z_b, (run, *to), row)
                ))
        return carry

    lax.fori_loop(0, runs, one_run, 0)
    for row in chunks(ny):
        for at in range(n - 2):
            value = flat(part, (at,), row)
            if at == n - 3:
                value = each(lambda a, b: a - 0.5 * b, value, flat(sum_x, (0,), row))
            put_plain(result, (place[at],), row, value)
        for at in range(2):
            sides = flat(sum_z, (at,), row)
            value = each(
                lambda a, b, c, d, e, f: -0.5 * ((a + b) + (c + d) + (e + f)),
                flat(sum_x, (at,), row), flat(sum_x, (at + 1,), row),
                padded(sum_y, (at,), row), padded(sum_y, (at,), row, -1), sides, before_z(sides),
            )
            put_plain(result, (place[n - 2 + at],), row, value)


def misfit_kernel(shares, misfit):
    misfit[...] = jnp.sum(shares[...], axis=0)


def call(kernel, outs, scratch, args, flops):
    moved = 4 * (sum(a.size for a in args) + sum(math.prod(o) for o in outs))
    return pl.pallas_call(
        kernel,
        out_shape=tuple(jax.ShapeDtypeStruct(o, jnp.float32) for o in outs),
        in_specs=[VMEM] * len(args),
        out_specs=tuple([VMEM] * len(outs)),
        scratch_shapes=[pltpu.VMEM(s, jnp.float32) for s in scratch],
        compiler_params=pltpu.CompilerParams(vmem_limit_bytes=16 * 1024 * 1024),
        cost_estimate=pl.CostEstimate(flops=flops, bytes_accessed=moved, transcendentals=0),
    )(*args)


def on_device(initial, observed, mobility):
    runs, n, ny, nz = initial.shape
    blocks = nz // LANES
    count = lax.axis_size("gx")
    over_chips = [(i, (i - 1 + 2 * (i % 2)) % count) for i in range(count)]
    over_cores = [(i, i ^ 1) for i in range(count)]
    cell = ny * nz

    def neighbours(to_chip, to_core):
        of_core = lax.ppermute(to_core, "gx", over_cores)
        return lax.ppermute(to_chip, "gx", over_chips), of_core

    def lies(*lead):
        return (*lead, blocks, ny, LANES)

    def lies_padded(*lead):
        return (*lead, blocks, ny + 2 * PAD, LANES)

    if n == 4:
        near = (initial, initial)
    else:
        near = [lax.dynamic_slice_in_dim(initial, at, 4, 1) for at in (either(0, n - 4), either(n - 4, 0))]
    of_chip, of_core = neighbours(*near)
    conc, mob, to_chip, to_core = call(
        own_kernel, (lies_padded(runs, n), lies_padded(n), lies(3), lies(3)), (), (initial, mobility),
        runs * n * cell,
    )
    m_chip, m_core = neighbours(to_chip, to_core)
    conc_core, chem0_a, *faces_a = call(
        core_kernel,
        (
            lies_padded(runs, 4), lies_padded(runs, n + 2),
            lies(n + 2), lies_padded(n + 2), lies(n + 2), lies(n + 2), lies(n + 1),
        ),
        (lies_padded(3),),
        (of_core, m_core, conc, mob),
        20 * runs * (n + 2) * cell,
    )
    conc_chip, chem0_b, state1_a, chem1_a, adjoint2_a, squares = call(
        chip_kernel,
        (
            lies_padded(runs, 4), lies_padded(runs, 4), lies_padded(runs, n + 1),
            lies_padded(runs, n - 1), lies_padded(runs, n - 3), (CHUNK, LANES),
        ),
        (),
        (of_chip, conc, conc_core, chem0_a, observed, *faces_a),
        60 * runs * (n - 1) * cell,
    )
    *faces_b, state1_b, chem1_b, adjoint2_b, to_core, to_chip, share = call(
        forward_kernel,
        (
            lies(3), lies_padded(2), lies(2), lies(2), lies(3),
            lies_padded(runs, 3), lies_padded(runs, 3), lies_padded(runs, 3),
            lies(runs, 3), lies(runs, 3), (LANES, LANES),
        ),
        (lies_padded(3), (CHUNK, LANES)),
        (m_chip, mob, conc, conc_chip, chem0_a, chem0_b, state1_a, chem1_a, adjoint2_a, squares, observed, *faces_a),
        60 * runs * 3 * cell,
    )
    faces = (*faces_a, *faces_b)
    of_chip, of_core = neighbours(to_chip, to_core)
    shares = lax.all_gather(share, "gx")
    flow_a, flow_part, adjoint1_a, weight_b, step_z_b, part, *sums_b = call(
        early_kernel,
        (
            lies_padded(runs, n + 1), lies_padded(runs, 1), lies_padded(runs, n - 1), lies(runs, 3), lies(runs, 2),
            lies(n - 2), lies(2), lies(2), lies(2),
        ),
        (lies_padded(runs, 3), lies(n), lies_padded(n), lies(n)),
        (of_core, *faces, chem0_a, chem0_b, state1_a, state1_b, chem1_a, chem1_b, adjoint2_a, adjoint2_b),
        60 * runs * n * cell,
    )
    (result,) = call(
        late_kernel,
        ((n, ny, nz),),
        (
            lies_padded(runs, 3), lies_padded(runs, 3), lies_padded(runs, 3),
            lies(3), lies_padded(2), lies(2),
        ),
        (
            of_chip, *faces, chem0_a, chem0_b, chem1_b, adjoint2_b, flow_a, flow_part, adjoint1_a,
            weight_b, step_z_b, part, *sums_b,
        ),
        60 * runs * 3 * cell,
    )
    (misfit,) = call(misfit_kernel, ((1, LANES),), (), (shares[:, :1],), count)
    return (result, misfit[0, :1])


def solution(mesh):
    placed = (
        P("group", "gx", None, None),
        P("group", "gx", None, None),
        P(("group", "gx"), None, None),
    )
    return jax.shard_map(
        on_device,
        mesh=mesh,
        in_specs=placed,
        out_specs=(P(("group", "gx"), None, None), P("group")),
        check_vma=False,
    )
```

```python
import functools
import math

import jax
import jax.numpy as jnp
from jax import lax
from jax.experimental import pallas as pl
from jax.experimental.pallas import tpu as pltpu
from jax.sharding import PartitionSpec as P

stiffness = 0.5
time_step = 0.005
VMEM = pl.BlockSpec(memory_space=pltpu.VMEM)
SMEM = pl.BlockSpec(memory_space=pltpu.SMEM)
LANES = 128
ROWS = 8
PAD = ROWS
CHUNK = 16


def chunks(ny):
    return range(0, ny, CHUNK)


def plain(ref, lead, row):
    return [
        ref[(*lead, pl.ds(row, CHUNK), pl.ds(at, LANES))] for at in range(0, ref.shape[-1], LANES)
    ]


def put_plain(ref, lead, row, value):
    for block, part in enumerate(value):
        ref[(*lead, pl.ds(row, CHUNK), pl.ds(block * LANES, LANES))] = part


def flat(ref, lead, row):
    return [ref[(*lead, block, pl.ds(row, CHUNK))] for block in range(ref.shape[-3])]


def put_flat(ref, lead, row, value):
    for block, part in enumerate(value):
        ref[(*lead, block, pl.ds(row, CHUNK))] = part


def padded(ref, lead, row, shift=0):
    return [ref[(*lead, block, pl.ds(PAD + row + shift, CHUNK))] for block in range(ref.shape[-3])]


def put_padded(ref, lead, row, value):
    ny = ref.shape[-2] - 2 * PAD
    for block, part in enumerate(value):
        ref[(*lead, block, pl.ds(PAD + row, CHUNK))] = part
        if row == 0:
            ref[(*lead, block, pl.ds(PAD + ny, 1))] = part[:1]
        if row + CHUNK == ny:
            ref[(*lead, block, pl.ds(PAD - 1, 1))] = part[CHUNK - 1 :]


def lane():
    return lax.broadcasted_iota(jnp.int32, (CHUNK, LANES), 1)


def after_z(value):
    turned = [pltpu.roll(part, LANES - 1, 1) for part in value]
    turned.append(turned[0])
    edge = lane() == LANES - 1
    return [jnp.where(edge, turned[at + 1], turned[at]) for at in range(len(value))]


def before_z(value):
    turned = [pltpu.roll(part, 1, 1) for part in value]
    edge = lane() == 0
    return [jnp.where(edge, turned[at - 1], turned[at]) for at in range(len(value))]


def side():
    return lax.rem(lax.axis_index("gx"), 2)


def either(first, second):
    return first + side() * (second - first)


class Line:
    def __init__(self, *parts):
        self.parts = parts

    def __call__(self, at, *lead):
        for ref, first, last in self.parts:
            if first <= at <= last:
                return ref, (*lead, at - first)
        raise IndexError(at)


def each(function, *values):
    return [function(*parts) for parts in zip(*values)]


def beside(low, high, up, down, mid):
    return each(
        lambda a, b, c, d, e, f: (a + b) + (c + d) + (e + f),
        low, high, up, down, after_z(mid), before_z(mid),
    )


def potential(low, mid, high, up, down):
    return each(
        lambda c, total: c * (c * c + (6.0 * stiffness - 1.0)) - stiffness * total,
        mid, beside(low, high, up, down, mid),
    )


class Faces:
    def __init__(self, n, refs):
        mx_a, my_a, mz_a, mz_low_a, all_a, *late = refs
        two = lambda ref, first, last, at: ((ref, first, last), *(((late[at], last + 1, n + 1),) if late else ()))
        self.mx = Line(*two(mx_a, -3, n - 2, 0))
        self.my = Line(*two(my_a, -2, n - 1, 1))
        self.mz = Line(*two(mz_a, -2, n - 1, 2))
        self.mz_low = Line(*two(mz_low_a, -2, n - 1, 3))
        self.all = Line(*two(all_a, -2, n - 2, 4))

    def flow(self, row, at, mid, up, down, low=None, high=None):
        total = each(
            lambda a, b, c, d, e, u, v, w, x, y: (a * u + b * v) + (c * w + d * x) - e * y,
            padded(*self.my(at), row), padded(*self.my(at), row, -1), flat(*self.mz(at), row),
            flat(*self.mz_low(at), row), flat(*self.all(at), row), up, down, after_z(mid), before_z(mid), mid,
        )
        if low is not None:
            total = add_product(total, flat(*self.mx(at - 1), row), low)
        if high is not None:
            total = add_product(total, flat(*self.mx(at), row), high)
        return total


def add_product(total, a, b):
    return each(lambda t, x, y: t + x * y, total, a, b)


def sub(a, b):
    return each(lambda x, y: x - y, a, b)


def own_kernel(initial, mobility, conc, mob, to_chip, to_core):
    runs, n, ny, _ = initial.shape
    place = [either(n - 1 - at, at) for at in range(n)]

    def one_run(run, carry):
        for row in chunks(ny):
            for at in range(n):
                put_padded(conc, (run, at), row, plain(initial, (run, place[at]), row))
        return carry

    lax.fori_loop(0, runs, one_run, 0)
    for row in chunks(ny):
        for at in range(n):
            value = plain(mobility, (place[at],), row)
            put_padded(mob, (at,), row, value)
            if at < 3:
                put_flat(to_core, (at,), row, value)
            if at >= n - 3:
                put_flat(to_chip, (n - 1 - at,), row, value)


def mean(a, b):
    return 0.5 * (a + b)


def put_faces(row, mob, places, my, mz, mz_low):
    for at in places:
        mid = padded(*mob(at), row)
        put_padded(*my(at), row, each(mean, mid, padded(*mob(at), row, 1)))
        put_flat(*mz(at), row, each(mean, mid, after_z(mid)))
        put_flat(*mz_low(at), row, each(mean, mid, before_z(mid)))


def put_all(row, faces, places):
    for at in places:
        put_flat(*faces.all(at), row, each(
            lambda a, b, c, d, e, f: (a + b) + (c + d) + (e + f),
            flat(*faces.mx(at - 1), row), flat(*faces.mx(at), row), padded(*faces.my(at), row),
            padded(*faces.my(at), row, -1), flat(*faces.mz(at), row), flat(*faces.mz_low(at), row),
        ))


def put_potential(row, field, run, places, target):
    mids = {at: padded(*field(at, run), row) for at in range(places[0] - 1, places[-1] + 2)}
    for at in places:
        value = potential(
            mids[at - 1], mids[at], mids[at + 1],
            padded(*field(at, run), row, 1), padded(*field(at, run), row, -1),
        )
        put_padded(*target(at, run), row, value)


def put_step(row, faces, chem, state, run, places, target):
    mids = {at: padded(*chem(at, run), row) for at in range(places[0] - 1, places[-1] + 2)}
    for at in places:
        flow = faces.flow(
            row, at, mids[at], padded(*chem(at, run), row, 1), padded(*chem(at, run), row, -1),
            mids[at - 1], mids[at + 1],
        )
        value = each(lambda a, b: a + time_step * b, padded(*state(at, run), row), flow)
        target(at, value)


def put_miss(row, runs, observed, place, run, at, value, adjoint2):
    miss = sub(value, plain(observed, (run, place[at]), row))
    adjoint = each(lambda a: a * (1.0 / runs), miss)
    put_padded(*adjoint2(at, run), row, adjoint)
    return adjoint, sum(part * part for part in miss)


def core_kernel(of_core, m_core, conc_own, mob_own, conc_core, chem0, mx, my, mz, mz_low, m_all, rim):
    runs, n = conc_own.shape[:2]
    ny = of_core.shape[2]
    mob = Line((rim, -3, -1), (mob_own, 0, n - 1))
    faces = Faces(n, (mx, my, mz, mz_low, m_all))
    for row in chunks(ny):
        for at in range(3):
            put_padded(rim, (2 - at,), row, flat(m_core, (at,), row))
    for row in chunks(ny):
        mids = [padded(*mob(at), row) for at in range(-3, n)]
        for at in range(n + 2):
            put_flat(mx, (at,), row, each(mean, mids[at], mids[at + 1]))
        put_faces(row, mob, range(-2, n), faces.my, faces.mz, faces.mz_low)
    for row in chunks(ny):
        put_all(row, faces, range(-2, n - 1))
    place = [either(at, 3 - at) for at in range(4)]
    conc = Line((conc_core, -4, -1), (conc_own, 0, n - 1))

    def one_run(run, carry):
        for row in chunks(ny):
            for at in range(4):
                put_padded(conc_core, (run, 3 - at), row, plain(of_core, (run, place[at]), row))
        for row in chunks(ny):
            put_potential(row, conc, run, range(-3, n - 1), Line((chem0, -3, n - 2)))
        return carry

    lax.fori_loop(0, runs, one_run, 0)


def chip_kernel(
    of_chip, conc_own, conc_core, chem0_a, observed, mx, my, mz, mz_low, m_all,
    conc_chip, chem0_b, state1_a, chem1_a, adjoint2_a, squares,
):
    runs, n = conc_own.shape[:2]
    ny = observed.shape[2]
    faces = Faces(n, (mx, my, mz, mz_low, m_all))
    message = [either(3 - at, at) for at in range(4)]
    place = [either(n - 1 - at, at) for at in range(n)]
    conc = Line((conc_core, -4, -1), (conc_own, 0, n - 1), (conc_chip, n, n + 3))
    chem0 = Line((chem0_a, -3, n - 2), (chem0_b, n - 1, n + 2))
    state1 = Line((state1_a, -2, n - 2))
    chem1 = Line((chem1_a, -1, n - 3))
    adjoint2 = Line((adjoint2_a, 0, n - 4))
    squares[...] = jnp.zeros_like(squares)

    def one_run(run, carry):
        for row in chunks(ny):
            for at in range(4):
                put_padded(conc_chip, (run, at), row, plain(of_chip, (run, message[at]), row))
        for row in chunks(ny):
            put_potential(row, conc, run, range(n - 1, n + 3), chem0)
        for row in chunks(ny):
            put_step(
                row, faces, chem0, conc, run, range(-2, n - 1),
                lambda at, value: put_padded(*state1(at, run), row, value),
            )
        for row in chunks(ny):
            put_potential(row, state1, run, range(-1, n - 2), chem1)
        for row in chunks(ny):

            def target(at, value):
                squares[...] += put_miss(row, runs, observed, place, run, at, value, adjoint2)[1]

            put_step(row, faces, chem1, state1, run, range(0, n - 3), target)
        return carry

    lax.fori_loop(0, runs, one_run, 0)


def forward_kernel(
    m_chip, mob_own, conc_own, conc_chip, chem0_a, chem0_b, state1_a, chem1_a, adjoint2_a, squares, observed,
    mx_a, my_a, mz_a, mz_low_a, all_a,
    mx_b, my_b, mz_b, mz_low_b, all_b, state1_b, chem1_b, adjoint2_b, to_core, to_chip, share, rim, total,
):
    runs, n = conc_own.shape[:2]
    ny = observed.shape[2]
    faces = Faces(n, (mx_a, my_a, mz_a, mz_low_a, all_a, mx_b, my_b, mz_b, mz_low_b, all_b))
    mob = Line((mob_own, 0, n - 1), (rim, n, n + 2))
    place = [either(n - 1 - at, at) for at in range(n)]
    conc = Line((conc_own, 0, n - 1), (conc_chip, n, n + 3))
    chem0 = Line((chem0_a, -3, n - 2), (chem0_b, n - 1, n + 2))
    state1 = Line((state1_a, -2, n - 2), (state1_b, n - 1, n + 1))
    chem1 = Line((chem1_a, -1, n - 3), (chem1_b, n - 2, n))
    adjoint2 = Line((adjoint2_a, 0, n - 4), (adjoint2_b, n - 3, n - 1))
    for row in chunks(ny):
        for at in range(3):
            put_padded(rim, (at,), row, flat(m_chip, (at,), row))
    for row in chunks(ny):
        mids = [padded(*mob(at), row) for at in range(n - 1, n + 3)]
        for at in range(3):
            put_flat(mx_b, (at,), row, each(mean, mids[at], mids[at + 1]))
        put_faces(row, mob, range(n, n + 2), faces.my, faces.mz, faces.mz_low)
    for row in chunks(ny):
        put_all(row, faces, range(n - 1, n + 2))
    total[...] = squares[...]

    def one_run(run, carry):
        for row in chunks(ny):
            put_step(
                row, faces, chem0, conc, run, range(n - 1, n + 2),
                lambda at, value: put_padded(*state1(at, run), row, value),
            )
        for row in chunks(ny):
            put_potential(row, state1, run, range(n - 2, n + 1), chem1)
        for row in chunks(ny):

            def target(at, value):
                adjoint, square = put_miss(row, runs, observed, place, run, at, value, adjoint2)
                total[...] += square
                put_flat(to_chip, (run, n - 1 - at), row, adjoint)
                if at < 3:
                    put_flat(to_core, (run, at), row, adjoint)

            put_step(row, faces, chem1, state1, run, range(n - 3, n), target)
            for at in range(min(3, n - 3)):
                put_flat(to_core, (run, at), row, padded(*adjoint2(at, run), row))
        return carry

    lax.fori_loop(0, runs, one_run, 0)
    columns = (0.5 / runs) * jnp.sum(total[...], axis=0, keepdims=True)
    mine = jnp.broadcast_to(jnp.sum(columns, axis=1, keepdims=True), share.shape)
    share[...] = mine
    to_core[0, 0, 0, ny:] = mine


def put_adjoint1(row, flow, adjoint2, run, places, weight, target):
    mids = {at: padded(*flow(at, run), row) for at in range(places[0] - 1, places[-1] + 2)}
    for at in places:
        total = beside(
            mids[at - 1], mids[at + 1], padded(*flow(at, run), row, 1), padded(*flow(at, run), row, -1), mids[at]
        )
        value = each(
            lambda a, w, f, t: a + w * f - (time_step * stiffness) * t,
            padded(*adjoint2(at, run), row), weight(at), mids[at], total,
        )
        put_padded(*target(at, run), row, value)


def slope(state):
    return each(lambda c: time_step * (3.0 * c * c + (6.0 * stiffness - 1.0)), state)


def step_x(field, run, at, row):
    return sub(padded(*field(at + 1, run), row), padded(*field(at, run), row))


def step_y(field, run, at, row):
    return sub(padded(*field(at, run), row, 1), padded(*field(at, run), row))


def step_z(field, run, at, row):
    mid = padded(*field(at, run), row)
    return sub(after_z(mid), mid)


def early_kernel(
    of_core, mx_a, my_a, mz_a, mz_low_a, all_a, mx_b, my_b, mz_b, mz_low_b, all_b,
    chem0_a, chem0_b, state1_a, state1_b, chem1_a, chem1_b, adjoint2_a, adjoint2_b,
    share_in, flow_a, flow_part, adjoint1_a, weight_b, step_z_b, part, sum_x_b, sum_y_b, sum_z_b, share,
    rim, sum_x, sum_y, sum_z,
):
    share[...] = share_in[...]
    runs = of_core.shape[0]
    n = part.shape[0] + 2
    ny = part.shape[-2]
    faces = Faces(n, (mx_a, my_a, mz_a, mz_low_a, all_a, mx_b, my_b, mz_b, mz_low_b, all_b))
    chem0 = Line((chem0_a, -3, n - 2), (chem0_b, n - 1, n + 2))
    state1 = Line((state1_a, -2, n - 2), (state1_b, n - 1, n + 1))
    chem1 = Line((chem1_a, -1, n - 3), (chem1_b, n - 2, n))
    adjoint2 = Line((rim, -3, -1), (adjoint2_a, 0, n - 4), (adjoint2_b, n - 3, n - 1))
    flow = Line((flow_a, -2, n - 2), (flow_part, n - 1, n - 1))
    adjoint1 = Line((adjoint1_a, -1, n - 3))
    for sums in (sum_x, sum_y, sum_z):
        sums[...] = jnp.zeros_like(sums)

    def one_run(run, carry):
        for row in chunks(ny):
            for at in range(3):
                put_padded(rim, (run, 2 - at), row, flat(of_core, (run, at), row))
        for row in chunks(ny):
            mids = {at: padded(*adjoint2(at, run), row) for at in range(-3, n)}
            for at in range(-2, n):
                value = faces.flow(
                    row, at, mids[at], padded(*adjoint2(at, run), row, 1), padded(*adjoint2(at, run), row, -1),
                    mids[at - 1], mids.get(at + 1),
                )
                put_padded(*flow(at, run), row, value)
        for row in chunks(ny):
            put_adjoint1(
                row, flow, adjoint2, run, range(-1, n - 2),
                lambda at: slope(padded(*state1(at, run), row)), adjoint1,
            )
            for at in range(n - 2, n + 1):
                put_flat(weight_b, (run, at - (n - 2)), row, slope(padded(*state1(at, run), row)))
        for row in chunks(ny):
            for at in range(-1, n - 1):
                total = add_product(
                    flat(sum_x, (at + 1,), row), step_x(adjoint2, run, at, row), step_x(chem1, run, at, row)
                )
                if at < n - 3:
                    total = add_product(total, step_x(adjoint1, run, at, row), step_x(chem0, run, at, row))
                put_flat(sum_x, (at + 1,), row, total)
            for at in range(n):
                total_y = add_product(
                    padded(sum_y, (at,), row), step_y(adjoint2, run, at, row), step_y(chem1, run, at, row)
                )
                total_z = add_product(
                    flat(sum_z, (at,), row), step_z(adjoint2, run, at, row), step_z(chem1, run, at, row)
                )
                slant = step_z(chem0, run, at, row)
                if at < n - 2:
                    total_y = add_product(total_y, step_y(adjoint1, run, at, row), step_y(chem0, run, at, row))
                    total_z = add_product(total_z, step_z(adjoint1, run, at, row), slant)
                else:
                    put_flat(step_z_b, (run, at - (n - 2)), row, slant)
                put_padded(sum_y, (at,), row, total_y)
                put_flat(sum_z, (at,), row, total_z)
        return carry

    lax.fori_loop(0, runs, one_run, 0)
    for row in chunks(ny):
        for at in range(n - 2):
            sides = flat(sum_z, (at,), row)
            value = each(
                lambda a, b, c, d, e: -0.5 * ((a + b) + (c + d) + e),
                padded(sum_y, (at,), row), padded(sum_y, (at,), row, -1), sides, before_z(sides),
                flat(sum_x, (at,), row),
            )
            if at < n - 3:
                value = each(lambda a, b: a - 0.5 * b, value, flat(sum_x, (at + 1,), row))
            put_flat(part, (at,), row, value)
        for at in range(2):
            put_flat(sum_x_b, (at,), row, flat(sum_x, (n - 2 + at,), row))
            put_flat(sum_y_b, (at,), row, padded(sum_y, (n - 2 + at,), row))
            put_flat(sum_z_b, (at,), row, flat(sum_z, (n - 2 + at,), row))


def late_kernel(
    of_chip, mx_a, my_a, mz_a, mz_low_a, all_a, mx_b, my_b, mz_b, mz_low_b, all_b,
    chem0_a, chem0_b, chem1_b, adjoint2_b, flow_a, flow_part, adjoint1_a, weight_b, step_z_b,
    part, sum_x_b, sum_y_b, sum_z_b, share, far, result, misfit, rim, flow_b, adjoint1_b, sum_x, sum_y, sum_z,
):
    misfit[0] = (share[...] + far[...])[0, 0]
    runs = of_chip.shape[0]
    n, ny, _ = result.shape
    faces = Faces(n, (mx_a, my_a, mz_a, mz_low_a, all_a, mx_b, my_b, mz_b, mz_low_b, all_b))
    place = [either(n - 1 - at, at) for at in range(n)]
    chem0 = Line((chem0_a, -3, n - 2), (chem0_b, n - 1, n + 2))
    chem1 = Line((chem1_b, n - 2, n))
    adjoint2 = Line((adjoint2_b, n - 3, n - 1), (rim, n, n + 2))
    flow = Line((flow_a, -2, n - 2), (flow_b, n - 1, n + 1))
    adjoint1 = Line((adjoint1_a, -1, n - 3), (adjoint1_b, n - 2, n))
    for row in chunks(ny):
        for at in range(2):
            put_flat(sum_x, (at,), row, flat(sum_x_b, (at,), row))
            put_padded(sum_y, (at,), row, flat(sum_y_b, (at,), row))
            put_flat(sum_z, (at,), row, flat(sum_z_b, (at,), row))
    sum_x[2] = jnp.zeros_like(sum_x[2])

    def one_run(run, carry):
        for row in chunks(ny):
            for at in range(3):
                put_padded(rim, (run, at), row, flat(of_chip, (run, at), row))
        for row in chunks(ny):
            mids = {at: padded(*adjoint2(at, run), row) for at in range(n - 1, n + 3)}
            value = add_product(padded(flow_part, (run, 0), row), flat(*faces.mx(n - 1), row), mids[n])
            put_padded(*flow(n - 1, run), row, value)
            for at in range(n, n + 2):
                value = faces.flow(
                    row, at, mids[at], padded(*adjoint2(at, run), row, 1), padded(*adjoint2(at, run), row, -1),
                    mids[at - 1], mids[at + 1],
                )
                put_padded(*flow(at, run), row, value)
        for row in chunks(ny):
            put_adjoint1(
                row, flow, adjoint2, run, range(n - 2, n + 1),
                lambda at: flat(weight_b, (run, at - (n - 2)), row), adjoint1,
            )
        for row in chunks(ny):
            for at in range(n - 3, n):
                total = add_product(
                    flat(sum_x, (at - (n - 3),), row), step_x(adjoint1, run, at, row), step_x(chem0, run, at, row)
                )
                if at == n - 1:
                    total = add_product(total, step_x(adjoint2, run, at, row), step_x(chem1, run, at, row))
                put_flat(sum_x, (at - (n - 3),), row, total)
            for at in range(n - 2, n):
                to = (at - (n - 2),)
                put_padded(sum_y, to, row, add_product(
                    padded(sum_y, to, row), step_y(adjoint1, run, at, row), step_y(chem0, run, at, row)
                ))
                put_flat(sum_z, to, row, add_product(
                    flat(sum_z, to, row), step_z(adjoint1, run, at, row), flat(step_z_b, (run, *to), row)
                ))
        return carry

    lax.fori_loop(0, runs, one_run, 0)
    for row in chunks(ny):
        for at in range(n - 2):
            value = flat(part, (at,), row)
            if at == n - 3:
                value = each(lambda a, b: a - 0.5 * b, value, flat(sum_x, (0,), row))
            put_plain(result, (place[at],), row, value)
        for at in range(2):
            sides = flat(sum_z, (at,), row)
            value = each(
                lambda a, b, c, d, e, f: -0.5 * ((a + b) + (c + d) + (e + f)),
                flat(sum_x, (at,), row), flat(sum_x, (at + 1,), row),
                padded(sum_y, (at,), row), padded(sum_y, (at,), row, -1), sides, before_z(sides),
            )
            put_plain(result, (place[n - 2 + at],), row, value)


def call(kernel, outs, scratch, args, flops, scalar=None):
    moved = 4 * (sum(a.size for a in args) + sum(math.prod(o) for o in outs))
    return pl.pallas_call(
        kernel,
        out_shape=tuple(jax.ShapeDtypeStruct(o, jnp.float32) for o in outs),
        in_specs=[VMEM] * len(args),
        out_specs=tuple(SMEM if at == scalar else VMEM for at in range(len(outs))),
        scratch_shapes=[pltpu.VMEM(s, jnp.float32) for s in scratch],
        compiler_params=pltpu.CompilerParams(vmem_limit_bytes=16 * 1024 * 1024),
        cost_estimate=pl.CostEstimate(flops=flops, bytes_accessed=moved, transcendentals=0),
    )(*args)


def on_device(initial, observed, mobility):
    runs, n, ny, nz = initial.shape
    blocks = nz // LANES
    count = lax.axis_size("gx")
    over_chips = [(i, (i - 1 + 2 * (i % 2)) % count) for i in range(count)]
    over_cores = [(i, i ^ 1) for i in range(count)]
    cell = ny * nz

    def neighbours(to_chip, to_core):
        of_core = lax.ppermute(to_core, "gx", over_cores)
        return lax.ppermute(to_chip, "gx", over_chips), of_core

    def lies(*lead):
        return (*lead, blocks, ny, LANES)

    def lies_padded(*lead):
        return (*lead, blocks, ny + 2 * PAD, LANES)

    if n == 4:
        near = (initial, initial)
    else:
        near = [lax.dynamic_slice_in_dim(initial, at, 4, 1) for at in (either(0, n - 4), either(n - 4, 0))]
    of_chip, of_core = neighbours(*near)
    conc, mob, to_chip, to_core = call(
        own_kernel, (lies_padded(runs, n), lies_padded(n), lies(3), lies(3)), (), (initial, mobility),
        runs * n * cell,
    )
    m_chip, m_core = neighbours(to_chip, to_core)
    conc_core, chem0_a, *faces_a = call(
        core_kernel,
        (
            lies_padded(runs, 4), lies_padded(runs, n + 2),
            lies(n + 2), lies_padded(n + 2), lies(n + 2), lies(n + 2), lies(n + 1),
        ),
        (lies_padded(3),),
        (of_core, m_core, conc, mob),
        20 * runs * (n + 2) * cell,
    )
    conc_chip, chem0_b, state1_a, chem1_a, adjoint2_a, squares = call(
        chip_kernel,
        (
            lies_padded(runs, 4), lies_padded(runs, 4), lies_padded(runs, n + 1),
            lies_padded(runs, n - 1), lies_padded(runs, n - 3), (CHUNK, LANES),
        ),
        (),
        (of_chip, conc, conc_core, chem0_a, observed, *faces_a),
        60 * runs * (n - 1) * cell,
    )
    *faces_b, state1_b, chem1_b, adjoint2_b, to_core, to_chip, share = call(
        forward_kernel,
        (
            lies(3), lies_padded(2), lies(2), lies(2), lies(3),
            lies_padded(runs, 3), lies_padded(runs, 3), lies_padded(runs, 3),
            (runs, 3, blocks, ny + ROWS, LANES), lies(runs, 3), (ROWS, LANES),
        ),
        (lies_padded(3), (CHUNK, LANES)),
        (m_chip, mob, conc, conc_chip, chem0_a, chem0_b, state1_a, chem1_a, adjoint2_a, squares, observed, *faces_a),
        60 * runs * 3 * cell,
    )
    faces = (*faces_a, *faces_b)
    of_chip, of_core = neighbours(to_chip, to_core)
    bits = range(count.bit_length() - 2)

    def target(at, step):
        apart = (at ^ at >> 1) & 1
        bit = bits[-1 - step] if apart else bits[step]
        return at ^ (3 if bit == 0 else 2 << bit)

    def hop(value, step):
        return lax.ppermute(value, "gx", [(at, target(at, step)) for at in range(count)])

    share = share + of_core[0, 0, 0, ny:]
    far = hop(share, 0)
    flow_a, flow_part, adjoint1_a, weight_b, step_z_b, part, *sums_b, share = call(
        early_kernel,
        (
            lies_padded(runs, n + 1), lies_padded(runs, 1), lies_padded(runs, n - 1), lies(runs, 3), lies(runs, 2),
            lies(n - 2), lies(2), lies(2), lies(2), (ROWS, LANES),
        ),
        (lies_padded(runs, 3), lies(n), lies_padded(n), lies(n)),
        (of_core, *faces, chem0_a, chem0_b, state1_a, state1_b, chem1_a, chem1_b, adjoint2_a, adjoint2_b, share),
        60 * runs * n * cell,
    )
    for step in bits[1:]:
        share = share + far
        far = hop(share, step)
    return call(
        late_kernel,
        ((n, ny, nz), (1,)),
        (
            lies_padded(runs, 3), lies_padded(runs, 3), lies_padded(runs, 3),
            lies(3), lies_padded(2), lies(2),
        ),
        (
            of_chip, *faces, chem0_a, chem0_b, chem1_b, adjoint2_b, flow_a, flow_part, adjoint1_a,
            weight_b, step_z_b, part, *sums_b, share, far,
        ),
        60 * runs * 3 * cell,
        scalar=1,
    )


def solution(mesh):
    placed = (
        P("group", "gx", None, None),
        P("group", "gx", None, None),
        P(("group", "gx"), None, None),
    )
    return jax.shard_map(
        on_device,
        mesh=mesh,
        in_specs=placed,
        out_specs=(P(("group", "gx"), None, None), P("group")),
        check_vma=False,
    )
```

```python
import functools
import math

import jax
import jax.numpy as jnp
from jax import lax
from jax.experimental import pallas as pl
from jax.experimental.pallas import tpu as pltpu
from jax.sharding import PartitionSpec as P

stiffness = 0.5
time_step = 0.005
VMEM = pl.BlockSpec(memory_space=pltpu.VMEM)
SMEM = pl.BlockSpec(memory_space=pltpu.SMEM)
LANES = 128
ROWS = 8
PAD = ROWS
CHUNK = 16


def chunks(ny):
    return range(0, ny, CHUNK)


def plain(ref, lead, row):
    return [
        ref[(*lead, pl.ds(row, CHUNK), pl.ds(at, LANES))] for at in range(0, ref.shape[-1], LANES)
    ]


def put_plain(ref, lead, row, value):
    for block, part in enumerate(value):
        ref[(*lead, pl.ds(row, CHUNK), pl.ds(block * LANES, LANES))] = part


def flat(ref, lead, row):
    return [ref[(*lead, block, pl.ds(row, CHUNK))] for block in range(ref.shape[-3])]


def put_flat(ref, lead, row, value):
    for block, part in enumerate(value):
        ref[(*lead, block, pl.ds(row, CHUNK))] = part


def padded(ref, lead, row, shift=0):
    return [ref[(*lead, block, pl.ds(PAD + row + shift, CHUNK))] for block in range(ref.shape[-3])]


def put_padded(ref, lead, row, value):
    ny = ref.shape[-2] - 2 * PAD
    for block, part in enumerate(value):
        ref[(*lead, block, pl.ds(PAD + row, CHUNK))] = part
        if row == 0:
            ref[(*lead, block, pl.ds(PAD + ny, 1))] = part[:1]
        if row + CHUNK == ny:
            ref[(*lead, block, pl.ds(PAD - 1, 1))] = part[CHUNK - 1 :]


def lane():
    return lax.broadcasted_iota(jnp.int32, (CHUNK, LANES), 1)


def after_z(value):
    turned = [pltpu.roll(part, LANES - 1, 1) for part in value]
    turned.append(turned[0])
    edge = lane() == LANES - 1
    return [jnp.where(edge, turned[at + 1], turned[at]) for at in range(len(value))]


def before_z(value):
    turned = [pltpu.roll(part, 1, 1) for part in value]
    edge = lane() == 0
    return [jnp.where(edge, turned[at - 1], turned[at]) for at in range(len(value))]


def side():
    return lax.rem(lax.axis_index("gx"), 2)


def either(first, second):
    return first + side() * (second - first)


class Line:
    def __init__(self, *parts):
        self.parts = parts

    def __call__(self, at, *lead):
        for ref, first, last in self.parts:
            if first <= at <= last:
                return ref, (*lead, at - first)
        raise IndexError(at)


def each(function, *values):
    return [function(*parts) for parts in zip(*values)]


def beside(low, high, up, down, mid):
    return each(
        lambda a, b, c, d, e, f: (a + b) + (c + d) + (e + f),
        low, high, up, down, after_z(mid), before_z(mid),
    )


def potential(low, mid, high, up, down):
    return each(
        lambda c, total: c * (c * c + (6.0 * stiffness - 1.0)) - stiffness * total,
        mid, beside(low, high, up, down, mid),
    )


class Faces:
    def __init__(self, n, refs):
        mx_a, my_a, mz_a, mz_low_a, all_a, *late = refs
        two = lambda ref, first, last, at: ((ref, first, last), *(((late[at], last + 1, n + 1),) if late else ()))
        self.mx = Line(*two(mx_a, -3, n - 2, 0))
        self.my = Line(*two(my_a, -2, n - 1, 1))
        self.mz = Line(*two(mz_a, -2, n - 1, 2))
        self.mz_low = Line(*two(mz_low_a, -2, n - 1, 3))
        self.all = Line(*two(all_a, -2, n - 2, 4))

    def flow(self, row, at, mid, up, down, low=None, high=None):
        total = each(
            lambda a, b, c, d, e, u, v, w, x, y: (a * u + b * v) + (c * w + d * x) - e * y,
            padded(*self.my(at), row), padded(*self.my(at), row, -1), flat(*self.mz(at), row),
            flat(*self.mz_low(at), row), flat(*self.all(at), row), up, down, after_z(mid), before_z(mid), mid,
        )
        if low is not None:
            total = add_product(total, flat(*self.mx(at - 1), row), low)
        if high is not None:
            total = add_product(total, flat(*self.mx(at), row), high)
        return total


def add_product(total, a, b):
    return each(lambda t, x, y: t + x * y, total, a, b)


def sub(a, b):
    return each(lambda x, y: x - y, a, b)


def own_kernel(initial, mobility, conc, mob, to_chip, to_core):
    runs, n, ny, _ = initial.shape
    place = [either(n - 1 - at, at) for at in range(n)]

    def one_run(run, carry):
        for row in chunks(ny):
            for at in range(n):
                put_padded(conc, (run, at), row, plain(initial, (run, place[at]), row))
        return carry

    lax.fori_loop(0, runs, one_run, 0)
    for row in chunks(ny):
        for at in range(n):
            value = plain(mobility, (place[at],), row)
            put_padded(mob, (at,), row, value)
            if at < 3:
                put_flat(to_core, (at,), row, value)
            if at >= n - 3:
                put_flat(to_chip, (n - 1 - at,), row, value)


def mean(a, b):
    return 0.5 * (a + b)


def put_faces(row, mob, places, my, mz, mz_low):
    for at in places:
        mid = padded(*mob(at), row)
        put_padded(*my(at), row, each(mean, mid, padded(*mob(at), row, 1)))
        put_flat(*mz(at), row, each(mean, mid, after_z(mid)))
        put_flat(*mz_low(at), row, each(mean, mid, before_z(mid)))


def put_all(row, faces, places):
    for at in places:
        put_flat(*faces.all(at), row, each(
            lambda a, b, c, d, e, f: (a + b) + (c + d) + (e + f),
            flat(*faces.mx(at - 1), row), flat(*faces.mx(at), row), padded(*faces.my(at), row),
            padded(*faces.my(at), row, -1), flat(*faces.mz(at), row), flat(*faces.mz_low(at), row),
        ))


def put_potential(row, field, run, places, target):
    mids = {at: padded(*field(at, run), row) for at in range(places[0] - 1, places[-1] + 2)}
    for at in places:
        value = potential(
            mids[at - 1], mids[at], mids[at + 1],
            padded(*field(at, run), row, 1), padded(*field(at, run), row, -1),
        )
        put_padded(*target(at, run), row, value)


def put_step(row, faces, chem, state, run, places, target):
    mids = {at: padded(*chem(at, run), row) for at in range(places[0] - 1, places[-1] + 2)}
    for at in places:
        flow = faces.flow(
            row, at, mids[at], padded(*chem(at, run), row, 1), padded(*chem(at, run), row, -1),
            mids[at - 1], mids[at + 1],
        )
        value = each(lambda a, b: a + time_step * b, padded(*state(at, run), row), flow)
        target(at, value)


def put_miss(row, runs, observed, place, run, at, value, adjoint2):
    miss = sub(value, plain(observed, (run, place[at]), row))
    adjoint = each(lambda a: a * (1.0 / runs), miss)
    put_padded(*adjoint2(at, run), row, adjoint)
    return adjoint, sum(part * part for part in miss)


def core_kernel(of_core, m_core, conc_own, mob_own, conc_core, chem0, mx, my, mz, mz_low, m_all, rim):
    runs, n = conc_own.shape[:2]
    ny = of_core.shape[2]
    mob = Line((rim, -3, -1), (mob_own, 0, n - 1))
    faces = Faces(n, (mx, my, mz, mz_low, m_all))
    for row in chunks(ny):
        for at in range(3):
            put_padded(rim, (2 - at,), row, flat(m_core, (at,), row))
    for row in chunks(ny):
        mids = [padded(*mob(at), row) for at in range(-3, n)]
        for at in range(n + 2):
            put_flat(mx, (at,), row, each(mean, mids[at], mids[at + 1]))
        put_faces(row, mob, range(-2, n), faces.my, faces.mz, faces.mz_low)
    for row in chunks(ny):
        put_all(row, faces, range(-2, n - 1))
    place = [either(at, 3 - at) for at in range(4)]
    conc = Line((conc_core, -4, -1), (conc_own, 0, n - 1))

    def one_run(run, carry):
        for row in chunks(ny):
            for at in range(4):
                put_padded(conc_core, (run, 3 - at), row, plain(of_core, (run, place[at]), row))
        for row in chunks(ny):
            put_potential(row, conc, run, range(-3, n - 1), Line((chem0, -3, n - 2)))
        return carry

    lax.fori_loop(0, runs, one_run, 0)


def chip_kernel(
    of_chip, conc_own, conc_core, chem0_a, observed, mx, my, mz, mz_low, m_all,
    conc_chip, chem0_b, state1_a, chem1_a, adjoint2_a, squares,
):
    runs, n = conc_own.shape[:2]
    ny = observed.shape[2]
    faces = Faces(n, (mx, my, mz, mz_low, m_all))
    message = [either(3 - at, at) for at in range(4)]
    place = [either(n - 1 - at, at) for at in range(n)]
    conc = Line((conc_core, -4, -1), (conc_own, 0, n - 1), (conc_chip, n, n + 3))
    chem0 = Line((chem0_a, -3, n - 2), (chem0_b, n - 1, n + 2))
    state1 = Line((state1_a, -2, n - 2))
    chem1 = Line((chem1_a, -1, n - 3))
    adjoint2 = Line((adjoint2_a, 0, n - 4))
    squares[...] = jnp.zeros_like(squares)

    def one_run(run, carry):
        for row in chunks(ny):
            for at in range(4):
                put_padded(conc_chip, (run, at), row, plain(of_chip, (run, message[at]), row))
        for row in chunks(ny):
            put_potential(row, conc, run, range(n - 1, n + 3), chem0)
        for row in chunks(ny):
            put_step(
                row, faces, chem0, conc, run, range(-2, n - 1),
                lambda at, value: put_padded(*state1(at, run), row, value),
            )
        for row in chunks(ny):
            put_potential(row, state1, run, range(-1, n - 2), chem1)
        for row in chunks(ny):

            def target(at, value):
                squares[...] += put_miss(row, runs, observed, place, run, at, value, adjoint2)[1]

            put_step(row, faces, chem1, state1, run, range(0, n - 3), target)
        return carry

    lax.fori_loop(0, runs, one_run, 0)


def forward_kernel(
    m_chip, mob_own, conc_own, conc_chip, chem0_a, chem0_b, state1_a, chem1_a, adjoint2_a, squares, observed,
    mx_a, my_a, mz_a, mz_low_a, all_a,
    mx_b, my_b, mz_b, mz_low_b, all_b, state1_b, chem1_b, adjoint2_b, to_core, to_chip, share, rim, total,
):
    runs, n = conc_own.shape[:2]
    ny = observed.shape[2]
    faces = Faces(n, (mx_a, my_a, mz_a, mz_low_a, all_a, mx_b, my_b, mz_b, mz_low_b, all_b))
    mob = Line((mob_own, 0, n - 1), (rim, n, n + 2))
    place = [either(n - 1 - at, at) for at in range(n)]
    conc = Line((conc_own, 0, n - 1), (conc_chip, n, n + 3))
    chem0 = Line((chem0_a, -3, n - 2), (chem0_b, n - 1, n + 2))
    state1 = Line((state1_a, -2, n - 2), (state1_b, n - 1, n + 1))
    chem1 = Line((chem1_a, -1, n - 3), (chem1_b, n - 2, n))
    adjoint2 = Line((adjoint2_a, 0, n - 4), (adjoint2_b, n - 3, n - 1))
    for row in chunks(ny):
        for at in range(3):
            put_padded(rim, (at,), row, flat(m_chip, (at,), row))
    for row in chunks(ny):
        mids = [padded(*mob(at), row) for at in range(n - 1, n + 3)]
        for at in range(3):
            put_flat(mx_b, (at,), row, each(mean, mids[at], mids[at + 1]))
        put_faces(row, mob, range(n, n + 2), faces.my, faces.mz, faces.mz_low)
    for row in chunks(ny):
        put_all(row, faces, range(n - 1, n + 2))
    total[...] = squares[...]

    def one_run(run, carry):
        for row in chunks(ny):
            put_step(
                row, faces, chem0, conc, run, range(n - 1, n + 2),
                lambda at, value: put_padded(*state1(at, run), row, value),
            )
        for row in chunks(ny):
            put_potential(row, state1, run, range(n - 2, n + 1), chem1)
        for row in chunks(ny):

            def target(at, value):
                adjoint, square = put_miss(row, runs, observed, place, run, at, value, adjoint2)
                total[...] += square
                put_flat(to_chip, (run, n - 1 - at), row, adjoint)
                if at < 3:
                    put_flat(to_core, (run, at), row, adjoint)

            put_step(row, faces, chem1, state1, run, range(n - 3, n), target)
            for at in range(min(3, n - 3)):
                put_flat(to_core, (run, at), row, padded(*adjoint2(at, run), row))
        return carry

    lax.fori_loop(0, runs, one_run, 0)
    columns = (0.5 / runs) * jnp.sum(total[...], axis=0, keepdims=True)
    mine = jnp.broadcast_to(jnp.sum(columns, axis=1, keepdims=True), share.shape)
    share[...] = mine
    to_core[0, 0, 0, ny:] = mine


def put_adjoint1(row, flow, adjoint2, run, places, weight, target):
    mids = {at: padded(*flow(at, run), row) for at in range(places[0] - 1, places[-1] + 2)}
    for at in places:
        total = beside(
            mids[at - 1], mids[at + 1], padded(*flow(at, run), row, 1), padded(*flow(at, run), row, -1), mids[at]
        )
        value = each(
            lambda a, w, f, t: a + w * f - (time_step * stiffness) * t,
            padded(*adjoint2(at, run), row), weight(at), mids[at], total,
        )
        put_padded(*target(at, run), row, value)


def slope(state):
    return each(lambda c: time_step * (3.0 * c * c + (6.0 * stiffness - 1.0)), state)


def step_x(field, run, at, row):
    return sub(padded(*field(at + 1, run), row), padded(*field(at, run), row))


def step_y(field, run, at, row):
    return sub(padded(*field(at, run), row, 1), padded(*field(at, run), row))


def step_z(field, run, at, row):
    mid = padded(*field(at, run), row)
    return sub(after_z(mid), mid)


def early_kernel(
    of_core, mx_a, my_a, mz_a, mz_low_a, all_a, mx_b, my_b, mz_b, mz_low_b, all_b,
    chem0_a, chem0_b, state1_a, state1_b, chem1_a, chem1_b, adjoint2_a, adjoint2_b,
    share, flow_a, flow_part, adjoint1_a, weight_b, step_z_b, part, sum_x_b, sum_y_b, sum_z_b, shares,
    rim, sum_x, sum_y, sum_z,
):
    ny = part.shape[-2]
    chip = share[:1] + of_core[0, 0, 0, ny : ny + 1]
    shares[...] = jnp.broadcast_to(chip[None], shares.shape)
    runs = of_core.shape[0]
    n = part.shape[0] + 2
    ny = part.shape[-2]
    faces = Faces(n, (mx_a, my_a, mz_a, mz_low_a, all_a, mx_b, my_b, mz_b, mz_low_b, all_b))
    chem0 = Line((chem0_a, -3, n - 2), (chem0_b, n - 1, n + 2))
    state1 = Line((state1_a, -2, n - 2), (state1_b, n - 1, n + 1))
    chem1 = Line((chem1_a, -1, n - 3), (chem1_b, n - 2, n))
    adjoint2 = Line((rim, -3, -1), (adjoint2_a, 0, n - 4), (adjoint2_b, n - 3, n - 1))
    flow = Line((flow_a, -2, n - 2), (flow_part, n - 1, n - 1))
    adjoint1 = Line((adjoint1_a, -1, n - 3))
    for sums in (sum_x, sum_y, sum_z):
        sums[...] = jnp.zeros_like(sums)

    def one_run(run, carry):
        for row in chunks(ny):
            for at in range(3):
                put_padded(rim, (run, 2 - at), row, flat(of_core, (run, at), row))
        for row in chunks(ny):
            mids = {at: padded(*adjoint2(at, run), row) for at in range(-3, n)}
            for at in range(-2, n):
                value = faces.flow(
                    row, at, mids[at], padded(*adjoint2(at, run), row, 1), padded(*adjoint2(at, run), row, -1),
                    mids[at - 1], mids.get(at + 1),
                )
                put_padded(*flow(at, run), row, value)
        for row in chunks(ny):
            put_adjoint1(
                row, flow, adjoint2, run, range(-1, n - 2),
                lambda at: slope(padded(*state1(at, run), row)), adjoint1,
            )
            for at in range(n - 2, n + 1):
                put_flat(weight_b, (run, at - (n - 2)), row, slope(padded(*state1(at, run), row)))
        for row in chunks(ny):
            for at in range(-1, n - 1):
                total = add_product(
                    flat(sum_x, (at + 1,), row), step_x(adjoint2, run, at, row), step_x(chem1, run, at, row)
                )
                if at < n - 3:
                    total = add_product(total, step_x(adjoint1, run, at, row), step_x(chem0, run, at, row))
                put_flat(sum_x, (at + 1,), row, total)
            for at in range(n):
                total_y = add_product(
                    padded(sum_y, (at,), row), step_y(adjoint2, run, at, row), step_y(chem1, run, at, row)
                )
                total_z = add_product(
                    flat(sum_z, (at,), row), step_z(adjoint2, run, at, row), step_z(chem1, run, at, row)
                )
                slant = step_z(chem0, run, at, row)
                if at < n - 2:
                    total_y = add_product(total_y, step_y(adjoint1, run, at, row), step_y(chem0, run, at, row))
                    total_z = add_product(total_z, step_z(adjoint1, run, at, row), slant)
                else:
                    put_flat(step_z_b, (run, at - (n - 2)), row, slant)
                put_padded(sum_y, (at,), row, total_y)
                put_flat(sum_z, (at,), row, total_z)
        return carry

    lax.fori_loop(0, runs, one_run, 0)
    for row in chunks(ny):
        for at in range(n - 2):
            sides = flat(sum_z, (at,), row)
            value = each(
                lambda a, b, c, d, e: -0.5 * ((a + b) + (c + d) + e),
                padded(sum_y, (at,), row), padded(sum_y, (at,), row, -1), sides, before_z(sides),
                flat(sum_x, (at,), row),
            )
            if at < n - 3:
                value = each(lambda a, b: a - 0.5 * b, value, flat(sum_x, (at + 1,), row))
            put_flat(part, (at,), row, value)
        for at in range(2):
            put_flat(sum_x_b, (at,), row, flat(sum_x, (n - 2 + at,), row))
            put_flat(sum_y_b, (at,), row, padded(sum_y, (n - 2 + at,), row))
            put_flat(sum_z_b, (at,), row, flat(sum_z, (n - 2 + at,), row))


def late_kernel(
    of_chip, mx_a, my_a, mz_a, mz_low_a, all_a, mx_b, my_b, mz_b, mz_low_b, all_b,
    chem0_a, chem0_b, chem1_b, adjoint2_b, flow_a, flow_part, adjoint1_a, weight_b, step_z_b,
    part, sum_x_b, sum_y_b, sum_z_b, shares, result, misfit, rim, flow_b, adjoint1_b, sum_x, sum_y, sum_z,
):
    misfit[0] = jnp.sum(shares[...], axis=0)[0, 0]
    runs = of_chip.shape[0]
    n, ny, _ = result.shape
    faces = Faces(n, (mx_a, my_a, mz_a, mz_low_a, all_a, mx_b, my_b, mz_b, mz_low_b, all_b))
    place = [either(n - 1 - at, at) for at in range(n)]
    chem0 = Line((chem0_a, -3, n - 2), (chem0_b, n - 1, n + 2))
    chem1 = Line((chem1_b, n - 2, n))
    adjoint2 = Line((adjoint2_b, n - 3, n - 1), (rim, n, n + 2))
    flow = Line((flow_a, -2, n - 2), (flow_b, n - 1, n + 1))
    adjoint1 = Line((adjoint1_a, -1, n - 3), (adjoint1_b, n - 2, n))
    for row in chunks(ny):
        for at in range(2):
            put_flat(sum_x, (at,), row, flat(sum_x_b, (at,), row))
            put_padded(sum_y, (at,), row, flat(sum_y_b, (at,), row))
            put_flat(sum_z, (at,), row, flat(sum_z_b, (at,), row))
    sum_x[2] = jnp.zeros_like(sum_x[2])

    def one_run(run, carry):
        for row in chunks(ny):
            for at in range(3):
                put_padded(rim, (run, at), row, flat(of_chip, (run, at), row))
        for row in chunks(ny):
            mids = {at: padded(*adjoint2(at, run), row) for at in range(n - 1, n + 3)}
            value = add_product(padded(flow_part, (run, 0), row), flat(*faces.mx(n - 1), row), mids[n])
            put_padded(*flow(n - 1, run), row, value)
            for at in range(n, n + 2):
                value = faces.flow(
                    row, at, mids[at], padded(*adjoint2(at, run), row, 1), padded(*adjoint2(at, run), row, -1),
                    mids[at - 1], mids[at + 1],
                )
                put_padded(*flow(at, run), row, value)
        for row in chunks(ny):
            put_adjoint1(
                row, flow, adjoint2, run, range(n - 2, n + 1),
                lambda at: flat(weight_b, (run, at - (n - 2)), row), adjoint1,
            )
        for row in chunks(ny):
            for at in range(n - 3, n):
                total = add_product(
                    flat(sum_x, (at - (n - 3),), row), step_x(adjoint1, run, at, row), step_x(chem0, run, at, row)
                )
                if at == n - 1:
                    total = add_product(total, step_x(adjoint2, run, at, row), step_x(chem1, run, at, row))
                put_flat(sum_x, (at - (n - 3),), row, total)
            for at in range(n - 2, n):
                to = (at - (n - 2),)
                put_padded(sum_y, to, row, add_product(
                    padded(sum_y, to, row), step_y(adjoint1, run, at, row), step_y(chem0, run, at, row)
                ))
                put_flat(sum_z, to, row, add_product(
                    flat(sum_z, to, row), step_z(adjoint1, run, at, row), flat(step_z_b, (run, *to), row)
                ))
        return carry

    lax.fori_loop(0, runs, one_run, 0)
    for row in chunks(ny):
        for at in range(n - 2):
            value = flat(part, (at,), row)
            if at == n - 3:
                value = each(lambda a, b: a - 0.5 * b, value, flat(sum_x, (0,), row))
            put_plain(result, (place[at],), row, value)
        for at in range(2):
            sides = flat(sum_z, (at,), row)
            value = each(
                lambda a, b, c, d, e, f: -0.5 * ((a + b) + (c + d) + (e + f)),
                flat(sum_x, (at,), row), flat(sum_x, (at + 1,), row),
                padded(sum_y, (at,), row), padded(sum_y, (at,), row, -1), sides, before_z(sides),
            )
            put_plain(result, (place[n - 2 + at],), row, value)


def call(kernel, outs, scratch, args, flops, scalar=None):
    moved = 4 * (sum(a.size for a in args) + sum(math.prod(o) for o in outs))
    return pl.pallas_call(
        kernel,
        out_shape=tuple(jax.ShapeDtypeStruct(o, jnp.float32) for o in outs),
        in_specs=[VMEM] * len(args),
        out_specs=tuple(SMEM if at == scalar else VMEM for at in range(len(outs))),
        scratch_shapes=[pltpu.VMEM(s, jnp.float32) for s in scratch],
        compiler_params=pltpu.CompilerParams(vmem_limit_bytes=16 * 1024 * 1024),
        cost_estimate=pl.CostEstimate(flops=flops, bytes_accessed=moved, transcendentals=0),
    )(*args)


def on_device(initial, observed, mobility):
    runs, n, ny, nz = initial.shape
    blocks = nz // LANES
    count = lax.axis_size("gx")
    over_chips = [(i, (i - 1 + 2 * (i % 2)) % count) for i in range(count)]
    over_cores = [(i, i ^ 1) for i in range(count)]
    cell = ny * nz

    def neighbours(to_chip, to_core):
        of_core = lax.ppermute(to_core, "gx", over_cores)
        return lax.ppermute(to_chip, "gx", over_chips), of_core

    def lies(*lead):
        return (*lead, blocks, ny, LANES)

    def lies_padded(*lead):
        return (*lead, blocks, ny + 2 * PAD, LANES)

    if n == 4:
        near = (initial, initial)
    else:
        near = [lax.dynamic_slice_in_dim(initial, at, 4, 1) for at in (either(0, n - 4), either(n - 4, 0))]
    of_chip, of_core = neighbours(*near)
    conc, mob, to_chip, to_core = call(
        own_kernel, (lies_padded(runs, n), lies_padded(n), lies(3), lies(3)), (), (initial, mobility),
        runs * n * cell,
    )
    m_chip, m_core = neighbours(to_chip, to_core)
    conc_core, chem0_a, *faces_a = call(
        core_kernel,
        (
            lies_padded(runs, 4), lies_padded(runs, n + 2),
            lies(n + 2), lies_padded(n + 2), lies(n + 2), lies(n + 2), lies(n + 1),
        ),
        (lies_padded(3),),
        (of_core, m_core, conc, mob),
        20 * runs * (n + 2) * cell,
    )
    conc_chip, chem0_b, state1_a, chem1_a, adjoint2_a, squares = call(
        chip_kernel,
        (
            lies_padded(runs, 4), lies_padded(runs, 4), lies_padded(runs, n + 1),
            lies_padded(runs, n - 1), lies_padded(runs, n - 3), (CHUNK, LANES),
        ),
        (),
        (of_chip, conc, conc_core, chem0_a, observed, *faces_a),
        60 * runs * (n - 1) * cell,
    )
    *faces_b, state1_b, chem1_b, adjoint2_b, to_core, to_chip, share = call(
        forward_kernel,
        (
            lies(3), lies_padded(2), lies(2), lies(2), lies(3),
            lies_padded(runs, 3), lies_padded(runs, 3), lies_padded(runs, 3),
            (runs, 3, blocks, ny + ROWS, LANES), lies(runs, 3), (ROWS, LANES),
        ),
        (lies_padded(3), (CHUNK, LANES)),
        (m_chip, mob, conc, conc_chip, chem0_a, chem0_b, state1_a, chem1_a, adjoint2_a, squares, observed, *faces_a),
        60 * runs * 3 * cell,
    )
    faces = (*faces_a, *faces_b)
    of_chip, of_core = neighbours(to_chip, to_core)
    sets = [[at for at in range(count) if (at ^ at >> 1) & 1 == which] for which in (0, 1)]
    flow_a, flow_part, adjoint1_a, weight_b, step_z_b, part, *sums_b, shares = call(
        early_kernel,
        (
            lies_padded(runs, n + 1), lies_padded(runs, 1), lies_padded(runs, n - 1), lies(runs, 3), lies(runs, 2),
            lies(n - 2), lies(2), lies(2), lies(2), (count // 2, 1, LANES),
        ),
        (lies_padded(runs, 3), lies(n), lies_padded(n), lies(n)),
        (of_core, *faces, chem0_a, chem0_b, state1_a, state1_b, chem1_a, chem1_b, adjoint2_a, adjoint2_b, share),
        60 * runs * n * cell,
    )
    shares = lax.all_to_all(shares, "gx", 0, 0, axis_index_groups=sets)
    return call(
        late_kernel,
        ((n, ny, nz), (1,)),
        (
            lies_padded(runs, 3), lies_padded(runs, 3), lies_padded(runs, 3),
            lies(3), lies_padded(2), lies(2),
        ),
        (
            of_chip, *faces, chem0_a, chem0_b, chem1_b, adjoint2_b, flow_a, flow_part, adjoint1_a,
            weight_b, step_z_b, part, *sums_b, shares,
        ),
        60 * runs * 3 * cell,
        scalar=1,
    )


def solution(mesh):
    placed = (
        P("group", "gx", None, None),
        P("group", "gx", None, None),
        P(("group", "gx"), None, None),
    )
    return jax.shard_map(
        on_device,
        mesh=mesh,
        in_specs=placed,
        out_specs=(P(("group", "gx"), None, None), P("group")),
        check_vma=False,
    )
```

```python
import functools
import math

import jax
import jax.numpy as jnp
from jax import lax
from jax.experimental import pallas as pl
from jax.experimental.pallas import tpu as pltpu
from jax.sharding import PartitionSpec as P

stiffness = 0.5
time_step = 0.005
VMEM = pl.BlockSpec(memory_space=pltpu.VMEM)
SMEM = pl.BlockSpec(memory_space=pltpu.SMEM)
LANES = 128
ROWS = 8
PAD = ROWS
CHUNK = 16


def chunks(ny):
    return range(0, ny, CHUNK)


def plain(ref, lead, row):
    return [
        ref[(*lead, pl.ds(row, CHUNK), pl.ds(at, LANES))] for at in range(0, ref.shape[-1], LANES)
    ]


def put_plain(ref, lead, row, value):
    for block, part in enumerate(value):
        ref[(*lead, pl.ds(row, CHUNK), pl.ds(block * LANES, LANES))] = part


def flat(ref, lead, row):
    return [ref[(*lead, block, pl.ds(row, CHUNK))] for block in range(ref.shape[-3])]


def put_flat(ref, lead, row, value):
    for block, part in enumerate(value):
        ref[(*lead, block, pl.ds(row, CHUNK))] = part


def padded(ref, lead, row, shift=0):
    return [ref[(*lead, block, pl.ds(PAD + row + shift, CHUNK))] for block in range(ref.shape[-3])]


def put_padded(ref, lead, row, value):
    ny = ref.shape[-2] - 2 * PAD
    for block, part in enumerate(value):
        ref[(*lead, block, pl.ds(PAD + row, CHUNK))] = part
        if row == 0:
            ref[(*lead, block, pl.ds(PAD + ny, 1))] = part[:1]
        if row + CHUNK == ny:
            ref[(*lead, block, pl.ds(PAD - 1, 1))] = part[CHUNK - 1 :]


def lane():
    return lax.broadcasted_iota(jnp.int32, (CHUNK, LANES), 1)


def after_z(value):
    turned = [pltpu.roll(part, LANES - 1, 1) for part in value]
    turned.append(turned[0])
    edge = lane() == LANES - 1
    return [jnp.where(edge, turned[at + 1], turned[at]) for at in range(len(value))]


def before_z(value):
    turned = [pltpu.roll(part, 1, 1) for part in value]
    edge = lane() == 0
    return [jnp.where(edge, turned[at - 1], turned[at]) for at in range(len(value))]


def side():
    return lax.rem(lax.axis_index("gx"), 2)


def either(first, second):
    return first + side() * (second - first)


class Line:
    def __init__(self, *parts):
        self.parts = parts

    def __call__(self, at, *lead):
        for ref, first, last in self.parts:
            if first <= at <= last:
                return ref, (*lead, at - first)
        raise IndexError(at)


def each(function, *values):
    return [function(*parts) for parts in zip(*values)]


def beside(low, high, up, down, mid):
    return each(
        lambda a, b, c, d, e, f: (a + b) + (c + d) + (e + f),
        low, high, up, down, after_z(mid), before_z(mid),
    )


def potential(low, mid, high, up, down):
    return each(
        lambda c, total: c * (c * c + (6.0 * stiffness - 1.0)) - stiffness * total,
        mid, beside(low, high, up, down, mid),
    )


class Faces:
    def __init__(self, n, refs):
        mx_a, my_a, mz_a, mz_low_a, all_a, *late = refs
        two = lambda ref, first, last, at: ((ref, first, last), *(((late[at], last + 1, n + 1),) if late else ()))
        self.mx = Line(*two(mx_a, -3, n - 2, 0))
        self.my = Line(*two(my_a, -2, n - 1, 1))
        self.mz = Line(*two(mz_a, -2, n - 1, 2))
        self.mz_low = Line(*two(mz_low_a, -2, n - 1, 3))
        self.all = Line(*two(all_a, -2, n - 2, 4))

    def flow(self, row, at, mid, up, down, low=None, high=None):
        total = each(
            lambda a, b, c, d, e, u, v, w, x, y: (a * u + b * v) + (c * w + d * x) - e * y,
            padded(*self.my(at), row), padded(*self.my(at), row, -1), flat(*self.mz(at), row),
            flat(*self.mz_low(at), row), flat(*self.all(at), row), up, down, after_z(mid), before_z(mid), mid,
        )
        if low is not None:
            total = add_product(total, flat(*self.mx(at - 1), row), low)
        if high is not None:
            total = add_product(total, flat(*self.mx(at), row), high)
        return total


def add_product(total, a, b):
    return each(lambda t, x, y: t + x * y, total, a, b)


def sub(a, b):
    return each(lambda x, y: x - y, a, b)


def own_kernel(initial, mobility, conc, mob, to_chip, to_core):
    runs, n, ny, _ = initial.shape
    place = [either(n - 1 - at, at) for at in range(n)]

    def one_run(run, carry):
        for row in chunks(ny):
            for at in range(n):
                put_padded(conc, (run, at), row, plain(initial, (run, place[at]), row))
        return carry

    lax.fori_loop(0, runs, one_run, 0)
    for row in chunks(ny):
        for at in range(n):
            value = plain(mobility, (place[at],), row)
            put_padded(mob, (at,), row, value)
            if at < 3:
                put_flat(to_core, (at,), row, value)
            if at >= n - 3:
                put_flat(to_chip, (n - 1 - at,), row, value)


def mean(a, b):
    return 0.5 * (a + b)


def put_faces(row, mob, places, my, mz, mz_low):
    for at in places:
        mid = padded(*mob(at), row)
        put_padded(*my(at), row, each(mean, mid, padded(*mob(at), row, 1)))
        put_flat(*mz(at), row, each(mean, mid, after_z(mid)))
        put_flat(*mz_low(at), row, each(mean, mid, before_z(mid)))


def put_all(row, faces, places):
    for at in places:
        put_flat(*faces.all(at), row, each(
            lambda a, b, c, d, e, f: (a + b) + (c + d) + (e + f),
            flat(*faces.mx(at - 1), row), flat(*faces.mx(at), row), padded(*faces.my(at), row),
            padded(*faces.my(at), row, -1), flat(*faces.mz(at), row), flat(*faces.mz_low(at), row),
        ))


def put_potential(row, field, run, places, target):
    mids = {at: padded(*field(at, run), row) for at in range(places[0] - 1, places[-1] + 2)}
    for at in places:
        value = potential(
            mids[at - 1], mids[at], mids[at + 1],
            padded(*field(at, run), row, 1), padded(*field(at, run), row, -1),
        )
        put_padded(*target(at, run), row, value)


def put_step(row, faces, chem, state, run, places, target):
    mids = {at: padded(*chem(at, run), row) for at in range(places[0] - 1, places[-1] + 2)}
    for at in places:
        flow = faces.flow(
            row, at, mids[at], padded(*chem(at, run), row, 1), padded(*chem(at, run), row, -1),
            mids[at - 1], mids[at + 1],
        )
        value = each(lambda a, b: a + time_step * b, padded(*state(at, run), row), flow)
        target(at, value)


def put_miss(row, runs, observed, place, run, at, value, adjoint2):
    miss = sub(value, plain(observed, (run, place[at]), row))
    adjoint = each(lambda a: a * (1.0 / runs), miss)
    put_padded(*adjoint2(at, run), row, adjoint)
    return adjoint, sum(part * part for part in miss)


def core_kernel(of_core, m_core, conc_own, mob_own, conc_core, chem0, mx, my, mz, mz_low, m_all, rim):
    runs, n = conc_own.shape[:2]
    ny = of_core.shape[2]
    mob = Line((rim, -3, -1), (mob_own, 0, n - 1))
    faces = Faces(n, (mx, my, mz, mz_low, m_all))
    for row in chunks(ny):
        for at in range(3):
            put_padded(rim, (2 - at,), row, flat(m_core, (at,), row))
    for row in chunks(ny):
        mids = [padded(*mob(at), row) for at in range(-3, n)]
        for at in range(n + 2):
            put_flat(mx, (at,), row, each(mean, mids[at], mids[at + 1]))
        put_faces(row, mob, range(-2, n), faces.my, faces.mz, faces.mz_low)
    for row in chunks(ny):
        put_all(row, faces, range(-2, n - 1))
    place = [either(at, 3 - at) for at in range(4)]
    conc = Line((conc_core, -4, -1), (conc_own, 0, n - 1))

    def one_run(run, carry):
        for row in chunks(ny):
            for at in range(4):
                put_padded(conc_core, (run, 3 - at), row, plain(of_core, (run, place[at]), row))
        for row in chunks(ny):
            put_potential(row, conc, run, range(-3, n - 1), Line((chem0, -3, n - 2)))
        return carry

    lax.fori_loop(0, runs, one_run, 0)


def chip_kernel(
    of_chip, conc_own, conc_core, chem0_a, observed, mx, my, mz, mz_low, m_all,
    conc_chip, chem0_b, state1_a, chem1_a, adjoint2_a, squares,
):
    runs, n = conc_own.shape[:2]
    ny = observed.shape[2]
    faces = Faces(n, (mx, my, mz, mz_low, m_all))
    message = [either(3 - at, at) for at in range(4)]
    place = [either(n - 1 - at, at) for at in range(n)]
    conc = Line((conc_core, -4, -1), (conc_own, 0, n - 1), (conc_chip, n, n + 3))
    chem0 = Line((chem0_a, -3, n - 2), (chem0_b, n - 1, n + 2))
    state1 = Line((state1_a, -2, n - 2))
    chem1 = Line((chem1_a, -1, n - 3))
    adjoint2 = Line((adjoint2_a, 0, n - 4))
    squares[...] = jnp.zeros_like(squares)

    def one_run(run, carry):
        for row in chunks(ny):
            for at in range(4):
                put_padded(conc_chip, (run, at), row, plain(of_chip, (run, message[at]), row))
        for row in chunks(ny):
            put_potential(row, conc, run, range(n - 1, n + 3), chem0)
        for row in chunks(ny):
            put_step(
                row, faces, chem0, conc, run, range(-2, n - 1),
                lambda at, value: put_padded(*state1(at, run), row, value),
            )
        for row in chunks(ny):
            put_potential(row, state1, run, range(-1, n - 2), chem1)
        for row in chunks(ny):

            def target(at, value):
                squares[...] += put_miss(row, runs, observed, place, run, at, value, adjoint2)[1]

            put_step(row, faces, chem1, state1, run, range(0, n - 3), target)
        return carry

    lax.fori_loop(0, runs, one_run, 0)


def forward_kernel(
    m_chip, mob_own, conc_own, conc_chip, chem0_a, chem0_b, state1_a, chem1_a, adjoint2_a, squares, observed,
    mx_a, my_a, mz_a, mz_low_a, all_a,
    mx_b, my_b, mz_b, mz_low_b, all_b, state1_b, chem1_b, adjoint2_b, to_core, to_chip, share, rim, total,
):
    runs, n = conc_own.shape[:2]
    ny = observed.shape[2]
    faces = Faces(n, (mx_a, my_a, mz_a, mz_low_a, all_a, mx_b, my_b, mz_b, mz_low_b, all_b))
    mob = Line((mob_own, 0, n - 1), (rim, n, n + 2))
    place = [either(n - 1 - at, at) for at in range(n)]
    conc = Line((conc_own, 0, n - 1), (conc_chip, n, n + 3))
    chem0 = Line((chem0_a, -3, n - 2), (chem0_b, n - 1, n + 2))
    state1 = Line((state1_a, -2, n - 2), (state1_b, n - 1, n + 1))
    chem1 = Line((chem1_a, -1, n - 3), (chem1_b, n - 2, n))
    adjoint2 = Line((adjoint2_a, 0, n - 4), (adjoint2_b, n - 3, n - 1))
    for row in chunks(ny):
        for at in range(3):
            put_padded(rim, (at,), row, flat(m_chip, (at,), row))
    for row in chunks(ny):
        mids = [padded(*mob(at), row) for at in range(n - 1, n + 3)]
        for at in range(3):
            put_flat(mx_b, (at,), row, each(mean, mids[at], mids[at + 1]))
        put_faces(row, mob, range(n, n + 2), faces.my, faces.mz, faces.mz_low)
    for row in chunks(ny):
        put_all(row, faces, range(n - 1, n + 2))
    total[...] = squares[...]

    def one_run(run, carry):
        for row in chunks(ny):
            put_step(
                row, faces, chem0, conc, run, range(n - 1, n + 2),
                lambda at, value: put_padded(*state1(at, run), row, value),
            )
        for row in chunks(ny):
            put_potential(row, state1, run, range(n - 2, n + 1), chem1)
        for row in chunks(ny):

            def target(at, value):
                adjoint, square = put_miss(row, runs, observed, place, run, at, value, adjoint2)
                total[...] += square
                put_flat(to_chip, (run, n - 1 - at), row, adjoint)
                if at < 3:
                    put_flat(to_core, (run, at), row, adjoint)

            put_step(row, faces, chem1, state1, run, range(n - 3, n), target)
            for at in range(min(3, n - 3)):
                put_flat(to_core, (run, at), row, padded(*adjoint2(at, run), row))
        return carry

    lax.fori_loop(0, runs, one_run, 0)
    columns = (0.5 / runs) * jnp.sum(total[...], axis=0, keepdims=True)
    mine = jnp.broadcast_to(jnp.sum(columns, axis=1, keepdims=True), share.shape)
    share[...] = mine
    to_core[0, 0, 0, ny:] = mine


def put_adjoint1(row, flow, adjoint2, run, places, weight, target):
    mids = {at: padded(*flow(at, run), row) for at in range(places[0] - 1, places[-1] + 2)}
    for at in places:
        total = beside(
            mids[at - 1], mids[at + 1], padded(*flow(at, run), row, 1), padded(*flow(at, run), row, -1), mids[at]
        )
        value = each(
            lambda a, w, f, t: a + w * f - (time_step * stiffness) * t,
            padded(*adjoint2(at, run), row), weight(at), mids[at], total,
        )
        put_padded(*target(at, run), row, value)


def slope(state):
    return each(lambda c: time_step * (3.0 * c * c + (6.0 * stiffness - 1.0)), state)


def step_x(field, run, at, row):
    return sub(padded(*field(at + 1, run), row), padded(*field(at, run), row))


def step_y(field, run, at, row):
    return sub(padded(*field(at, run), row, 1), padded(*field(at, run), row))


def step_z(field, run, at, row):
    mid = padded(*field(at, run), row)
    return sub(after_z(mid), mid)


def early_kernel(
    of_core, mx_a, my_a, mz_a, mz_low_a, all_a, mx_b, my_b, mz_b, mz_low_b, all_b,
    chem0_a, chem0_b, state1_a, state1_b, chem1_a, chem1_b, adjoint2_a, adjoint2_b,
    share_in, flow_a, flow_part, adjoint1_a, weight_b, step_z_b, part, sum_x_b, sum_y_b, sum_z_b, share,
    rim, sum_x, sum_y, sum_z,
):
    share[...] = share_in[...]
    runs = of_core.shape[0]
    n = part.shape[0] + 2
    ny = part.shape[-2]
    faces = Faces(n, (mx_a, my_a, mz_a, mz_low_a, all_a, mx_b, my_b, mz_b, mz_low_b, all_b))
    chem0 = Line((chem0_a, -3, n - 2), (chem0_b, n - 1, n + 2))
    state1 = Line((state1_a, -2, n - 2), (state1_b, n - 1, n + 1))
    chem1 = Line((chem1_a, -1, n - 3), (chem1_b, n - 2, n))
    adjoint2 = Line((rim, -3, -1), (adjoint2_a, 0, n - 4), (adjoint2_b, n - 3, n - 1))
    flow = Line((flow_a, -2, n - 2), (flow_part, n - 1, n - 1))
    adjoint1 = Line((adjoint1_a, -1, n - 3))
    for sums in (sum_x, sum_y, sum_z):
        sums[...] = jnp.zeros_like(sums)

    def one_run(run, carry):
        for row in chunks(ny):
            for at in range(3):
                put_padded(rim, (run, 2 - at), row, flat(of_core, (run, at), row))
        for row in chunks(ny):
            mids = {at: padded(*adjoint2(at, run), row) for at in range(-3, n)}
            for at in range(-2, n):
                value = faces.flow(
                    row, at, mids[at], padded(*adjoint2(at, run), row, 1), padded(*adjoint2(at, run), row, -1),
                    mids[at - 1], mids.get(at + 1),
                )
                put_padded(*flow(at, run), row, value)
        for row in chunks(ny):
            put_adjoint1(
                row, flow, adjoint2, run, range(-1, n - 2),
                lambda at: slope(padded(*state1(at, run), row)), adjoint1,
            )
            for at in range(n - 2, n + 1):
                put_flat(weight_b, (run, at - (n - 2)), row, slope(padded(*state1(at, run), row)))
        for row in chunks(ny):
            for at in range(-1, n - 1):
                total = add_product(
                    flat(sum_x, (at + 1,), row), step_x(adjoint2, run, at, row), step_x(chem1, run, at, row)
                )
                if at < n - 3:
                    total = add_product(total, step_x(adjoint1, run, at, row), step_x(chem0, run, at, row))
                put_flat(sum_x, (at + 1,), row, total)
            for at in range(n):
                total_y = add_product(
                    padded(sum_y, (at,), row), step_y(adjoint2, run, at, row), step_y(chem1, run, at, row)
                )
                total_z = add_product(
                    flat(sum_z, (at,), row), step_z(adjoint2, run, at, row), step_z(chem1, run, at, row)
                )
                slant = step_z(chem0, run, at, row)
                if at < n - 2:
                    total_y = add_product(total_y, step_y(adjoint1, run, at, row), step_y(chem0, run, at, row))
                    total_z = add_product(total_z, step_z(adjoint1, run, at, row), slant)
                else:
                    put_flat(step_z_b, (run, at - (n - 2)), row, slant)
                put_padded(sum_y, (at,), row, total_y)
                put_flat(sum_z, (at,), row, total_z)
        return carry

    lax.fori_loop(0, runs, one_run, 0)
    for row in chunks(ny):
        for at in range(n - 2):
            sides = flat(sum_z, (at,), row)
            value = each(
                lambda a, b, c, d, e: -0.5 * ((a + b) + (c + d) + e),
                padded(sum_y, (at,), row), padded(sum_y, (at,), row, -1), sides, before_z(sides),
                flat(sum_x, (at,), row),
            )
            if at < n - 3:
                value = each(lambda a, b: a - 0.5 * b, value, flat(sum_x, (at + 1,), row))
            put_flat(part, (at,), row, value)
        for at in range(2):
            put_flat(sum_x_b, (at,), row, flat(sum_x, (n - 2 + at,), row))
            put_flat(sum_y_b, (at,), row, padded(sum_y, (n - 2 + at,), row))
            put_flat(sum_z_b, (at,), row, flat(sum_z, (n - 2 + at,), row))


def late_kernel(
    of_chip, mx_a, my_a, mz_a, mz_low_a, all_a, mx_b, my_b, mz_b, mz_low_b, all_b,
    chem0_a, chem0_b, chem1_b, adjoint2_b, flow_a, flow_part, adjoint1_a, weight_b, step_z_b,
    part, sum_x_b, sum_y_b, sum_z_b, result, rim, flow_b, adjoint1_b, sum_x, sum_y, sum_z,
):
    runs = of_chip.shape[0]
    n, ny, _ = result.shape
    faces = Faces(n, (mx_a, my_a, mz_a, mz_low_a, all_a, mx_b, my_b, mz_b, mz_low_b, all_b))
    place = [either(n - 1 - at, at) for at in range(n)]
    chem0 = Line((chem0_a, -3, n - 2), (chem0_b, n - 1, n + 2))
    chem1 = Line((chem1_b, n - 2, n))
    adjoint2 = Line((adjoint2_b, n - 3, n - 1), (rim, n, n + 2))
    flow = Line((flow_a, -2, n - 2), (flow_b, n - 1, n + 1))
    adjoint1 = Line((adjoint1_a, -1, n - 3), (adjoint1_b, n - 2, n))
    for row in chunks(ny):
        for at in range(2):
            put_flat(sum_x, (at,), row, flat(sum_x_b, (at,), row))
            put_padded(sum_y, (at,), row, flat(sum_y_b, (at,), row))
            put_flat(sum_z, (at,), row, flat(sum_z_b, (at,), row))
    sum_x[2] = jnp.zeros_like(sum_x[2])

    def one_run(run, carry):
        for row in chunks(ny):
            for at in range(3):
                put_padded(rim, (run, at), row, flat(of_chip, (run, at), row))
        for row in chunks(ny):
            mids = {at: padded(*adjoint2(at, run), row) for at in range(n - 1, n + 3)}
            value = add_product(padded(flow_part, (run, 0), row), flat(*faces.mx(n - 1), row), mids[n])
            put_padded(*flow(n - 1, run), row, value)
            for at in range(n, n + 2):
                value = faces.flow(
                    row, at, mids[at], padded(*adjoint2(at, run), row, 1), padded(*adjoint2(at, run), row, -1),
                    mids[at - 1], mids[at + 1],
                )
                put_padded(*flow(at, run), row, value)
        for row in chunks(ny):
            put_adjoint1(
                row, flow, adjoint2, run, range(n - 2, n + 1),
                lambda at: flat(weight_b, (run, at - (n - 2)), row), adjoint1,
            )
        for row in chunks(ny):
            for at in range(n - 3, n):
                total = add_product(
                    flat(sum_x, (at - (n - 3),), row), step_x(adjoint1, run, at, row), step_x(chem0, run, at, row)
                )
                if at == n - 1:
                    total = add_product(total, step_x(adjoint2, run, at, row), step_x(chem1, run, at, row))
                put_flat(sum_x, (at - (n - 3),), row, total)
            for at in range(n - 2, n):
                to = (at - (n - 2),)
                put_padded(sum_y, to, row, add_product(
                    padded(sum_y, to, row), step_y(adjoint1, run, at, row), step_y(chem0, run, at, row)
                ))
                put_flat(sum_z, to, row, add_product(
                    flat(sum_z, to, row), step_z(adjoint1, run, at, row), flat(step_z_b, (run, *to), row)
                ))
        return carry

    lax.fori_loop(0, runs, one_run, 0)
    for row in chunks(ny):
        for at in range(n - 2):
            value = flat(part, (at,), row)
            if at == n - 3:
                value = each(lambda a, b: a - 0.5 * b, value, flat(sum_x, (0,), row))
            put_plain(result, (place[at],), row, value)
        for at in range(2):
            sides = flat(sum_z, (at,), row)
            value = each(
                lambda a, b, c, d, e, f: -0.5 * ((a + b) + (c + d) + (e + f)),
                flat(sum_x, (at,), row), flat(sum_x, (at + 1,), row),
                padded(sum_y, (at,), row), padded(sum_y, (at,), row, -1), sides, before_z(sides),
            )
            put_plain(result, (place[n - 2 + at],), row, value)


def counts(at):
    return (at ^ (at >> 1)) & 1


def misfit_kernel(total, handed, misfit):
    misfit[0] = jnp.where(counts(lax.axis_index("gx")) == 1, total[0, 0], handed[0, 0])


def call(kernel, outs, scratch, args, flops, scalar=None):
    moved = 4 * (sum(a.size for a in args) + sum(math.prod(o) for o in outs))
    return pl.pallas_call(
        kernel,
        out_shape=tuple(jax.ShapeDtypeStruct(o, jnp.float32) for o in outs),
        in_specs=[VMEM] * len(args),
        out_specs=tuple(SMEM if at == scalar else VMEM for at in range(len(outs))),
        scratch_shapes=[pltpu.VMEM(s, jnp.float32) for s in scratch],
        compiler_params=pltpu.CompilerParams(vmem_limit_bytes=16 * 1024 * 1024),
        cost_estimate=pl.CostEstimate(flops=flops, bytes_accessed=moved, transcendentals=0),
    )(*args)


def on_device(initial, observed, mobility):
    runs, n, ny, nz = initial.shape
    blocks = nz // LANES
    count = lax.axis_size("gx")
    over_chips = [(i, (i - 1 + 2 * (i % 2)) % count) for i in range(count)]
    over_cores = [(i, i ^ 1) for i in range(count)]
    cell = ny * nz

    def neighbours(to_chip, to_core):
        of_core = lax.ppermute(to_core, "gx", over_cores)
        return lax.ppermute(to_chip, "gx", over_chips), of_core

    def lies(*lead):
        return (*lead, blocks, ny, LANES)

    def lies_padded(*lead):
        return (*lead, blocks, ny + 2 * PAD, LANES)

    if n == 4:
        near = (initial, initial)
    else:
        near = [lax.dynamic_slice_in_dim(initial, at, 4, 1) for at in (either(0, n - 4), either(n - 4, 0))]
    of_chip, of_core = neighbours(*near)
    conc, mob, to_chip, to_core = call(
        own_kernel, (lies_padded(runs, n), lies_padded(n), lies(3), lies(3)), (), (initial, mobility),
        runs * n * cell,
    )
    m_chip, m_core = neighbours(to_chip, to_core)
    conc_core, chem0_a, *faces_a = call(
        core_kernel,
        (
            lies_padded(runs, 4), lies_padded(runs, n + 2),
            lies(n + 2), lies_padded(n + 2), lies(n + 2), lies(n + 2), lies(n + 1),
        ),
        (lies_padded(3),),
        (of_core, m_core, conc, mob),
        20 * runs * (n + 2) * cell,
    )
    conc_chip, chem0_b, state1_a, chem1_a, adjoint2_a, squares = call(
        chip_kernel,
        (
            lies_padded(runs, 4), lies_padded(runs, 4), lies_padded(runs, n + 1),
            lies_padded(runs, n - 1), lies_padded(runs, n - 3), (CHUNK, LANES),
        ),
        (),
        (of_chip, conc, conc_core, chem0_a, observed, *faces_a),
        60 * runs * (n - 1) * cell,
    )
    *faces_b, state1_b, chem1_b, adjoint2_b, to_core, to_chip, share = call(
        forward_kernel,
        (
            lies(3), lies_padded(2), lies(2), lies(2), lies(3),
            lies_padded(runs, 3), lies_padded(runs, 3), lies_padded(runs, 3),
            (runs, 3, blocks, ny + ROWS, LANES), lies(runs, 3), (ROWS, LANES),
        ),
        (lies_padded(3), (CHUNK, LANES)),
        (m_chip, mob, conc, conc_chip, chem0_a, chem0_b, state1_a, chem1_a, adjoint2_a, squares, observed, *faces_a),
        60 * runs * 3 * cell,
    )
    faces = (*faces_a, *faces_b)
    of_chip, of_core = neighbours(to_chip, to_core)
    bits = range(count.bit_length() - 2)

    def hop(value, bit):
        apart = 3 if bit == 0 else 2 << bit
        return lax.ppermute(value, "gx", [(at, at ^ apart) for at in range(count) if counts(at)])

    share = share + of_core[0, 0, 0, ny:]
    far = hop(share, bits[-1])
    flow_a, flow_part, adjoint1_a, weight_b, step_z_b, part, *sums_b, share = call(
        early_kernel,
        (
            lies_padded(runs, n + 1), lies_padded(runs, 1), lies_padded(runs, n - 1), lies(runs, 3), lies(runs, 2),
            lies(n - 2), lies(2), lies(2), lies(2), (ROWS, LANES),
        ),
        (lies_padded(runs, 3), lies(n), lies_padded(n), lies(n)),
        (of_core, *faces, chem0_a, chem0_b, state1_a, state1_b, chem1_a, chem1_b, adjoint2_a, adjoint2_b, share),
        60 * runs * n * cell,
    )
    for bit in bits[-2::-1]:
        share = share + far
        far = hop(share, bit)
    share = share + far
    handed = lax.ppermute(share, "gx", over_cores)
    (result,) = call(
        late_kernel,
        ((n, ny, nz),),
        (
            lies_padded(runs, 3), lies_padded(runs, 3), lies_padded(runs, 3),
            lies(3), lies_padded(2), lies(2),
        ),
        (
            of_chip, *faces, chem0_a, chem0_b, chem1_b, adjoint2_b, flow_a, flow_part, adjoint1_a,
            weight_b, step_z_b, part, *sums_b,
        ),
        60 * runs * 3 * cell,
    )
    (misfit,) = call(misfit_kernel, ((1,),), (), (share, handed), 1, scalar=0)
    return (result, misfit)


def solution(mesh):
    placed = (
        P("group", "gx", None, None),
        P("group", "gx", None, None),
        P(("group", "gx"), None, None),
    )
    return jax.shard_map(
        on_device,
        mesh=mesh,
        in_specs=placed,
        out_specs=(P(("group", "gx"), None, None), P("group")),
        check_vma=False,
    )
```

```python
import functools
import math

import jax
import jax.numpy as jnp
from jax import lax
from jax.experimental import pallas as pl
from jax.experimental.pallas import tpu as pltpu
from jax.sharding import PartitionSpec as P

stiffness = 0.5
time_step = 0.005
VMEM = pl.BlockSpec(memory_space=pltpu.VMEM)
SMEM = pl.BlockSpec(memory_space=pltpu.SMEM)
LANES = 128
ROWS = 8
PAD = ROWS
CHUNK = 16


def chunks(ny):
    return range(0, ny, CHUNK)


def plain(ref, lead, row):
    return [
        ref[(*lead, pl.ds(row, CHUNK), pl.ds(at, LANES))] for at in range(0, ref.shape[-1], LANES)
    ]


def put_plain(ref, lead, row, value):
    for block, part in enumerate(value):
        ref[(*lead, pl.ds(row, CHUNK), pl.ds(block * LANES, LANES))] = part


def flat(ref, lead, row):
    return [ref[(*lead, block, pl.ds(row, CHUNK))] for block in range(ref.shape[-3])]


def put_flat(ref, lead, row, value):
    for block, part in enumerate(value):
        ref[(*lead, block, pl.ds(row, CHUNK))] = part


def padded(ref, lead, row, shift=0):
    return [ref[(*lead, block, pl.ds(PAD + row + shift, CHUNK))] for block in range(ref.shape[-3])]


def put_padded(ref, lead, row, value):
    ny = ref.shape[-2] - 2 * PAD
    for block, part in enumerate(value):
        ref[(*lead, block, pl.ds(PAD + row, CHUNK))] = part
        if row == 0:
            ref[(*lead, block, pl.ds(PAD + ny, 1))] = part[:1]
        if row + CHUNK == ny:
            ref[(*lead, block, pl.ds(PAD - 1, 1))] = part[CHUNK - 1 :]


def lane():
    return lax.broadcasted_iota(jnp.int32, (CHUNK, LANES), 1)


def after_z(value):
    turned = [pltpu.roll(part, LANES - 1, 1) for part in value]
    turned.append(turned[0])
    edge = lane() == LANES - 1
    return [jnp.where(edge, turned[at + 1], turned[at]) for at in range(len(value))]


def before_z(value):
    turned = [pltpu.roll(part, 1, 1) for part in value]
    edge = lane() == 0
    return [jnp.where(edge, turned[at - 1], turned[at]) for at in range(len(value))]


def side():
    return lax.rem(lax.axis_index("gx"), 2)


def either(first, second):
    return first + side() * (second - first)


class Line:
    def __init__(self, *parts):
        self.parts = parts

    def __call__(self, at, *lead):
        for ref, first, last in self.parts:
            if first <= at <= last:
                return ref, (*lead, at - first)
        raise IndexError(at)


def each(function, *values):
    return [function(*parts) for parts in zip(*values)]


def beside(low, high, up, down, mid):
    return each(
        lambda a, b, c, d, e, f: (a + b) + (c + d) + (e + f),
        low, high, up, down, after_z(mid), before_z(mid),
    )


def potential(low, mid, high, up, down):
    return each(
        lambda c, total: c * (c * c + (6.0 * stiffness - 1.0)) - stiffness * total,
        mid, beside(low, high, up, down, mid),
    )


class Faces:
    def __init__(self, mx, my, mz, mz_low, m_all):
        self.mx, self.my, self.mz, self.mz_low, self.all = mx, my, mz, mz_low, m_all

    def flow(self, row, at, mid, up, down, low=None, high=None):
        total = each(
            lambda a, b, c, d, e, u, v, w, x, y: (a * u + b * v) + (c * w + d * x) - e * y,
            padded(*self.my(at), row), padded(*self.my(at), row, -1), flat(*self.mz(at), row),
            flat(*self.mz_low(at), row), flat(*self.all(at), row), up, down, after_z(mid), before_z(mid), mid,
        )
        if low is not None:
            total = add_product(total, flat(*self.mx(at - 1), row), low)
        if high is not None:
            total = add_product(total, flat(*self.mx(at), row), high)
        return total


def add_product(total, a, b):
    return each(lambda t, x, y: t + x * y, total, a, b)


def sub(a, b):
    return each(lambda x, y: x - y, a, b)


def own_kernel(initial, mobility, conc, mob, to_chip, to_core):
    runs, n, ny, _ = initial.shape
    place = [either(n - 1 - at, at) for at in range(n)]

    def one_run(run, carry):
        for row in chunks(ny):
            for at in range(n):
                value = plain(initial, (run, place[at]), row)
                put_padded(conc, (run, at), row, value)
                if at < 2:
                    put_flat(to_core, (2 * run + at,), row, value)
                if at >= n - 2:
                    put_flat(to_chip, (2 * run + n - 1 - at,), row, value)
        return carry

    lax.fori_loop(0, runs, one_run, 0)
    for row in chunks(ny):
        for at in range(n):
            value = plain(mobility, (place[at],), row)
            put_padded(mob, (at,), row, value)
            if at == 0:
                put_flat(to_core, (2 * runs,), row, value)
            if at == n - 1:
                put_flat(to_chip, (2 * runs,), row, value)


def mean(a, b):
    return 0.5 * (a + b)


def put_faces(row, mob, places, my, mz, mz_low):
    for at in places:
        mid = padded(*mob(at), row)
        put_padded(*my(at), row, each(mean, mid, padded(*mob(at), row, 1)))
        put_flat(*mz(at), row, each(mean, mid, after_z(mid)))
        put_flat(*mz_low(at), row, each(mean, mid, before_z(mid)))


def put_all(row, faces, places):
    for at in places:
        put_flat(*faces.all(at), row, each(
            lambda a, b, c, d, e, f: (a + b) + (c + d) + (e + f),
            flat(*faces.mx(at - 1), row), flat(*faces.mx(at), row), padded(*faces.my(at), row),
            padded(*faces.my(at), row, -1), flat(*faces.mz(at), row), flat(*faces.mz_low(at), row),
        ))


def put_potential(row, field, run, places, target):
    mids = {at: padded(*field(at, run), row) for at in range(places[0] - 1, places[-1] + 2)}
    for at in places:
        value = potential(
            mids[at - 1], mids[at], mids[at + 1],
            padded(*field(at, run), row, 1), padded(*field(at, run), row, -1),
        )
        put_padded(*target(at, run), row, value)


def put_step(row, faces, chem, state, run, places, target):
    mids = {at: padded(*chem(at, run), row) for at in range(places[0] - 1, places[-1] + 2)}
    for at in places:
        flow = faces.flow(
            row, at, mids[at], padded(*chem(at, run), row, 1), padded(*chem(at, run), row, -1),
            mids[at - 1], mids[at + 1],
        )
        value = each(lambda a, b: a + time_step * b, padded(*state(at, run), row), flow)
        target(at, value)


def put_miss(row, runs, observed, place, run, at, value, adjoint2):
    miss = sub(value, plain(observed, (run, place[at]), row))
    adjoint = each(lambda a: a * (1.0 / runs), miss)
    put_padded(*adjoint2(at, run), row, adjoint)
    return adjoint, sum(part * part for part in miss)


def core_kernel(
    of_core, conc_own, mob_own, mob_low, mx, my, mz, mz_low, m_all, chem0, state1, rim,
):
    runs, n = conc_own.shape[:2]
    ny = of_core.shape[-2]
    mob = Line((mob_low, -1, -1), (mob_own, 0, n - 1))
    faces = Faces(
        Line((mx, -1, n - 2)), Line((my, 0, n - 1)), Line((mz, 0, n - 1)), Line((mz_low, 0, n - 1)),
        Line((m_all, 0, n - 2)),
    )
    conc = Line((rim, -2, -1), (conc_own, 0, n - 1))
    chem = Line((chem0, -1, n - 2))
    for row in chunks(ny):
        put_padded(mob_low, (0,), row, flat(of_core, (2 * runs,), row))
    for row in chunks(ny):
        mids = [padded(*mob(at), row) for at in range(-1, n)]
        for at in range(n):
            put_flat(mx, (at,), row, each(mean, mids[at], mids[at + 1]))
        put_faces(row, mob, range(n), faces.my, faces.mz, faces.mz_low)
    for row in chunks(ny):
        put_all(row, faces, range(n - 1))

    def one_run(run, carry):
        for row in chunks(ny):
            for at in range(2):
                put_padded(rim, (run, 1 - at), row, flat(of_core, (2 * run + at,), row))
        for row in chunks(ny):
            put_potential(row, conc, run, range(-1, n - 1), chem)
        for row in chunks(ny):
            put_step(
                row, faces, chem, conc, run, range(n - 2),
                lambda at, value: put_padded(state1, (run, at), row, value),
            )
        return carry

    lax.fori_loop(0, runs, one_run, 0)


def chip_kernel(
    of_chip, conc_own, mob_own, mx_a, my_a, mz_a, mz_low_a, all_a, chem0_a, state1_a,
    mob_high, mx_b, all_b, chem0_b, state1_b, to_chip, to_core, rim,
):
    runs, n = conc_own.shape[:2]
    ny = of_chip.shape[-2]
    mob = Line((mob_own, 0, n - 1), (mob_high, n, n))
    faces = Faces(
        Line((mx_a, -1, n - 2), (mx_b, n - 1, n - 1)), Line((my_a, 0, n - 1)), Line((mz_a, 0, n - 1)),
        Line((mz_low_a, 0, n - 1)), Line((all_a, 0, n - 2), (all_b, n - 1, n - 1)),
    )
    conc = Line((conc_own, 0, n - 1), (rim, n, n + 1))
    chem = Line((chem0_a, -1, n - 2), (chem0_b, n - 1, n))
    state1 = Line((state1_a, 0, n - 3), (state1_b, n - 2, n - 1))
    for row in chunks(ny):
        value = flat(of_chip, (2 * runs,), row)
        put_padded(mob_high, (0,), row, value)
        put_flat(mx_b, (0,), row, each(mean, padded(*mob(n - 1), row), value))
        put_all(row, faces, range(n - 1, n))

    def one_run(run, carry):
        for row in chunks(ny):
            for at in range(2):
                put_padded(rim, (run, at), row, flat(of_chip, (2 * run + at,), row))
        for row in chunks(ny):
            put_potential(row, conc, run, range(n - 1, n + 1), chem)
        for row in chunks(ny):

            def target(at, value):
                put_padded(state1_b, (run, at - (n - 2)), row, value)
                put_flat(to_chip, (2 * run + n - 1 - at,), row, value)

            put_step(row, faces, chem, conc, run, range(n - 2, n), target)
            for at in range(2):
                put_flat(to_core, (2 * run + at,), row, padded(*state1(at, run), row))
        return carry

    lax.fori_loop(0, runs, one_run, 0)


def second_core_kernel(
    of_core, state1_a, state1_b, observed, mx_a, my_a, mz_a, mz_low_a, all_a,
    state1_low, chem1, adjoint2, squares,
):
    runs, n, ny, _ = observed.shape
    faces = Faces(
        Line((mx_a, -1, n - 2)), Line((my_a, 0, n - 1)), Line((mz_a, 0, n - 1)), Line((mz_low_a, 0, n - 1)),
        Line((all_a, 0, n - 2)),
    )
    place = [either(n - 1 - at, at) for at in range(n)]
    state1 = Line((state1_low, -2, -1), (state1_a, 0, n - 3), (state1_b, n - 2, n - 1))
    chem = Line((chem1, -1, n - 2))
    squares[...] = jnp.zeros_like(squares)

    def one_run(run, carry):
        for row in chunks(ny):
            for at in range(2):
                put_padded(state1_low, (run, 1 - at), row, flat(of_core, (2 * run + at,), row))
        for row in chunks(ny):
            put_potential(row, state1, run, range(-1, n - 1), chem)
        for row in chunks(ny):

            def target(at, value):
                squares[...] += put_miss(row, runs, observed, place, run, at, value, Line((adjoint2, 0, n - 3)))[1]

            put_step(row, faces, chem, state1, run, range(n - 2), target)
        return carry

    lax.fori_loop(0, runs, one_run, 0)


def second_chip_kernel(
    of_chip, state1_a, state1_b, chem1_a, adjoint2_a, squares, observed, mob,
    mx_a, my_a, mz_a, mz_low_a, all_a, mx_b, all_b,
    state1_high, chem1_b, adjoint2_b, to_core, to_chip, share, total,
):
    runs, n, ny, _ = observed.shape
    faces = Faces(
        Line((mx_a, -1, n - 2), (mx_b, n - 1, n - 1)), Line((my_a, 0, n - 1)), Line((mz_a, 0, n - 1)),
        Line((mz_low_a, 0, n - 1)), Line((all_a, 0, n - 2), (all_b, n - 1, n - 1)),
    )
    place = [either(n - 1 - at, at) for at in range(n)]
    state1 = Line((state1_a, 0, n - 3), (state1_b, n - 2, n - 1), (state1_high, n, n + 1))
    chem = Line((chem1_a, -1, n - 2), (chem1_b, n - 1, n))
    adjoint2 = Line((adjoint2_a, 0, n - 3), (adjoint2_b, n - 2, n - 1))
    total[...] = squares[...]

    def one_run(run, carry):
        for row in chunks(ny):
            for at in range(2):
                put_padded(state1_high, (run, at), row, flat(of_chip, (2 * run + at,), row))
        for row in chunks(ny):
            put_potential(row, state1, run, range(n - 1, n + 1), chem)
        for row in chunks(ny):

            def target(at, value):
                adjoint, square = put_miss(row, runs, observed, place, run, at, value, adjoint2)
                total[...] += square
                put_flat(to_chip, (3 * run + n - 1 - at,), row, adjoint)
                if at < 3:
                    put_flat(to_core, (3 * run + at,), row, adjoint)

            put_step(row, faces, chem, state1, run, range(n - 2, n), target)
            put_flat(to_chip, (3 * run + 2,), row, padded(*adjoint2(n - 3, run), row))
            for at in range(min(3, n - 2)):
                put_flat(to_core, (3 * run + at,), row, padded(*adjoint2(at, run), row))
        return carry

    lax.fori_loop(0, runs, one_run, 0)
    for row in chunks(ny):
        for at in range(2):
            put_flat(to_chip, (3 * runs + at,), row, padded(mob, (n - 2 - at,), row))
            put_flat(to_core, (3 * runs + at,), row, padded(mob, (1 + at,), row))
    columns = (0.5 / runs) * jnp.sum(total[...], axis=0, keepdims=True)
    mine = jnp.broadcast_to(jnp.sum(columns, axis=1, keepdims=True), share.shape)
    share[...] = mine
    to_core[0, 0, ny:] = mine


def put_adjoint1(row, flow, adjoint2, run, places, weight, target):
    mids = {at: padded(*flow(at, run), row) for at in range(places[0] - 1, places[-1] + 2)}
    for at in places:
        total = beside(
            mids[at - 1], mids[at + 1], padded(*flow(at, run), row, 1), padded(*flow(at, run), row, -1), mids[at]
        )
        value = each(
            lambda a, w, f, t: a + w * f - (time_step * stiffness) * t,
            padded(*adjoint2(at, run), row), weight(at), mids[at], total,
        )
        put_padded(*target(at, run), row, value)


def slope(state):
    return each(lambda c: time_step * (3.0 * c * c + (6.0 * stiffness - 1.0)), state)


def step_x(field, run, at, row):
    return sub(padded(*field(at + 1, run), row), padded(*field(at, run), row))


def step_y(field, run, at, row):
    return sub(padded(*field(at, run), row, 1), padded(*field(at, run), row))


def step_z(field, run, at, row):
    mid = padded(*field(at, run), row)
    return sub(after_z(mid), mid)


class Backward:
    names = (
        "mx_a", "my_a", "mz_a", "mz_low_a", "all_a", "mx_b", "all_b",
        "chem0_a", "chem0_b", "state1_low", "state1_a", "state1_b", "state1_high", "chem1_a", "chem1_b",
        "adjoint2_a", "adjoint2_b",
    )

    def __init__(self, n, refs, low=None, high=None):
        at = dict(zip(self.names, refs))

        def line(which, shift, *own):
            outer = ((low[which], shift - 2, shift - 1),) if low else ((high[which], n, n + 1),)
            return Line(*own, *outer)

        self.faces = Faces(
            line(0, -1, (at["mx_a"], -1, n - 2), (at["mx_b"], n - 1, n - 1)),
            *(line(1 + which, 0, (at[name], 0, n - 1)) for which, name in enumerate(("my_a", "mz_a", "mz_low_a"))),
            line(4, 0, (at["all_a"], 0, n - 2), (at["all_b"], n - 1, n - 1)),
        )
        self.chem0 = Line((at["chem0_a"], -1, n - 2), (at["chem0_b"], n - 1, n))
        self.state1 = Line(
            (at["state1_low"], -2, -1), (at["state1_a"], 0, n - 3), (at["state1_b"], n - 2, n - 1),
            (at["state1_high"], n, n + 1),
        )
        self.chem1 = Line((at["chem1_a"], -1, n - 2), (at["chem1_b"], n - 1, n))
        self.adjoint2 = ((at["adjoint2_a"], 0, n - 3), (at["adjoint2_b"], n - 2, n - 1))


def put_outer(ny, message, first, mob, to, faces, places):
    for row in chunks(ny):
        for at in range(2):
            put_padded(*mob(to[at]), row, flat(message, (first + at,), row))
    for row in chunks(ny):
        mids = {at: padded(*mob(at), row) for at in range(min(places[0], *to), max(places[1], *to) + 1)}
        for at in sorted(mids)[:-1]:
            put_flat(*faces.mx(at), row, each(mean, mids[at], mids[at + 1]))
        put_faces(row, mob, places, faces.my, faces.mz, faces.mz_low)
    for row in chunks(ny):
        put_all(row, faces, places)


def early_kernel(of_core, mob_low, share_in, *refs):
    count = len(Backward.names)
    kept, refs = refs[:count], refs[count:]
    flow_a, flow_part, adjoint1_a, weight_b, step_z_b, part, sum_x_b, sum_y_b, sum_z_b, share = refs[:10]
    rim, sum_x, sum_y, sum_z, m_rim, *low = refs[10:]
    share[...] = share_in[...]
    n = part.shape[0] + 2
    runs = flow_a.shape[0]
    ny = part.shape[-2]
    at_ = Backward(n, kept, low=low)
    faces, chem0, state1, chem1 = at_.faces, at_.chem0, at_.state1, at_.chem1
    adjoint2 = Line((rim, -3, -1), *at_.adjoint2)
    flow = Line((flow_a, -2, n - 2), (flow_part, n - 1, n - 1))
    adjoint1 = Line((adjoint1_a, -1, n - 3))
    mob = Line((m_rim, -3, -2), (mob_low, -1, -1))
    put_outer(ny, of_core, 3 * runs, mob, (-2, -3), faces, (-2, -1))
    for sums in (sum_x, sum_y, sum_z):
        sums[...] = jnp.zeros_like(sums)

    def one_run(run, carry):
        for row in chunks(ny):
            for at in range(3):
                put_padded(rim, (run, 2 - at), row, flat(of_core, (3 * run + at,), row))
        for row in chunks(ny):
            mids = {at: padded(*adjoint2(at, run), row) for at in range(-3, n)}
            for at in range(-2, n):
                value = faces.flow(
                    row, at, mids[at], padded(*adjoint2(at, run), row, 1), padded(*adjoint2(at, run), row, -1),
                    mids[at - 1], mids.get(at + 1),
                )
                put_padded(*flow(at, run), row, value)
        for row in chunks(ny):
            put_adjoint1(
                row, flow, adjoint2, run, range(-1, n - 2),
                lambda at: slope(padded(*state1(at, run), row)), adjoint1,
            )
            for at in range(n - 2, n + 1):
                put_flat(weight_b, (run, at - (n - 2)), row, slope(padded(*state1(at, run), row)))
        for row in chunks(ny):
            for at in range(-1, n - 1):
                total = add_product(
                    flat(sum_x, (at + 1,), row), step_x(adjoint2, run, at, row), step_x(chem1, run, at, row)
                )
                if at < n - 3:
                    total = add_product(total, step_x(adjoint1, run, at, row), step_x(chem0, run, at, row))
                put_flat(sum_x, (at + 1,), row, total)
            for at in range(n):
                total_y = add_product(
                    padded(sum_y, (at,), row), step_y(adjoint2, run, at, row), step_y(chem1, run, at, row)
                )
                total_z = add_product(
                    flat(sum_z, (at,), row), step_z(adjoint2, run, at, row), step_z(chem1, run, at, row)
                )
                slant = step_z(chem0, run, at, row)
                if at < n - 2:
                    total_y = add_product(total_y, step_y(adjoint1, run, at, row), step_y(chem0, run, at, row))
                    total_z = add_product(total_z, step_z(adjoint1, run, at, row), slant)
                else:
                    put_flat(step_z_b, (run, at - (n - 2)), row, slant)
                put_padded(sum_y, (at,), row, total_y)
                put_flat(sum_z, (at,), row, total_z)
        return carry

    lax.fori_loop(0, runs, one_run, 0)
    for row in chunks(ny):
        for at in range(n - 2):
            sides_z = flat(sum_z, (at,), row)
            value = each(
                lambda a, b, c, d, e: -0.5 * ((a + b) + (c + d) + e),
                padded(sum_y, (at,), row), padded(sum_y, (at,), row, -1), sides_z, before_z(sides_z),
                flat(sum_x, (at,), row),
            )
            if at < n - 3:
                value = each(lambda a, b: a - 0.5 * b, value, flat(sum_x, (at + 1,), row))
            put_flat(part, (at,), row, value)
        for at in range(2):
            put_flat(sum_x_b, (at,), row, flat(sum_x, (n - 2 + at,), row))
            put_flat(sum_y_b, (at,), row, padded(sum_y, (n - 2 + at,), row))
            put_flat(sum_z_b, (at,), row, flat(sum_z, (n - 2 + at,), row))


def late_kernel(of_chip, mob_high, *refs):
    count = len(Backward.names)
    kept, refs = refs[:count], refs[count:]
    flow_a, flow_part, adjoint1_a, weight_b, step_z_b, part, sum_x_b, sum_y_b, sum_z_b, result = refs[:10]
    rim, flow_b, adjoint1_b, sum_x, sum_y, sum_z, m_rim, *high = refs[10:]
    runs = flow_a.shape[0]
    n, ny, _ = result.shape
    at_ = Backward(n, kept, high=high)
    faces, chem0, chem1 = at_.faces, at_.chem0, at_.chem1
    mob = Line((mob_high, n, n), (m_rim, n + 1, n + 2))
    put_outer(ny, of_chip, 3 * runs, mob, (n + 1, n + 2), faces, (n, n + 1))
    place = [either(n - 1 - at, at) for at in range(n)]
    adjoint2 = Line(*at_.adjoint2, (rim, n, n + 2))
    flow = Line((flow_a, -2, n - 2), (flow_b, n - 1, n + 1))
    adjoint1 = Line((adjoint1_a, -1, n - 3), (adjoint1_b, n - 2, n))
    for row in chunks(ny):
        for at in range(2):
            put_flat(sum_x, (at,), row, flat(sum_x_b, (at,), row))
            put_padded(sum_y, (at,), row, flat(sum_y_b, (at,), row))
            put_flat(sum_z, (at,), row, flat(sum_z_b, (at,), row))
    sum_x[2] = jnp.zeros_like(sum_x[2])

    def one_run(run, carry):
        for row in chunks(ny):
            for at in range(3):
                put_padded(rim, (run, at), row, flat(of_chip, (3 * run + at,), row))
        for row in chunks(ny):
            mids = {at: padded(*adjoint2(at, run), row) for at in range(n - 1, n + 3)}
            value = add_product(padded(flow_part, (run, 0), row), flat(*faces.mx(n - 1), row), mids[n])
            put_padded(*flow(n - 1, run), row, value)
            for at in range(n, n + 2):
                value = faces.flow(
                    row, at, mids[at], padded(*adjoint2(at, run), row, 1), padded(*adjoint2(at, run), row, -1),
                    mids[at - 1], mids[at + 1],
                )
                put_padded(*flow(at, run), row, value)
        for row in chunks(ny):
            put_adjoint1(
                row, flow, adjoint2, run, range(n - 2, n + 1),
                lambda at: flat(weight_b, (run, at - (n - 2)), row), adjoint1,
            )
        for row in chunks(ny):
            for at in range(n - 3, n):
                total = add_product(
                    flat(sum_x, (at - (n - 3),), row), step_x(adjoint1, run, at, row), step_x(chem0, run, at, row)
                )
                if at == n - 1:
                    total = add_product(total, step_x(adjoint2, run, at, row), step_x(chem1, run, at, row))
                put_flat(sum_x, (at - (n - 3),), row, total)
            for at in range(n - 2, n):
                to = (at - (n - 2),)
                put_padded(sum_y, to, row, add_product(
                    padded(sum_y, to, row), step_y(adjoint1, run, at, row), step_y(chem0, run, at, row)
                ))
                put_flat(sum_z, to, row, add_product(
                    flat(sum_z, to, row), step_z(adjoint1, run, at, row), flat(step_z_b, (run, *to), row)
                ))
        return carry

    lax.fori_loop(0, runs, one_run, 0)
    for row in chunks(ny):
        for at in range(n - 2):
            value = flat(part, (at,), row)
            if at == n - 3:
                value = each(lambda a, b: a - 0.5 * b, value, flat(sum_x, (0,), row))
            put_plain(result, (place[at],), row, value)
        for at in range(2):
            sides = flat(sum_z, (at,), row)
            value = each(
                lambda a, b, c, d, e, f: -0.5 * ((a + b) + (c + d) + (e + f)),
                flat(sum_x, (at,), row), flat(sum_x, (at + 1,), row),
                padded(sum_y, (at,), row), padded(sum_y, (at,), row, -1), sides, before_z(sides),
            )
            put_plain(result, (place[n - 2 + at],), row, value)


def misfit_kernel(share, far, misfit):
    misfit[0] = (share[...] + far[...])[0, 0]


def call(kernel, outs, scratch, args, flops, spaces=(VMEM, VMEM)):
    moved = 4 * (sum(a.size for a in args) + sum(math.prod(o) for o in outs))
    return pl.pallas_call(
        kernel,
        out_shape=tuple(jax.ShapeDtypeStruct(o, jnp.float32) for o in outs),
        in_specs=[spaces[0]] * len(args),
        out_specs=tuple([spaces[1]] * len(outs)),
        scratch_shapes=[pltpu.VMEM(s, jnp.float32) for s in scratch],
        compiler_params=pltpu.CompilerParams(vmem_limit_bytes=16 * 1024 * 1024),
        cost_estimate=pl.CostEstimate(flops=flops, bytes_accessed=moved, transcendentals=0),
    )(*args)


def on_device(initial, observed, mobility):
    runs, n, ny, nz = initial.shape
    blocks = nz // LANES
    count = lax.axis_size("gx")
    over_chips = [(i, (i - 1 + 2 * (i % 2)) % count) for i in range(count)]
    over_cores = [(i, i ^ 1) for i in range(count)]
    cell = ny * nz

    def neighbours(to_chip, to_core):
        of_core = lax.ppermute(to_core, "gx", over_cores)
        return lax.ppermute(to_chip, "gx", over_chips), of_core

    def lies(*lead):
        return (*lead, blocks, ny, LANES)

    def lies_padded(*lead):
        return (*lead, blocks, ny + 2 * PAD, LANES)

    conc, mob, to_chip, to_core = call(
        own_kernel,
        (
            lies_padded(runs, n), lies_padded(n), lies(2 * runs + 1), lies(2 * runs + 1),
        ),
        (),
        (initial, mobility),
        runs * n * cell,
    )
    of_chip, of_core = neighbours(to_chip, to_core)
    mob_low, *faces_a, chem0_a, state1_a = call(
        core_kernel,
        (
            lies_padded(1), lies(n), lies_padded(n), lies(n), lies(n), lies(n - 1),
            lies_padded(runs, n), lies_padded(runs, n - 2),
        ),
        (lies_padded(runs, 2),),
        (of_core, conc, mob),
        30 * runs * 2 * n * cell,
    )
    mob_high, *faces_b, chem0_b, state1_b, to_chip, to_core = call(
        chip_kernel,
        (
            lies_padded(1), lies(1), lies(1), lies_padded(runs, 2), lies_padded(runs, 2),
            lies(2 * runs), lies(2 * runs),
        ),
        (lies_padded(runs, 2),),
        (of_chip, conc, mob, *faces_a, chem0_a, state1_a),
        30 * runs * 4 * cell,
    )
    of_chip, of_core = neighbours(to_chip, to_core)
    state1_low, chem1_a, adjoint2_a, squares = call(
        second_core_kernel,
        (lies_padded(runs, 2), lies_padded(runs, n), lies_padded(runs, n - 2), (CHUNK, LANES)),
        (),
        (of_core, state1_a, state1_b, observed, *faces_a),
        30 * runs * (2 * n - 2) * cell,
    )
    state1_high, chem1_b, adjoint2_b, to_core, to_chip, share = call(
        second_chip_kernel,
        (
            lies_padded(runs, 2), lies_padded(runs, 2), lies_padded(runs, 2),
            (3 * runs + 2, blocks, ny + ROWS, LANES), lies(3 * runs + 2), (ROWS, LANES),
        ),
        ((CHUNK, LANES),),
        (of_chip, state1_a, state1_b, chem1_a, adjoint2_a, squares, observed, mob, *faces_a, *faces_b),
        30 * runs * 4 * cell,
    )
    kept = (
        *faces_a, *faces_b, chem0_a, chem0_b, state1_low, state1_a, state1_b, state1_high, chem1_a, chem1_b,
        adjoint2_a, adjoint2_b,
    )
    of_chip, of_core = neighbours(to_chip, to_core)
    hops = [1 << bit for bit in range(count.bit_length() - 2, 0, -1)]

    def hop_of(value, hop):
        return lax.ppermute(value, "gx", [(i, i ^ hop) for i in range(count)])

    share = share + of_core[0, 0, ny:]
    far = hop_of(share, hops[0])
    outer = (lies_padded(2), lies(2), lies_padded(2), lies(2), lies(2), lies(2))
    *done, share = call(
        early_kernel,
        (
            lies_padded(runs, n + 1), lies_padded(runs, 1), lies_padded(runs, n - 1), lies(runs, 3), lies(runs, 2),
            lies(n - 2), lies(2), lies(2), lies(2), (ROWS, LANES),
        ),
        (lies_padded(runs, 3), lies(n), lies_padded(n), lies(n), *outer),
        (of_core, mob_low, share, *kept),
        60 * runs * n * cell,
    )
    for hop in hops[1:]:
        share = share + far
        far = hop_of(share, hop)
    (result,) = call(
        late_kernel,
        ((n, ny, nz),),
        (
            lies_padded(runs, 3), lies_padded(runs, 3), lies_padded(runs, 3),
            lies(3), lies_padded(2), lies(2), *outer,
        ),
        (of_chip, mob_high, *kept, *done),
        60 * runs * 3 * cell,
    )
    (misfit,) = call(misfit_kernel, ((1,),), (), (share, far), 1, (VMEM, SMEM))
    return (result, misfit)


def solution(mesh):
    placed = (
        P("group", "gx", None, None),
        P("group", "gx", None, None),
        P(("group", "gx"), None, None),
    )
    return jax.shard_map(
        on_device,
        mesh=mesh,
        in_specs=placed,
        out_specs=(P(("group", "gx"), None, None), P("group")),
        check_vma=False,
    )
```

```python
import functools
import math

import jax
import jax.numpy as jnp
from jax import lax
from jax.experimental import pallas as pl
from jax.experimental.pallas import tpu as pltpu
from jax.sharding import PartitionSpec as P

stiffness = 0.5
time_step = 0.005
VMEM = pl.BlockSpec(memory_space=pltpu.VMEM)
SMEM = pl.BlockSpec(memory_space=pltpu.SMEM)
LANES = 128
ROWS = 8
PAD = ROWS
CHUNK = 16


def chunks(ny):
    return range(0, ny, CHUNK)


def plain(ref, lead, row):
    return [
        ref[(*lead, pl.ds(row, CHUNK), pl.ds(at, LANES))] for at in range(0, ref.shape[-1], LANES)
    ]


def put_plain(ref, lead, row, value):
    for block, part in enumerate(value):
        ref[(*lead, pl.ds(row, CHUNK), pl.ds(block * LANES, LANES))] = part


def flat(ref, lead, row):
    return [ref[(*lead, block, pl.ds(row, CHUNK))] for block in range(ref.shape[-3])]


def put_flat(ref, lead, row, value):
    for block, part in enumerate(value):
        ref[(*lead, block, pl.ds(row, CHUNK))] = part


def padded(ref, lead, row, shift=0):
    return [ref[(*lead, block, pl.ds(PAD + row + shift, CHUNK))] for block in range(ref.shape[-3])]


def put_padded(ref, lead, row, value):
    ny = ref.shape[-2] - 2 * PAD
    for block, part in enumerate(value):
        ref[(*lead, block, pl.ds(PAD + row, CHUNK))] = part
        if row == 0:
            ref[(*lead, block, pl.ds(PAD + ny, 1))] = part[:1]
        if row + CHUNK == ny:
            ref[(*lead, block, pl.ds(PAD - 1, 1))] = part[CHUNK - 1 :]


def lane():
    return lax.broadcasted_iota(jnp.int32, (CHUNK, LANES), 1)


def after_z(value):
    turned = [pltpu.roll(part, LANES - 1, 1) for part in value]
    turned.append(turned[0])
    edge = lane() == LANES - 1
    return [jnp.where(edge, turned[at + 1], turned[at]) for at in range(len(value))]


def before_z(value):
    turned = [pltpu.roll(part, 1, 1) for part in value]
    edge = lane() == 0
    return [jnp.where(edge, turned[at - 1], turned[at]) for at in range(len(value))]


def side():
    return lax.rem(lax.axis_index("gx"), 2)


def either(first, second):
    return first + side() * (second - first)


class Line:
    def __init__(self, *parts):
        self.parts = parts

    def __call__(self, at, *lead):
        for ref, first, last in self.parts:
            if first <= at <= last:
                return ref, (*lead, at - first)
        raise IndexError(at)


def each(function, *values):
    return [function(*parts) for parts in zip(*values)]


def beside(low, high, up, down, mid):
    return each(
        lambda a, b, c, d, e, f: (a + b) + (c + d) + (e + f),
        low, high, up, down, after_z(mid), before_z(mid),
    )


def potential(low, mid, high, up, down):
    return each(
        lambda c, total: c * (c * c + (6.0 * stiffness - 1.0)) - stiffness * total,
        mid, beside(low, high, up, down, mid),
    )


class Faces:
    def __init__(self, mx, my, mz, mz_low, m_all):
        self.mx, self.my, self.mz, self.mz_low, self.all = mx, my, mz, mz_low, m_all

    def flow(self, row, at, mid, up, down, low=None, high=None):
        total = each(
            lambda a, b, c, d, e, u, v, w, x, y: (a * u + b * v) + (c * w + d * x) - e * y,
            padded(*self.my(at), row), padded(*self.my(at), row, -1), flat(*self.mz(at), row),
            flat(*self.mz_low(at), row), flat(*self.all(at), row), up, down, after_z(mid), before_z(mid), mid,
        )
        if low is not None:
            total = add_product(total, flat(*self.mx(at - 1), row), low)
        if high is not None:
            total = add_product(total, flat(*self.mx(at), row), high)
        return total


def add_product(total, a, b):
    return each(lambda t, x, y: t + x * y, total, a, b)


def sub(a, b):
    return each(lambda x, y: x - y, a, b)


def own_kernel(initial, mobility, conc, mob, to_chip, to_core):
    runs, n, ny, _ = initial.shape
    place = [either(n - 1 - at, at) for at in range(n)]

    def one_run(run, carry):
        for row in chunks(ny):
            for at in range(n):
                value = plain(initial, (run, place[at]), row)
                put_padded(conc, (run, at), row, value)
                if at < 2:
                    put_flat(to_core, (2 * run + at,), row, value)
                if at >= n - 2:
                    put_flat(to_chip, (2 * run + n - 1 - at,), row, value)
        return carry

    lax.fori_loop(0, runs, one_run, 0)
    for row in chunks(ny):
        for at in range(n):
            value = plain(mobility, (place[at],), row)
            put_padded(mob, (at,), row, value)
            if at == 0:
                put_flat(to_core, (2 * runs,), row, value)
            if at == n - 1:
                put_flat(to_chip, (2 * runs,), row, value)


def mean(a, b):
    return 0.5 * (a + b)


def put_faces(row, mob, places, my, mz, mz_low):
    for at in places:
        mid = padded(*mob(at), row)
        put_padded(*my(at), row, each(mean, mid, padded(*mob(at), row, 1)))
        put_flat(*mz(at), row, each(mean, mid, after_z(mid)))
        put_flat(*mz_low(at), row, each(mean, mid, before_z(mid)))


def put_all(row, faces, places):
    for at in places:
        put_flat(*faces.all(at), row, each(
            lambda a, b, c, d, e, f: (a + b) + (c + d) + (e + f),
            flat(*faces.mx(at - 1), row), flat(*faces.mx(at), row), padded(*faces.my(at), row),
            padded(*faces.my(at), row, -1), flat(*faces.mz(at), row), flat(*faces.mz_low(at), row),
        ))


def put_potential(row, field, run, places, target):
    mids = {at: padded(*field(at, run), row) for at in range(places[0] - 1, places[-1] + 2)}
    for at in places:
        value = potential(
            mids[at - 1], mids[at], mids[at + 1],
            padded(*field(at, run), row, 1), padded(*field(at, run), row, -1),
        )
        put_padded(*target(at, run), row, value)


def put_step(row, faces, chem, state, run, places, target):
    mids = {at: padded(*chem(at, run), row) for at in range(places[0] - 1, places[-1] + 2)}
    for at in places:
        flow = faces.flow(
            row, at, mids[at], padded(*chem(at, run), row, 1), padded(*chem(at, run), row, -1),
            mids[at - 1], mids[at + 1],
        )
        value = each(lambda a, b: a + time_step * b, padded(*state(at, run), row), flow)
        target(at, value)


def put_miss(row, runs, observed, place, run, at, value, adjoint2):
    miss = sub(value, plain(observed, (run, place[at]), row))
    adjoint = each(lambda a: a * (1.0 / runs), miss)
    put_padded(*adjoint2(at, run), row, adjoint)
    return adjoint, sum(part * part for part in miss)


def first_own_kernel(conc_own, mob_own, mx, my, mz, mz_low, m_all, chem0):
    runs, n = conc_own.shape[:2]
    ny = conc_own.shape[-2] - 2 * PAD
    mob = Line((mob_own, 0, n - 1))
    conc = Line((conc_own, 0, n - 1))
    faces = Faces(
        Line((mx, 0, n - 2)), Line((my, 0, n - 1)), Line((mz, 0, n - 1)), Line((mz_low, 0, n - 1)),
        Line((m_all, 1, n - 2)),
    )
    for row in chunks(ny):
        mids = [padded(*mob(at), row) for at in range(n)]
        for at in range(n - 1):
            put_flat(mx, (at,), row, each(mean, mids[at], mids[at + 1]))
        put_faces(row, mob, range(n), faces.my, faces.mz, faces.mz_low)
    for row in chunks(ny):
        put_all(row, faces, range(1, n - 1))

    def one_run(run, carry):
        for row in chunks(ny):
            put_potential(row, conc, run, range(1, n - 1), Line((chem0, 1, n - 2)))
        return carry

    lax.fori_loop(0, runs, one_run, 0)


def all_faces(n, refs):
    mx, my, mz, mz_low, m_all, mx_low, mx_high, all_low, all_high = refs
    return Faces(
        Line((mx_low, -1, -1), (mx, 0, n - 2), (mx_high, n - 1, n - 1)),
        Line((my, 0, n - 1)), Line((mz, 0, n - 1)), Line((mz_low, 0, n - 1)),
        Line((all_low, 0, 0), (m_all, 1, n - 2), (all_high, n - 1, n - 1)),
    )


def ends(n, low, own, high):
    return Line((low, -1, 0), (own, 1, n - 2), (high, n - 1, n))


def first_kernel(
    of_chip, of_core, conc_own, mob_own, chem0_own, mx, my, mz, mz_low, m_all,
    mob_low, mob_high, mx_low, mx_high, all_low, all_high, chem0_low, chem0_high, state1, to_chip, to_core,
    rim_low, rim_high,
):
    runs, n = conc_own.shape[:2]
    ny = of_chip.shape[-2]
    mob = Line((mob_low, -1, -1), (mob_own, 0, n - 1), (mob_high, n, n))
    conc = Line((rim_low, -2, -1), (conc_own, 0, n - 1), (rim_high, n, n + 1))
    faces = all_faces(n, (mx, my, mz, mz_low, m_all, mx_low, mx_high, all_low, all_high))
    chem = ends(n, chem0_low, chem0_own, chem0_high)
    for row in chunks(ny):
        put_padded(mob_low, (0,), row, flat(of_core, (2 * runs,), row))
        put_padded(mob_high, (0,), row, flat(of_chip, (2 * runs,), row))
        for at in (-1, n - 1):
            put_flat(*faces.mx(at), row, each(mean, padded(*mob(at), row), padded(*mob(at + 1), row)))
        put_all(row, faces, (0, n - 1))

    def one_run(run, carry):
        for row in chunks(ny):
            for at in range(2):
                put_padded(rim_low, (run, 1 - at), row, flat(of_core, (2 * run + at,), row))
                put_padded(rim_high, (run, at), row, flat(of_chip, (2 * run + at,), row))
        for row in chunks(ny):
            put_potential(row, conc, run, range(-1, 1), chem)
            put_potential(row, conc, run, range(n - 1, n + 1), chem)
        for row in chunks(ny):

            def target(at, value):
                put_padded(state1, (run, at), row, value)
                if at < 2:
                    put_flat(to_core, (2 * run + at,), row, value)
                if at >= n - 2:
                    put_flat(to_chip, (2 * run + n - 1 - at,), row, value)

            put_step(row, faces, chem, conc, run, range(n), target)
        return carry

    lax.fori_loop(0, runs, one_run, 0)


def second_own_kernel(state1, chem1):
    runs, n = state1.shape[:2]

    def one_run(run, carry):
        for row in chunks(state1.shape[-2] - 2 * PAD):
            put_potential(row, Line((state1, 0, n - 1)), run, range(1, n - 1), Line((chem1, 1, n - 2)))
        return carry

    lax.fori_loop(0, runs, one_run, 0)


def second_kernel(
    of_chip, of_core, state1_own, chem1_own, observed, mob, *refs,
):
    faces, refs = refs[:9], refs[9:]
    state1_low, state1_high, chem1_low, chem1_high, adjoint2, to_chip, to_core, share, total = refs
    runs, n, ny, _ = observed.shape
    faces = all_faces(n, faces)
    place = [either(n - 1 - at, at) for at in range(n)]
    state1 = Line((state1_low, -2, -1), (state1_own, 0, n - 1), (state1_high, n, n + 1))
    chem = ends(n, chem1_low, chem1_own, chem1_high)
    total[...] = jnp.zeros_like(total)

    def one_run(run, carry):
        for row in chunks(ny):
            for at in range(2):
                put_padded(state1_low, (run, 1 - at), row, flat(of_core, (2 * run + at,), row))
                put_padded(state1_high, (run, at), row, flat(of_chip, (2 * run + at,), row))
        for row in chunks(ny):
            put_potential(row, state1, run, range(-1, 1), chem)
            put_potential(row, state1, run, range(n - 1, n + 1), chem)
        for row in chunks(ny):
            squares = []

            def target(at, value):
                adjoint, square = put_miss(row, runs, observed, place, run, at, value, Line((adjoint2, 0, n - 1)))
                squares.append(square)
                if at < 3:
                    put_flat(to_core, (3 * run + at,), row, adjoint)
                if at >= n - 3:
                    put_flat(to_chip, (3 * run + n - 1 - at,), row, adjoint)

            put_step(row, faces, chem, state1, run, range(n), target)
            total[...] += sum(squares)
        return carry

    lax.fori_loop(0, runs, one_run, 0)
    for row in chunks(ny):
        for at in range(2):
            put_flat(to_chip, (3 * runs + at,), row, padded(mob, (n - 2 - at,), row))
            put_flat(to_core, (3 * runs + at,), row, padded(mob, (1 + at,), row))
    columns = (0.5 / runs) * jnp.sum(total[...], axis=0, keepdims=True)
    share[...] = jnp.broadcast_to(jnp.sum(columns, axis=1, keepdims=True), share.shape)


def put_adjoint1(row, flow, adjoint2, run, places, weight, target):
    mids = {at: padded(*flow(at, run), row) for at in range(places[0] - 1, places[-1] + 2)}
    for at in places:
        total = beside(
            mids[at - 1], mids[at + 1], padded(*flow(at, run), row, 1), padded(*flow(at, run), row, -1), mids[at]
        )
        value = each(
            lambda a, w, f, t: a + w * f - (time_step * stiffness) * t,
            padded(*adjoint2(at, run), row), weight(at), mids[at], total,
        )
        put_padded(*target(at, run), row, value)


def slope(state):
    return each(lambda c: time_step * (3.0 * c * c + (6.0 * stiffness - 1.0)), state)


def step_x(field, run, at, row):
    return sub(padded(*field(at + 1, run), row), padded(*field(at, run), row))


def step_y(field, run, at, row):
    return sub(padded(*field(at, run), row, 1), padded(*field(at, run), row))


def step_z(field, run, at, row):
    mid = padded(*field(at, run), row)
    return sub(after_z(mid), mid)


def third_own_kernel(
    adjoint2_own, state1_low, state1_own, state1_high, chem0_low, chem0_own, chem0_high,
    chem1_low, chem1_own, chem1_high, share, *refs,
):
    faces, refs = refs[:9], refs[9:]
    flow_own, weight, step_z0, sum_x, sum_y, sum_z, shares = refs
    runs, n = adjoint2_own.shape[:2]
    ny = weight.shape[-2]
    faces = all_faces(n, faces)
    state1 = Line((state1_low, -2, -1), (state1_own, 0, n - 1), (state1_high, n, n + 1))
    chem0 = ends(n, chem0_low, chem0_own, chem0_high)
    chem1 = ends(n, chem1_low, chem1_own, chem1_high)
    adjoint2 = Line((adjoint2_own, 0, n - 1))
    shares[...] = jnp.broadcast_to(share[:1][None], shares.shape)
    for sums in (sum_x, sum_y, sum_z):
        sums[...] = jnp.zeros_like(sums)

    def one_run(run, carry):
        for row in chunks(ny):
            mids = {at: padded(*adjoint2(at, run), row) for at in range(n)}
            for at in range(n):
                value = faces.flow(
                    row, at, mids[at], padded(*adjoint2(at, run), row, 1), padded(*adjoint2(at, run), row, -1),
                    mids.get(at - 1), mids.get(at + 1),
                )
                put_padded(flow_own, (run, at), row, value)
                put_flat(sum_y, (at,), row, add_product(
                    flat(sum_y, (at,), row), step_y(adjoint2, run, at, row), step_y(chem1, run, at, row)
                ))
                put_flat(sum_z, (at,), row, add_product(
                    flat(sum_z, (at,), row), step_z(adjoint2, run, at, row), step_z(chem1, run, at, row)
                ))
                put_flat(step_z0, (run, at), row, step_z(chem0, run, at, row))
            for at in range(n - 1):
                put_flat(sum_x, (at + 1,), row, add_product(
                    flat(sum_x, (at + 1,), row), sub(mids[at + 1], mids[at]), step_x(chem1, run, at, row)
                ))
            for at in range(-1, n + 1):
                put_flat(weight, (run, at + 1), row, slope(padded(*state1(at, run), row)))
        return carry

    lax.fori_loop(0, runs, one_run, 0)


def third_kernel(
    of_chip, of_core, shares, mob_low, mob_high, adjoint2_own, chem0_low, chem0_own, chem0_high,
    chem1_low, chem1_own, chem1_high, flow_own, weight, step_z0, sum_x_in, sum_y_in, sum_z_in, *refs,
):
    faces, refs = refs[:9], refs[9:]
    result, misfit, rim_low, rim_high, flow_low, flow_high, adjoint1, sum_x, sum_y, sum_z, m_low, m_high, *outer = refs
    runs = flow_own.shape[0]
    n, ny, _ = result.shape
    faces = all_faces(n, faces)
    for line, low, high, shift in zip(
        (faces.mx, faces.my, faces.mz, faces.mz_low, faces.all), outer[:5], outer[5:], (1, 0, 0, 0, 0)
    ):
        line.parts += ((low, -2 - shift, -1 - shift), (high, n, n + 1))
    place = [either(n - 1 - at, at) for at in range(n)]
    mob = Line((m_low, -3, -2), (mob_low, -1, -1), (mob_high, n, n), (m_high, n + 1, n + 2))
    chem0 = ends(n, chem0_low, chem0_own, chem0_high)
    chem1 = ends(n, chem1_low, chem1_own, chem1_high)
    adjoint2 = Line((rim_low, -3, -1), (adjoint2_own, 0, n - 1), (rim_high, n, n + 2))
    flow = Line((flow_low, -2, 0), (flow_high, n - 1, n + 1), (flow_own, 0, n - 1))
    misfit[0] = jnp.sum(shares[...], axis=0)[0, 0]
    for row in chunks(ny):
        for at in range(2):
            put_padded(m_low, (1 - at,), row, flat(of_core, (3 * runs + at,), row))
            put_padded(m_high, (at,), row, flat(of_chip, (3 * runs + at,), row))
    for row in chunks(ny):
        for first in (-3, n):
            mids = [padded(*mob(first + at), row) for at in range(3)]
            for at in range(2):
                put_flat(*faces.mx(first + at), row, each(mean, mids[at], mids[at + 1]))
        for first in (-2, n):
            put_faces(row, mob, range(first, first + 2), faces.my, faces.mz, faces.mz_low)
    for row in chunks(ny):
        put_all(row, faces, (-2, -1, n, n + 1))
    sum_x[...] = sum_x_in[...]
    sum_z[...] = sum_z_in[...]
    for row in chunks(ny):
        for at in range(n):
            put_padded(sum_y, (at,), row, flat(sum_y_in, (at,), row))

    def one_run(run, carry):
        for row in chunks(ny):
            for at in range(3):
                put_padded(rim_low, (run, 2 - at), row, flat(of_core, (3 * run + at,), row))
                put_padded(rim_high, (run, at), row, flat(of_chip, (3 * run + at,), row))
        for row in chunks(ny):
            mids = {at: padded(*adjoint2(at, run), row) for at in (-3, -2, -1, 0, n - 1, n, n + 1, n + 2)}
            for at in (-2, -1, n, n + 1):
                value = faces.flow(
                    row, at, mids[at], padded(*adjoint2(at, run), row, 1), padded(*adjoint2(at, run), row, -1),
                    mids[at - 1], mids[at + 1],
                )
                put_padded(*flow(at, run), row, value)
            for at, face, beyond in ((0, -1, -1), (n - 1, n - 1, n)):
                value = add_product(padded(flow_own, (run, at), row), flat(*faces.mx(face), row), mids[beyond])
                put_padded(*flow(at, run), row, value)
        for row in chunks(ny):
            put_adjoint1(
                row, flow, adjoint2, run, range(-1, n + 1),
                lambda at: flat(weight, (run, at + 1), row), Line((adjoint1, -1, n)),
            )
        adj1 = Line((adjoint1, -1, n))
        for row in chunks(ny):
            for at in range(-1, n):
                total = add_product(
                    flat(sum_x, (at + 1,), row), step_x(adj1, run, at, row), step_x(chem0, run, at, row)
                )
                if at in (-1, n - 1):
                    total = add_product(total, step_x(adjoint2, run, at, row), step_x(chem1, run, at, row))
                put_flat(sum_x, (at + 1,), row, total)
            for at in range(n):
                put_padded(sum_y, (at,), row, add_product(
                    padded(sum_y, (at,), row), step_y(adj1, run, at, row), step_y(chem0, run, at, row)
                ))
                put_flat(sum_z, (at,), row, add_product(
                    flat(sum_z, (at,), row), step_z(adj1, run, at, row), flat(step_z0, (run, at), row)
                ))
        return carry

    lax.fori_loop(0, runs, one_run, 0)
    for row in chunks(ny):
        for at in range(n):
            sides = flat(sum_z, (at,), row)
            value = each(
                lambda a, b, c, d, e, f: -0.5 * ((a + b) + (c + d) + (e + f)),
                flat(sum_x, (at,), row), flat(sum_x, (at + 1,), row),
                padded(sum_y, (at,), row), padded(sum_y, (at,), row, -1), sides, before_z(sides),
            )
            put_plain(result, (place[at],), row, value)


def call(kernel, outs, scratch, args, flops, scalar=None):
    moved = 4 * (sum(a.size for a in args) + sum(math.prod(o) for o in outs))
    return pl.pallas_call(
        kernel,
        out_shape=tuple(jax.ShapeDtypeStruct(o, jnp.float32) for o in outs),
        in_specs=[VMEM] * len(args),
        out_specs=tuple(SMEM if at == scalar else VMEM for at in range(len(outs))),
        scratch_shapes=[pltpu.VMEM(s, jnp.float32) for s in scratch],
        compiler_params=pltpu.CompilerParams(vmem_limit_bytes=16 * 1024 * 1024),
        cost_estimate=pl.CostEstimate(flops=flops, bytes_accessed=moved, transcendentals=0),
    )(*args)


def on_device(initial, observed, mobility):
    runs, n, ny, nz = initial.shape
    blocks = nz // LANES
    count = lax.axis_size("gx")
    over_chips = [(i, (i - 1 + 2 * (i % 2)) % count) for i in range(count)]
    over_cores = [(i, i ^ 1) for i in range(count)]
    cell = ny * nz

    def neighbours(to_chip, to_core):
        return lax.ppermute(to_chip, "gx", over_chips), lax.ppermute(to_core, "gx", over_cores)

    def lies(*lead):
        return (*lead, blocks, ny, LANES)

    def lies_padded(*lead):
        return (*lead, blocks, ny + 2 * PAD, LANES)

    conc, mob, to_chip, to_core = call(
        own_kernel,
        (
            lies_padded(runs, n), lies_padded(n), lies(2 * runs + 1), lies(2 * runs + 1),
        ),
        (),
        (initial, mobility),
        runs * n * cell,
    )
    of_chip, of_core = neighbours(to_chip, to_core)
    *faces, chem0_own = call(
        first_own_kernel,
        (lies(n - 1), lies_padded(n), lies(n), lies(n), lies(n - 2), lies_padded(runs, n - 2)),
        (),
        (conc, mob),
        15 * runs * n * cell,
    )
    mob_low, mob_high, *more_faces, chem0_low, chem0_high, state1, to_chip, to_core = call(
        first_kernel,
        (
            lies_padded(1), lies_padded(1), lies(1), lies(1), lies(1), lies(1),
            lies_padded(runs, 2), lies_padded(runs, 2), lies_padded(runs, n), lies(2 * runs), lies(2 * runs),
        ),
        (lies_padded(runs, 2), lies_padded(runs, 2)),
        (of_chip, of_core, conc, mob, chem0_own, *faces),
        30 * runs * (n + 4) * cell,
    )
    faces = (*faces, *more_faces)
    of_chip, of_core = neighbours(to_chip, to_core)
    (chem1_own,) = call(
        second_own_kernel, (lies_padded(runs, n - 2),), (), (state1,), 20 * runs * (n - 2) * cell
    )
    state1_low, state1_high, chem1_low, chem1_high, adjoint2, to_chip, to_core, share = call(
        second_kernel,
        (
            lies_padded(runs, 2), lies_padded(runs, 2), lies_padded(runs, 2), lies_padded(runs, 2),
            lies_padded(runs, n), lies(3 * runs + 2), lies(3 * runs + 2), (ROWS, LANES),
        ),
        ((CHUNK, LANES),),
        (of_chip, of_core, state1, chem1_own, observed, mob, *faces),
        30 * runs * (n + 4) * cell,
    )
    of_chip, of_core = neighbours(to_chip, to_core)
    potentials = (chem0_low, chem0_own, chem0_high, chem1_low, chem1_own, chem1_high)
    *done, shares = call(
        third_own_kernel,
        (
            lies_padded(runs, n), lies(runs, n + 2), lies(runs, n), lies(n + 1), lies(n), lies(n),
            (count, 1, LANES),
        ),
        (),
        (adjoint2, state1_low, state1, state1_high, *potentials, share, *faces),
        40 * runs * n * cell,
    )
    shares = lax.all_to_all(shares, "gx", 0, 0)
    outer = (lies(2), lies_padded(2), lies(2), lies(2), lies(2))
    return call(
        third_kernel,
        ((n, ny, nz), (1,)),
        (
            lies_padded(runs, 3), lies_padded(runs, 3), lies_padded(runs, 3), lies_padded(runs, 3),
            lies_padded(runs, n + 2), lies(n + 1), lies_padded(n), lies(n), lies_padded(2), lies_padded(2),
            *outer, *outer,
        ),
        (of_chip, of_core, shares, mob_low, mob_high, adjoint2, *potentials, *done, *faces),
        40 * runs * (n + 2) * cell,
        scalar=1,
    )


def solution(mesh):
    placed = (
        P("group", "gx", None, None),
        P("group", "gx", None, None),
        P(("group", "gx"), None, None),
    )
    return jax.shard_map(
        on_device,
        mesh=mesh,
        in_specs=placed,
        out_specs=(P(("group", "gx"), None, None), P("group")),
        check_vma=False,
    )
```

```python
import functools
import math

import jax
import jax.numpy as jnp
from jax import lax
from jax.experimental import pallas as pl
from jax.experimental.pallas import tpu as pltpu
from jax.sharding import PartitionSpec as P

stiffness = 0.5
time_step = 0.005
VMEM = pl.BlockSpec(memory_space=pltpu.VMEM)
SMEM = pl.BlockSpec(memory_space=pltpu.SMEM)
LANES = 128
ROWS = 8
PAD = ROWS
CHUNK = 16


def chunks(ny):
    return range(0, ny, CHUNK)


def plain(ref, lead, row):
    return [
        ref[(*lead, pl.ds(row, CHUNK), pl.ds(at, LANES))] for at in range(0, ref.shape[-1], LANES)
    ]


def put_plain(ref, lead, row, value):
    for block, part in enumerate(value):
        ref[(*lead, pl.ds(row, CHUNK), pl.ds(block * LANES, LANES))] = part


def flat(ref, lead, row):
    return [ref[(*lead, block, pl.ds(row, CHUNK))] for block in range(ref.shape[-3])]


def put_flat(ref, lead, row, value):
    for block, part in enumerate(value):
        ref[(*lead, block, pl.ds(row, CHUNK))] = part


def padded(ref, lead, row, shift=0):
    return [ref[(*lead, block, pl.ds(PAD + row + shift, CHUNK))] for block in range(ref.shape[-3])]


def put_padded(ref, lead, row, value):
    ny = ref.shape[-2] - 2 * PAD
    for block, part in enumerate(value):
        ref[(*lead, block, pl.ds(PAD + row, CHUNK))] = part
        if row == 0:
            ref[(*lead, block, pl.ds(PAD + ny, 1))] = part[:1]
        if row + CHUNK == ny:
            ref[(*lead, block, pl.ds(PAD - 1, 1))] = part[CHUNK - 1 :]


def lane():
    return lax.broadcasted_iota(jnp.int32, (CHUNK, LANES), 1)


def after_z(value):
    turned = [pltpu.roll(part, LANES - 1, 1) for part in value]
    turned.append(turned[0])
    edge = lane() == LANES - 1
    return [jnp.where(edge, turned[at + 1], turned[at]) for at in range(len(value))]


def before_z(value):
    turned = [pltpu.roll(part, 1, 1) for part in value]
    edge = lane() == 0
    return [jnp.where(edge, turned[at - 1], turned[at]) for at in range(len(value))]


def side():
    return lax.rem(lax.axis_index("gx"), 2)


def either(first, second):
    return first + side() * (second - first)


class Line:
    def __init__(self, *parts):
        self.parts = parts

    def __call__(self, at, *lead):
        for ref, first, last in self.parts:
            if first <= at <= last:
                return ref, (*lead, at - first)
        raise IndexError(at)


def each(function, *values):
    return [function(*parts) for parts in zip(*values)]


def beside(low, high, up, down, mid):
    return each(
        lambda a, b, c, d, e, f: (a + b) + (c + d) + (e + f),
        low, high, up, down, after_z(mid), before_z(mid),
    )


def potential(low, mid, high, up, down):
    return each(
        lambda c, total: c * (c * c + (6.0 * stiffness - 1.0)) - stiffness * total,
        mid, beside(low, high, up, down, mid),
    )


class Faces:
    def __init__(self, n, refs):
        mx_a, my_a, mz_a, mz_low_a, all_a, *late = refs
        two = lambda ref, first, last, at: ((ref, first, last), *(((late[at], last + 1, n + 1),) if late else ()))
        self.mx = Line(*two(mx_a, -3, n - 2, 0))
        self.my = Line(*two(my_a, -2, n - 1, 1))
        self.mz = Line(*two(mz_a, -2, n - 1, 2))
        self.mz_low = Line(*two(mz_low_a, -2, n - 1, 3))
        self.all = Line(*two(all_a, -2, n - 2, 4))

    def flow(self, row, at, mid, up, down, low=None, high=None):
        total = each(
            lambda a, b, c, d, e, u, v, w, x, y: (a * u + b * v) + (c * w + d * x) - e * y,
            padded(*self.my(at), row), padded(*self.my(at), row, -1), flat(*self.mz(at), row),
            flat(*self.mz_low(at), row), flat(*self.all(at), row), up, down, after_z(mid), before_z(mid), mid,
        )
        if low is not None:
            total = add_product(total, flat(*self.mx(at - 1), row), low)
        if high is not None:
            total = add_product(total, flat(*self.mx(at), row), high)
        return total


def add_product(total, a, b):
    return each(lambda t, x, y: t + x * y, total, a, b)


def sub(a, b):
    return each(lambda x, y: x - y, a, b)


def own_kernel(initial, mobility, conc, mob, to_chip, to_core):
    runs, n, ny, _ = initial.shape
    place = [either(n - 1 - at, at) for at in range(n)]

    def one_run(run, carry):
        for row in chunks(ny):
            for at in range(n):
                put_padded(conc, (run, at), row, plain(initial, (run, place[at]), row))
        return carry

    lax.fori_loop(0, runs, one_run, 0)
    for row in chunks(ny):
        for at in range(n):
            value = plain(mobility, (place[at],), row)
            put_padded(mob, (at,), row, value)
            if at < 3:
                put_flat(to_core, (at,), row, value)
            if at >= n - 3:
                put_flat(to_chip, (n - 1 - at,), row, value)


def mean(a, b):
    return 0.5 * (a + b)


def put_faces(row, mob, places, my, mz, mz_low):
    for at in places:
        mid = padded(*mob(at), row)
        put_padded(*my(at), row, each(mean, mid, padded(*mob(at), row, 1)))
        put_flat(*mz(at), row, each(mean, mid, after_z(mid)))
        put_flat(*mz_low(at), row, each(mean, mid, before_z(mid)))


def put_all(row, faces, places):
    for at in places:
        put_flat(*faces.all(at), row, each(
            lambda a, b, c, d, e, f: (a + b) + (c + d) + (e + f),
            flat(*faces.mx(at - 1), row), flat(*faces.mx(at), row), padded(*faces.my(at), row),
            padded(*faces.my(at), row, -1), flat(*faces.mz(at), row), flat(*faces.mz_low(at), row),
        ))


def put_potential(row, field, run, places, target):
    mids = {at: padded(*field(at, run), row) for at in range(places[0] - 1, places[-1] + 2)}
    for at in places:
        value = potential(
            mids[at - 1], mids[at], mids[at + 1],
            padded(*field(at, run), row, 1), padded(*field(at, run), row, -1),
        )
        put_padded(*target(at, run), row, value)


def put_step(row, faces, chem, state, run, places, target):
    mids = {at: padded(*chem(at, run), row) for at in range(places[0] - 1, places[-1] + 2)}
    for at in places:
        flow = faces.flow(
            row, at, mids[at], padded(*chem(at, run), row, 1), padded(*chem(at, run), row, -1),
            mids[at - 1], mids[at + 1],
        )
        value = each(lambda a, b: a + time_step * b, padded(*state(at, run), row), flow)
        target(at, value)


def put_miss(row, runs, observed, place, run, at, value, adjoint2):
    miss = sub(value, plain(observed, (run, place[at]), row))
    adjoint = each(lambda a: a * (1.0 / runs), miss)
    put_padded(*adjoint2(at, run), row, adjoint)
    return adjoint, sum(part * part for part in miss)


def core_kernel(of_core, m_core, conc_own, mob_own, conc_core, chem0, mx, my, mz, mz_low, m_all, rim):
    runs, n = conc_own.shape[:2]
    ny = of_core.shape[2]
    mob = Line((rim, -3, -1), (mob_own, 0, n - 1))
    faces = Faces(n, (mx, my, mz, mz_low, m_all))
    for row in chunks(ny):
        for at in range(3):
            put_padded(rim, (2 - at,), row, flat(m_core, (at,), row))
    for row in chunks(ny):
        mids = [padded(*mob(at), row) for at in range(-3, n)]
        for at in range(n + 2):
            put_flat(mx, (at,), row, each(mean, mids[at], mids[at + 1]))
        put_faces(row, mob, range(-2, n), faces.my, faces.mz, faces.mz_low)
    for row in chunks(ny):
        put_all(row, faces, range(-2, n - 1))
    place = [either(at, 3 - at) for at in range(4)]
    conc = Line((conc_core, -4, -1), (conc_own, 0, n - 1))

    def one_run(run, carry):
        for row in chunks(ny):
            for at in range(4):
                put_padded(conc_core, (run, 3 - at), row, plain(of_core, (run, place[at]), row))
        for row in chunks(ny):
            put_potential(row, conc, run, range(-3, n - 1), Line((chem0, -3, n - 2)))
        return carry

    lax.fori_loop(0, runs, one_run, 0)


def chip_kernel(
    of_chip, conc_own, conc_core, chem0_a, observed, mx, my, mz, mz_low, m_all,
    conc_chip, chem0_b, state1_a, chem1_a, adjoint2_a, squares,
):
    runs, n = conc_own.shape[:2]
    ny = observed.shape[2]
    faces = Faces(n, (mx, my, mz, mz_low, m_all))
    message = [either(3 - at, at) for at in range(4)]
    place = [either(n - 1 - at, at) for at in range(n)]
    conc = Line((conc_core, -4, -1), (conc_own, 0, n - 1), (conc_chip, n, n + 3))
    chem0 = Line((chem0_a, -3, n - 2), (chem0_b, n - 1, n + 2))
    state1 = Line((state1_a, -2, n - 2))
    chem1 = Line((chem1_a, -1, n - 3))
    adjoint2 = Line((adjoint2_a, 0, n - 4))
    squares[...] = jnp.zeros_like(squares)

    def one_run(run, carry):
        for row in chunks(ny):
            for at in range(4):
                put_padded(conc_chip, (run, at), row, plain(of_chip, (run, message[at]), row))
        for row in chunks(ny):
            put_potential(row, conc, run, range(n - 1, n + 3), chem0)
        for row in chunks(ny):
            put_step(
                row, faces, chem0, conc, run, range(-2, n - 1),
                lambda at, value: put_padded(*state1(at, run), row, value),
            )
        for row in chunks(ny):
            put_potential(row, state1, run, range(-1, n - 2), chem1)
        for row in chunks(ny):

            def target(at, value):
                squares[...] += put_miss(row, runs, observed, place, run, at, value, adjoint2)[1]

            put_step(row, faces, chem1, state1, run, range(0, n - 3), target)
        return carry

    lax.fori_loop(0, runs, one_run, 0)


def forward_kernel(
    m_chip, mob_own, conc_own, conc_chip, chem0_a, chem0_b, state1_a, chem1_a, adjoint2_a, squares, observed,
    mx_a, my_a, mz_a, mz_low_a, all_a,
    mx_b, my_b, mz_b, mz_low_b, all_b, state1_b, chem1_b, adjoint2_b, to_core, to_chip, share, rim, total,
):
    runs, n = conc_own.shape[:2]
    ny = observed.shape[2]
    faces = Faces(n, (mx_a, my_a, mz_a, mz_low_a, all_a, mx_b, my_b, mz_b, mz_low_b, all_b))
    mob = Line((mob_own, 0, n - 1), (rim, n, n + 2))
    place = [either(n - 1 - at, at) for at in range(n)]
    conc = Line((conc_own, 0, n - 1), (conc_chip, n, n + 3))
    chem0 = Line((chem0_a, -3, n - 2), (chem0_b, n - 1, n + 2))
    state1 = Line((state1_a, -2, n - 2), (state1_b, n - 1, n + 1))
    chem1 = Line((chem1_a, -1, n - 3), (chem1_b, n - 2, n))
    adjoint2 = Line((adjoint2_a, 0, n - 4), (adjoint2_b, n - 3, n - 1))
    for row in chunks(ny):
        for at in range(3):
            put_padded(rim, (at,), row, flat(m_chip, (at,), row))
    for row in chunks(ny):
        mids = [padded(*mob(at), row) for at in range(n - 1, n + 3)]
        for at in range(3):
            put_flat(mx_b, (at,), row, each(mean, mids[at], mids[at + 1]))
        put_faces(row, mob, range(n, n + 2), faces.my, faces.mz, faces.mz_low)
    for row in chunks(ny):
        put_all(row, faces, range(n - 1, n + 2))
    total[...] = squares[...]

    def one_run(run, carry):
        for row in chunks(ny):
            put_step(
                row, faces, chem0, conc, run, range(n - 1, n + 2),
                lambda at, value: put_padded(*state1(at, run), row, value),
            )
        for row in chunks(ny):
            put_potential(row, state1, run, range(n - 2, n + 1), chem1)
        for row in chunks(ny):

            def target(at, value):
                adjoint, square = put_miss(row, runs, observed, place, run, at, value, adjoint2)
                total[...] += square
                put_flat(to_chip, (run, n - 1 - at), row, adjoint)
                if at < 3:
                    put_flat(to_core, (run, at), row, adjoint)

            put_step(row, faces, chem1, state1, run, range(n - 3, n), target)
            for at in range(min(3, n - 3)):
                put_flat(to_core, (run, at), row, padded(*adjoint2(at, run), row))
        return carry

    lax.fori_loop(0, runs, one_run, 0)
    columns = (0.5 / runs) * jnp.sum(total[...], axis=0, keepdims=True)
    mine = jnp.broadcast_to(jnp.sum(columns, axis=1, keepdims=True), share.shape)
    share[...] = mine
    to_core[0, 0, 0, ny:] = mine


def put_adjoint1(row, flow, adjoint2, run, places, weight, target):
    mids = {at: padded(*flow(at, run), row) for at in range(places[0] - 1, places[-1] + 2)}
    for at in places:
        total = beside(
            mids[at - 1], mids[at + 1], padded(*flow(at, run), row, 1), padded(*flow(at, run), row, -1), mids[at]
        )
        value = each(
            lambda a, w, f, t: a + w * f - (time_step * stiffness) * t,
            padded(*adjoint2(at, run), row), weight(at), mids[at], total,
        )
        put_padded(*target(at, run), row, value)


def slope(state):
    return each(lambda c: time_step * (3.0 * c * c + (6.0 * stiffness - 1.0)), state)


def step_x(field, run, at, row):
    return sub(padded(*field(at + 1, run), row), padded(*field(at, run), row))


def step_y(field, run, at, row):
    return sub(padded(*field(at, run), row, 1), padded(*field(at, run), row))


def step_z(field, run, at, row):
    mid = padded(*field(at, run), row)
    return sub(after_z(mid), mid)


def early_kernel(
    of_core, mx_a, my_a, mz_a, mz_low_a, all_a, mx_b, my_b, mz_b, mz_low_b, all_b,
    chem0_a, chem0_b, state1_a, state1_b, chem1_a, chem1_b, adjoint2_a, adjoint2_b,
    share_in, flow_a, flow_part, adjoint1_a, weight_b, step_z_b, part, sum_x_b, sum_y_b, sum_z_b, share,
    rim, sum_x, sum_y, sum_z,
):
    share[...] = share_in[...]
    runs = of_core.shape[0]
    n = part.shape[0] + 2
    ny = part.shape[-2]
    faces = Faces(n, (mx_a, my_a, mz_a, mz_low_a, all_a, mx_b, my_b, mz_b, mz_low_b, all_b))
    chem0 = Line((chem0_a, -3, n - 2), (chem0_b, n - 1, n + 2))
    state1 = Line((state1_a, -2, n - 2), (state1_b, n - 1, n + 1))
    chem1 = Line((chem1_a, -1, n - 3), (chem1_b, n - 2, n))
    adjoint2 = Line((rim, -3, -1), (adjoint2_a, 0, n - 4), (adjoint2_b, n - 3, n - 1))
    flow = Line((flow_a, -2, n - 2), (flow_part, n - 1, n - 1))
    adjoint1 = Line((adjoint1_a, -1, n - 3))
    for sums in (sum_x, sum_y, sum_z):
        sums[...] = jnp.zeros_like(sums)

    def one_run(run, carry):
        for row in chunks(ny):
            for at in range(3):
                put_padded(rim, (run, 2 - at), row, flat(of_core, (run, at), row))
        for row in chunks(ny):
            mids = {at: padded(*adjoint2(at, run), row) for at in range(-3, n)}
            for at in range(-2, n):
                value = faces.flow(
                    row, at, mids[at], padded(*adjoint2(at, run), row, 1), padded(*adjoint2(at, run), row, -1),
                    mids[at - 1], mids.get(at + 1),
                )
                put_padded(*flow(at, run), row, value)
        for row in chunks(ny):
            put_adjoint1(
                row, flow, adjoint2, run, range(-1, n - 2),
                lambda at: slope(padded(*state1(at, run), row)), adjoint1,
            )
            for at in range(n - 2, n + 1):
                put_flat(weight_b, (run, at - (n - 2)), row, slope(padded(*state1(at, run), row)))
        for row in chunks(ny):
            for at in range(-1, n - 1):
                total = add_product(
                    flat(sum_x, (at + 1,), row), step_x(adjoint2, run, at, row), step_x(chem1, run, at, row)
                )
                if at < n - 3:
                    total = add_product(total, step_x(adjoint1, run, at, row), step_x(chem0, run, at, row))
                put_flat(sum_x, (at + 1,), row, total)
            for at in range(n):
                total_y = add_product(
                    padded(sum_y, (at,), row), step_y(adjoint2, run, at, row), step_y(chem1, run, at, row)
                )
                total_z = add_product(
                    flat(sum_z, (at,), row), step_z(adjoint2, run, at, row), step_z(chem1, run, at, row)
                )
                slant = step_z(chem0, run, at, row)
                if at < n - 2:
                    total_y = add_product(total_y, step_y(adjoint1, run, at, row), step_y(chem0, run, at, row))
                    total_z = add_product(total_z, step_z(adjoint1, run, at, row), slant)
                else:
                    put_flat(step_z_b, (run, at - (n - 2)), row, slant)
                put_padded(sum_y, (at,), row, total_y)
                put_flat(sum_z, (at,), row, total_z)
        return carry

    lax.fori_loop(0, runs, one_run, 0)
    for row in chunks(ny):
        for at in range(n - 2):
            sides = flat(sum_z, (at,), row)
            value = each(
                lambda a, b, c, d, e: -0.5 * ((a + b) + (c + d) + e),
                padded(sum_y, (at,), row), padded(sum_y, (at,), row, -1), sides, before_z(sides),
                flat(sum_x, (at,), row),
            )
            if at < n - 3:
                value = each(lambda a, b: a - 0.5 * b, value, flat(sum_x, (at + 1,), row))
            put_flat(part, (at,), row, value)
        for at in range(2):
            put_flat(sum_x_b, (at,), row, flat(sum_x, (n - 2 + at,), row))
            put_flat(sum_y_b, (at,), row, padded(sum_y, (n - 2 + at,), row))
            put_flat(sum_z_b, (at,), row, flat(sum_z, (n - 2 + at,), row))


def late_kernel(
    of_chip, mx_a, my_a, mz_a, mz_low_a, all_a, mx_b, my_b, mz_b, mz_low_b, all_b,
    chem0_a, chem0_b, chem1_b, adjoint2_b, flow_a, flow_part, adjoint1_a, weight_b, step_z_b,
    part, sum_x_b, sum_y_b, sum_z_b, result, rim, flow_b, adjoint1_b, sum_x, sum_y, sum_z,
):
    runs = of_chip.shape[0]
    n, ny, _ = result.shape
    faces = Faces(n, (mx_a, my_a, mz_a, mz_low_a, all_a, mx_b, my_b, mz_b, mz_low_b, all_b))
    place = [either(n - 1 - at, at) for at in range(n)]
    chem0 = Line((chem0_a, -3, n - 2), (chem0_b, n - 1, n + 2))
    chem1 = Line((chem1_b, n - 2, n))
    adjoint2 = Line((adjoint2_b, n - 3, n - 1), (rim, n, n + 2))
    flow = Line((flow_a, -2, n - 2), (flow_b, n - 1, n + 1))
    adjoint1 = Line((adjoint1_a, -1, n - 3), (adjoint1_b, n - 2, n))
    for row in chunks(ny):
        for at in range(2):
            put_flat(sum_x, (at,), row, flat(sum_x_b, (at,), row))
            put_padded(sum_y, (at,), row, flat(sum_y_b, (at,), row))
            put_flat(sum_z, (at,), row, flat(sum_z_b, (at,), row))
    sum_x[2] = jnp.zeros_like(sum_x[2])

    def one_run(run, carry):
        for row in chunks(ny):
            for at in range(3):
                put_padded(rim, (run, at), row, flat(of_chip, (run, at), row))
        for row in chunks(ny):
            mids = {at: padded(*adjoint2(at, run), row) for at in range(n - 1, n + 3)}
            value = add_product(padded(flow_part, (run, 0), row), flat(*faces.mx(n - 1), row), mids[n])
            put_padded(*flow(n - 1, run), row, value)
            for at in range(n, n + 2):
                value = faces.flow(
                    row, at, mids[at], padded(*adjoint2(at, run), row, 1), padded(*adjoint2(at, run), row, -1),
                    mids[at - 1], mids[at + 1],
                )
                put_padded(*flow(at, run), row, value)
        for row in chunks(ny):
            put_adjoint1(
                row, flow, adjoint2, run, range(n - 2, n + 1),
                lambda at: flat(weight_b, (run, at - (n - 2)), row), adjoint1,
            )
        for row in chunks(ny):
            for at in range(n - 3, n):
                total = add_product(
                    flat(sum_x, (at - (n - 3),), row), step_x(adjoint1, run, at, row), step_x(chem0, run, at, row)
                )
                if at == n - 1:
                    total = add_product(total, step_x(adjoint2, run, at, row), step_x(chem1, run, at, row))
                put_flat(sum_x, (at - (n - 3),), row, total)
            for at in range(n - 2, n):
                to = (at - (n - 2),)
                put_padded(sum_y, to, row, add_product(
                    padded(sum_y, to, row), step_y(adjoint1, run, at, row), step_y(chem0, run, at, row)
                ))
                put_flat(sum_z, to, row, add_product(
                    flat(sum_z, to, row), step_z(adjoint1, run, at, row), flat(step_z_b, (run, *to), row)
                ))
        return carry

    lax.fori_loop(0, runs, one_run, 0)
    for row in chunks(ny):
        for at in range(n - 2):
            value = flat(part, (at,), row)
            if at == n - 3:
                value = each(lambda a, b: a - 0.5 * b, value, flat(sum_x, (0,), row))
            put_plain(result, (place[at],), row, value)
        for at in range(2):
            sides = flat(sum_z, (at,), row)
            value = each(
                lambda a, b, c, d, e, f: -0.5 * ((a + b) + (c + d) + (e + f)),
                flat(sum_x, (at,), row), flat(sum_x, (at + 1,), row),
                padded(sum_y, (at,), row), padded(sum_y, (at,), row, -1), sides, before_z(sides),
            )
            put_plain(result, (place[n - 2 + at],), row, value)


def counts(at):
    return (at ^ (at >> 1)) & 1


def misfit_kernel(total, handed, misfit):
    misfit[0] = jnp.where(counts(lax.axis_index("gx")) == 1, total[0, 0], handed[0, 0])


def call(kernel, outs, scratch, args, flops, scalar=None):
    moved = 4 * (sum(a.size for a in args) + sum(math.prod(o) for o in outs))
    return pl.pallas_call(
        kernel,
        out_shape=tuple(jax.ShapeDtypeStruct(o, jnp.float32) for o in outs),
        in_specs=[VMEM] * len(args),
        out_specs=tuple(SMEM if at == scalar else VMEM for at in range(len(outs))),
        scratch_shapes=[pltpu.VMEM(s, jnp.float32) for s in scratch],
        compiler_params=pltpu.CompilerParams(vmem_limit_bytes=16 * 1024 * 1024),
        cost_estimate=pl.CostEstimate(flops=flops, bytes_accessed=moved, transcendentals=0),
    )(*args)


def on_device(initial, observed, mobility):
    runs, n, ny, nz = initial.shape
    blocks = nz // LANES
    count = lax.axis_size("gx")
    over_chips = [(i, (i - 1 + 2 * (i % 2)) % count) for i in range(count)]
    over_cores = [(i, i ^ 1) for i in range(count)]
    cell = ny * nz

    def neighbours(to_chip, to_core):
        of_core = lax.ppermute(to_core, "gx", over_cores)
        return lax.ppermute(to_chip, "gx", over_chips), of_core

    def lies(*lead):
        return (*lead, blocks, ny, LANES)

    def lies_padded(*lead):
        return (*lead, blocks, ny + 2 * PAD, LANES)

    if n == 4:
        near = (initial, initial)
    else:
        near = [lax.dynamic_slice_in_dim(initial, at, 4, 1) for at in (either(0, n - 4), either(n - 4, 0))]
    of_chip, of_core = neighbours(*near)
    conc, mob, to_chip, to_core = call(
        own_kernel, (lies_padded(runs, n), lies_padded(n), lies(3), lies(3)), (), (initial, mobility),
        runs * n * cell,
    )
    m_chip, m_core = neighbours(to_chip, to_core)
    conc_core, chem0_a, *faces_a = call(
        core_kernel,
        (
            lies_padded(runs, 4), lies_padded(runs, n + 2),
            lies(n + 2), lies_padded(n + 2), lies(n + 2), lies(n + 2), lies(n + 1),
        ),
        (lies_padded(3),),
        (of_core, m_core, conc, mob),
        20 * runs * (n + 2) * cell,
    )
    conc_chip, chem0_b, state1_a, chem1_a, adjoint2_a, squares = call(
        chip_kernel,
        (
            lies_padded(runs, 4), lies_padded(runs, 4), lies_padded(runs, n + 1),
            lies_padded(runs, n - 1), lies_padded(runs, n - 3), (CHUNK, LANES),
        ),
        (),
        (of_chip, conc, conc_core, chem0_a, observed, *faces_a),
        60 * runs * (n - 1) * cell,
    )
    *faces_b, state1_b, chem1_b, adjoint2_b, to_core, to_chip, share = call(
        forward_kernel,
        (
            lies(3), lies_padded(2), lies(2), lies(2), lies(3),
            lies_padded(runs, 3), lies_padded(runs, 3), lies_padded(runs, 3),
            (runs, 3, blocks, ny + ROWS, LANES), lies(runs, 3), (ROWS, LANES),
        ),
        (lies_padded(3), (CHUNK, LANES)),
        (m_chip, mob, conc, conc_chip, chem0_a, chem0_b, state1_a, chem1_a, adjoint2_a, squares, observed, *faces_a),
        60 * runs * 3 * cell,
    )
    faces = (*faces_a, *faces_b)
    of_chip, of_core = neighbours(to_chip, to_core)
    bits = range(count.bit_length() - 2)

    def hop(value, bit):
        apart = 3 if bit == 0 else 2 << bit
        return lax.ppermute(value, "gx", [(at, at ^ apart * counts(at)) for at in range(count)])

    share = share + of_core[0, 0, 0, ny:]
    far = hop(share, bits[-1])
    flow_a, flow_part, adjoint1_a, weight_b, step_z_b, part, *sums_b, share = call(
        early_kernel,
        (
            lies_padded(runs, n + 1), lies_padded(runs, 1), lies_padded(runs, n - 1), lies(runs, 3), lies(runs, 2),
            lies(n - 2), lies(2), lies(2), lies(2), (ROWS, LANES),
        ),
        (lies_padded(runs, 3), lies(n), lies_padded(n), lies(n)),
        (of_core, *faces, chem0_a, chem0_b, state1_a, state1_b, chem1_a, chem1_b, adjoint2_a, adjoint2_b, share),
        60 * runs * n * cell,
    )
    for bit in bits[-2::-1]:
        share = share + far
        far = hop(share, bit)
    share = share + far
    handed = lax.ppermute(share, "gx", over_cores)
    (result,) = call(
        late_kernel,
        ((n, ny, nz),),
        (
            lies_padded(runs, 3), lies_padded(runs, 3), lies_padded(runs, 3),
            lies(3), lies_padded(2), lies(2),
        ),
        (
            of_chip, *faces, chem0_a, chem0_b, chem1_b, adjoint2_b, flow_a, flow_part, adjoint1_a,
            weight_b, step_z_b, part, *sums_b,
        ),
        60 * runs * 3 * cell,
    )
    (misfit,) = call(misfit_kernel, ((1,),), (), (share, handed), 1, scalar=0)
    return (result, misfit)


def solution(mesh):
    placed = (
        P("group", "gx", None, None),
        P("group", "gx", None, None),
        P(("group", "gx"), None, None),
    )
    return jax.shard_map(
        on_device,
        mesh=mesh,
        in_specs=placed,
        out_specs=(P(("group", "gx"), None, None), P("group")),
        check_vma=False,
    )
```

```python
import functools
import math

import jax
import jax.numpy as jnp
from jax import lax
from jax.experimental import pallas as pl
from jax.experimental.pallas import tpu as pltpu
from jax.sharding import PartitionSpec as P

stiffness = 0.5
time_step = 0.005
VMEM = pl.BlockSpec(memory_space=pltpu.VMEM)
SMEM = pl.BlockSpec(memory_space=pltpu.SMEM)
LANES = 128
ROWS = 8
PAD = ROWS
CHUNK = 16


def chunks(ny):
    return range(0, ny, CHUNK)


def plain(ref, lead, row):
    return [
        ref[(*lead, pl.ds(row, CHUNK), pl.ds(at, LANES))] for at in range(0, ref.shape[-1], LANES)
    ]


def put_plain(ref, lead, row, value):
    for block, part in enumerate(value):
        ref[(*lead, pl.ds(row, CHUNK), pl.ds(block * LANES, LANES))] = part


def flat(ref, lead, row):
    return [ref[(*lead, block, pl.ds(row, CHUNK))] for block in range(ref.shape[-3])]


def put_flat(ref, lead, row, value):
    for block, part in enumerate(value):
        ref[(*lead, block, pl.ds(row, CHUNK))] = part


def padded(ref, lead, row, shift=0):
    return [ref[(*lead, block, pl.ds(PAD + row + shift, CHUNK))] for block in range(ref.shape[-3])]


def put_padded(ref, lead, row, value):
    ny = ref.shape[-2] - 2 * PAD
    for block, part in enumerate(value):
        ref[(*lead, block, pl.ds(PAD + row, CHUNK))] = part
        if row == 0:
            ref[(*lead, block, pl.ds(PAD + ny, 1))] = part[:1]
        if row + CHUNK == ny:
            ref[(*lead, block, pl.ds(PAD - 1, 1))] = part[CHUNK - 1 :]


def lane():
    return lax.broadcasted_iota(jnp.int32, (CHUNK, LANES), 1)


def after_z(value):
    turned = [pltpu.roll(part, LANES - 1, 1) for part in value]
    turned.append(turned[0])
    edge = lane() == LANES - 1
    return [jnp.where(edge, turned[at + 1], turned[at]) for at in range(len(value))]


def before_z(value):
    turned = [pltpu.roll(part, 1, 1) for part in value]
    edge = lane() == 0
    return [jnp.where(edge, turned[at - 1], turned[at]) for at in range(len(value))]


def side():
    return lax.rem(lax.axis_index("gx"), 2)


def either(first, second):
    return first + side() * (second - first)


class Line:
    def __init__(self, *parts):
        self.parts = parts

    def __call__(self, at, *lead):
        for ref, first, last in self.parts:
            if first <= at <= last:
                return ref, (*lead, at - first)
        raise IndexError(at)


def each(function, *values):
    return [function(*parts) for parts in zip(*values)]


def beside(low, high, up, down, mid):
    return each(
        lambda a, b, c, d, e, f: (a + b) + (c + d) + (e + f),
        low, high, up, down, after_z(mid), before_z(mid),
    )


def potential(low, mid, high, up, down):
    return each(
        lambda c, total: c * (c * c + (6.0 * stiffness - 1.0)) - stiffness * total,
        mid, beside(low, high, up, down, mid),
    )


class Faces:
    def __init__(self, n, refs):
        mx_a, my_a, mz_a, mz_low_a, all_a, *late = refs
        two = lambda ref, first, last, at: ((ref, first, last), *(((late[at], last + 1, n + 1),) if late else ()))
        self.mx = Line(*two(mx_a, -3, n - 2, 0))
        self.my = Line(*two(my_a, -2, n - 1, 1))
        self.mz = Line(*two(mz_a, -2, n - 1, 2))
        self.mz_low = Line(*two(mz_low_a, -2, n - 1, 3))
        self.all = Line(*two(all_a, -2, n - 2, 4))

    def flow(self, row, at, mid, up, down, low=None, high=None):
        total = each(
            lambda a, b, c, d, e, u, v, w, x, y: (a * u + b * v) + (c * w + d * x) - e * y,
            padded(*self.my(at), row), padded(*self.my(at), row, -1), flat(*self.mz(at), row),
            flat(*self.mz_low(at), row), flat(*self.all(at), row), up, down, after_z(mid), before_z(mid), mid,
        )
        if low is not None:
            total = add_product(total, flat(*self.mx(at - 1), row), low)
        if high is not None:
            total = add_product(total, flat(*self.mx(at), row), high)
        return total


def add_product(total, a, b):
    return each(lambda t, x, y: t + x * y, total, a, b)


def sub(a, b):
    return each(lambda x, y: x - y, a, b)


def own_kernel(initial, mobility, conc, mob, to_chip, to_core):
    runs, n, ny, _ = initial.shape
    place = [either(n - 1 - at, at) for at in range(n)]

    def one_run(run, carry):
        for row in chunks(ny):
            for at in range(n):
                put_padded(conc, (run, at), row, plain(initial, (run, place[at]), row))
        return carry

    lax.fori_loop(0, runs, one_run, 0)
    for row in chunks(ny):
        for at in range(n):
            value = plain(mobility, (place[at],), row)
            put_padded(mob, (at,), row, value)
            if at < 3:
                put_flat(to_core, (at,), row, value)
            if at >= n - 3:
                put_flat(to_chip, (n - 1 - at,), row, value)


def mean(a, b):
    return 0.5 * (a + b)


def put_faces(row, mob, places, my, mz, mz_low):
    for at in places:
        mid = padded(*mob(at), row)
        put_padded(*my(at), row, each(mean, mid, padded(*mob(at), row, 1)))
        put_flat(*mz(at), row, each(mean, mid, after_z(mid)))
        put_flat(*mz_low(at), row, each(mean, mid, before_z(mid)))


def put_all(row, faces, places):
    for at in places:
        put_flat(*faces.all(at), row, each(
            lambda a, b, c, d, e, f: (a + b) + (c + d) + (e + f),
            flat(*faces.mx(at - 1), row), flat(*faces.mx(at), row), padded(*faces.my(at), row),
            padded(*faces.my(at), row, -1), flat(*faces.mz(at), row), flat(*faces.mz_low(at), row),
        ))


def put_potential(row, field, run, places, target):
    mids = {at: padded(*field(at, run), row) for at in range(places[0] - 1, places[-1] + 2)}
    for at in places:
        value = potential(
            mids[at - 1], mids[at], mids[at + 1],
            padded(*field(at, run), row, 1), padded(*field(at, run), row, -1),
        )
        put_padded(*target(at, run), row, value)


def put_step(row, faces, chem, state, run, places, target):
    mids = {at: padded(*chem(at, run), row) for at in range(places[0] - 1, places[-1] + 2)}
    for at in places:
        flow = faces.flow(
            row, at, mids[at], padded(*chem(at, run), row, 1), padded(*chem(at, run), row, -1),
            mids[at - 1], mids[at + 1],
        )
        value = each(lambda a, b: a + time_step * b, padded(*state(at, run), row), flow)
        target(at, value)


def put_miss(row, runs, observed, place, run, at, value, adjoint2):
    miss = sub(value, plain(observed, (run, place[at]), row))
    adjoint = each(lambda a: a * (1.0 / runs), miss)
    put_padded(*adjoint2(at, run), row, adjoint)
    return adjoint, sum(part * part for part in miss)


def core_kernel(of_core, m_core, conc_own, mob_own, conc_core, chem0, mx, my, mz, mz_low, m_all, rim):
    runs, n = conc_own.shape[:2]
    ny = of_core.shape[2]
    mob = Line((rim, -3, -1), (mob_own, 0, n - 1))
    faces = Faces(n, (mx, my, mz, mz_low, m_all))
    for row in chunks(ny):
        for at in range(3):
            put_padded(rim, (2 - at,), row, flat(m_core, (at,), row))
    for row in chunks(ny):
        mids = [padded(*mob(at), row) for at in range(-3, n)]
        for at in range(n + 2):
            put_flat(mx, (at,), row, each(mean, mids[at], mids[at + 1]))
        put_faces(row, mob, range(-2, n), faces.my, faces.mz, faces.mz_low)
    for row in chunks(ny):
        put_all(row, faces, range(-2, n - 1))
    place = [either(at, 3 - at) for at in range(4)]
    conc = Line((conc_core, -4, -1), (conc_own, 0, n - 1))

    def one_run(run, carry):
        for row in chunks(ny):
            for at in range(4):
                put_padded(conc_core, (run, 3 - at), row, plain(of_core, (run, place[at]), row))
        for row in chunks(ny):
            put_potential(row, conc, run, range(-3, n - 1), Line((chem0, -3, n - 2)))
        return carry

    lax.fori_loop(0, runs, one_run, 0)


def chip_kernel(
    of_chip, conc_own, conc_core, chem0_a, observed, mx, my, mz, mz_low, m_all,
    conc_chip, chem0_b, state1_a, chem1_a, adjoint2_a, squares,
):
    runs, n = conc_own.shape[:2]
    ny = observed.shape[2]
    faces = Faces(n, (mx, my, mz, mz_low, m_all))
    message = [either(3 - at, at) for at in range(4)]
    place = [either(n - 1 - at, at) for at in range(n)]
    conc = Line((conc_core, -4, -1), (conc_own, 0, n - 1), (conc_chip, n, n + 3))
    chem0 = Line((chem0_a, -3, n - 2), (chem0_b, n - 1, n + 2))
    state1 = Line((state1_a, -2, n - 2))
    chem1 = Line((chem1_a, -1, n - 3))
    adjoint2 = Line((adjoint2_a, 0, n - 4))
    squares[...] = jnp.zeros_like(squares)

    def one_run(run, carry):
        for row in chunks(ny):
            for at in range(4):
                put_padded(conc_chip, (run, at), row, plain(of_chip, (run, message[at]), row))
        for row in chunks(ny):
            put_potential(row, conc, run, range(n - 1, n + 3), chem0)
        for row in chunks(ny):
            put_step(
                row, faces, chem0, conc, run, range(-2, n - 1),
                lambda at, value: put_padded(*state1(at, run), row, value),
            )
        for row in chunks(ny):
            put_potential(row, state1, run, range(-1, n - 2), chem1)
        for row in chunks(ny):

            def target(at, value):
                squares[...] += put_miss(row, runs, observed, place, run, at, value, adjoint2)[1]

            put_step(row, faces, chem1, state1, run, range(0, n - 3), target)
        return carry

    lax.fori_loop(0, runs, one_run, 0)


def forward_kernel(
    m_chip, mob_own, conc_own, conc_chip, chem0_a, chem0_b, state1_a, chem1_a, adjoint2_a, squares, observed,
    mx_a, my_a, mz_a, mz_low_a, all_a,
    mx_b, my_b, mz_b, mz_low_b, all_b, state1_b, chem1_b, adjoint2_b, to_core, to_chip, share, rim, total,
):
    runs, n = conc_own.shape[:2]
    ny = observed.shape[2]
    faces = Faces(n, (mx_a, my_a, mz_a, mz_low_a, all_a, mx_b, my_b, mz_b, mz_low_b, all_b))
    mob = Line((mob_own, 0, n - 1), (rim, n, n + 2))
    place = [either(n - 1 - at, at) for at in range(n)]
    conc = Line((conc_own, 0, n - 1), (conc_chip, n, n + 3))
    chem0 = Line((chem0_a, -3, n - 2), (chem0_b, n - 1, n + 2))
    state1 = Line((state1_a, -2, n - 2), (state1_b, n - 1, n + 1))
    chem1 = Line((chem1_a, -1, n - 3), (chem1_b, n - 2, n))
    adjoint2 = Line((adjoint2_a, 0, n - 4), (adjoint2_b, n - 3, n - 1))
    for row in chunks(ny):
        for at in range(3):
            put_padded(rim, (at,), row, flat(m_chip, (at,), row))
    for row in chunks(ny):
        mids = [padded(*mob(at), row) for at in range(n - 1, n + 3)]
        for at in range(3):
            put_flat(mx_b, (at,), row, each(mean, mids[at], mids[at + 1]))
        put_faces(row, mob, range(n, n + 2), faces.my, faces.mz, faces.mz_low)
    for row in chunks(ny):
        put_all(row, faces, range(n - 1, n + 2))
    total[...] = squares[...]

    def one_run(run, carry):
        for row in chunks(ny):
            put_step(
                row, faces, chem0, conc, run, range(n - 1, n + 2),
                lambda at, value: put_padded(*state1(at, run), row, value),
            )
        for row in chunks(ny):
            put_potential(row, state1, run, range(n - 2, n + 1), chem1)
        for row in chunks(ny):

            def target(at, value):
                adjoint, square = put_miss(row, runs, observed, place, run, at, value, adjoint2)
                total[...] += square
                put_flat(to_chip, (run, n - 1 - at), row, adjoint)
                if at < 3:
                    put_flat(to_core, (run, at), row, adjoint)

            put_step(row, faces, chem1, state1, run, range(n - 3, n), target)
            for at in range(min(3, n - 3)):
                put_flat(to_core, (run, at), row, padded(*adjoint2(at, run), row))
        return carry

    lax.fori_loop(0, runs, one_run, 0)
    columns = (0.5 / runs) * jnp.sum(total[...], axis=0, keepdims=True)
    mine = jnp.broadcast_to(jnp.sum(columns, axis=1, keepdims=True), share.shape)
    share[...] = mine
    to_core[0, 0, 0, ny:] = mine


def put_adjoint1(row, flow, adjoint2, run, places, weight, target):
    mids = {at: padded(*flow(at, run), row) for at in range(places[0] - 1, places[-1] + 2)}
    for at in places:
        total = beside(
            mids[at - 1], mids[at + 1], padded(*flow(at, run), row, 1), padded(*flow(at, run), row, -1), mids[at]
        )
        value = each(
            lambda a, w, f, t: a + w * f - (time_step * stiffness) * t,
            padded(*adjoint2(at, run), row), weight(at), mids[at], total,
        )
        put_padded(*target(at, run), row, value)


def slope(state):
    return each(lambda c: time_step * (3.0 * c * c + (6.0 * stiffness - 1.0)), state)


def step_x(field, run, at, row):
    return sub(padded(*field(at + 1, run), row), padded(*field(at, run), row))


def step_y(field, run, at, row):
    return sub(padded(*field(at, run), row, 1), padded(*field(at, run), row))


def step_z(field, run, at, row):
    mid = padded(*field(at, run), row)
    return sub(after_z(mid), mid)


def early_kernel(
    of_core, mx_a, my_a, mz_a, mz_low_a, all_a, mx_b, my_b, mz_b, mz_low_b, all_b,
    chem0_a, chem0_b, state1_a, state1_b, chem1_a, chem1_b, adjoint2_a, adjoint2_b,
    share_in, flow_a, flow_part, adjoint1_a, weight_b, step_z_b, part, sum_x_b, sum_y_b, sum_z_b, share,
    rim, sum_x, sum_y, sum_z,
):
    share[...] = share_in[...]
    runs = of_core.shape[0]
    n = part.shape[0] + 2
    ny = part.shape[-2]
    faces = Faces(n, (mx_a, my_a, mz_a, mz_low_a, all_a, mx_b, my_b, mz_b, mz_low_b, all_b))
    chem0 = Line((chem0_a, -3, n - 2), (chem0_b, n - 1, n + 2))
    state1 = Line((state1_a, -2, n - 2), (state1_b, n - 1, n + 1))
    chem1 = Line((chem1_a, -1, n - 3), (chem1_b, n - 2, n))
    adjoint2 = Line((rim, -3, -1), (adjoint2_a, 0, n - 4), (adjoint2_b, n - 3, n - 1))
    flow = Line((flow_a, -2, n - 2), (flow_part, n - 1, n - 1))
    adjoint1 = Line((adjoint1_a, -1, n - 3))
    for sums in (sum_x, sum_y, sum_z):
        sums[...] = jnp.zeros_like(sums)

    def one_run(run, carry):
        for row in chunks(ny):
            for at in range(3):
                put_padded(rim, (run, 2 - at), row, flat(of_core, (run, at), row))
        for row in chunks(ny):
            mids = {at: padded(*adjoint2(at, run), row) for at in range(-3, n)}
            for at in range(-2, n):
                value = faces.flow(
                    row, at, mids[at], padded(*adjoint2(at, run), row, 1), padded(*adjoint2(at, run), row, -1),
                    mids[at - 1], mids.get(at + 1),
                )
                put_padded(*flow(at, run), row, value)
        for row in chunks(ny):
            put_adjoint1(
                row, flow, adjoint2, run, range(-1, n - 2),
                lambda at: slope(padded(*state1(at, run), row)), adjoint1,
            )
            for at in range(n - 2, n + 1):
                put_flat(weight_b, (run, at - (n - 2)), row, slope(padded(*state1(at, run), row)))
        for row in chunks(ny):
            for at in range(-1, n - 1):
                total = add_product(
                    flat(sum_x, (at + 1,), row), step_x(adjoint2, run, at, row), step_x(chem1, run, at, row)
                )
                if at < n - 3:
                    total = add_product(total, step_x(adjoint1, run, at, row), step_x(chem0, run, at, row))
                put_flat(sum_x, (at + 1,), row, total)
            for at in range(n):
                total_y = add_product(
                    padded(sum_y, (at,), row), step_y(adjoint2, run, at, row), step_y(chem1, run, at, row)
                )
                total_z = add_product(
                    flat(sum_z, (at,), row), step_z(adjoint2, run, at, row), step_z(chem1, run, at, row)
                )
                slant = step_z(chem0, run, at, row)
                if at < n - 2:
                    total_y = add_product(total_y, step_y(adjoint1, run, at, row), step_y(chem0, run, at, row))
                    total_z = add_product(total_z, step_z(adjoint1, run, at, row), slant)
                else:
                    put_flat(step_z_b, (run, at - (n - 2)), row, slant)
                put_padded(sum_y, (at,), row, total_y)
                put_flat(sum_z, (at,), row, total_z)
        return carry

    lax.fori_loop(0, runs, one_run, 0)
    for row in chunks(ny):
        for at in range(n - 2):
            sides = flat(sum_z, (at,), row)
            value = each(
                lambda a, b, c, d, e: -0.5 * ((a + b) + (c + d) + e),
                padded(sum_y, (at,), row), padded(sum_y, (at,), row, -1), sides, before_z(sides),
                flat(sum_x, (at,), row),
            )
            if at < n - 3:
                value = each(lambda a, b: a - 0.5 * b, value, flat(sum_x, (at + 1,), row))
            put_flat(part, (at,), row, value)
        for at in range(2):
            put_flat(sum_x_b, (at,), row, flat(sum_x, (n - 2 + at,), row))
            put_flat(sum_y_b, (at,), row, padded(sum_y, (n - 2 + at,), row))
            put_flat(sum_z_b, (at,), row, flat(sum_z, (n - 2 + at,), row))


def late_kernel(
    of_chip, mx_a, my_a, mz_a, mz_low_a, all_a, mx_b, my_b, mz_b, mz_low_b, all_b,
    chem0_a, chem0_b, chem1_b, adjoint2_b, flow_a, flow_part, adjoint1_a, weight_b, step_z_b,
    part, sum_x_b, sum_y_b, sum_z_b, result, rim, flow_b, adjoint1_b, sum_x, sum_y, sum_z,
):
    runs = of_chip.shape[0]
    n, ny, _ = result.shape
    faces = Faces(n, (mx_a, my_a, mz_a, mz_low_a, all_a, mx_b, my_b, mz_b, mz_low_b, all_b))
    place = [either(n - 1 - at, at) for at in range(n)]
    chem0 = Line((chem0_a, -3, n - 2), (chem0_b, n - 1, n + 2))
    chem1 = Line((chem1_b, n - 2, n))
    adjoint2 = Line((adjoint2_b, n - 3, n - 1), (rim, n, n + 2))
    flow = Line((flow_a, -2, n - 2), (flow_b, n - 1, n + 1))
    adjoint1 = Line((adjoint1_a, -1, n - 3), (adjoint1_b, n - 2, n))
    for row in chunks(ny):
        for at in range(2):
            put_flat(sum_x, (at,), row, flat(sum_x_b, (at,), row))
            put_padded(sum_y, (at,), row, flat(sum_y_b, (at,), row))
            put_flat(sum_z, (at,), row, flat(sum_z_b, (at,), row))
    sum_x[2] = jnp.zeros_like(sum_x[2])

    def one_run(run, carry):
        for row in chunks(ny):
            for at in range(3):
                put_padded(rim, (run, at), row, flat(of_chip, (run, at), row))
        for row in chunks(ny):
            mids = {at: padded(*adjoint2(at, run), row) for at in range(n - 1, n + 3)}
            value = add_product(padded(flow_part, (run, 0), row), flat(*faces.mx(n - 1), row), mids[n])
            put_padded(*flow(n - 1, run), row, value)
            for at in range(n, n + 2):
                value = faces.flow(
                    row, at, mids[at], padded(*adjoint2(at, run), row, 1), padded(*adjoint2(at, run), row, -1),
                    mids[at - 1], mids[at + 1],
                )
                put_padded(*flow(at, run), row, value)
        for row in chunks(ny):
            put_adjoint1(
                row, flow, adjoint2, run, range(n - 2, n + 1),
                lambda at: flat(weight_b, (run, at - (n - 2)), row), adjoint1,
            )
        for row in chunks(ny):
            for at in range(n - 3, n):
                total = add_product(
                    flat(sum_x, (at - (n - 3),), row), step_x(adjoint1, run, at, row), step_x(chem0, run, at, row)
                )
                if at == n - 1:
                    total = add_product(total, step_x(adjoint2, run, at, row), step_x(chem1, run, at, row))
                put_flat(sum_x, (at - (n - 3),), row, total)
            for at in range(n - 2, n):
                to = (at - (n - 2),)
                put_padded(sum_y, to, row, add_product(
                    padded(sum_y, to, row), step_y(adjoint1, run, at, row), step_y(chem0, run, at, row)
                ))
                put_flat(sum_z, to, row, add_product(
                    flat(sum_z, to, row), step_z(adjoint1, run, at, row), flat(step_z_b, (run, *to), row)
                ))
        return carry

    lax.fori_loop(0, runs, one_run, 0)
    for row in chunks(ny):
        for at in range(n - 2):
            value = flat(part, (at,), row)
            if at == n - 3:
                value = each(lambda a, b: a - 0.5 * b, value, flat(sum_x, (0,), row))
            put_plain(result, (place[at],), row, value)
        for at in range(2):
            sides = flat(sum_z, (at,), row)
            value = each(
                lambda a, b, c, d, e, f: -0.5 * ((a + b) + (c + d) + (e + f)),
                flat(sum_x, (at,), row), flat(sum_x, (at + 1,), row),
                padded(sum_y, (at,), row), padded(sum_y, (at,), row, -1), sides, before_z(sides),
            )
            put_plain(result, (place[n - 2 + at],), row, value)


def counts(at):
    return (at ^ (at >> 1)) & 1


def misfit_kernel(total, handed, misfit):
    misfit[0] = jnp.where(counts(lax.axis_index("gx")) == 1, total[0, 0], handed[0, 0])


def call(kernel, outs, scratch, args, flops, scalar=None):
    moved = 4 * (sum(a.size for a in args) + sum(math.prod(o) for o in outs))
    return pl.pallas_call(
        kernel,
        out_shape=tuple(jax.ShapeDtypeStruct(o, jnp.float32) for o in outs),
        in_specs=[VMEM] * len(args),
        out_specs=tuple(SMEM if at == scalar else VMEM for at in range(len(outs))),
        scratch_shapes=[pltpu.VMEM(s, jnp.float32) for s in scratch],
        compiler_params=pltpu.CompilerParams(vmem_limit_bytes=16 * 1024 * 1024),
        cost_estimate=pl.CostEstimate(flops=flops, bytes_accessed=moved, transcendentals=0),
    )(*args)


def on_device(initial, observed, mobility):
    runs, n, ny, nz = initial.shape
    blocks = nz // LANES
    count = lax.axis_size("gx")
    over_chips = [(i, (i - 1 + 2 * (i % 2)) % count) for i in range(count)]
    over_cores = [(i, i ^ 1) for i in range(count)]
    cell = ny * nz

    def neighbours(to_chip, to_core):
        of_core = lax.ppermute(to_core, "gx", over_cores)
        return lax.ppermute(to_chip, "gx", over_chips), of_core

    def lies(*lead):
        return (*lead, blocks, ny, LANES)

    def lies_padded(*lead):
        return (*lead, blocks, ny + 2 * PAD, LANES)

    if n == 4:
        near = (initial, initial)
    else:
        near = [lax.dynamic_slice_in_dim(initial, at, 4, 1) for at in (either(0, n - 4), either(n - 4, 0))]
    of_chip, of_core = neighbours(*near)
    conc, mob, to_chip, to_core = call(
        own_kernel, (lies_padded(runs, n), lies_padded(n), lies(3), lies(3)), (), (initial, mobility),
        runs * n * cell,
    )
    m_chip, m_core = neighbours(to_chip, to_core)
    conc_core, chem0_a, *faces_a = call(
        core_kernel,
        (
            lies_padded(runs, 4), lies_padded(runs, n + 2),
            lies(n + 2), lies_padded(n + 2), lies(n + 2), lies(n + 2), lies(n + 1),
        ),
        (lies_padded(3),),
        (of_core, m_core, conc, mob),
        20 * runs * (n + 2) * cell,
    )
    conc_chip, chem0_b, state1_a, chem1_a, adjoint2_a, squares = call(
        chip_kernel,
        (
            lies_padded(runs, 4), lies_padded(runs, 4), lies_padded(runs, n + 1),
            lies_padded(runs, n - 1), lies_padded(runs, n - 3), (CHUNK, LANES),
        ),
        (),
        (of_chip, conc, conc_core, chem0_a, observed, *faces_a),
        60 * runs * (n - 1) * cell,
    )
    *faces_b, state1_b, chem1_b, adjoint2_b, to_core, to_chip, share = call(
        forward_kernel,
        (
            lies(3), lies_padded(2), lies(2), lies(2), lies(3),
            lies_padded(runs, 3), lies_padded(runs, 3), lies_padded(runs, 3),
            (runs, 3, blocks, ny + ROWS, LANES), lies(runs, 3), (ROWS, LANES),
        ),
        (lies_padded(3), (CHUNK, LANES)),
        (m_chip, mob, conc, conc_chip, chem0_a, chem0_b, state1_a, chem1_a, adjoint2_a, squares, observed, *faces_a),
        60 * runs * 3 * cell,
    )
    faces = (*faces_a, *faces_b)
    of_chip, of_core = neighbours(to_chip, to_core)
    bits = range(count.bit_length() - 2)

    groups = lax.axis_size("group")

    def target(group, at, apart):
        if counts(at):
            return group * count + (at ^ apart)
        return min(group ^ 1, groups - 1) * count + at

    def hop(value, bit):
        apart = 3 if bit == 0 else 2 << bit
        pairs = [
            (group * count + at, target(group, at, apart)) for group in range(groups) for at in range(count)
        ]
        return lax.ppermute(value, ("group", "gx"), pairs)

    share = share + of_core[0, 0, 0, ny:]
    far = hop(share, bits[-1])
    flow_a, flow_part, adjoint1_a, weight_b, step_z_b, part, *sums_b, share = call(
        early_kernel,
        (
            lies_padded(runs, n + 1), lies_padded(runs, 1), lies_padded(runs, n - 1), lies(runs, 3), lies(runs, 2),
            lies(n - 2), lies(2), lies(2), lies(2), (ROWS, LANES),
        ),
        (lies_padded(runs, 3), lies(n), lies_padded(n), lies(n)),
        (of_core, *faces, chem0_a, chem0_b, state1_a, state1_b, chem1_a, chem1_b, adjoint2_a, adjoint2_b, share),
        60 * runs * n * cell,
    )
    for bit in bits[-2::-1]:
        share = share + far
        far = hop(share, bit)
    share = share + far
    handed = lax.ppermute(share, "gx", over_cores)
    (result,) = call(
        late_kernel,
        ((n, ny, nz),),
        (
            lies_padded(runs, 3), lies_padded(runs, 3), lies_padded(runs, 3),
            lies(3), lies_padded(2), lies(2),
        ),
        (
            of_chip, *faces, chem0_a, chem0_b, chem1_b, adjoint2_b, flow_a, flow_part, adjoint1_a,
            weight_b, step_z_b, part, *sums_b,
        ),
        60 * runs * 3 * cell,
    )
    (misfit,) = call(misfit_kernel, ((1,),), (), (share, handed), 1, scalar=0)
    return (result, misfit)


def solution(mesh):
    placed = (
        P("group", "gx", None, None),
        P("group", "gx", None, None),
        P(("group", "gx"), None, None),
    )
    return jax.shard_map(
        on_device,
        mesh=mesh,
        in_specs=placed,
        out_specs=(P(("group", "gx"), None, None), P("group")),
        check_vma=False,
    )
```

```python
import functools
import math

import jax
import jax.numpy as jnp
from jax import lax
from jax.experimental import pallas as pl
from jax.experimental.pallas import tpu as pltpu
from jax.sharding import PartitionSpec as P

stiffness = 0.5
time_step = 0.005
VMEM = pl.BlockSpec(memory_space=pltpu.VMEM)
SMEM = pl.BlockSpec(memory_space=pltpu.SMEM)
LANES = 128
ROWS = 8
PAD = ROWS
CHUNK = 8


def chunks(ny):
    return range(0, ny, CHUNK)


def plain(ref, lead, row):
    return [
        ref[(*lead, pl.ds(row, CHUNK), pl.ds(at, LANES))] for at in range(0, ref.shape[-1], LANES)
    ]


def put_plain(ref, lead, row, value):
    for block, part in enumerate(value):
        ref[(*lead, pl.ds(row, CHUNK), pl.ds(block * LANES, LANES))] = part


def flat(ref, lead, row):
    return [ref[(*lead, block, pl.ds(row, CHUNK))] for block in range(ref.shape[-3])]


def put_flat(ref, lead, row, value):
    for block, part in enumerate(value):
        ref[(*lead, block, pl.ds(row, CHUNK))] = part


def padded(ref, lead, row, shift=0):
    return [ref[(*lead, block, pl.ds(PAD + row + shift, CHUNK))] for block in range(ref.shape[-3])]


def put_padded(ref, lead, row, value):
    ny = ref.shape[-2] - 2 * PAD
    for block, part in enumerate(value):
        ref[(*lead, block, pl.ds(PAD + row, CHUNK))] = part
        if row == 0:
            ref[(*lead, block, pl.ds(PAD + ny, 1))] = part[:1]
        if row + CHUNK == ny:
            ref[(*lead, block, pl.ds(PAD - 1, 1))] = part[CHUNK - 1 :]


def lane():
    return lax.broadcasted_iota(jnp.int32, (CHUNK, LANES), 1)


def after_z(value):
    turned = [pltpu.roll(part, LANES - 1, 1) for part in value]
    turned.append(turned[0])
    edge = lane() == LANES - 1
    return [jnp.where(edge, turned[at + 1], turned[at]) for at in range(len(value))]


def before_z(value):
    turned = [pltpu.roll(part, 1, 1) for part in value]
    edge = lane() == 0
    return [jnp.where(edge, turned[at - 1], turned[at]) for at in range(len(value))]


def side():
    return lax.rem(lax.axis_index("gx"), 2)


def either(first, second):
    return first + side() * (second - first)


class Line:
    def __init__(self, *parts):
        self.parts = parts

    def __call__(self, at, *lead):
        for ref, first, last in self.parts:
            if first <= at <= last:
                return ref, (*lead, at - first)
        raise IndexError(at)


def each(function, *values):
    return [function(*parts) for parts in zip(*values)]


def beside(low, high, up, down, mid):
    return each(
        lambda a, b, c, d, e, f: (a + b) + (c + d) + (e + f),
        low, high, up, down, after_z(mid), before_z(mid),
    )


def potential(low, mid, high, up, down):
    return each(
        lambda c, total: c * (c * c + (6.0 * stiffness - 1.0)) - stiffness * total,
        mid, beside(low, high, up, down, mid),
    )


class Faces:
    def __init__(self, n, refs):
        mx_a, my_a, mz_a, mz_low_a, all_a, *late = refs
        two = lambda ref, first, last, at: ((ref, first, last), *(((late[at], last + 1, n + 1),) if late else ()))
        self.mx = Line(*two(mx_a, -3, n - 2, 0))
        self.my = Line(*two(my_a, -2, n - 1, 1))
        self.mz = Line(*two(mz_a, -2, n - 1, 2))
        self.mz_low = Line(*two(mz_low_a, -2, n - 1, 3))
        self.all = Line(*two(all_a, -2, n - 2, 4))

    def flow(self, row, at, mid, up, down, low=None, high=None):
        total = each(
            lambda a, b, c, d, e, u, v, w, x, y: (a * u + b * v) + (c * w + d * x) - e * y,
            padded(*self.my(at), row), padded(*self.my(at), row, -1), flat(*self.mz(at), row),
            flat(*self.mz_low(at), row), flat(*self.all(at), row), up, down, after_z(mid), before_z(mid), mid,
        )
        if low is not None:
            total = add_product(total, flat(*self.mx(at - 1), row), low)
        if high is not None:
            total = add_product(total, flat(*self.mx(at), row), high)
        return total


def add_product(total, a, b):
    return each(lambda t, x, y: t + x * y, total, a, b)


def sub(a, b):
    return each(lambda x, y: x - y, a, b)


def own_kernel(initial, mobility, conc, mob, to_chip, to_core):
    runs, n, ny, _ = initial.shape
    place = [either(n - 1 - at, at) for at in range(n)]

    def one_run(run, carry):
        for row in chunks(ny):
            for at in range(n):
                put_padded(conc, (run, at), row, plain(initial, (run, place[at]), row))
        return carry

    lax.fori_loop(0, runs, one_run, 0)
    for row in chunks(ny):
        for at in range(n):
            value = plain(mobility, (place[at],), row)
            put_padded(mob, (at,), row, value)
            if at < 3:
                put_flat(to_core, (at,), row, value)
            if at >= n - 3:
                put_flat(to_chip, (n - 1 - at,), row, value)


def mean(a, b):
    return 0.5 * (a + b)


def put_faces(row, mob, places, my, mz, mz_low):
    for at in places:
        mid = padded(*mob(at), row)
        put_padded(*my(at), row, each(mean, mid, padded(*mob(at), row, 1)))
        put_flat(*mz(at), row, each(mean, mid, after_z(mid)))
        put_flat(*mz_low(at), row, each(mean, mid, before_z(mid)))


def put_all(row, faces, places):
    for at in places:
        put_flat(*faces.all(at), row, each(
            lambda a, b, c, d, e, f: (a + b) + (c + d) + (e + f),
            flat(*faces.mx(at - 1), row), flat(*faces.mx(at), row), padded(*faces.my(at), row),
            padded(*faces.my(at), row, -1), flat(*faces.mz(at), row), flat(*faces.mz_low(at), row),
        ))


def put_potential(row, field, run, places, target):
    mids = {at: padded(*field(at, run), row) for at in range(places[0] - 1, places[-1] + 2)}
    for at in places:
        value = potential(
            mids[at - 1], mids[at], mids[at + 1],
            padded(*field(at, run), row, 1), padded(*field(at, run), row, -1),
        )
        put_padded(*target(at, run), row, value)


def put_step(row, faces, chem, state, run, places, target):
    mids = {at: padded(*chem(at, run), row) for at in range(places[0] - 1, places[-1] + 2)}
    for at in places:
        flow = faces.flow(
            row, at, mids[at], padded(*chem(at, run), row, 1), padded(*chem(at, run), row, -1),
            mids[at - 1], mids[at + 1],
        )
        value = each(lambda a, b: a + time_step * b, padded(*state(at, run), row), flow)
        target(at, value)


def put_miss(row, runs, observed, place, run, at, value, adjoint2):
    miss = sub(value, plain(observed, (run, place[at]), row))
    adjoint = each(lambda a: a * (1.0 / runs), miss)
    put_padded(*adjoint2(at, run), row, adjoint)
    return adjoint, sum(part * part for part in miss)


def core_kernel(of_core, m_core, conc_own, mob_own, conc_core, chem0, mx, my, mz, mz_low, m_all, rim):
    runs, n = conc_own.shape[:2]
    ny = of_core.shape[2]
    mob = Line((rim, -3, -1), (mob_own, 0, n - 1))
    faces = Faces(n, (mx, my, mz, mz_low, m_all))
    for row in chunks(ny):
        for at in range(3):
            put_padded(rim, (2 - at,), row, flat(m_core, (at,), row))
    for row in chunks(ny):
        mids = [padded(*mob(at), row) for at in range(-3, n)]
        for at in range(n + 2):
            put_flat(mx, (at,), row, each(mean, mids[at], mids[at + 1]))
        put_faces(row, mob, range(-2, n), faces.my, faces.mz, faces.mz_low)
    for row in chunks(ny):
        put_all(row, faces, range(-2, n - 1))
    place = [either(at, 3 - at) for at in range(4)]
    conc = Line((conc_core, -4, -1), (conc_own, 0, n - 1))

    def one_run(run, carry):
        for row in chunks(ny):
            for at in range(4):
                put_padded(conc_core, (run, 3 - at), row, plain(of_core, (run, place[at]), row))
        for row in chunks(ny):
            put_potential(row, conc, run, range(-3, n - 1), Line((chem0, -3, n - 2)))
        return carry

    lax.fori_loop(0, runs, one_run, 0)


def chip_kernel(
    of_chip, conc_own, conc_core, chem0_a, observed, mx, my, mz, mz_low, m_all,
    conc_chip, chem0_b, state1_a, chem1_a, adjoint2_a, squares,
):
    runs, n = conc_own.shape[:2]
    ny = observed.shape[2]
    faces = Faces(n, (mx, my, mz, mz_low, m_all))
    message = [either(3 - at, at) for at in range(4)]
    place = [either(n - 1 - at, at) for at in range(n)]
    conc = Line((conc_core, -4, -1), (conc_own, 0, n - 1), (conc_chip, n, n + 3))
    chem0 = Line((chem0_a, -3, n - 2), (chem0_b, n - 1, n + 2))
    state1 = Line((state1_a, -2, n - 2))
    chem1 = Line((chem1_a, -1, n - 3))
    adjoint2 = Line((adjoint2_a, 0, n - 4))
    squares[...] = jnp.zeros_like(squares)

    def one_run(run, carry):
        for row in chunks(ny):
            for at in range(4):
                put_padded(conc_chip, (run, at), row, plain(of_chip, (run, message[at]), row))
        for row in chunks(ny):
            put_potential(row, conc, run, range(n - 1, n + 3), chem0)
        for row in chunks(ny):
            put_step(
                row, faces, chem0, conc, run, range(-2, n - 1),
                lambda at, value: put_padded(*state1(at, run), row, value),
            )
        for row in chunks(ny):
            put_potential(row, state1, run, range(-1, n - 2), chem1)
        for row in chunks(ny):

            def target(at, value):
                squares[...] += put_miss(row, runs, observed, place, run, at, value, adjoint2)[1]

            put_step(row, faces, chem1, state1, run, range(0, n - 3), target)
        return carry

    lax.fori_loop(0, runs, one_run, 0)


def forward_kernel(
    m_chip, mob_own, conc_own, conc_chip, chem0_a, chem0_b, state1_a, chem1_a, adjoint2_a, squares, observed,
    mx_a, my_a, mz_a, mz_low_a, all_a,
    mx_b, my_b, mz_b, mz_low_b, all_b, state1_b, chem1_b, adjoint2_b, to_core, to_chip, share, rim, total,
):
    runs, n = conc_own.shape[:2]
    ny = observed.shape[2]
    faces = Faces(n, (mx_a, my_a, mz_a, mz_low_a, all_a, mx_b, my_b, mz_b, mz_low_b, all_b))
    mob = Line((mob_own, 0, n - 1), (rim, n, n + 2))
    place = [either(n - 1 - at, at) for at in range(n)]
    conc = Line((conc_own, 0, n - 1), (conc_chip, n, n + 3))
    chem0 = Line((chem0_a, -3, n - 2), (chem0_b, n - 1, n + 2))
    state1 = Line((state1_a, -2, n - 2), (state1_b, n - 1, n + 1))
    chem1 = Line((chem1_a, -1, n - 3), (chem1_b, n - 2, n))
    adjoint2 = Line((adjoint2_a, 0, n - 4), (adjoint2_b, n - 3, n - 1))
    for row in chunks(ny):
        for at in range(3):
            put_padded(rim, (at,), row, flat(m_chip, (at,), row))
    for row in chunks(ny):
        mids = [padded(*mob(at), row) for at in range(n - 1, n + 3)]
        for at in range(3):
            put_flat(mx_b, (at,), row, each(mean, mids[at], mids[at + 1]))
        put_faces(row, mob, range(n, n + 2), faces.my, faces.mz, faces.mz_low)
    for row in chunks(ny):
        put_all(row, faces, range(n - 1, n + 2))
    total[...] = squares[...]

    def one_run(run, carry):
        for row in chunks(ny):
            put_step(
                row, faces, chem0, conc, run, range(n - 1, n + 2),
                lambda at, value: put_padded(*state1(at, run), row, value),
            )
        for row in chunks(ny):
            put_potential(row, state1, run, range(n - 2, n + 1), chem1)
        for row in chunks(ny):

            def target(at, value):
                adjoint, square = put_miss(row, runs, observed, place, run, at, value, adjoint2)
                total[...] += square
                put_flat(to_chip, (run, n - 1 - at), row, adjoint)
                if at < 3:
                    put_flat(to_core, (run, at), row, adjoint)

            put_step(row, faces, chem1, state1, run, range(n - 3, n), target)
            for at in range(min(3, n - 3)):
                put_flat(to_core, (run, at), row, padded(*adjoint2(at, run), row))
        return carry

    lax.fori_loop(0, runs, one_run, 0)
    columns = (0.5 / runs) * jnp.sum(total[...], axis=0, keepdims=True)
    mine = jnp.broadcast_to(jnp.sum(columns, axis=1, keepdims=True), share.shape)
    share[...] = mine
    to_core[0, 0, 0, ny:] = mine


def put_adjoint1(row, flow, adjoint2, run, places, weight, target):
    mids = {at: padded(*flow(at, run), row) for at in range(places[0] - 1, places[-1] + 2)}
    for at in places:
        total = beside(
            mids[at - 1], mids[at + 1], padded(*flow(at, run), row, 1), padded(*flow(at, run), row, -1), mids[at]
        )
        value = each(
            lambda a, w, f, t: a + w * f - (time_step * stiffness) * t,
            padded(*adjoint2(at, run), row), weight(at), mids[at], total,
        )
        put_padded(*target(at, run), row, value)


def slope(state):
    return each(lambda c: time_step * (3.0 * c * c + (6.0 * stiffness - 1.0)), state)


def step_x(field, run, at, row):
    return sub(padded(*field(at + 1, run), row), padded(*field(at, run), row))


def step_y(field, run, at, row):
    return sub(padded(*field(at, run), row, 1), padded(*field(at, run), row))


def step_z(field, run, at, row):
    mid = padded(*field(at, run), row)
    return sub(after_z(mid), mid)


def early_kernel(
    of_core, mx_a, my_a, mz_a, mz_low_a, all_a, mx_b, my_b, mz_b, mz_low_b, all_b,
    chem0_a, chem0_b, state1_a, state1_b, chem1_a, chem1_b, adjoint2_a, adjoint2_b,
    share_in, flow_a, flow_part, adjoint1_a, weight_b, step_z_b, part, sum_x_b, sum_y_b, sum_z_b, share,
    rim, sum_x, sum_y, sum_z,
):
    share[...] = share_in[...]
    runs = of_core.shape[0]
    n = part.shape[0] + 2
    ny = part.shape[-2]
    faces = Faces(n, (mx_a, my_a, mz_a, mz_low_a, all_a, mx_b, my_b, mz_b, mz_low_b, all_b))
    chem0 = Line((chem0_a, -3, n - 2), (chem0_b, n - 1, n + 2))
    state1 = Line((state1_a, -2, n - 2), (state1_b, n - 1, n + 1))
    chem1 = Line((chem1_a, -1, n - 3), (chem1_b, n - 2, n))
    adjoint2 = Line((rim, -3, -1), (adjoint2_a, 0, n - 4), (adjoint2_b, n - 3, n - 1))
    flow = Line((flow_a, -2, n - 2), (flow_part, n - 1, n - 1))
    adjoint1 = Line((adjoint1_a, -1, n - 3))
    for sums in (sum_x, sum_y, sum_z):
        sums[...] = jnp.zeros_like(sums)

    def one_run(run, carry):
        for row in chunks(ny):
            for at in range(3):
                put_padded(rim, (run, 2 - at), row, flat(of_core, (run, at), row))
        for row in chunks(ny):
            mids = {at: padded(*adjoint2(at, run), row) for at in range(-3, n)}
            for at in range(-2, n):
                value = faces.flow(
                    row, at, mids[at], padded(*adjoint2(at, run), row, 1), padded(*adjoint2(at, run), row, -1),
                    mids[at - 1], mids.get(at + 1),
                )
                put_padded(*flow(at, run), row, value)
        for row in chunks(ny):
            put_adjoint1(
                row, flow, adjoint2, run, range(-1, n - 2),
                lambda at: slope(padded(*state1(at, run), row)), adjoint1,
            )
            for at in range(n - 2, n + 1):
                put_flat(weight_b, (run, at - (n - 2)), row, slope(padded(*state1(at, run), row)))
        for row in chunks(ny):
            for at in range(-1, n - 1):
                total = add_product(
                    flat(sum_x, (at + 1,), row), step_x(adjoint2, run, at, row), step_x(chem1, run, at, row)
                )
                if at < n - 3:
                    total = add_product(total, step_x(adjoint1, run, at, row), step_x(chem0, run, at, row))
                put_flat(sum_x, (at + 1,), row, total)
            for at in range(n):
                total_y = add_product(
                    padded(sum_y, (at,), row), step_y(adjoint2, run, at, row), step_y(chem1, run, at, row)
                )
                total_z = add_product(
                    flat(sum_z, (at,), row), step_z(adjoint2, run, at, row), step_z(chem1, run, at, row)
                )
                slant = step_z(chem0, run, at, row)
                if at < n - 2:
                    total_y = add_product(total_y, step_y(adjoint1, run, at, row), step_y(chem0, run, at, row))
                    total_z = add_product(total_z, step_z(adjoint1, run, at, row), slant)
                else:
                    put_flat(step_z_b, (run, at - (n - 2)), row, slant)
                put_padded(sum_y, (at,), row, total_y)
                put_flat(sum_z, (at,), row, total_z)
        return carry

    lax.fori_loop(0, runs, one_run, 0)
    for row in chunks(ny):
        for at in range(n - 2):
            sides = flat(sum_z, (at,), row)
            value = each(
                lambda a, b, c, d, e: -0.5 * ((a + b) + (c + d) + e),
                padded(sum_y, (at,), row), padded(sum_y, (at,), row, -1), sides, before_z(sides),
                flat(sum_x, (at,), row),
            )
            if at < n - 3:
                value = each(lambda a, b: a - 0.5 * b, value, flat(sum_x, (at + 1,), row))
            put_flat(part, (at,), row, value)
        for at in range(2):
            put_flat(sum_x_b, (at,), row, flat(sum_x, (n - 2 + at,), row))
            put_flat(sum_y_b, (at,), row, padded(sum_y, (n - 2 + at,), row))
            put_flat(sum_z_b, (at,), row, flat(sum_z, (n - 2 + at,), row))


def late_kernel(
    of_chip, mx_a, my_a, mz_a, mz_low_a, all_a, mx_b, my_b, mz_b, mz_low_b, all_b,
    chem0_a, chem0_b, chem1_b, adjoint2_b, flow_a, flow_part, adjoint1_a, weight_b, step_z_b,
    part, sum_x_b, sum_y_b, sum_z_b, share_in, result, share, rim, flow_b, adjoint1_b, sum_x, sum_y, sum_z,
):
    share[...] = share_in[...]
    runs = of_chip.shape[0]
    n, ny, _ = result.shape
    faces = Faces(n, (mx_a, my_a, mz_a, mz_low_a, all_a, mx_b, my_b, mz_b, mz_low_b, all_b))
    place = [either(n - 1 - at, at) for at in range(n)]
    chem0 = Line((chem0_a, -3, n - 2), (chem0_b, n - 1, n + 2))
    chem1 = Line((chem1_b, n - 2, n))
    adjoint2 = Line((adjoint2_b, n - 3, n - 1), (rim, n, n + 2))
    flow = Line((flow_a, -2, n - 2), (flow_b, n - 1, n + 1))
    adjoint1 = Line((adjoint1_a, -1, n - 3), (adjoint1_b, n - 2, n))
    for row in chunks(ny):
        for at in range(2):
            put_flat(sum_x, (at,), row, flat(sum_x_b, (at,), row))
            put_padded(sum_y, (at,), row, flat(sum_y_b, (at,), row))
            put_flat(sum_z, (at,), row, flat(sum_z_b, (at,), row))
    sum_x[2] = jnp.zeros_like(sum_x[2])

    def one_run(run, carry):
        for row in chunks(ny):
            for at in range(3):
                put_padded(rim, (run, at), row, flat(of_chip, (run, at), row))
        for row in chunks(ny):
            mids = {at: padded(*adjoint2(at, run), row) for at in range(n - 1, n + 3)}
            value = add_product(padded(flow_part, (run, 0), row), flat(*faces.mx(n - 1), row), mids[n])
            put_padded(*flow(n - 1, run), row, value)
            for at in range(n, n + 2):
                value = faces.flow(
                    row, at, mids[at], padded(*adjoint2(at, run), row, 1), padded(*adjoint2(at, run), row, -1),
                    mids[at - 1], mids[at + 1],
                )
                put_padded(*flow(at, run), row, value)
        for row in chunks(ny):
            put_adjoint1(
                row, flow, adjoint2, run, range(n - 2, n + 1),
                lambda at: flat(weight_b, (run, at - (n - 2)), row), adjoint1,
            )
        for row in chunks(ny):
            for at in range(n - 3, n):
                total = add_product(
                    flat(sum_x, (at - (n - 3),), row), step_x(adjoint1, run, at, row), step_x(chem0, run, at, row)
                )
                if at == n - 1:
                    total = add_product(total, step_x(adjoint2, run, at, row), step_x(chem1, run, at, row))
                put_flat(sum_x, (at - (n - 3),), row, total)
            for at in range(n - 2, n):
                to = (at - (n - 2),)
                put_padded(sum_y, to, row, add_product(
                    padded(sum_y, to, row), step_y(adjoint1, run, at, row), step_y(chem0, run, at, row)
                ))
                put_flat(sum_z, to, row, add_product(
                    flat(sum_z, to, row), step_z(adjoint1, run, at, row), flat(step_z_b, (run, *to), row)
                ))
        return carry

    lax.fori_loop(0, runs, one_run, 0)
    for row in chunks(ny):
        for at in range(n - 2):
            value = flat(part, (at,), row)
            if at == n - 3:
                value = each(lambda a, b: a - 0.5 * b, value, flat(sum_x, (0,), row))
            put_plain(result, (place[at],), row, value)
        for at in range(2):
            sides = flat(sum_z, (at,), row)
            value = each(
                lambda a, b, c, d, e, f: -0.5 * ((a + b) + (c + d) + (e + f)),
                flat(sum_x, (at,), row), flat(sum_x, (at + 1,), row),
                padded(sum_y, (at,), row), padded(sum_y, (at,), row, -1), sides, before_z(sides),
            )
            put_plain(result, (place[n - 2 + at],), row, value)


def counts(at):
    return (at ^ (at >> 1)) & 1


def misfit_kernel(total, handed, misfit):
    misfit[0] = jnp.where(counts(lax.axis_index("gx")) == 1, total[0, 0], handed[0, 0])


def call(kernel, outs, scratch, args, flops, scalar=None):
    moved = 4 * (sum(a.size for a in args) + sum(math.prod(o) for o in outs))
    return pl.pallas_call(
        kernel,
        out_shape=tuple(jax.ShapeDtypeStruct(o, jnp.float32) for o in outs),
        in_specs=[VMEM] * len(args),
        out_specs=tuple(SMEM if at == scalar else VMEM for at in range(len(outs))),
        scratch_shapes=[pltpu.VMEM(s, jnp.float32) for s in scratch],
        compiler_params=pltpu.CompilerParams(vmem_limit_bytes=16 * 1024 * 1024),
        cost_estimate=pl.CostEstimate(flops=flops, bytes_accessed=moved, transcendentals=0),
    )(*args)


def on_device(initial, observed, mobility):
    runs, n, ny, nz = initial.shape
    blocks = nz // LANES
    count = lax.axis_size("gx")
    over_chips = [(i, (i - 1 + 2 * (i % 2)) % count) for i in range(count)]
    over_cores = [(i, i ^ 1) for i in range(count)]
    cell = ny * nz

    def neighbours(to_chip, to_core):
        of_core = lax.ppermute(to_core, "gx", over_cores)
        return lax.ppermute(to_chip, "gx", over_chips), of_core

    def lies(*lead):
        return (*lead, blocks, ny, LANES)

    def lies_padded(*lead):
        return (*lead, blocks, ny + 2 * PAD, LANES)

    if n == 4:
        near = (initial, initial)
    else:
        near = [lax.dynamic_slice_in_dim(initial, at, 4, 1) for at in (either(0, n - 4), either(n - 4, 0))]
    of_chip, of_core = neighbours(*near)
    conc, mob, to_chip, to_core = call(
        own_kernel, (lies_padded(runs, n), lies_padded(n), lies(3), lies(3)), (), (initial, mobility),
        runs * n * cell,
    )
    m_chip, m_core = neighbours(to_chip, to_core)
    conc_core, chem0_a, *faces_a = call(
        core_kernel,
        (
            lies_padded(runs, 4), lies_padded(runs, n + 2),
            lies(n + 2), lies_padded(n + 2), lies(n + 2), lies(n + 2), lies(n + 1),
        ),
        (lies_padded(3),),
        (of_core, m_core, conc, mob),
        20 * runs * (n + 2) * cell,
    )
    conc_chip, chem0_b, state1_a, chem1_a, adjoint2_a, squares = call(
        chip_kernel,
        (
            lies_padded(runs, 4), lies_padded(runs, 4), lies_padded(runs, n + 1),
            lies_padded(runs, n - 1), lies_padded(runs, n - 3), (CHUNK, LANES),
        ),
        (),
        (of_chip, conc, conc_core, chem0_a, observed, *faces_a),
        60 * runs * (n - 1) * cell,
    )
    *faces_b, state1_b, chem1_b, adjoint2_b, to_core, to_chip, share = call(
        forward_kernel,
        (
            lies(3), lies_padded(2), lies(2), lies(2), lies(3),
            lies_padded(runs, 3), lies_padded(runs, 3), lies_padded(runs, 3),
            (runs, 3, blocks, ny + ROWS, LANES), lies(runs, 3), (ROWS, LANES),
        ),
        (lies_padded(3), (CHUNK, LANES)),
        (m_chip, mob, conc, conc_chip, chem0_a, chem0_b, state1_a, chem1_a, adjoint2_a, squares, observed, *faces_a),
        60 * runs * 3 * cell,
    )
    faces = (*faces_a, *faces_b)
    of_chip, of_core = neighbours(to_chip, to_core)
    bits = range(count.bit_length() - 2)

    groups = lax.axis_size("group")

    def target(group, at, apart):
        if counts(at):
            return group * count + (at ^ apart)
        return min(group ^ 1, groups - 1) * count + at

    def hop(value, bit):
        apart = 3 if bit == 0 else 2 << bit
        pairs = [
            (group * count + at, target(group, at, apart)) for group in range(groups) for at in range(count)
        ]
        return lax.ppermute(value, ("group", "gx"), pairs)

    share = share + of_core[0, 0, 0, ny:]
    far = hop(share, bits[-1])
    flow_a, flow_part, adjoint1_a, weight_b, step_z_b, part, *sums_b, share = call(
        early_kernel,
        (
            lies_padded(runs, n + 1), lies_padded(runs, 1), lies_padded(runs, n - 1), lies(runs, 3), lies(runs, 2),
            lies(n - 2), lies(2), lies(2), lies(2), (ROWS, LANES),
        ),
        (lies_padded(runs, 3), lies(n), lies_padded(n), lies(n)),
        (of_core, *faces, chem0_a, chem0_b, state1_a, state1_b, chem1_a, chem1_b, adjoint2_a, adjoint2_b, share),
        60 * runs * n * cell,
    )
    for bit in bits[-2::-1]:
        share = share + far
        far = hop(share, bit)
    result, share = call(
        late_kernel,
        ((n, ny, nz), (ROWS, LANES)),
        (
            lies_padded(runs, 3), lies_padded(runs, 3), lies_padded(runs, 3),
            lies(3), lies_padded(2), lies(2),
        ),
        (
            of_chip, *faces, chem0_a, chem0_b, chem1_b, adjoint2_b, flow_a, flow_part, adjoint1_a,
            weight_b, step_z_b, part, *sums_b, share,
        ),
        60 * runs * 3 * cell,
    )
    share = share + far
    handed = lax.ppermute(share, "gx", over_cores)
    (misfit,) = call(misfit_kernel, ((1,),), (), (share, handed), 1, scalar=0)
    return (result, misfit)


def solution(mesh):
    placed = (
        P("group", "gx", None, None),
        P("group", "gx", None, None),
        P(("group", "gx"), None, None),
    )
    return jax.shard_map(
        on_device,
        mesh=mesh,
        in_specs=placed,
        out_specs=(P(("group", "gx"), None, None), P("group")),
        check_vma=False,
    )
```

```python
import functools
import math

import jax
import jax.numpy as jnp
from jax import lax
from jax.experimental import pallas as pl
from jax.experimental.pallas import tpu as pltpu
from jax.sharding import PartitionSpec as P

stiffness = 0.5
time_step = 0.005
VMEM = pl.BlockSpec(memory_space=pltpu.VMEM)
SMEM = pl.BlockSpec(memory_space=pltpu.SMEM)
LANES = 128
ROWS = 8
PAD = ROWS
CHUNK = 8


def chunks(ny):
    return range(0, ny, CHUNK)


def plain(ref, lead, row):
    return [
        ref[(*lead, pl.ds(row, CHUNK), pl.ds(at, LANES))] for at in range(0, ref.shape[-1], LANES)
    ]


def put_plain(ref, lead, row, value):
    for block, part in enumerate(value):
        ref[(*lead, pl.ds(row, CHUNK), pl.ds(block * LANES, LANES))] = part


def flat(ref, lead, row):
    return [ref[(*lead, block, pl.ds(row, CHUNK))] for block in range(ref.shape[-3])]


def put_flat(ref, lead, row, value):
    for block, part in enumerate(value):
        ref[(*lead, block, pl.ds(row, CHUNK))] = part


def padded(ref, lead, row, shift=0):
    return [ref[(*lead, block, pl.ds(PAD + row + shift, CHUNK))] for block in range(ref.shape[-3])]


def put_padded(ref, lead, row, value):
    ny = ref.shape[-2] - 2 * PAD
    for block, part in enumerate(value):
        ref[(*lead, block, pl.ds(PAD + row, CHUNK))] = part
        if row == 0:
            ref[(*lead, block, pl.ds(PAD + ny, 1))] = part[:1]
        if row + CHUNK == ny:
            ref[(*lead, block, pl.ds(PAD - 1, 1))] = part[CHUNK - 1 :]


def lane():
    return lax.broadcasted_iota(jnp.int32, (CHUNK, LANES), 1)


def after_z(value):
    turned = [pltpu.roll(part, LANES - 1, 1) for part in value]
    turned.append(turned[0])
    edge = lane() == LANES - 1
    return [jnp.where(edge, turned[at + 1], turned[at]) for at in range(len(value))]


def before_z(value):
    turned = [pltpu.roll(part, 1, 1) for part in value]
    edge = lane() == 0
    return [jnp.where(edge, turned[at - 1], turned[at]) for at in range(len(value))]


def side():
    return lax.rem(lax.axis_index("gx"), 2)


def either(first, second):
    return first + side() * (second - first)


class Line:
    def __init__(self, *parts):
        self.parts = parts

    def __call__(self, at, *lead):
        for ref, first, last in self.parts:
            if first <= at <= last:
                return ref, (*lead, at - first)
        raise IndexError(at)


def each(function, *values):
    return [function(*parts) for parts in zip(*values)]


def beside(low, high, up, down, mid):
    return each(
        lambda a, b, c, d, e, f: (a + b) + (c + d) + (e + f),
        low, high, up, down, after_z(mid), before_z(mid),
    )


def potential(low, mid, high, up, down):
    return each(
        lambda c, total: c * (c * c + (6.0 * stiffness - 1.0)) - stiffness * total,
        mid, beside(low, high, up, down, mid),
    )


class Faces:
    def __init__(self, n, refs):
        mx_a, my_a, my_low_a, mz_a, mz_low_a, all_a, *late = refs
        two = lambda ref, first, last, at: ((ref, first, last), *(((late[at], last + 1, n + 1),) if late else ()))
        self.mx = Line(*two(mx_a, -3, n - 2, 0))
        self.my = Line(*two(my_a, -2, n - 1, 1))
        self.my_low = Line(*two(my_low_a, -2, n - 1, 2))
        self.mz = Line(*two(mz_a, -2, n - 1, 3))
        self.mz_low = Line(*two(mz_low_a, -2, n - 1, 4))
        self.all = Line(*two(all_a, -2, n - 2, 5))

    def flow(self, row, at, mid, up, down, low=None, high=None):
        total = each(
            lambda a, b, c, d, e, u, v, w, x, y: (a * u + b * v) + (c * w + d * x) - e * y,
            flat(*self.my(at), row), flat(*self.my_low(at), row), flat(*self.mz(at), row),
            flat(*self.mz_low(at), row), flat(*self.all(at), row), up, down, after_z(mid), before_z(mid), mid,
        )
        if low is not None:
            total = add_product(total, flat(*self.mx(at - 1), row), low)
        if high is not None:
            total = add_product(total, flat(*self.mx(at), row), high)
        return total


def add_product(total, a, b):
    return each(lambda t, x, y: t + x * y, total, a, b)


def sub(a, b):
    return each(lambda x, y: x - y, a, b)


def own_kernel(initial, mobility, conc, mob, to_chip, to_core):
    runs, n, ny, _ = initial.shape
    place = [either(n - 1 - at, at) for at in range(n)]

    def one_run(run, carry):
        for row in chunks(ny):
            for at in range(n):
                put_padded(conc, (run, at), row, plain(initial, (run, place[at]), row))
        return carry

    lax.fori_loop(0, runs, one_run, 0)
    for row in chunks(ny):
        for at in range(n):
            value = plain(mobility, (place[at],), row)
            put_padded(mob, (at,), row, value)
            if at < 3:
                put_flat(to_core, (at,), row, value)
            if at >= n - 3:
                put_flat(to_chip, (n - 1 - at,), row, value)


def mean(a, b):
    return 0.5 * (a + b)


def put_faces(row, mob, places, faces):
    for at in places:
        mid = padded(*mob(at), row)
        put_flat(*faces.my(at), row, each(mean, mid, padded(*mob(at), row, 1)))
        put_flat(*faces.my_low(at), row, each(mean, mid, padded(*mob(at), row, -1)))
        put_flat(*faces.mz(at), row, each(mean, mid, after_z(mid)))
        put_flat(*faces.mz_low(at), row, each(mean, mid, before_z(mid)))


def put_all(row, faces, places):
    for at in places:
        put_flat(*faces.all(at), row, each(
            lambda a, b, c, d, e, f: (a + b) + (c + d) + (e + f),
            flat(*faces.mx(at - 1), row), flat(*faces.mx(at), row), flat(*faces.my(at), row),
            flat(*faces.my_low(at), row), flat(*faces.mz(at), row), flat(*faces.mz_low(at), row),
        ))


def put_potential(row, field, run, places, target):
    mids = {at: padded(*field(at, run), row) for at in range(places[0] - 1, places[-1] + 2)}
    for at in places:
        value = potential(
            mids[at - 1], mids[at], mids[at + 1],
            padded(*field(at, run), row, 1), padded(*field(at, run), row, -1),
        )
        put_padded(*target(at, run), row, value)


def put_step(row, faces, chem, state, run, places, target):
    mids = {at: padded(*chem(at, run), row) for at in range(places[0] - 1, places[-1] + 2)}
    for at in places:
        flow = faces.flow(
            row, at, mids[at], padded(*chem(at, run), row, 1), padded(*chem(at, run), row, -1),
            mids[at - 1], mids[at + 1],
        )
        value = each(lambda a, b: a + time_step * b, padded(*state(at, run), row), flow)
        target(at, value)


def put_miss(row, runs, observed, place, run, at, value, adjoint2):
    miss = sub(value, plain(observed, (run, place[at]), row))
    adjoint = each(lambda a: a * (1.0 / runs), miss)
    put_padded(*adjoint2(at, run), row, adjoint)
    return adjoint, sum(part * part for part in miss)


def core_kernel(of_core, m_core, conc_own, mob_own, conc_core, chem0, mx, my, my_low, mz, mz_low, m_all, rim):
    runs, n = conc_own.shape[:2]
    ny = of_core.shape[2]
    mob = Line((rim, -3, -1), (mob_own, 0, n - 1))
    faces = Faces(n, (mx, my, my_low, mz, mz_low, m_all))
    for row in chunks(ny):
        for at in range(3):
            put_padded(rim, (2 - at,), row, flat(m_core, (at,), row))
    for row in chunks(ny):
        mids = [padded(*mob(at), row) for at in range(-3, n)]
        for at in range(n + 2):
            put_flat(mx, (at,), row, each(mean, mids[at], mids[at + 1]))
        put_faces(row, mob, range(-2, n), faces)
    for row in chunks(ny):
        put_all(row, faces, range(-2, n - 1))
    place = [either(at, 3 - at) for at in range(4)]
    conc = Line((conc_core, -4, -1), (conc_own, 0, n - 1))

    def one_run(run, carry):
        for row in chunks(ny):
            for at in range(4):
                put_padded(conc_core, (run, 3 - at), row, plain(of_core, (run, place[at]), row))
        for row in chunks(ny):
            put_potential(row, conc, run, range(-3, n - 1), Line((chem0, -3, n - 2)))
        return carry

    lax.fori_loop(0, runs, one_run, 0)


def chip_kernel(
    of_chip, conc_own, conc_core, chem0_a, observed, mx, my, my_low, mz, mz_low, m_all,
    conc_chip, chem0_b, state1_a, chem1_a, adjoint2_a, squares,
):
    runs, n = conc_own.shape[:2]
    ny = observed.shape[2]
    faces = Faces(n, (mx, my, my_low, mz, mz_low, m_all))
    message = [either(3 - at, at) for at in range(4)]
    place = [either(n - 1 - at, at) for at in range(n)]
    conc = Line((conc_core, -4, -1), (conc_own, 0, n - 1), (conc_chip, n, n + 3))
    chem0 = Line((chem0_a, -3, n - 2), (chem0_b, n - 1, n + 2))
    state1 = Line((state1_a, -2, n - 2))
    chem1 = Line((chem1_a, -1, n - 3))
    adjoint2 = Line((adjoint2_a, 0, n - 4))
    squares[...] = jnp.zeros_like(squares)

    def one_run(run, carry):
        for row in chunks(ny):
            for at in range(4):
                put_padded(conc_chip, (run, at), row, plain(of_chip, (run, message[at]), row))
        for row in chunks(ny):
            put_potential(row, conc, run, range(n - 1, n + 3), chem0)
        for row in chunks(ny):
            put_step(
                row, faces, chem0, conc, run, range(-2, n - 1),
                lambda at, value: put_padded(*state1(at, run), row, value),
            )
        for row in chunks(ny):
            put_potential(row, state1, run, range(-1, n - 2), chem1)
        for row in chunks(ny):

            def target(at, value):
                squares[...] += put_miss(row, runs, observed, place, run, at, value, adjoint2)[1]

            put_step(row, faces, chem1, state1, run, range(0, n - 3), target)
        return carry

    lax.fori_loop(0, runs, one_run, 0)


def forward_kernel(
    m_chip, mob_own, conc_own, conc_chip, chem0_a, chem0_b, state1_a, chem1_a, adjoint2_a, squares, observed,
    mx_a, my_a, my_low_a, mz_a, mz_low_a, all_a,
    mx_b, my_b, my_low_b, mz_b, mz_low_b, all_b, state1_b, chem1_b, adjoint2_b, to_core, to_chip, share, rim, total,
):
    runs, n = conc_own.shape[:2]
    ny = observed.shape[2]
    faces = Faces(n, (mx_a, my_a, my_low_a, mz_a, mz_low_a, all_a, mx_b, my_b, my_low_b, mz_b, mz_low_b, all_b))
    mob = Line((mob_own, 0, n - 1), (rim, n, n + 2))
    place = [either(n - 1 - at, at) for at in range(n)]
    conc = Line((conc_own, 0, n - 1), (conc_chip, n, n + 3))
    chem0 = Line((chem0_a, -3, n - 2), (chem0_b, n - 1, n + 2))
    state1 = Line((state1_a, -2, n - 2), (state1_b, n - 1, n + 1))
    chem1 = Line((chem1_a, -1, n - 3), (chem1_b, n - 2, n))
    adjoint2 = Line((adjoint2_a, 0, n - 4), (adjoint2_b, n - 3, n - 1))
    for row in chunks(ny):
        for at in range(3):
            put_padded(rim, (at,), row, flat(m_chip, (at,), row))
    for row in chunks(ny):
        mids = [padded(*mob(at), row) for at in range(n - 1, n + 3)]
        for at in range(3):
            put_flat(mx_b, (at,), row, each(mean, mids[at], mids[at + 1]))
        put_faces(row, mob, range(n, n + 2), faces)
    for row in chunks(ny):
        put_all(row, faces, range(n - 1, n + 2))
    total[...] = squares[...]

    def one_run(run, carry):
        for row in chunks(ny):
            put_step(
                row, faces, chem0, conc, run, range(n - 1, n + 2),
                lambda at, value: put_padded(*state1(at, run), row, value),
            )
        for row in chunks(ny):
            put_potential(row, state1, run, range(n - 2, n + 1), chem1)
        for row in chunks(ny):

            def target(at, value):
                adjoint, square = put_miss(row, runs, observed, place, run, at, value, adjoint2)
                total[...] += square
                put_flat(to_chip, (run, n - 1 - at), row, adjoint)
                if at < 3:
                    put_flat(to_core, (run, at), row, adjoint)

            put_step(row, faces, chem1, state1, run, range(n - 3, n), target)
            for at in range(min(3, n - 3)):
                put_flat(to_core, (run, at), row, padded(*adjoint2(at, run), row))
        return carry

    lax.fori_loop(0, runs, one_run, 0)
    columns = (0.5 / runs) * jnp.sum(total[...], axis=0, keepdims=True)
    mine = jnp.broadcast_to(jnp.sum(columns, axis=1, keepdims=True), share.shape)
    share[...] = mine
    to_core[0, 0, 0, ny:] = mine


def put_adjoint1(row, flow, adjoint2, run, places, weight, target):
    mids = {at: padded(*flow(at, run), row) for at in range(places[0] - 1, places[-1] + 2)}
    for at in places:
        total = beside(
            mids[at - 1], mids[at + 1], padded(*flow(at, run), row, 1), padded(*flow(at, run), row, -1), mids[at]
        )
        value = each(
            lambda a, w, f, t: a + w * f - (time_step * stiffness) * t,
            padded(*adjoint2(at, run), row), weight(at), mids[at], total,
        )
        put_padded(*target(at, run), row, value)


def slope(state):
    return each(lambda c: time_step * (3.0 * c * c + (6.0 * stiffness - 1.0)), state)


def step_x(field, run, at, row):
    return sub(padded(*field(at + 1, run), row), padded(*field(at, run), row))


def step_y(field, run, at, row):
    return sub(padded(*field(at, run), row, 1), padded(*field(at, run), row))


def step_z(field, run, at, row):
    mid = padded(*field(at, run), row)
    return sub(after_z(mid), mid)


def early_kernel(
    of_core, mx_a, my_a, my_low_a, mz_a, mz_low_a, all_a, mx_b, my_b, my_low_b, mz_b, mz_low_b, all_b,
    chem0_a, chem0_b, state1_a, state1_b, chem1_a, chem1_b, adjoint2_a, adjoint2_b,
    share_in, flow_a, flow_part, adjoint1_a, weight_b, step_z_b, part, sum_x_b, sum_y_b, sum_z_b, share,
    rim, sum_x, sum_y, sum_z,
):
    share[...] = share_in[...]
    runs = of_core.shape[0]
    n = part.shape[0] + 2
    ny = part.shape[-2]
    faces = Faces(n, (mx_a, my_a, my_low_a, mz_a, mz_low_a, all_a, mx_b, my_b, my_low_b, mz_b, mz_low_b, all_b))
    chem0 = Line((chem0_a, -3, n - 2), (chem0_b, n - 1, n + 2))
    state1 = Line((state1_a, -2, n - 2), (state1_b, n - 1, n + 1))
    chem1 = Line((chem1_a, -1, n - 3), (chem1_b, n - 2, n))
    adjoint2 = Line((rim, -3, -1), (adjoint2_a, 0, n - 4), (adjoint2_b, n - 3, n - 1))
    flow = Line((flow_a, -2, n - 2), (flow_part, n - 1, n - 1))
    adjoint1 = Line((adjoint1_a, -1, n - 3))
    for sums in (sum_x, sum_y, sum_z):
        sums[...] = jnp.zeros_like(sums)

    def one_run(run, carry):
        for row in chunks(ny):
            for at in range(3):
                put_padded(rim, (run, 2 - at), row, flat(of_core, (run, at), row))
        for row in chunks(ny):
            mids = {at: padded(*adjoint2(at, run), row) for at in range(-3, n)}
            for at in range(-2, n):
                value = faces.flow(
                    row, at, mids[at], padded(*adjoint2(at, run), row, 1), padded(*adjoint2(at, run), row, -1),
                    mids[at - 1], mids.get(at + 1),
                )
                put_padded(*flow(at, run), row, value)
        for row in chunks(ny):
            put_adjoint1(
                row, flow, adjoint2, run, range(-1, n - 2),
                lambda at: slope(padded(*state1(at, run), row)), adjoint1,
            )
            for at in range(n - 2, n + 1):
                put_flat(weight_b, (run, at - (n - 2)), row, slope(padded(*state1(at, run), row)))
        for row in chunks(ny):
            for at in range(-1, n - 1):
                total = add_product(
                    flat(sum_x, (at + 1,), row), step_x(adjoint2, run, at, row), step_x(chem1, run, at, row)
                )
                if at < n - 3:
                    total = add_product(total, step_x(adjoint1, run, at, row), step_x(chem0, run, at, row))
                put_flat(sum_x, (at + 1,), row, total)
            for at in range(n):
                total_y = add_product(
                    padded(sum_y, (at,), row), step_y(adjoint2, run, at, row), step_y(chem1, run, at, row)
                )
                total_z = add_product(
                    flat(sum_z, (at,), row), step_z(adjoint2, run, at, row), step_z(chem1, run, at, row)
                )
                slant = step_z(chem0, run, at, row)
                if at < n - 2:
                    total_y = add_product(total_y, step_y(adjoint1, run, at, row), step_y(chem0, run, at, row))
                    total_z = add_product(total_z, step_z(adjoint1, run, at, row), slant)
                else:
                    put_flat(step_z_b, (run, at - (n - 2)), row, slant)
                put_padded(sum_y, (at,), row, total_y)
                put_flat(sum_z, (at,), row, total_z)
        return carry

    lax.fori_loop(0, runs, one_run, 0)
    for row in chunks(ny):
        for at in range(n - 2):
            sides = flat(sum_z, (at,), row)
            value = each(
                lambda a, b, c, d, e: -0.5 * ((a + b) + (c + d) + e),
                padded(sum_y, (at,), row), padded(sum_y, (at,), row, -1), sides, before_z(sides),
                flat(sum_x, (at,), row),
            )
            if at < n - 3:
                value = each(lambda a, b: a - 0.5 * b, value, flat(sum_x, (at + 1,), row))
            put_flat(part, (at,), row, value)
        for at in range(2):
            put_flat(sum_x_b, (at,), row, flat(sum_x, (n - 2 + at,), row))
            put_flat(sum_y_b, (at,), row, padded(sum_y, (n - 2 + at,), row))
            put_flat(sum_z_b, (at,), row, flat(sum_z, (n - 2 + at,), row))


def late_kernel(
    of_chip, mx_a, my_a, my_low_a, mz_a, mz_low_a, all_a, mx_b, my_b, my_low_b, mz_b, mz_low_b, all_b,
    chem0_a, chem0_b, chem1_b, adjoint2_b, flow_a, flow_part, adjoint1_a, weight_b, step_z_b,
    part, sum_x_b, sum_y_b, sum_z_b, share_in, result, share, rim, flow_b, adjoint1_b, sum_x, sum_y, sum_z,
):
    share[...] = share_in[...]
    runs = of_chip.shape[0]
    n, ny, _ = result.shape
    faces = Faces(n, (mx_a, my_a, my_low_a, mz_a, mz_low_a, all_a, mx_b, my_b, my_low_b, mz_b, mz_low_b, all_b))
    place = [either(n - 1 - at, at) for at in range(n)]
    chem0 = Line((chem0_a, -3, n - 2), (chem0_b, n - 1, n + 2))
    chem1 = Line((chem1_b, n - 2, n))
    adjoint2 = Line((adjoint2_b, n - 3, n - 1), (rim, n, n + 2))
    flow = Line((flow_a, -2, n - 2), (flow_b, n - 1, n + 1))
    adjoint1 = Line((adjoint1_a, -1, n - 3), (adjoint1_b, n - 2, n))
    for row in chunks(ny):
        for at in range(2):
            put_flat(sum_x, (at,), row, flat(sum_x_b, (at,), row))
            put_padded(sum_y, (at,), row, flat(sum_y_b, (at,), row))
            put_flat(sum_z, (at,), row, flat(sum_z_b, (at,), row))
    sum_x[2] = jnp.zeros_like(sum_x[2])

    def one_run(run, carry):
        for row in chunks(ny):
            for at in range(3):
                put_padded(rim, (run, at), row, flat(of_chip, (run, at), row))
        for row in chunks(ny):
            mids = {at: padded(*adjoint2(at, run), row) for at in range(n - 1, n + 3)}
            value = add_product(padded(flow_part, (run, 0), row), flat(*faces.mx(n - 1), row), mids[n])
            put_padded(*flow(n - 1, run), row, value)
            for at in range(n, n + 2):
                value = faces.flow(
                    row, at, mids[at], padded(*adjoint2(at, run), row, 1), padded(*adjoint2(at, run), row, -1),
                    mids[at - 1], mids[at + 1],
                )
                put_padded(*flow(at, run), row, value)
        for row in chunks(ny):
            put_adjoint1(
                row, flow, adjoint2, run, range(n - 2, n + 1),
                lambda at: flat(weight_b, (run, at - (n - 2)), row), adjoint1,
            )
        for row in chunks(ny):
            for at in range(n - 3, n):
                total = add_product(
                    flat(sum_x, (at - (n - 3),), row), step_x(adjoint1, run, at, row), step_x(chem0, run, at, row)
                )
                if at == n - 1:
                    total = add_product(total, step_x(adjoint2, run, at, row), step_x(chem1, run, at, row))
                put_flat(sum_x, (at - (n - 3),), row, total)
            for at in range(n - 2, n):
                to = (at - (n - 2),)
                put_padded(sum_y, to, row, add_product(
                    padded(sum_y, to, row), step_y(adjoint1, run, at, row), step_y(chem0, run, at, row)
                ))
                put_flat(sum_z, to, row, add_product(
                    flat(sum_z, to, row), step_z(adjoint1, run, at, row), flat(step_z_b, (run, *to), row)
                ))
        return carry

    lax.fori_loop(0, runs, one_run, 0)
    for row in chunks(ny):
        for at in range(n - 2):
            value = flat(part, (at,), row)
            if at == n - 3:
                value = each(lambda a, b: a - 0.5 * b, value, flat(sum_x, (0,), row))
            put_plain(result, (place[at],), row, value)
        for at in range(2):
            sides = flat(sum_z, (at,), row)
            value = each(
                lambda a, b, c, d, e, f: -0.5 * ((a + b) + (c + d) + (e + f)),
                flat(sum_x, (at,), row), flat(sum_x, (at + 1,), row),
                padded(sum_y, (at,), row), padded(sum_y, (at,), row, -1), sides, before_z(sides),
            )
            put_plain(result, (place[n - 2 + at],), row, value)


def counts(at):
    return (at ^ (at >> 1)) & 1


def misfit_kernel(total, handed, misfit):
    misfit[0] = jnp.where(counts(lax.axis_index("gx")) == 1, total[0, 0], handed[0, 0])


def call(kernel, outs, scratch, args, flops, scalar=None):
    moved = 4 * (sum(a.size for a in args) + sum(math.prod(o) for o in outs))
    return pl.pallas_call(
        kernel,
        out_shape=tuple(jax.ShapeDtypeStruct(o, jnp.float32) for o in outs),
        in_specs=[VMEM] * len(args),
        out_specs=tuple(SMEM if at == scalar else VMEM for at in range(len(outs))),
        scratch_shapes=[pltpu.VMEM(s, jnp.float32) for s in scratch],
        compiler_params=pltpu.CompilerParams(vmem_limit_bytes=16 * 1024 * 1024),
        cost_estimate=pl.CostEstimate(flops=flops, bytes_accessed=moved, transcendentals=0),
    )(*args)


def on_device(initial, observed, mobility):
    runs, n, ny, nz = initial.shape
    blocks = nz // LANES
    count = lax.axis_size("gx")
    over_chips = [(i, (i - 1 + 2 * (i % 2)) % count) for i in range(count)]
    over_cores = [(i, i ^ 1) for i in range(count)]
    cell = ny * nz

    def neighbours(to_chip, to_core):
        of_core = lax.ppermute(to_core, "gx", over_cores)
        return lax.ppermute(to_chip, "gx", over_chips), of_core

    def lies(*lead):
        return (*lead, blocks, ny, LANES)

    def lies_padded(*lead):
        return (*lead, blocks, ny + 2 * PAD, LANES)

    if n == 4:
        near = (initial, initial)
    else:
        near = [lax.dynamic_slice_in_dim(initial, at, 4, 1) for at in (either(0, n - 4), either(n - 4, 0))]
    of_chip, of_core = neighbours(*near)
    conc, mob, to_chip, to_core = call(
        own_kernel, (lies_padded(runs, n), lies_padded(n), lies(3), lies(3)), (), (initial, mobility),
        runs * n * cell,
    )
    m_chip, m_core = neighbours(to_chip, to_core)
    conc_core, chem0_a, *faces_a = call(
        core_kernel,
        (
            lies_padded(runs, 4), lies_padded(runs, n + 2),
            lies(n + 2), lies(n + 2), lies(n + 2), lies(n + 2), lies(n + 2), lies(n + 1),
        ),
        (lies_padded(3),),
        (of_core, m_core, conc, mob),
        20 * runs * (n + 2) * cell,
    )
    conc_chip, chem0_b, state1_a, chem1_a, adjoint2_a, squares = call(
        chip_kernel,
        (
            lies_padded(runs, 4), lies_padded(runs, 4), lies_padded(runs, n + 1),
            lies_padded(runs, n - 1), lies_padded(runs, n - 3), (CHUNK, LANES),
        ),
        (),
        (of_chip, conc, conc_core, chem0_a, observed, *faces_a),
        60 * runs * (n - 1) * cell,
    )
    *faces_b, state1_b, chem1_b, adjoint2_b, to_core, to_chip, share = call(
        forward_kernel,
        (
            lies(3), lies(2), lies(2), lies(2), lies(2), lies(3),
            lies_padded(runs, 3), lies_padded(runs, 3), lies_padded(runs, 3),
            (runs, 3, blocks, ny + ROWS, LANES), lies(runs, 3), (ROWS, LANES),
        ),
        (lies_padded(3), (CHUNK, LANES)),
        (m_chip, mob, conc, conc_chip, chem0_a, chem0_b, state1_a, chem1_a, adjoint2_a, squares, observed, *faces_a),
        60 * runs * 3 * cell,
    )
    faces = (*faces_a, *faces_b)
    of_chip, of_core = neighbours(to_chip, to_core)
    groups = lax.axis_size("group")

    def target(group, at, apart):
        if counts(at):
            return group * count + (at ^ apart)
        return min(group ^ 1, groups - 1) * count + at

    def hop(value, apart):
        pairs = [
            (group * count + at, target(group, at, apart)) for group in range(groups) for at in range(count)
        ]
        return lax.ppermute(value, ("group", "gx"), pairs)

    def hops(value, bits):
        aparts = [sum(2 << bit for at, bit in enumerate(bits) if which >> at & 1) for which in range(1, 1 << len(bits))]
        return [hop(value, apart) for apart in aparts]

    share = share + of_core[0, 0, 0, ny:]
    upper = range(count.bit_length() - 3, 0, -1)
    steps = [upper[at : at + 2] for at in range(0, len(upper), 2)]
    fars = hops(share, steps[0])
    flow_a, flow_part, adjoint1_a, weight_b, step_z_b, part, *sums_b, share = call(
        early_kernel,
        (
            lies_padded(runs, n + 1), lies_padded(runs, 1), lies_padded(runs, n - 1), lies(runs, 3), lies(runs, 2),
            lies(n - 2), lies(2), lies(2), lies(2), (ROWS, LANES),
        ),
        (lies_padded(runs, 3), lies(n), lies_padded(n), lies(n)),
        (of_core, *faces, chem0_a, chem0_b, state1_a, state1_b, chem1_a, chem1_b, adjoint2_a, adjoint2_b, share),
        60 * runs * n * cell,
    )
    for bits in steps[1:]:
        share = share + sum(fars)
        fars = hops(share, bits)
    share = share + sum(fars)
    far = hop(share, 3)
    result, share = call(
        late_kernel,
        ((n, ny, nz), (ROWS, LANES)),
        (
            lies_padded(runs, 3), lies_padded(runs, 3), lies_padded(runs, 3),
            lies(3), lies_padded(2), lies(2),
        ),
        (
            of_chip, *faces, chem0_a, chem0_b, chem1_b, adjoint2_b, flow_a, flow_part, adjoint1_a,
            weight_b, step_z_b, part, *sums_b, share,
        ),
        60 * runs * 3 * cell,
    )
    share = share + far
    handed = lax.ppermute(share, "gx", over_cores)
    (misfit,) = call(misfit_kernel, ((1,),), (), (share, handed), 1, scalar=0)
    return (result, misfit)


def solution(mesh):
    placed = (
        P("group", "gx", None, None),
        P("group", "gx", None, None),
        P(("group", "gx"), None, None),
    )
    return jax.shard_map(
        on_device,
        mesh=mesh,
        in_specs=placed,
        out_specs=(P(("group", "gx"), None, None), P("group")),
        check_vma=False,
    )
```

```python
import functools
import math

import jax
import jax.numpy as jnp
from jax import lax
from jax.experimental import pallas as pl
from jax.experimental.pallas import tpu as pltpu
from jax.sharding import PartitionSpec as P

stiffness = 0.5
time_step = 0.005
VMEM = pl.BlockSpec(memory_space=pltpu.VMEM)
SMEM = pl.BlockSpec(memory_space=pltpu.SMEM)
LANES = 128
ROWS = 8
PAD = ROWS
CHUNK = 8


def chunks(ny):
    return range(0, ny, CHUNK)


def plain(ref, lead, row):
    return [
        ref[(*lead, pl.ds(row, CHUNK), pl.ds(at, LANES))] for at in range(0, ref.shape[-1], LANES)
    ]


def put_plain(ref, lead, row, value):
    for block, part in enumerate(value):
        ref[(*lead, pl.ds(row, CHUNK), pl.ds(block * LANES, LANES))] = part


def flat(ref, lead, row):
    return [ref[(*lead, block, pl.ds(row, CHUNK))] for block in range(ref.shape[-3])]


def put_flat(ref, lead, row, value):
    for block, part in enumerate(value):
        ref[(*lead, block, pl.ds(row, CHUNK))] = part


def padded(ref, lead, row, shift=0):
    return [ref[(*lead, block, pl.ds(PAD + row + shift, CHUNK))] for block in range(ref.shape[-3])]


def put_padded(ref, lead, row, value):
    ny = ref.shape[-2] - 2 * PAD
    for block, part in enumerate(value):
        ref[(*lead, block, pl.ds(PAD + row, CHUNK))] = part
        if row == 0:
            ref[(*lead, block, pl.ds(PAD + ny, 1))] = part[:1]
        if row + CHUNK == ny:
            ref[(*lead, block, pl.ds(PAD - 1, 1))] = part[CHUNK - 1 :]


def lane():
    return lax.broadcasted_iota(jnp.int32, (CHUNK, LANES), 1)


def after_z(value):
    turned = [pltpu.roll(part, LANES - 1, 1) for part in value]
    turned.append(turned[0])
    edge = lane() == LANES - 1
    return [jnp.where(edge, turned[at + 1], turned[at]) for at in range(len(value))]


def before_z(value):
    turned = [pltpu.roll(part, 1, 1) for part in value]
    edge = lane() == 0
    return [jnp.where(edge, turned[at - 1], turned[at]) for at in range(len(value))]


def side():
    return lax.rem(lax.axis_index("gx"), 2)


def either(first, second):
    return first + side() * (second - first)


class Line:
    def __init__(self, *parts):
        self.parts = parts

    def __call__(self, at, *lead):
        for ref, first, last in self.parts:
            if first <= at <= last:
                return ref, (*lead, at - first)
        raise IndexError(at)


def each(function, *values):
    return [function(*parts) for parts in zip(*values)]


def beside(low, high, up, down, mid):
    return each(
        lambda a, b, c, d, e, f: (a + b) + (c + d) + (e + f),
        low, high, up, down, after_z(mid), before_z(mid),
    )


def potential(low, mid, high, up, down):
    return each(
        lambda c, total: c * (c * c + (6.0 * stiffness - 1.0)) - stiffness * total,
        mid, beside(low, high, up, down, mid),
    )


class Faces:
    def __init__(self, n, refs):
        mx_a, my_a, my_low_a, mz_a, mz_low_a, all_a, *late = refs
        two = lambda ref, first, last, at: ((ref, first, last), *(((late[at], last + 1, n + 1),) if late else ()))
        self.mx = Line(*two(mx_a, -3, n - 2, 0))
        self.my = Line(*two(my_a, -2, n - 1, 1))
        self.my_low = Line(*two(my_low_a, -2, n - 1, 2))
        self.mz = Line(*two(mz_a, -2, n - 1, 3))
        self.mz_low = Line(*two(mz_low_a, -2, n - 1, 4))
        self.all = Line(*two(all_a, -2, n - 2, 5))

    def flow(self, row, at, mid, up, down, low=None, high=None):
        total = each(
            lambda a, b, c, d, e, u, v, w, x, y: (a * u + b * v) + (c * w + d * x) - e * y,
            flat(*self.my(at), row), flat(*self.my_low(at), row), flat(*self.mz(at), row),
            flat(*self.mz_low(at), row), flat(*self.all(at), row), up, down, after_z(mid), before_z(mid), mid,
        )
        if low is not None:
            total = add_product(total, flat(*self.mx(at - 1), row), low)
        if high is not None:
            total = add_product(total, flat(*self.mx(at), row), high)
        return total


def add_product(total, a, b):
    return each(lambda t, x, y: t + x * y, total, a, b)


def sub(a, b):
    return each(lambda x, y: x - y, a, b)


def own_kernel(initial, mobility, conc, mob, to_chip, to_core):
    runs, n, ny, _ = initial.shape
    place = [either(n - 1 - at, at) for at in range(n)]

    def one_run(run, carry):
        for row in chunks(ny):
            for at in range(n):
                put_padded(conc, (run, at), row, plain(initial, (run, place[at]), row))
        return carry

    for run in range(runs):
        one_run(run, 0)
    for row in chunks(ny):
        for at in range(n):
            value = plain(mobility, (place[at],), row)
            put_padded(mob, (at,), row, value)
            if at < 3:
                put_flat(to_core, (at,), row, value)
            if at >= n - 3:
                put_flat(to_chip, (n - 1 - at,), row, value)


def mean(a, b):
    return 0.5 * (a + b)


def put_faces(row, mob, places, faces):
    for at in places:
        mid = padded(*mob(at), row)
        put_flat(*faces.my(at), row, each(mean, mid, padded(*mob(at), row, 1)))
        put_flat(*faces.my_low(at), row, each(mean, mid, padded(*mob(at), row, -1)))
        put_flat(*faces.mz(at), row, each(mean, mid, after_z(mid)))
        put_flat(*faces.mz_low(at), row, each(mean, mid, before_z(mid)))


def put_all(row, faces, places):
    for at in places:
        put_flat(*faces.all(at), row, each(
            lambda a, b, c, d, e, f: (a + b) + (c + d) + (e + f),
            flat(*faces.mx(at - 1), row), flat(*faces.mx(at), row), flat(*faces.my(at), row),
            flat(*faces.my_low(at), row), flat(*faces.mz(at), row), flat(*faces.mz_low(at), row),
        ))


def put_potential(row, field, run, places, target):
    mids = {at: padded(*field(at, run), row) for at in range(places[0] - 1, places[-1] + 2)}
    for at in places:
        value = potential(
            mids[at - 1], mids[at], mids[at + 1],
            padded(*field(at, run), row, 1), padded(*field(at, run), row, -1),
        )
        put_padded(*target(at, run), row, value)


def put_step(row, faces, chem, state, run, places, target):
    mids = {at: padded(*chem(at, run), row) for at in range(places[0] - 1, places[-1] + 2)}
    for at in places:
        flow = faces.flow(
            row, at, mids[at], padded(*chem(at, run), row, 1), padded(*chem(at, run), row, -1),
            mids[at - 1], mids[at + 1],
        )
        value = each(lambda a, b: a + time_step * b, padded(*state(at, run), row), flow)
        target(at, value)


def put_miss(row, runs, observed, place, run, at, value, adjoint2):
    miss = sub(value, plain(observed, (run, place[at]), row))
    adjoint = each(lambda a: a * (1.0 / runs), miss)
    put_padded(*adjoint2(at, run), row, adjoint)
    return adjoint, sum(part * part for part in miss)


def core_kernel(of_core, m_core, conc_own, mob_own, conc_core, chem0, mx, my, my_low, mz, mz_low, m_all, rim):
    runs, n = conc_own.shape[:2]
    ny = of_core.shape[2]
    mob = Line((rim, -3, -1), (mob_own, 0, n - 1))
    faces = Faces(n, (mx, my, my_low, mz, mz_low, m_all))
    for row in chunks(ny):
        for at in range(3):
            put_padded(rim, (2 - at,), row, flat(m_core, (at,), row))
    for row in chunks(ny):
        mids = [padded(*mob(at), row) for at in range(-3, n)]
        for at in range(n + 2):
            put_flat(mx, (at,), row, each(mean, mids[at], mids[at + 1]))
        put_faces(row, mob, range(-2, n), faces)
    for row in chunks(ny):
        put_all(row, faces, range(-2, n - 1))
    place = [either(at, 3 - at) for at in range(4)]
    conc = Line((conc_core, -4, -1), (conc_own, 0, n - 1))

    def one_run(run, carry):
        for row in chunks(ny):
            for at in range(4):
                put_padded(conc_core, (run, 3 - at), row, plain(of_core, (run, place[at]), row))
        for row in chunks(ny):
            put_potential(row, conc, run, range(-3, n - 1), Line((chem0, -3, n - 2)))
        return carry

    for run in range(runs):
        one_run(run, 0)


def chip_kernel(
    of_chip, conc_own, conc_core, chem0_a, observed, mx, my, my_low, mz, mz_low, m_all,
    conc_chip, chem0_b, state1_a, chem1_a, adjoint2_a, squares,
):
    runs, n = conc_own.shape[:2]
    ny = observed.shape[2]
    faces = Faces(n, (mx, my, my_low, mz, mz_low, m_all))
    message = [either(3 - at, at) for at in range(4)]
    place = [either(n - 1 - at, at) for at in range(n)]
    conc = Line((conc_core, -4, -1), (conc_own, 0, n - 1), (conc_chip, n, n + 3))
    chem0 = Line((chem0_a, -3, n - 2), (chem0_b, n - 1, n + 2))
    state1 = Line((state1_a, -2, n - 2))
    chem1 = Line((chem1_a, -1, n - 3))
    adjoint2 = Line((adjoint2_a, 0, n - 4))
    squares[...] = jnp.zeros_like(squares)

    def one_run(run, carry):
        for row in chunks(ny):
            for at in range(4):
                put_padded(conc_chip, (run, at), row, plain(of_chip, (run, message[at]), row))
        for row in chunks(ny):
            put_potential(row, conc, run, range(n - 1, n + 3), chem0)
        for row in chunks(ny):
            put_step(
                row, faces, chem0, conc, run, range(-2, n - 1),
                lambda at, value: put_padded(*state1(at, run), row, value),
            )
        for row in chunks(ny):
            put_potential(row, state1, run, range(-1, n - 2), chem1)
        for row in chunks(ny):

            def target(at, value):
                squares[...] += put_miss(row, runs, observed, place, run, at, value, adjoint2)[1]

            put_step(row, faces, chem1, state1, run, range(0, n - 3), target)
        return carry

    for run in range(runs):
        one_run(run, 0)


def forward_kernel(
    m_chip, mob_own, conc_own, conc_chip, chem0_a, chem0_b, state1_a, chem1_a, adjoint2_a, squares, observed,
    mx_a, my_a, my_low_a, mz_a, mz_low_a, all_a,
    mx_b, my_b, my_low_b, mz_b, mz_low_b, all_b, state1_b, chem1_b, adjoint2_b, to_core, to_chip, share, rim, total,
):
    runs, n = conc_own.shape[:2]
    ny = observed.shape[2]
    faces = Faces(n, (mx_a, my_a, my_low_a, mz_a, mz_low_a, all_a, mx_b, my_b, my_low_b, mz_b, mz_low_b, all_b))
    mob = Line((mob_own, 0, n - 1), (rim, n, n + 2))
    place = [either(n - 1 - at, at) for at in range(n)]
    conc = Line((conc_own, 0, n - 1), (conc_chip, n, n + 3))
    chem0 = Line((chem0_a, -3, n - 2), (chem0_b, n - 1, n + 2))
    state1 = Line((state1_a, -2, n - 2), (state1_b, n - 1, n + 1))
    chem1 = Line((chem1_a, -1, n - 3), (chem1_b, n - 2, n))
    adjoint2 = Line((adjoint2_a, 0, n - 4), (adjoint2_b, n - 3, n - 1))
    for row in chunks(ny):
        for at in range(3):
            put_padded(rim, (at,), row, flat(m_chip, (at,), row))
    for row in chunks(ny):
        mids = [padded(*mob(at), row) for at in range(n - 1, n + 3)]
        for at in range(3):
            put_flat(mx_b, (at,), row, each(mean, mids[at], mids[at + 1]))
        put_faces(row, mob, range(n, n + 2), faces)
    for row in chunks(ny):
        put_all(row, faces, range(n - 1, n + 2))
    total[...] = squares[...]

    def one_run(run, carry):
        for row in chunks(ny):
            put_step(
                row, faces, chem0, conc, run, range(n - 1, n + 2),
                lambda at, value: put_padded(*state1(at, run), row, value),
            )
        for row in chunks(ny):
            put_potential(row, state1, run, range(n - 2, n + 1), chem1)
        for row in chunks(ny):

            def target(at, value):
                adjoint, square = put_miss(row, runs, observed, place, run, at, value, adjoint2)
                total[...] += square
                put_flat(to_chip, (run, n - 1 - at), row, adjoint)
                if at < 3:
                    put_flat(to_core, (run, at), row, adjoint)

            put_step(row, faces, chem1, state1, run, range(n - 3, n), target)
            for at in range(min(3, n - 3)):
                put_flat(to_core, (run, at), row, padded(*adjoint2(at, run), row))
        return carry

    for run in range(runs):
        one_run(run, 0)
    columns = (0.5 / runs) * jnp.sum(total[...], axis=0, keepdims=True)
    mine = jnp.broadcast_to(jnp.sum(columns, axis=1, keepdims=True), share.shape)
    share[...] = mine
    to_core[0, 0, 0, ny:] = mine


def put_adjoint1(row, flow, adjoint2, run, places, weight, target):
    mids = {at: padded(*flow(at, run), row) for at in range(places[0] - 1, places[-1] + 2)}
    for at in places:
        total = beside(
            mids[at - 1], mids[at + 1], padded(*flow(at, run), row, 1), padded(*flow(at, run), row, -1), mids[at]
        )
        value = each(
            lambda a, w, f, t: a + w * f - (time_step * stiffness) * t,
            padded(*adjoint2(at, run), row), weight(at), mids[at], total,
        )
        put_padded(*target(at, run), row, value)


def slope(state):
    return each(lambda c: time_step * (3.0 * c * c + (6.0 * stiffness - 1.0)), state)


def step_x(field, run, at, row):
    return sub(padded(*field(at + 1, run), row), padded(*field(at, run), row))


def step_y(field, run, at, row):
    return sub(padded(*field(at, run), row, 1), padded(*field(at, run), row))


def step_z(field, run, at, row):
    mid = padded(*field(at, run), row)
    return sub(after_z(mid), mid)


def early_kernel(
    of_core, mx_a, my_a, my_low_a, mz_a, mz_low_a, all_a, mx_b, my_b, my_low_b, mz_b, mz_low_b, all_b,
    chem0_a, chem0_b, state1_a, state1_b, chem1_a, chem1_b, adjoint2_a, adjoint2_b,
    share_in, flow_a, flow_part, adjoint1_a, weight_b, step_z_b, part, sum_x_b, sum_y_b, sum_z_b, share,
    rim, sum_x, sum_y, sum_z,
):
    share[...] = share_in[...]
    runs = of_core.shape[0]
    n = part.shape[0] + 2
    ny = part.shape[-2]
    faces = Faces(n, (mx_a, my_a, my_low_a, mz_a, mz_low_a, all_a, mx_b, my_b, my_low_b, mz_b, mz_low_b, all_b))
    chem0 = Line((chem0_a, -3, n - 2), (chem0_b, n - 1, n + 2))
    state1 = Line((state1_a, -2, n - 2), (state1_b, n - 1, n + 1))
    chem1 = Line((chem1_a, -1, n - 3), (chem1_b, n - 2, n))
    adjoint2 = Line((rim, -3, -1), (adjoint2_a, 0, n - 4), (adjoint2_b, n - 3, n - 1))
    flow = Line((flow_a, -2, n - 2), (flow_part, n - 1, n - 1))
    adjoint1 = Line((adjoint1_a, -1, n - 3))
    for sums in (sum_x, sum_y, sum_z):
        sums[...] = jnp.zeros_like(sums)

    def one_run(run, carry):
        for row in chunks(ny):
            for at in range(3):
                put_padded(rim, (run, 2 - at), row, flat(of_core, (run, at), row))
        for row in chunks(ny):
            mids = {at: padded(*adjoint2(at, run), row) for at in range(-3, n)}
            for at in range(-2, n):
                value = faces.flow(
                    row, at, mids[at], padded(*adjoint2(at, run), row, 1), padded(*adjoint2(at, run), row, -1),
                    mids[at - 1], mids.get(at + 1),
                )
                put_padded(*flow(at, run), row, value)
        for row in chunks(ny):
            put_adjoint1(
                row, flow, adjoint2, run, range(-1, n - 2),
                lambda at: slope(padded(*state1(at, run), row)), adjoint1,
            )
            for at in range(n - 2, n + 1):
                put_flat(weight_b, (run, at - (n - 2)), row, slope(padded(*state1(at, run), row)))
        for row in chunks(ny):
            for at in range(-1, n - 1):
                total = add_product(
                    flat(sum_x, (at + 1,), row), step_x(adjoint2, run, at, row), step_x(chem1, run, at, row)
                )
                if at < n - 3:
                    total = add_product(total, step_x(adjoint1, run, at, row), step_x(chem0, run, at, row))
                put_flat(sum_x, (at + 1,), row, total)
            for at in range(n):
                total_y = add_product(
                    padded(sum_y, (at,), row), step_y(adjoint2, run, at, row), step_y(chem1, run, at, row)
                )
                total_z = add_product(
                    flat(sum_z, (at,), row), step_z(adjoint2, run, at, row), step_z(chem1, run, at, row)
                )
                slant = step_z(chem0, run, at, row)
                if at < n - 2:
                    total_y = add_product(total_y, step_y(adjoint1, run, at, row), step_y(chem0, run, at, row))
                    total_z = add_product(total_z, step_z(adjoint1, run, at, row), slant)
                else:
                    put_flat(step_z_b, (run, at - (n - 2)), row, slant)
                put_padded(sum_y, (at,), row, total_y)
                put_flat(sum_z, (at,), row, total_z)
        return carry

    for run in range(runs):
        one_run(run, 0)
    for row in chunks(ny):
        for at in range(n - 2):
            sides = flat(sum_z, (at,), row)
            value = each(
                lambda a, b, c, d, e: -0.5 * ((a + b) + (c + d) + e),
                padded(sum_y, (at,), row), padded(sum_y, (at,), row, -1), sides, before_z(sides),
                flat(sum_x, (at,), row),
            )
            if at < n - 3:
                value = each(lambda a, b: a - 0.5 * b, value, flat(sum_x, (at + 1,), row))
            put_flat(part, (at,), row, value)
        for at in range(2):
            put_flat(sum_x_b, (at,), row, flat(sum_x, (n - 2 + at,), row))
            put_flat(sum_y_b, (at,), row, padded(sum_y, (n - 2 + at,), row))
            put_flat(sum_z_b, (at,), row, flat(sum_z, (n - 2 + at,), row))


def late_kernel(
    of_chip, mx_a, my_a, my_low_a, mz_a, mz_low_a, all_a, mx_b, my_b, my_low_b, mz_b, mz_low_b, all_b,
    chem0_a, chem0_b, chem1_b, adjoint2_b, flow_a, flow_part, adjoint1_a, weight_b, step_z_b,
    part, sum_x_b, sum_y_b, sum_z_b, share_in, result, share, rim, flow_b, adjoint1_b, sum_x, sum_y, sum_z,
):
    share[...] = share_in[...]
    runs = of_chip.shape[0]
    n, ny, _ = result.shape
    faces = Faces(n, (mx_a, my_a, my_low_a, mz_a, mz_low_a, all_a, mx_b, my_b, my_low_b, mz_b, mz_low_b, all_b))
    place = [either(n - 1 - at, at) for at in range(n)]
    chem0 = Line((chem0_a, -3, n - 2), (chem0_b, n - 1, n + 2))
    chem1 = Line((chem1_b, n - 2, n))
    adjoint2 = Line((adjoint2_b, n - 3, n - 1), (rim, n, n + 2))
    flow = Line((flow_a, -2, n - 2), (flow_b, n - 1, n + 1))
    adjoint1 = Line((adjoint1_a, -1, n - 3), (adjoint1_b, n - 2, n))
    for row in chunks(ny):
        for at in range(2):
            put_flat(sum_x, (at,), row, flat(sum_x_b, (at,), row))
            put_padded(sum_y, (at,), row, flat(sum_y_b, (at,), row))
            put_flat(sum_z, (at,), row, flat(sum_z_b, (at,), row))
    sum_x[2] = jnp.zeros_like(sum_x[2])

    def one_run(run, carry):
        for row in chunks(ny):
            for at in range(3):
                put_padded(rim, (run, at), row, flat(of_chip, (run, at), row))
        for row in chunks(ny):
            mids = {at: padded(*adjoint2(at, run), row) for at in range(n - 1, n + 3)}
            value = add_product(padded(flow_part, (run, 0), row), flat(*faces.mx(n - 1), row), mids[n])
            put_padded(*flow(n - 1, run), row, value)
            for at in range(n, n + 2):
                value = faces.flow(
                    row, at, mids[at], padded(*adjoint2(at, run), row, 1), padded(*adjoint2(at, run), row, -1),
                    mids[at - 1], mids[at + 1],
                )
                put_padded(*flow(at, run), row, value)
        for row in chunks(ny):
            put_adjoint1(
                row, flow, adjoint2, run, range(n - 2, n + 1),
                lambda at: flat(weight_b, (run, at - (n - 2)), row), adjoint1,
            )
        for row in chunks(ny):
            for at in range(n - 3, n):
                total = add_product(
                    flat(sum_x, (at - (n - 3),), row), step_x(adjoint1, run, at, row), step_x(chem0, run, at, row)
                )
                if at == n - 1:
                    total = add_product(total, step_x(adjoint2, run, at, row), step_x(chem1, run, at, row))
                put_flat(sum_x, (at - (n - 3),), row, total)
            for at in range(n - 2, n):
                to = (at - (n - 2),)
                put_padded(sum_y, to, row, add_product(
                    padded(sum_y, to, row), step_y(adjoint1, run, at, row), step_y(chem0, run, at, row)
                ))
                put_flat(sum_z, to, row, add_product(
                    flat(sum_z, to, row), step_z(adjoint1, run, at, row), flat(step_z_b, (run, *to), row)
                ))
        return carry

    for run in range(runs):
        one_run(run, 0)
    for row in chunks(ny):
        for at in range(n - 2):
            value = flat(part, (at,), row)
            if at == n - 3:
                value = each(lambda a, b: a - 0.5 * b, value, flat(sum_x, (0,), row))
            put_plain(result, (place[at],), row, value)
        for at in range(2):
            sides = flat(sum_z, (at,), row)
            value = each(
                lambda a, b, c, d, e, f: -0.5 * ((a + b) + (c + d) + (e + f)),
                flat(sum_x, (at,), row), flat(sum_x, (at + 1,), row),
                padded(sum_y, (at,), row), padded(sum_y, (at,), row, -1), sides, before_z(sides),
            )
            put_plain(result, (place[n - 2 + at],), row, value)


def counts(at):
    return (at ^ (at >> 1)) & 1


def misfit_kernel(total, handed, misfit):
    misfit[0] = jnp.where(counts(lax.axis_index("gx")) == 1, total[0, 0], handed[0, 0])


def call(kernel, outs, scratch, args, flops, scalar=None):
    moved = 4 * (sum(a.size for a in args) + sum(math.prod(o) for o in outs))
    return pl.pallas_call(
        kernel,
        out_shape=tuple(jax.ShapeDtypeStruct(o, jnp.float32) for o in outs),
        in_specs=[VMEM] * len(args),
        out_specs=tuple(SMEM if at == scalar else VMEM for at in range(len(outs))),
        scratch_shapes=[pltpu.VMEM(s, jnp.float32) for s in scratch],
        compiler_params=pltpu.CompilerParams(vmem_limit_bytes=16 * 1024 * 1024),
        cost_estimate=pl.CostEstimate(flops=flops, bytes_accessed=moved, transcendentals=0),
    )(*args)


def on_device(initial, observed, mobility):
    runs, n, ny, nz = initial.shape
    blocks = nz // LANES
    count = lax.axis_size("gx")
    over_chips = [(i, (i - 1 + 2 * (i % 2)) % count) for i in range(count)]
    over_cores = [(i, i ^ 1) for i in range(count)]
    cell = ny * nz

    def neighbours(to_chip, to_core):
        of_core = lax.ppermute(to_core, "gx", over_cores)
        return lax.ppermute(to_chip, "gx", over_chips), of_core

    def lies(*lead):
        return (*lead, blocks, ny, LANES)

    def lies_padded(*lead):
        return (*lead, blocks, ny + 2 * PAD, LANES)

    if n == 4:
        near = (initial, initial)
    else:
        near = [lax.dynamic_slice_in_dim(initial, at, 4, 1) for at in (either(0, n - 4), either(n - 4, 0))]
    of_chip, of_core = neighbours(*near)
    conc, mob, to_chip, to_core = call(
        own_kernel, (lies_padded(runs, n), lies_padded(n), lies(3), lies(3)), (), (initial, mobility),
        runs * n * cell,
    )
    m_chip, m_core = neighbours(to_chip, to_core)
    conc_core, chem0_a, *faces_a = call(
        core_kernel,
        (
            lies_padded(runs, 4), lies_padded(runs, n + 2),
            lies(n + 2), lies(n + 2), lies(n + 2), lies(n + 2), lies(n + 2), lies(n + 1),
        ),
        (lies_padded(3),),
        (of_core, m_core, conc, mob),
        20 * runs * (n + 2) * cell,
    )
    conc_chip, chem0_b, state1_a, chem1_a, adjoint2_a, squares = call(
        chip_kernel,
        (
            lies_padded(runs, 4), lies_padded(runs, 4), lies_padded(runs, n + 1),
            lies_padded(runs, n - 1), lies_padded(runs, n - 3), (CHUNK, LANES),
        ),
        (),
        (of_chip, conc, conc_core, chem0_a, observed, *faces_a),
        60 * runs * (n - 1) * cell,
    )
    *faces_b, state1_b, chem1_b, adjoint2_b, to_core, to_chip, share = call(
        forward_kernel,
        (
            lies(3), lies(2), lies(2), lies(2), lies(2), lies(3),
            lies_padded(runs, 3), lies_padded(runs, 3), lies_padded(runs, 3),
            (runs, 3, blocks, ny + ROWS, LANES), lies(runs, 3), (ROWS, LANES),
        ),
        (lies_padded(3), (CHUNK, LANES)),
        (m_chip, mob, conc, conc_chip, chem0_a, chem0_b, state1_a, chem1_a, adjoint2_a, squares, observed, *faces_a),
        60 * runs * 3 * cell,
    )
    faces = (*faces_a, *faces_b)
    of_chip, of_core = neighbours(to_chip, to_core)
    groups = lax.axis_size("group")

    def target(group, at, apart):
        if counts(at):
            return group * count + (at ^ apart)
        return min(group ^ 1, groups - 1) * count + at

    def hop(value, apart):
        pairs = [
            (group * count + at, target(group, at, apart)) for group in range(groups) for at in range(count)
        ]
        return lax.ppermute(value, ("group", "gx"), pairs)

    def hops(value, bits):
        aparts = [sum(2 << bit for at, bit in enumerate(bits) if which >> at & 1) for which in range(1, 1 << len(bits))]
        return [hop(value, apart) for apart in aparts]

    share = share + of_core[0, 0, 0, ny:]
    upper = range(count.bit_length() - 3, 0, -1)
    steps = [upper[at : at + 2] for at in range(0, len(upper), 2)]
    fars = hops(share, steps[0])
    flow_a, flow_part, adjoint1_a, weight_b, step_z_b, part, *sums_b, share = call(
        early_kernel,
        (
            lies_padded(runs, n + 1), lies_padded(runs, 1), lies_padded(runs, n - 1), lies(runs, 3), lies(runs, 2),
            lies(n - 2), lies(2), lies(2), lies(2), (ROWS, LANES),
        ),
        (lies_padded(runs, 3), lies(n), lies_padded(n), lies(n)),
        (of_core, *faces, chem0_a, chem0_b, state1_a, state1_b, chem1_a, chem1_b, adjoint2_a, adjoint2_b, share),
        60 * runs * n * cell,
    )
    for bits in steps[1:]:
        share = share + sum(fars)
        fars = hops(share, bits)
    share = share + sum(fars)
    far = hop(share, 3)
    result, share = call(
        late_kernel,
        ((n, ny, nz), (ROWS, LANES)),
        (
            lies_padded(runs, 3), lies_padded(runs, 3), lies_padded(runs, 3),
            lies(3), lies_padded(2), lies(2),
        ),
        (
            of_chip, *faces, chem0_a, chem0_b, chem1_b, adjoint2_b, flow_a, flow_part, adjoint1_a,
            weight_b, step_z_b, part, *sums_b, share,
        ),
        60 * runs * 3 * cell,
    )
    share = share + far
    handed = lax.ppermute(share, "gx", over_cores)
    (misfit,) = call(misfit_kernel, ((1,),), (), (share, handed), 1, scalar=0)
    return (result, misfit)


def solution(mesh):
    placed = (
        P("group", "gx", None, None),
        P("group", "gx", None, None),
        P(("group", "gx"), None, None),
    )
    return jax.shard_map(
        on_device,
        mesh=mesh,
        in_specs=placed,
        out_specs=(P(("group", "gx"), None, None), P("group")),
        check_vma=False,
    )
```

```python
import functools
import math

import jax
import jax.numpy as jnp
from jax import lax
from jax.experimental import pallas as pl
from jax.experimental.pallas import tpu as pltpu
from jax.sharding import PartitionSpec as P

stiffness = 0.5
time_step = 0.005
VMEM = pl.BlockSpec(memory_space=pltpu.VMEM)
SMEM = pl.BlockSpec(memory_space=pltpu.SMEM)
LANES = 128
ROWS = 8
PAD = ROWS
CHUNK = 8


def chunks(ny):
    return range(0, ny, CHUNK)


def plain(ref, lead, row):
    return [
        ref[(*lead, pl.ds(row, CHUNK), pl.ds(at, LANES))] for at in range(0, ref.shape[-1], LANES)
    ]


def put_plain(ref, lead, row, value):
    for block, part in enumerate(value):
        ref[(*lead, pl.ds(row, CHUNK), pl.ds(block * LANES, LANES))] = part


def flat(ref, lead, row):
    return [ref[(*lead, block, pl.ds(row, CHUNK))] for block in range(ref.shape[-3])]


def put_flat(ref, lead, row, value):
    for block, part in enumerate(value):
        ref[(*lead, block, pl.ds(row, CHUNK))] = part


def padded(ref, lead, row, shift=0):
    return [ref[(*lead, block, pl.ds(PAD + row + shift, CHUNK))] for block in range(ref.shape[-3])]


def put_padded(ref, lead, row, value):
    ny = ref.shape[-2] - 2 * PAD
    for block, part in enumerate(value):
        ref[(*lead, block, pl.ds(PAD + row, CHUNK))] = part
        if row == 0:
            ref[(*lead, block, pl.ds(PAD + ny, 1))] = part[:1]
        if row + CHUNK == ny:
            ref[(*lead, block, pl.ds(PAD - 1, 1))] = part[CHUNK - 1 :]


def lane():
    return lax.broadcasted_iota(jnp.int32, (CHUNK, LANES), 1)


def after_z(value):
    turned = [pltpu.roll(part, LANES - 1, 1) for part in value]
    turned.append(turned[0])
    edge = lane() == LANES - 1
    return [jnp.where(edge, turned[at + 1], turned[at]) for at in range(len(value))]


def before_z(value):
    turned = [pltpu.roll(part, 1, 1) for part in value]
    edge = lane() == 0
    return [jnp.where(edge, turned[at - 1], turned[at]) for at in range(len(value))]


def side():
    return lax.rem(lax.axis_index("gx"), 2)


def either(first, second):
    return first + side() * (second - first)


class Line:
    def __init__(self, *parts):
        self.parts = parts

    def __call__(self, at, *lead):
        for ref, first, last in self.parts:
            if first <= at <= last:
                return ref, (*lead, at - first)
        raise IndexError(at)


def each(function, *values):
    return [function(*parts) for parts in zip(*values)]


def beside(low, high, up, down, mid):
    return each(
        lambda a, b, c, d, e, f: (a + b) + (c + d) + (e + f),
        low, high, up, down, after_z(mid), before_z(mid),
    )


def potential(low, mid, high, up, down):
    return each(
        lambda c, total: c * (c * c + (6.0 * stiffness - 1.0)) - stiffness * total,
        mid, beside(low, high, up, down, mid),
    )


class Faces:
    def __init__(self, n, refs):
        mx_a, my_a, my_low_a, mz_a, mz_low_a, all_a, *late = refs
        two = lambda ref, first, last, at: ((ref, first, last), *(((late[at], last + 1, n + 1),) if late else ()))
        self.mx = Line(*two(mx_a, -3, n - 2, 0))
        self.my = Line(*two(my_a, -2, n - 1, 1))
        self.my_low = Line(*two(my_low_a, -2, n - 1, 2))
        self.mz = Line(*two(mz_a, -2, n - 1, 3))
        self.mz_low = Line(*two(mz_low_a, -2, n - 1, 4))
        self.all = Line(*two(all_a, -2, n - 2, 5))

    def flow(self, row, at, mid, up, down, low=None, high=None):
        total = each(
            lambda a, b, c, d, e, u, v, w, x, y: (a * u + b * v) + (c * w + d * x) - e * y,
            flat(*self.my(at), row), flat(*self.my_low(at), row), flat(*self.mz(at), row),
            flat(*self.mz_low(at), row), flat(*self.all(at), row), up, down, after_z(mid), before_z(mid), mid,
        )
        if low is not None:
            total = add_product(total, flat(*self.mx(at - 1), row), low)
        if high is not None:
            total = add_product(total, flat(*self.mx(at), row), high)
        return total


def add_product(total, a, b):
    return each(lambda t, x, y: t + x * y, total, a, b)


def sub(a, b):
    return each(lambda x, y: x - y, a, b)


def own_kernel(initial, mobility, conc, mob, to_chip, to_core):
    runs, n, ny, _ = initial.shape
    place = [either(n - 1 - at, at) for at in range(n)]

    def one_run(run, carry):
        for row in chunks(ny):
            for at in range(n):
                put_padded(conc, (run, at), row, plain(initial, (run, place[at]), row))
        return carry

    for run in range(runs):
        one_run(run, 0)
    for row in chunks(ny):
        for at in range(n):
            value = plain(mobility, (place[at],), row)
            put_padded(mob, (at,), row, value)
            if at < 3:
                put_flat(to_core, (at,), row, value)
            if at >= n - 3:
                put_flat(to_chip, (n - 1 - at,), row, value)


def mean(a, b):
    return 0.5 * (a + b)


def put_faces(row, mob, places, faces):
    for at in places:
        mid = padded(*mob(at), row)
        put_flat(*faces.my(at), row, each(mean, mid, padded(*mob(at), row, 1)))
        put_flat(*faces.my_low(at), row, each(mean, mid, padded(*mob(at), row, -1)))
        put_flat(*faces.mz(at), row, each(mean, mid, after_z(mid)))
        put_flat(*faces.mz_low(at), row, each(mean, mid, before_z(mid)))


def put_all(row, faces, places):
    for at in places:
        put_flat(*faces.all(at), row, each(
            lambda a, b, c, d, e, f: (a + b) + (c + d) + (e + f),
            flat(*faces.mx(at - 1), row), flat(*faces.mx(at), row), flat(*faces.my(at), row),
            flat(*faces.my_low(at), row), flat(*faces.mz(at), row), flat(*faces.mz_low(at), row),
        ))


def put_potential(row, field, run, places, target):
    mids = {at: padded(*field(at, run), row) for at in range(places[0] - 1, places[-1] + 2)}
    for at in places:
        value = potential(
            mids[at - 1], mids[at], mids[at + 1],
            padded(*field(at, run), row, 1), padded(*field(at, run), row, -1),
        )
        put_padded(*target(at, run), row, value)


def put_step(row, faces, chem, state, run, places, target):
    mids = {at: padded(*chem(at, run), row) for at in range(places[0] - 1, places[-1] + 2)}
    for at in places:
        flow = faces.flow(
            row, at, mids[at], padded(*chem(at, run), row, 1), padded(*chem(at, run), row, -1),
            mids[at - 1], mids[at + 1],
        )
        value = each(lambda a, b: a + time_step * b, padded(*state(at, run), row), flow)
        target(at, value)


def put_miss(row, runs, observed, place, run, at, value, adjoint2):
    miss = sub(value, plain(observed, (run, place[at]), row))
    adjoint = each(lambda a: a * (1.0 / runs), miss)
    put_padded(*adjoint2(at, run), row, adjoint)
    return adjoint, sum(part * part for part in miss)


def core_kernel(of_core, m_core, conc_own, mob_own, conc_core, chem0, mx, my, my_low, mz, mz_low, m_all, rim):
    runs, n = conc_own.shape[:2]
    ny = of_core.shape[2]
    mob = Line((rim, -3, -1), (mob_own, 0, n - 1))
    faces = Faces(n, (mx, my, my_low, mz, mz_low, m_all))
    for row in chunks(ny):
        for at in range(3):
            put_padded(rim, (2 - at,), row, flat(m_core, (at,), row))
    for row in chunks(ny):
        mids = [padded(*mob(at), row) for at in range(-3, n)]
        for at in range(n + 2):
            put_flat(mx, (at,), row, each(mean, mids[at], mids[at + 1]))
        put_faces(row, mob, range(-2, n), faces)
    for row in chunks(ny):
        put_all(row, faces, range(-2, n - 1))
    place = [either(at, 3 - at) for at in range(4)]
    conc = Line((conc_core, -4, -1), (conc_own, 0, n - 1))

    def one_run(run, carry):
        for row in chunks(ny):
            for at in range(4):
                put_padded(conc_core, (run, 3 - at), row, plain(of_core, (run, place[at]), row))
        for row in chunks(ny):
            put_potential(row, conc, run, range(-3, n - 1), Line((chem0, -3, n - 2)))
        return carry

    for run in range(runs):
        one_run(run, 0)


def chip_kernel(
    of_chip, conc_own, conc_core, chem0_a, observed, mx, my, my_low, mz, mz_low, m_all,
    conc_chip, chem0_b, state1_a, chem1_a, adjoint2_a, squares,
):
    runs, n = conc_own.shape[:2]
    ny = observed.shape[2]
    faces = Faces(n, (mx, my, my_low, mz, mz_low, m_all))
    message = [either(3 - at, at) for at in range(4)]
    place = [either(n - 1 - at, at) for at in range(n)]
    conc = Line((conc_core, -4, -1), (conc_own, 0, n - 1), (conc_chip, n, n + 3))
    chem0 = Line((chem0_a, -3, n - 2), (chem0_b, n - 1, n + 2))
    state1 = Line((state1_a, -2, n - 2))
    chem1 = Line((chem1_a, -1, n - 3))
    adjoint2 = Line((adjoint2_a, 0, n - 4))
    squares[...] = jnp.zeros_like(squares)

    def one_run(run, carry):
        for row in chunks(ny):
            for at in range(4):
                put_padded(conc_chip, (run, at), row, plain(of_chip, (run, message[at]), row))
        for row in chunks(ny):
            put_potential(row, conc, run, range(n - 1, n + 3), chem0)
        for row in chunks(ny):
            put_step(
                row, faces, chem0, conc, run, range(-2, n - 1),
                lambda at, value: put_padded(*state1(at, run), row, value),
            )
        for row in chunks(ny):
            put_potential(row, state1, run, range(-1, n - 2), chem1)
        for row in chunks(ny):

            def target(at, value):
                squares[...] += put_miss(row, runs, observed, place, run, at, value, adjoint2)[1]

            put_step(row, faces, chem1, state1, run, range(0, n - 3), target)
        return carry

    for run in range(runs):
        one_run(run, 0)


def forward_kernel(
    m_chip, mob_own, conc_own, conc_chip, chem0_a, chem0_b, state1_a, chem1_a, adjoint2_a, squares, observed,
    mx_a, my_a, my_low_a, mz_a, mz_low_a, all_a,
    mx_b, my_b, my_low_b, mz_b, mz_low_b, all_b, state1_b, chem1_b, adjoint2_b, to_core, to_chip, share, rim, total,
):
    runs, n = conc_own.shape[:2]
    ny = observed.shape[2]
    faces = Faces(n, (mx_a, my_a, my_low_a, mz_a, mz_low_a, all_a, mx_b, my_b, my_low_b, mz_b, mz_low_b, all_b))
    mob = Line((mob_own, 0, n - 1), (rim, n, n + 2))
    place = [either(n - 1 - at, at) for at in range(n)]
    conc = Line((conc_own, 0, n - 1), (conc_chip, n, n + 3))
    chem0 = Line((chem0_a, -3, n - 2), (chem0_b, n - 1, n + 2))
    state1 = Line((state1_a, -2, n - 2), (state1_b, n - 1, n + 1))
    chem1 = Line((chem1_a, -1, n - 3), (chem1_b, n - 2, n))
    adjoint2 = Line((adjoint2_a, 0, n - 4), (adjoint2_b, n - 3, n - 1))
    for row in chunks(ny):
        for at in range(3):
            put_padded(rim, (at,), row, flat(m_chip, (at,), row))
    for row in chunks(ny):
        mids = [padded(*mob(at), row) for at in range(n - 1, n + 3)]
        for at in range(3):
            put_flat(mx_b, (at,), row, each(mean, mids[at], mids[at + 1]))
        put_faces(row, mob, range(n, n + 2), faces)
    for row in chunks(ny):
        put_all(row, faces, range(n - 1, n + 2))
    total[...] = squares[...]

    def one_run(run, carry):
        for row in chunks(ny):
            put_step(
                row, faces, chem0, conc, run, range(n - 1, n + 2),
                lambda at, value: put_padded(*state1(at, run), row, value),
            )
        for row in chunks(ny):
            put_potential(row, state1, run, range(n - 2, n + 1), chem1)
        for row in chunks(ny):

            def target(at, value):
                adjoint, square = put_miss(row, runs, observed, place, run, at, value, adjoint2)
                total[...] += square
                put_flat(to_chip, (run, n - 1 - at), row, adjoint)
                if at < 3:
                    put_flat(to_core, (run, at), row, adjoint)

            put_step(row, faces, chem1, state1, run, range(n - 3, n), target)
            for at in range(min(3, n - 3)):
                put_flat(to_core, (run, at), row, padded(*adjoint2(at, run), row))
        return carry

    for run in range(runs):
        one_run(run, 0)
    columns = (0.5 / runs) * jnp.sum(total[...], axis=0, keepdims=True)
    mine = jnp.broadcast_to(jnp.sum(columns, axis=1, keepdims=True), share.shape)
    sums = counts(lax.axis_index("gx")) == 1
    share[...] = jnp.where(sums, mine, 0.0)
    to_core[0, 0, 0, ny:] = jnp.where(sums, 0.0, mine)


def put_adjoint1(row, flow, adjoint2, run, places, weight, target):
    mids = {at: padded(*flow(at, run), row) for at in range(places[0] - 1, places[-1] + 2)}
    for at in places:
        total = beside(
            mids[at - 1], mids[at + 1], padded(*flow(at, run), row, 1), padded(*flow(at, run), row, -1), mids[at]
        )
        value = each(
            lambda a, w, f, t: a + w * f - (time_step * stiffness) * t,
            padded(*adjoint2(at, run), row), weight(at), mids[at], total,
        )
        put_padded(*target(at, run), row, value)


def slope(state):
    return each(lambda c: time_step * (3.0 * c * c + (6.0 * stiffness - 1.0)), state)


def step_x(field, run, at, row):
    return sub(padded(*field(at + 1, run), row), padded(*field(at, run), row))


def step_y(field, run, at, row):
    return sub(padded(*field(at, run), row, 1), padded(*field(at, run), row))


def step_z(field, run, at, row):
    mid = padded(*field(at, run), row)
    return sub(after_z(mid), mid)


def early_kernel(
    of_core, mx_a, my_a, my_low_a, mz_a, mz_low_a, all_a, mx_b, my_b, my_low_b, mz_b, mz_low_b, all_b,
    chem0_a, chem0_b, state1_a, state1_b, chem1_a, chem1_b, adjoint2_a, adjoint2_b,
    share_in, flow_a, flow_part, adjoint1_a, weight_b, step_z_b, part, sum_x_b, sum_y_b, sum_z_b, share,
    rim, sum_x, sum_y, sum_z,
):
    share[...] = share_in[...]
    runs = of_core.shape[0]
    n = part.shape[0] + 2
    ny = part.shape[-2]
    faces = Faces(n, (mx_a, my_a, my_low_a, mz_a, mz_low_a, all_a, mx_b, my_b, my_low_b, mz_b, mz_low_b, all_b))
    chem0 = Line((chem0_a, -3, n - 2), (chem0_b, n - 1, n + 2))
    state1 = Line((state1_a, -2, n - 2), (state1_b, n - 1, n + 1))
    chem1 = Line((chem1_a, -1, n - 3), (chem1_b, n - 2, n))
    adjoint2 = Line((rim, -3, -1), (adjoint2_a, 0, n - 4), (adjoint2_b, n - 3, n - 1))
    flow = Line((flow_a, -2, n - 2), (flow_part, n - 1, n - 1))
    adjoint1 = Line((adjoint1_a, -1, n - 3))
    for sums in (sum_x, sum_y, sum_z):
        sums[...] = jnp.zeros_like(sums)

    def one_run(run, carry):
        for row in chunks(ny):
            for at in range(3):
                put_padded(rim, (run, 2 - at), row, flat(of_core, (run, at), row))
        for row in chunks(ny):
            mids = {at: padded(*adjoint2(at, run), row) for at in range(-3, n)}
            for at in range(-2, n):
                value = faces.flow(
                    row, at, mids[at], padded(*adjoint2(at, run), row, 1), padded(*adjoint2(at, run), row, -1),
                    mids[at - 1], mids.get(at + 1),
                )
                put_padded(*flow(at, run), row, value)
        for row in chunks(ny):
            put_adjoint1(
                row, flow, adjoint2, run, range(-1, n - 2),
                lambda at: slope(padded(*state1(at, run), row)), adjoint1,
            )
            for at in range(n - 2, n + 1):
                put_flat(weight_b, (run, at - (n - 2)), row, slope(padded(*state1(at, run), row)))
        for row in chunks(ny):
            for at in range(-1, n - 1):
                total = add_product(
                    flat(sum_x, (at + 1,), row), step_x(adjoint2, run, at, row), step_x(chem1, run, at, row)
                )
                if at < n - 3:
                    total = add_product(total, step_x(adjoint1, run, at, row), step_x(chem0, run, at, row))
                put_flat(sum_x, (at + 1,), row, total)
            for at in range(n):
                total_y = add_product(
                    padded(sum_y, (at,), row), step_y(adjoint2, run, at, row), step_y(chem1, run, at, row)
                )
                total_z = add_product(
                    flat(sum_z, (at,), row), step_z(adjoint2, run, at, row), step_z(chem1, run, at, row)
                )
                slant = step_z(chem0, run, at, row)
                if at < n - 2:
                    total_y = add_product(total_y, step_y(adjoint1, run, at, row), step_y(chem0, run, at, row))
                    total_z = add_product(total_z, step_z(adjoint1, run, at, row), slant)
                else:
                    put_flat(step_z_b, (run, at - (n - 2)), row, slant)
                put_padded(sum_y, (at,), row, total_y)
                put_flat(sum_z, (at,), row, total_z)
        return carry

    for run in range(runs):
        one_run(run, 0)
    for row in chunks(ny):
        for at in range(n - 2):
            sides = flat(sum_z, (at,), row)
            value = each(
                lambda a, b, c, d, e: -0.5 * ((a + b) + (c + d) + e),
                padded(sum_y, (at,), row), padded(sum_y, (at,), row, -1), sides, before_z(sides),
                flat(sum_x, (at,), row),
            )
            if at < n - 3:
                value = each(lambda a, b: a - 0.5 * b, value, flat(sum_x, (at + 1,), row))
            put_flat(part, (at,), row, value)
        for at in range(2):
            put_flat(sum_x_b, (at,), row, flat(sum_x, (n - 2 + at,), row))
            put_flat(sum_y_b, (at,), row, padded(sum_y, (n - 2 + at,), row))
            put_flat(sum_z_b, (at,), row, flat(sum_z, (n - 2 + at,), row))


def late_kernel(
    of_chip, mx_a, my_a, my_low_a, mz_a, mz_low_a, all_a, mx_b, my_b, my_low_b, mz_b, mz_low_b, all_b,
    chem0_a, chem0_b, chem1_b, adjoint2_b, flow_a, flow_part, adjoint1_a, weight_b, step_z_b,
    part, sum_x_b, sum_y_b, sum_z_b, share_in, result, share, rim, flow_b, adjoint1_b, sum_x, sum_y, sum_z,
):
    share[...] = share_in[...]
    runs = of_chip.shape[0]
    n, ny, _ = result.shape
    faces = Faces(n, (mx_a, my_a, my_low_a, mz_a, mz_low_a, all_a, mx_b, my_b, my_low_b, mz_b, mz_low_b, all_b))
    place = [either(n - 1 - at, at) for at in range(n)]
    chem0 = Line((chem0_a, -3, n - 2), (chem0_b, n - 1, n + 2))
    chem1 = Line((chem1_b, n - 2, n))
    adjoint2 = Line((adjoint2_b, n - 3, n - 1), (rim, n, n + 2))
    flow = Line((flow_a, -2, n - 2), (flow_b, n - 1, n + 1))
    adjoint1 = Line((adjoint1_a, -1, n - 3), (adjoint1_b, n - 2, n))
    for row in chunks(ny):
        for at in range(2):
            put_flat(sum_x, (at,), row, flat(sum_x_b, (at,), row))
            put_padded(sum_y, (at,), row, flat(sum_y_b, (at,), row))
            put_flat(sum_z, (at,), row, flat(sum_z_b, (at,), row))
    sum_x[2] = jnp.zeros_like(sum_x[2])

    def one_run(run, carry):
        for row in chunks(ny):
            for at in range(3):
                put_padded(rim, (run, at), row, flat(of_chip, (run, at), row))
        for row in chunks(ny):
            mids = {at: padded(*adjoint2(at, run), row) for at in range(n - 1, n + 3)}
            value = add_product(padded(flow_part, (run, 0), row), flat(*faces.mx(n - 1), row), mids[n])
            put_padded(*flow(n - 1, run), row, value)
            for at in range(n, n + 2):
                value = faces.flow(
                    row, at, mids[at], padded(*adjoint2(at, run), row, 1), padded(*adjoint2(at, run), row, -1),
                    mids[at - 1], mids[at + 1],
                )
                put_padded(*flow(at, run), row, value)
        for row in chunks(ny):
            put_adjoint1(
                row, flow, adjoint2, run, range(n - 2, n + 1),
                lambda at: flat(weight_b, (run, at - (n - 2)), row), adjoint1,
            )
        for row in chunks(ny):
            for at in range(n - 3, n):
                total = add_product(
                    flat(sum_x, (at - (n - 3),), row), step_x(adjoint1, run, at, row), step_x(chem0, run, at, row)
                )
                if at == n - 1:
                    total = add_product(total, step_x(adjoint2, run, at, row), step_x(chem1, run, at, row))
                put_flat(sum_x, (at - (n - 3),), row, total)
            for at in range(n - 2, n):
                to = (at - (n - 2),)
                put_padded(sum_y, to, row, add_product(
                    padded(sum_y, to, row), step_y(adjoint1, run, at, row), step_y(chem0, run, at, row)
                ))
                put_flat(sum_z, to, row, add_product(
                    flat(sum_z, to, row), step_z(adjoint1, run, at, row), flat(step_z_b, (run, *to), row)
                ))
        return carry

    for run in range(runs):
        one_run(run, 0)
    for row in chunks(ny):
        for at in range(n - 2):
            value = flat(part, (at,), row)
            if at == n - 3:
                value = each(lambda a, b: a - 0.5 * b, value, flat(sum_x, (0,), row))
            put_plain(result, (place[at],), row, value)
        for at in range(2):
            sides = flat(sum_z, (at,), row)
            value = each(
                lambda a, b, c, d, e, f: -0.5 * ((a + b) + (c + d) + (e + f)),
                flat(sum_x, (at,), row), flat(sum_x, (at + 1,), row),
                padded(sum_y, (at,), row), padded(sum_y, (at,), row, -1), sides, before_z(sides),
            )
            put_plain(result, (place[n - 2 + at],), row, value)


def counts(at):
    return (at ^ (at >> 1)) & 1


def misfit_kernel(share, far, misfit):
    misfit[0] = (share[...] + far[...])[0, 0]


def call(kernel, outs, scratch, args, flops, scalar=None):
    moved = 4 * (sum(a.size for a in args) + sum(math.prod(o) for o in outs))
    return pl.pallas_call(
        kernel,
        out_shape=tuple(jax.ShapeDtypeStruct(o, jnp.float32) for o in outs),
        in_specs=[VMEM] * len(args),
        out_specs=tuple(SMEM if at == scalar else VMEM for at in range(len(outs))),
        scratch_shapes=[pltpu.VMEM(s, jnp.float32) for s in scratch],
        compiler_params=pltpu.CompilerParams(vmem_limit_bytes=16 * 1024 * 1024),
        cost_estimate=pl.CostEstimate(flops=flops, bytes_accessed=moved, transcendentals=0),
    )(*args)


def on_device(initial, observed, mobility):
    runs, n, ny, nz = initial.shape
    blocks = nz // LANES
    count = lax.axis_size("gx")
    over_chips = [(i, (i - 1 + 2 * (i % 2)) % count) for i in range(count)]
    over_cores = [(i, i ^ 1) for i in range(count)]
    cell = ny * nz

    def neighbours(to_chip, to_core):
        of_core = lax.ppermute(to_core, "gx", over_cores)
        return lax.ppermute(to_chip, "gx", over_chips), of_core

    def lies(*lead):
        return (*lead, blocks, ny, LANES)

    def lies_padded(*lead):
        return (*lead, blocks, ny + 2 * PAD, LANES)

    if n == 4:
        near = (initial, initial)
    else:
        near = [lax.dynamic_slice_in_dim(initial, at, 4, 1) for at in (either(0, n - 4), either(n - 4, 0))]
    of_chip, of_core = neighbours(*near)
    conc, mob, to_chip, to_core = call(
        own_kernel, (lies_padded(runs, n), lies_padded(n), lies(3), lies(3)), (), (initial, mobility),
        runs * n * cell,
    )
    m_chip, m_core = neighbours(to_chip, to_core)
    conc_core, chem0_a, *faces_a = call(
        core_kernel,
        (
            lies_padded(runs, 4), lies_padded(runs, n + 2),
            lies(n + 2), lies(n + 2), lies(n + 2), lies(n + 2), lies(n + 2), lies(n + 1),
        ),
        (lies_padded(3),),
        (of_core, m_core, conc, mob),
        20 * runs * (n + 2) * cell,
    )
    conc_chip, chem0_b, state1_a, chem1_a, adjoint2_a, squares = call(
        chip_kernel,
        (
            lies_padded(runs, 4), lies_padded(runs, 4), lies_padded(runs, n + 1),
            lies_padded(runs, n - 1), lies_padded(runs, n - 3), (CHUNK, LANES),
        ),
        (),
        (of_chip, conc, conc_core, chem0_a, observed, *faces_a),
        60 * runs * (n - 1) * cell,
    )
    *faces_b, state1_b, chem1_b, adjoint2_b, to_core, to_chip, share = call(
        forward_kernel,
        (
            lies(3), lies(2), lies(2), lies(2), lies(2), lies(3),
            lies_padded(runs, 3), lies_padded(runs, 3), lies_padded(runs, 3),
            (runs, 3, blocks, ny + ROWS, LANES), lies(runs, 3), (ROWS, LANES),
        ),
        (lies_padded(3), (CHUNK, LANES)),
        (m_chip, mob, conc, conc_chip, chem0_a, chem0_b, state1_a, chem1_a, adjoint2_a, squares, observed, *faces_a),
        60 * runs * 3 * cell,
    )
    faces = (*faces_a, *faces_b)
    of_chip, of_core = neighbours(to_chip, to_core)
    groups = lax.axis_size("group")

    def target(group, at, apart):
        if counts(at):
            return group * count + (at ^ apart)
        return min(group ^ 1, groups - 1) * count + at

    def hop(value, apart):
        pairs = [
            (group * count + at, target(group, at, apart)) for group in range(groups) for at in range(count)
        ]
        return lax.ppermute(value, ("group", "gx"), pairs)

    def hops(value, bits):
        aparts = [sum(2 << bit for at, bit in enumerate(bits) if which >> at & 1) for which in range(1, 1 << len(bits))]
        return [hop(value, apart) for apart in aparts]

    share = share + of_core[0, 0, 0, ny:]
    upper = range(count.bit_length() - 3, 0, -1)
    steps = [upper[at : at + 2] for at in range(0, len(upper), 2)]
    fars = hops(share, steps[0])
    flow_a, flow_part, adjoint1_a, weight_b, step_z_b, part, *sums_b, share = call(
        early_kernel,
        (
            lies_padded(runs, n + 1), lies_padded(runs, 1), lies_padded(runs, n - 1), lies(runs, 3), lies(runs, 2),
            lies(n - 2), lies(2), lies(2), lies(2), (ROWS, LANES),
        ),
        (lies_padded(runs, 3), lies(n), lies_padded(n), lies(n)),
        (of_core, *faces, chem0_a, chem0_b, state1_a, state1_b, chem1_a, chem1_b, adjoint2_a, adjoint2_b, share),
        60 * runs * n * cell,
    )
    for bits in steps[1:]:
        share = share + sum(fars)
        fars = hops(share, bits)
    share = share + sum(fars)
    share = share + lax.ppermute(share, "gx", over_cores)
    far = lax.ppermute(share, "gx", [(at, at ^ 3) for at in range(count)])
    result, share = call(
        late_kernel,
        ((n, ny, nz), (ROWS, LANES)),
        (
            lies_padded(runs, 3), lies_padded(runs, 3), lies_padded(runs, 3),
            lies(3), lies_padded(2), lies(2),
        ),
        (
            of_chip, *faces, chem0_a, chem0_b, chem1_b, adjoint2_b, flow_a, flow_part, adjoint1_a,
            weight_b, step_z_b, part, *sums_b, share,
        ),
        60 * runs * 3 * cell,
    )
    (misfit,) = call(misfit_kernel, ((1,),), (), (share, far), 1, scalar=0)
    return (result, misfit)


def solution(mesh):
    placed = (
        P("group", "gx", None, None),
        P("group", "gx", None, None),
        P(("group", "gx"), None, None),
    )
    return jax.shard_map(
        on_device,
        mesh=mesh,
        in_specs=placed,
        out_specs=(P(("group", "gx"), None, None), P("group")),
        check_vma=False,
    )
```

```python
import functools
import math

import jax
import jax.numpy as jnp
from jax import lax
from jax.experimental import pallas as pl
from jax.experimental.pallas import tpu as pltpu
from jax.sharding import PartitionSpec as P

stiffness = 0.5
time_step = 0.005
VMEM = pl.BlockSpec(memory_space=pltpu.VMEM)
SMEM = pl.BlockSpec(memory_space=pltpu.SMEM)
LANES = 128
ROWS = 8
PAD = ROWS
CHUNK = 8


def chunks(ny):
    return range(0, ny, CHUNK)


def plain(ref, lead, row):
    return [
        ref[(*lead, pl.ds(row, CHUNK), pl.ds(at, LANES))] for at in range(0, ref.shape[-1], LANES)
    ]


def put_plain(ref, lead, row, value):
    for block, part in enumerate(value):
        ref[(*lead, pl.ds(row, CHUNK), pl.ds(block * LANES, LANES))] = part


def flat(ref, lead, row):
    return [ref[(*lead, block, pl.ds(row, CHUNK))] for block in range(ref.shape[-3])]


def put_flat(ref, lead, row, value):
    for block, part in enumerate(value):
        ref[(*lead, block, pl.ds(row, CHUNK))] = part


def padded(ref, lead, row, shift=0):
    return [ref[(*lead, block, pl.ds(PAD + row + shift, CHUNK))] for block in range(ref.shape[-3])]


def put_padded(ref, lead, row, value):
    ny = ref.shape[-2] - 2 * PAD
    for block, part in enumerate(value):
        ref[(*lead, block, pl.ds(PAD + row, CHUNK))] = part
        if row == 0:
            ref[(*lead, block, pl.ds(PAD + ny, 1))] = part[:1]
        if row + CHUNK == ny:
            ref[(*lead, block, pl.ds(PAD - 1, 1))] = part[CHUNK - 1 :]


def lane():
    return lax.broadcasted_iota(jnp.int32, (CHUNK, LANES), 1)


def after_z(value):
    turned = [pltpu.roll(part, LANES - 1, 1) for part in value]
    turned.append(turned[0])
    edge = lane() == LANES - 1
    return [jnp.where(edge, turned[at + 1], turned[at]) for at in range(len(value))]


def before_z(value):
    turned = [pltpu.roll(part, 1, 1) for part in value]
    edge = lane() == 0
    return [jnp.where(edge, turned[at - 1], turned[at]) for at in range(len(value))]


def side():
    return lax.rem(lax.axis_index("gx"), 2)


def either(first, second):
    return first + side() * (second - first)


class Line:
    def __init__(self, *parts):
        self.parts = parts

    def __call__(self, at, *lead):
        for ref, first, last in self.parts:
            if first <= at <= last:
                return ref, (*lead, at - first)
        raise IndexError(at)


def each(function, *values):
    return [function(*parts) for parts in zip(*values)]


def beside(low, high, up, down, mid):
    return each(
        lambda a, b, c, d, e, f: (a + b) + (c + d) + (e + f),
        low, high, up, down, after_z(mid), before_z(mid),
    )


def potential(low, mid, high, up, down):
    return each(
        lambda c, total: c * (c * c + (6.0 * stiffness - 1.0)) - stiffness * total,
        mid, beside(low, high, up, down, mid),
    )


class Faces:
    def __init__(self, n, refs):
        mx_a, my_a, my_low_a, mz_a, mz_low_a, all_a, *late = refs
        two = lambda ref, first, last, at: ((ref, first, last), *(((late[at], last + 1, n + 1),) if late else ()))
        self.mx = Line(*two(mx_a, -3, n - 2, 0))
        self.my = Line(*two(my_a, -2, n - 1, 1))
        self.my_low = Line(*two(my_low_a, -2, n - 1, 2))
        self.mz = Line(*two(mz_a, -2, n - 1, 3))
        self.mz_low = Line(*two(mz_low_a, -2, n - 1, 4))
        self.all = Line(*two(all_a, -2, n - 2, 5))

    def flow(self, row, at, mid, up, down, low=None, high=None):
        total = each(
            lambda a, b, c, d, e, u, v, w, x, y: (a * u + b * v) + (c * w + d * x) - e * y,
            flat(*self.my(at), row), flat(*self.my_low(at), row), flat(*self.mz(at), row),
            flat(*self.mz_low(at), row), flat(*self.all(at), row), up, down, after_z(mid), before_z(mid), mid,
        )
        if low is not None:
            total = add_product(total, flat(*self.mx(at - 1), row), low)
        if high is not None:
            total = add_product(total, flat(*self.mx(at), row), high)
        return total


def add_product(total, a, b):
    return each(lambda t, x, y: t + x * y, total, a, b)


def sub(a, b):
    return each(lambda x, y: x - y, a, b)


def own_kernel(initial, mobility, conc, mob, to_chip, to_core):
    runs, n, ny, _ = initial.shape
    place = [either(n - 1 - at, at) for at in range(n)]

    def one_run(run, carry):
        for row in chunks(ny):
            for at in range(n):
                put_padded(conc, (run, at), row, plain(initial, (run, place[at]), row))
        return carry

    for run in range(runs):
        one_run(run, 0)
    for row in chunks(ny):
        for at in range(n):
            value = plain(mobility, (place[at],), row)
            put_padded(mob, (at,), row, value)
            if at < 3:
                put_flat(to_core, (at,), row, value)
            if at >= n - 3:
                put_flat(to_chip, (n - 1 - at,), row, value)


def mean(a, b):
    return 0.5 * (a + b)


def put_faces(row, mob, places, faces):
    for at in places:
        mid = padded(*mob(at), row)
        put_flat(*faces.my(at), row, each(mean, mid, padded(*mob(at), row, 1)))
        put_flat(*faces.my_low(at), row, each(mean, mid, padded(*mob(at), row, -1)))
        put_flat(*faces.mz(at), row, each(mean, mid, after_z(mid)))
        put_flat(*faces.mz_low(at), row, each(mean, mid, before_z(mid)))


def put_all(row, faces, places):
    for at in places:
        put_flat(*faces.all(at), row, each(
            lambda a, b, c, d, e, f: (a + b) + (c + d) + (e + f),
            flat(*faces.mx(at - 1), row), flat(*faces.mx(at), row), flat(*faces.my(at), row),
            flat(*faces.my_low(at), row), flat(*faces.mz(at), row), flat(*faces.mz_low(at), row),
        ))


def put_potential(row, field, run, places, target):
    mids = {at: padded(*field(at, run), row) for at in range(places[0] - 1, places[-1] + 2)}
    for at in places:
        value = potential(
            mids[at - 1], mids[at], mids[at + 1],
            padded(*field(at, run), row, 1), padded(*field(at, run), row, -1),
        )
        put_padded(*target(at, run), row, value)


def put_step(row, faces, chem, state, run, places, target):
    mids = {at: padded(*chem(at, run), row) for at in range(places[0] - 1, places[-1] + 2)}
    for at in places:
        flow = faces.flow(
            row, at, mids[at], padded(*chem(at, run), row, 1), padded(*chem(at, run), row, -1),
            mids[at - 1], mids[at + 1],
        )
        value = each(lambda a, b: a + time_step * b, padded(*state(at, run), row), flow)
        target(at, value)


def put_miss(row, runs, observed, place, run, at, value, adjoint2):
    miss = sub(value, plain(observed, (run, place[at]), row))
    adjoint = each(lambda a: a * (1.0 / runs), miss)
    put_padded(*adjoint2(at, run), row, adjoint)
    return adjoint, sum(part * part for part in miss)


def core_kernel(of_core, m_core, conc_own, mob_own, conc_core, chem0, mx, my, my_low, mz, mz_low, m_all, rim):
    runs, n = conc_own.shape[:2]
    ny = of_core.shape[2]
    mob = Line((rim, -3, -1), (mob_own, 0, n - 1))
    faces = Faces(n, (mx, my, my_low, mz, mz_low, m_all))
    for row in chunks(ny):
        for at in range(3):
            put_padded(rim, (2 - at,), row, flat(m_core, (at,), row))
    for row in chunks(ny):
        mids = [padded(*mob(at), row) for at in range(-3, n)]
        for at in range(n + 2):
            put_flat(mx, (at,), row, each(mean, mids[at], mids[at + 1]))
        put_faces(row, mob, range(-2, n), faces)
    for row in chunks(ny):
        put_all(row, faces, range(-2, n - 1))
    place = [either(at, 3 - at) for at in range(4)]
    conc = Line((conc_core, -4, -1), (conc_own, 0, n - 1))

    def one_run(run, carry):
        for row in chunks(ny):
            for at in range(4):
                put_padded(conc_core, (run, 3 - at), row, plain(of_core, (run, place[at]), row))
        for row in chunks(ny):
            put_potential(row, conc, run, range(-3, n - 1), Line((chem0, -3, n - 2)))
        return carry

    for run in range(runs):
        one_run(run, 0)


def chip_kernel(
    of_chip, conc_own, conc_core, chem0_a, observed, mx, my, my_low, mz, mz_low, m_all,
    conc_chip, chem0_b, state1_a, chem1_a, adjoint2_a, squares,
):
    runs, n = conc_own.shape[:2]
    ny = observed.shape[2]
    faces = Faces(n, (mx, my, my_low, mz, mz_low, m_all))
    message = [either(3 - at, at) for at in range(4)]
    place = [either(n - 1 - at, at) for at in range(n)]
    conc = Line((conc_core, -4, -1), (conc_own, 0, n - 1), (conc_chip, n, n + 3))
    chem0 = Line((chem0_a, -3, n - 2), (chem0_b, n - 1, n + 2))
    state1 = Line((state1_a, -2, n - 2))
    chem1 = Line((chem1_a, -1, n - 3))
    adjoint2 = Line((adjoint2_a, 0, n - 4))
    squares[...] = jnp.zeros_like(squares)

    def one_run(run, carry):
        for row in chunks(ny):
            for at in range(4):
                put_padded(conc_chip, (run, at), row, plain(of_chip, (run, message[at]), row))
        for row in chunks(ny):
            put_potential(row, conc, run, range(n - 1, n + 3), chem0)
        for row in chunks(ny):
            put_step(
                row, faces, chem0, conc, run, range(-2, n - 1),
                lambda at, value: put_padded(*state1(at, run), row, value),
            )
        for row in chunks(ny):
            put_potential(row, state1, run, range(-1, n - 2), chem1)
        for row in chunks(ny):

            def target(at, value):
                squares[...] += put_miss(row, runs, observed, place, run, at, value, adjoint2)[1]

            put_step(row, faces, chem1, state1, run, range(0, n - 3), target)
        return carry

    for run in range(runs):
        one_run(run, 0)


def forward_kernel(
    m_chip, mob_own, conc_own, conc_chip, chem0_a, chem0_b, state1_a, chem1_a, adjoint2_a, squares, observed,
    mx_a, my_a, my_low_a, mz_a, mz_low_a, all_a,
    mx_b, my_b, my_low_b, mz_b, mz_low_b, all_b, state1_b, chem1_b, adjoint2_b, first, to_core, to_chip, share, gift, rim, total,
):
    runs, n = conc_own.shape[:2]
    ny = observed.shape[2]
    faces = Faces(n, (mx_a, my_a, my_low_a, mz_a, mz_low_a, all_a, mx_b, my_b, my_low_b, mz_b, mz_low_b, all_b))
    mob = Line((mob_own, 0, n - 1), (rim, n, n + 2))
    place = [either(n - 1 - at, at) for at in range(n)]
    conc = Line((conc_own, 0, n - 1), (conc_chip, n, n + 3))
    chem0 = Line((chem0_a, -3, n - 2), (chem0_b, n - 1, n + 2))
    state1 = Line((state1_a, -2, n - 2), (state1_b, n - 1, n + 1))
    chem1 = Line((chem1_a, -1, n - 3), (chem1_b, n - 2, n))
    adjoint2 = Line((adjoint2_a, 0, n - 4), (adjoint2_b, n - 3, n - 1))
    for row in chunks(ny):
        for at in range(3):
            put_padded(rim, (at,), row, flat(m_chip, (at,), row))
    for row in chunks(ny):
        mids = [padded(*mob(at), row) for at in range(n - 1, n + 3)]
        for at in range(3):
            put_flat(mx_b, (at,), row, each(mean, mids[at], mids[at + 1]))
        put_faces(row, mob, range(n, n + 2), faces)
    for row in chunks(ny):
        put_all(row, faces, range(n - 1, n + 2))
    total[...] = squares[...]

    def one_run(run, carry):
        for row in chunks(ny):
            put_step(
                row, faces, chem0, conc, run, range(n - 1, n + 2),
                lambda at, value: put_padded(*state1(at, run), row, value),
            )
        for row in chunks(ny):
            put_potential(row, state1, run, range(n - 2, n + 1), chem1)
        for row in chunks(ny):

            def target(at, value):
                adjoint, square = put_miss(row, runs, observed, place, run, at, value, adjoint2)
                total[...] += square
                put_flat(to_chip, (run, n - 1 - at), row, adjoint)
                if at < 3:
                    put_flat(to_core, (run, at), row, adjoint)

            put_step(row, faces, chem1, state1, run, range(n - 3, n), target)
            for at in range(min(3, n - 3)):
                put_flat(to_core, (run, at), row, padded(*adjoint2(at, run), row))
            for at in range(3):
                put_flat(first, (run, at), row, choose(
                    at_wrap(1), flat(to_chip, (run, at), row), flat(to_core, (run, at), row)
                ))
        return carry

    for run in range(runs):
        one_run(run, 0)
    columns = (0.5 / runs) * jnp.sum(total[...], axis=0, keepdims=True)
    mine = jnp.broadcast_to(jnp.sum(columns, axis=1, keepdims=True), share.shape)
    sums = counts(lax.axis_index("gx")) == 1
    share[...] = jnp.where(sums, mine, 0.0)
    gift[...] = jnp.where(sums, 0.0, mine)


def put_adjoint1(row, flow, adjoint2, run, places, weight, target):
    mids = {at: padded(*flow(at, run), row) for at in range(places[0] - 1, places[-1] + 2)}
    for at in places:
        total = beside(
            mids[at - 1], mids[at + 1], padded(*flow(at, run), row, 1), padded(*flow(at, run), row, -1), mids[at]
        )
        value = each(
            lambda a, w, f, t: a + w * f - (time_step * stiffness) * t,
            padded(*adjoint2(at, run), row), weight(at), mids[at], total,
        )
        put_padded(*target(at, run), row, value)


def slope(state):
    return each(lambda c: time_step * (3.0 * c * c + (6.0 * stiffness - 1.0)), state)


def step_x(field, run, at, row):
    return sub(padded(*field(at + 1, run), row), padded(*field(at, run), row))


def step_y(field, run, at, row):
    return sub(padded(*field(at, run), row, 1), padded(*field(at, run), row))


def step_z(field, run, at, row):
    mid = padded(*field(at, run), row)
    return sub(after_z(mid), mid)


def early_kernel(
    of_first, of_core, mx_a, my_a, my_low_a, mz_a, mz_low_a, all_a, mx_b, my_b, my_low_b, mz_b, mz_low_b, all_b,
    chem0_a, chem0_b, state1_a, state1_b, chem1_a, chem1_b, adjoint2_a, adjoint2_b,
    share_in, flow_a, flow_part, adjoint1_a, weight_b, step_z_b, part, sum_x_b, sum_y_b, sum_z_b, share,
    rim, sum_x, sum_y, sum_z,
):
    share[...] = share_in[...]
    runs = of_core.shape[0]
    n = part.shape[0] + 2
    ny = part.shape[-2]
    faces = Faces(n, (mx_a, my_a, my_low_a, mz_a, mz_low_a, all_a, mx_b, my_b, my_low_b, mz_b, mz_low_b, all_b))
    chem0 = Line((chem0_a, -3, n - 2), (chem0_b, n - 1, n + 2))
    state1 = Line((state1_a, -2, n - 2), (state1_b, n - 1, n + 1))
    chem1 = Line((chem1_a, -1, n - 3), (chem1_b, n - 2, n))
    adjoint2 = Line((rim, -3, -1), (adjoint2_a, 0, n - 4), (adjoint2_b, n - 3, n - 1))
    flow = Line((flow_a, -2, n - 2), (flow_part, n - 1, n - 1))
    adjoint1 = Line((adjoint1_a, -1, n - 3))
    for sums in (sum_x, sum_y, sum_z):
        sums[...] = jnp.zeros_like(sums)

    def one_run(run, carry):
        for row in chunks(ny):
            for at in range(3):
                put_padded(rim, (run, 2 - at), row, choose(
                    at_wrap(2), flat(of_core, (run, at), row), flat(of_first, (run, at), row)
                ))
        for row in chunks(ny):
            mids = {at: padded(*adjoint2(at, run), row) for at in range(-3, n)}
            for at in range(-2, n):
                value = faces.flow(
                    row, at, mids[at], padded(*adjoint2(at, run), row, 1), padded(*adjoint2(at, run), row, -1),
                    mids[at - 1], mids.get(at + 1),
                )
                put_padded(*flow(at, run), row, value)
        for row in chunks(ny):
            put_adjoint1(
                row, flow, adjoint2, run, range(-1, n - 2),
                lambda at: slope(padded(*state1(at, run), row)), adjoint1,
            )
            for at in range(n - 2, n + 1):
                put_flat(weight_b, (run, at - (n - 2)), row, slope(padded(*state1(at, run), row)))
        for row in chunks(ny):
            for at in range(-1, n - 1):
                total = add_product(
                    flat(sum_x, (at + 1,), row), step_x(adjoint2, run, at, row), step_x(chem1, run, at, row)
                )
                if at < n - 3:
                    total = add_product(total, step_x(adjoint1, run, at, row), step_x(chem0, run, at, row))
                put_flat(sum_x, (at + 1,), row, total)
            for at in range(n):
                total_y = add_product(
                    padded(sum_y, (at,), row), step_y(adjoint2, run, at, row), step_y(chem1, run, at, row)
                )
                total_z = add_product(
                    flat(sum_z, (at,), row), step_z(adjoint2, run, at, row), step_z(chem1, run, at, row)
                )
                slant = step_z(chem0, run, at, row)
                if at < n - 2:
                    total_y = add_product(total_y, step_y(adjoint1, run, at, row), step_y(chem0, run, at, row))
                    total_z = add_product(total_z, step_z(adjoint1, run, at, row), slant)
                else:
                    put_flat(step_z_b, (run, at - (n - 2)), row, slant)
                put_padded(sum_y, (at,), row, total_y)
                put_flat(sum_z, (at,), row, total_z)
        return carry

    for run in range(runs):
        one_run(run, 0)
    for row in chunks(ny):
        for at in range(n - 2):
            sides = flat(sum_z, (at,), row)
            value = each(
                lambda a, b, c, d, e: -0.5 * ((a + b) + (c + d) + e),
                padded(sum_y, (at,), row), padded(sum_y, (at,), row, -1), sides, before_z(sides),
                flat(sum_x, (at,), row),
            )
            if at < n - 3:
                value = each(lambda a, b: a - 0.5 * b, value, flat(sum_x, (at + 1,), row))
            put_flat(part, (at,), row, value)
        for at in range(2):
            put_flat(sum_x_b, (at,), row, flat(sum_x, (n - 2 + at,), row))
            put_flat(sum_y_b, (at,), row, padded(sum_y, (n - 2 + at,), row))
            put_flat(sum_z_b, (at,), row, flat(sum_z, (n - 2 + at,), row))


def late_kernel(
    of_first, of_chip, mx_a, my_a, my_low_a, mz_a, mz_low_a, all_a, mx_b, my_b, my_low_b, mz_b, mz_low_b, all_b,
    chem0_a, chem0_b, chem1_b, adjoint2_b, flow_a, flow_part, adjoint1_a, weight_b, step_z_b,
    part, sum_x_b, sum_y_b, sum_z_b, share_in, result, share, rim, flow_b, adjoint1_b, sum_x, sum_y, sum_z,
):
    share[...] = share_in[...]
    runs = of_chip.shape[0]
    n, ny, _ = result.shape
    faces = Faces(n, (mx_a, my_a, my_low_a, mz_a, mz_low_a, all_a, mx_b, my_b, my_low_b, mz_b, mz_low_b, all_b))
    place = [either(n - 1 - at, at) for at in range(n)]
    chem0 = Line((chem0_a, -3, n - 2), (chem0_b, n - 1, n + 2))
    chem1 = Line((chem1_b, n - 2, n))
    adjoint2 = Line((adjoint2_b, n - 3, n - 1), (rim, n, n + 2))
    flow = Line((flow_a, -2, n - 2), (flow_b, n - 1, n + 1))
    adjoint1 = Line((adjoint1_a, -1, n - 3), (adjoint1_b, n - 2, n))
    for row in chunks(ny):
        for at in range(2):
            put_flat(sum_x, (at,), row, flat(sum_x_b, (at,), row))
            put_padded(sum_y, (at,), row, flat(sum_y_b, (at,), row))
            put_flat(sum_z, (at,), row, flat(sum_z_b, (at,), row))
    sum_x[2] = jnp.zeros_like(sum_x[2])

    def one_run(run, carry):
        for row in chunks(ny):
            for at in range(3):
                put_padded(rim, (run, at), row, choose(
                    at_wrap(1), flat(of_first, (run, at), row), flat(of_chip, (run, at), row)
                ))
        for row in chunks(ny):
            mids = {at: padded(*adjoint2(at, run), row) for at in range(n - 1, n + 3)}
            value = add_product(padded(flow_part, (run, 0), row), flat(*faces.mx(n - 1), row), mids[n])
            put_padded(*flow(n - 1, run), row, value)
            for at in range(n, n + 2):
                value = faces.flow(
                    row, at, mids[at], padded(*adjoint2(at, run), row, 1), padded(*adjoint2(at, run), row, -1),
                    mids[at - 1], mids[at + 1],
                )
                put_padded(*flow(at, run), row, value)
        for row in chunks(ny):
            put_adjoint1(
                row, flow, adjoint2, run, range(n - 2, n + 1),
                lambda at: flat(weight_b, (run, at - (n - 2)), row), adjoint1,
            )
        for row in chunks(ny):
            for at in range(n - 3, n):
                total = add_product(
                    flat(sum_x, (at - (n - 3),), row), step_x(adjoint1, run, at, row), step_x(chem0, run, at, row)
                )
                if at == n - 1:
                    total = add_product(total, step_x(adjoint2, run, at, row), step_x(chem1, run, at, row))
                put_flat(sum_x, (at - (n - 3),), row, total)
            for at in range(n - 2, n):
                to = (at - (n - 2),)
                put_padded(sum_y, to, row, add_product(
                    padded(sum_y, to, row), step_y(adjoint1, run, at, row), step_y(chem0, run, at, row)
                ))
                put_flat(sum_z, to, row, add_product(
                    flat(sum_z, to, row), step_z(adjoint1, run, at, row), flat(step_z_b, (run, *to), row)
                ))
        return carry

    for run in range(runs):
        one_run(run, 0)
    for row in chunks(ny):
        for at in range(n - 2):
            value = flat(part, (at,), row)
            if at == n - 3:
                value = each(lambda a, b: a - 0.5 * b, value, flat(sum_x, (0,), row))
            put_plain(result, (place[at],), row, value)
        for at in range(2):
            sides = flat(sum_z, (at,), row)
            value = each(
                lambda a, b, c, d, e, f: -0.5 * ((a + b) + (c + d) + (e + f)),
                flat(sum_x, (at,), row), flat(sum_x, (at + 1,), row),
                padded(sum_y, (at,), row), padded(sum_y, (at,), row, -1), sides, before_z(sides),
            )
            put_plain(result, (place[n - 2 + at],), row, value)


def counts(at):
    return (at ^ (at >> 1)) & 1


def at_wrap(cores):
    at = lax.axis_index("gx")
    return jnp.logical_or(at < cores, at >= lax.axis_size("gx") - cores)


def choose(which, first, second):
    return each(lambda a, b: jnp.where(which, a, b), first, second)


def misfit_kernel(share, far, misfit):
    misfit[0] = (share[...] + far[...])[0, 0]


def call(kernel, outs, scratch, args, flops, scalar=None):
    moved = 4 * (sum(a.size for a in args) + sum(math.prod(o) for o in outs))
    return pl.pallas_call(
        kernel,
        out_shape=tuple(jax.ShapeDtypeStruct(o, jnp.float32) for o in outs),
        in_specs=[VMEM] * len(args),
        out_specs=tuple(SMEM if at == scalar else VMEM for at in range(len(outs))),
        scratch_shapes=[pltpu.VMEM(s, jnp.float32) for s in scratch],
        compiler_params=pltpu.CompilerParams(vmem_limit_bytes=16 * 1024 * 1024),
        cost_estimate=pl.CostEstimate(flops=flops, bytes_accessed=moved, transcendentals=0),
    )(*args)


def on_device(initial, observed, mobility):
    runs, n, ny, nz = initial.shape
    blocks = nz // LANES
    count = lax.axis_size("gx")
    over_chips = [(i, (i - 1 + 2 * (i % 2)) % count) for i in range(count)]
    over_cores = [(i, i ^ 1) for i in range(count)]
    cell = ny * nz

    def neighbours(to_chip, to_core):
        of_core = lax.ppermute(to_core, "gx", over_cores)
        return lax.ppermute(to_chip, "gx", over_chips), of_core

    def lies(*lead):
        return (*lead, blocks, ny, LANES)

    def lies_padded(*lead):
        return (*lead, blocks, ny + 2 * PAD, LANES)

    if n == 4:
        near = (initial, initial)
    else:
        near = [lax.dynamic_slice_in_dim(initial, at, 4, 1) for at in (either(0, n - 4), either(n - 4, 0))]
    of_chip, of_core = neighbours(*near)
    conc, mob, to_chip, to_core = call(
        own_kernel, (lies_padded(runs, n), lies_padded(n), lies(3), lies(3)), (), (initial, mobility),
        runs * n * cell,
    )
    m_chip, m_core = neighbours(to_chip, to_core)
    conc_core, chem0_a, *faces_a = call(
        core_kernel,
        (
            lies_padded(runs, 4), lies_padded(runs, n + 2),
            lies(n + 2), lies(n + 2), lies(n + 2), lies(n + 2), lies(n + 2), lies(n + 1),
        ),
        (lies_padded(3),),
        (of_core, m_core, conc, mob),
        20 * runs * (n + 2) * cell,
    )
    conc_chip, chem0_b, state1_a, chem1_a, adjoint2_a, squares = call(
        chip_kernel,
        (
            lies_padded(runs, 4), lies_padded(runs, 4), lies_padded(runs, n + 1),
            lies_padded(runs, n - 1), lies_padded(runs, n - 3), (CHUNK, LANES),
        ),
        (),
        (of_chip, conc, conc_core, chem0_a, observed, *faces_a),
        60 * runs * (n - 1) * cell,
    )
    *faces_b, state1_b, chem1_b, adjoint2_b, first, to_core, to_chip, share, gift = call(
        forward_kernel,
        (
            lies(3), lies(2), lies(2), lies(2), lies(2), lies(3),
            lies_padded(runs, 3), lies_padded(runs, 3), lies_padded(runs, 3),
            lies(runs, 3), lies(runs, 3), lies(runs, 3), (ROWS, LANES), (ROWS, LANES),
        ),
        (lies_padded(3), (CHUNK, LANES)),
        (m_chip, mob, conc, conc_chip, chem0_a, chem0_b, state1_a, chem1_a, adjoint2_a, squares, observed, *faces_a),
        60 * runs * 3 * cell,
    )
    faces = (*faces_a, *faces_b)
    groups = lax.axis_size("group")

    def swap(value, partner):
        pairs = []
        for group in range(groups):
            for at in range(count):
                to = partner(at)
                aim = min(group ^ 1, groups - 1) * count + at if to is None else group * count + to
                pairs.append((group * count + at, aim))
        return lax.ppermute(value, ("group", "gx"), pairs)

    ends = {0: count - 1, count - 1: 0}
    of_first = swap(first, lambda at: ends.get(at, None if at in (1, count - 2) else at ^ 1))
    of_chip = swap(to_chip, lambda at: None if at in ends else dict(over_chips)[at])
    of_core = lax.ppermute(to_core, "gx", over_cores)

    def hop(value, apart):
        return swap(value, lambda at: at ^ apart if counts(at) else None)

    def hops(value, bits):
        aparts = [sum(2 << bit for at, bit in enumerate(bits) if which >> at & 1) for which in range(1, 1 << len(bits))]
        return [hop(value, apart) for apart in aparts]

    share = share + lax.ppermute(gift, "gx", over_cores)
    upper = range(count.bit_length() - 3, 0, -1)
    steps = [upper[at : at + 2] for at in range(0, len(upper), 2)]
    fars = hops(share, steps[0])
    flow_a, flow_part, adjoint1_a, weight_b, step_z_b, part, *sums_b, share = call(
        early_kernel,
        (
            lies_padded(runs, n + 1), lies_padded(runs, 1), lies_padded(runs, n - 1), lies(runs, 3), lies(runs, 2),
            lies(n - 2), lies(2), lies(2), lies(2), (ROWS, LANES),
        ),
        (lies_padded(runs, 3), lies(n), lies_padded(n), lies(n)),
        (of_first, of_core, *faces, chem0_a, chem0_b, state1_a, state1_b, chem1_a, chem1_b, adjoint2_a, adjoint2_b, share),
        60 * runs * n * cell,
    )
    for bits in steps[1:]:
        share = share + sum(fars)
        fars = hops(share, bits)
    share = share + sum(fars)
    share = share + lax.ppermute(share, "gx", over_cores)
    far = lax.ppermute(share, "gx", [(at, at ^ 3) for at in range(count)])
    result, share = call(
        late_kernel,
        ((n, ny, nz), (ROWS, LANES)),
        (
            lies_padded(runs, 3), lies_padded(runs, 3), lies_padded(runs, 3),
            lies(3), lies_padded(2), lies(2),
        ),
        (
            of_first, of_chip, *faces, chem0_a, chem0_b, chem1_b, adjoint2_b, flow_a, flow_part, adjoint1_a,
            weight_b, step_z_b, part, *sums_b, share,
        ),
        60 * runs * 3 * cell,
    )
    (misfit,) = call(misfit_kernel, ((1,),), (), (share, far), 1, scalar=0)
    return (result, misfit)


def solution(mesh):
    placed = (
        P("group", "gx", None, None),
        P("group", "gx", None, None),
        P(("group", "gx"), None, None),
    )
    return jax.shard_map(
        on_device,
        mesh=mesh,
        in_specs=placed,
        out_specs=(P(("group", "gx"), None, None), P("group")),
        check_vma=False,
    )
```

```python
import functools
import math

import jax
import jax.numpy as jnp
from jax import lax
from jax.experimental import pallas as pl
from jax.experimental.pallas import tpu as pltpu
from jax.sharding import PartitionSpec as P

stiffness = 0.5
time_step = 0.005
VMEM = pl.BlockSpec(memory_space=pltpu.VMEM)
SMEM = pl.BlockSpec(memory_space=pltpu.SMEM)
LANES = 128
ROWS = 8
PAD = ROWS
CHUNK = 8


def chunks(ny):
    return range(0, ny, CHUNK)


def plain(ref, lead, row):
    return [
        ref[(*lead, pl.ds(row, CHUNK), pl.ds(at, LANES))] for at in range(0, ref.shape[-1], LANES)
    ]


def put_plain(ref, lead, row, value):
    for block, part in enumerate(value):
        ref[(*lead, pl.ds(row, CHUNK), pl.ds(block * LANES, LANES))] = part


def flat(ref, lead, row):
    return [ref[(*lead, block, pl.ds(row, CHUNK))] for block in range(ref.shape[-3])]


def put_flat(ref, lead, row, value):
    for block, part in enumerate(value):
        ref[(*lead, block, pl.ds(row, CHUNK))] = part


def padded(ref, lead, row, shift=0):
    return [ref[(*lead, block, pl.ds(PAD + row + shift, CHUNK))] for block in range(ref.shape[-3])]


def put_padded(ref, lead, row, value):
    ny = ref.shape[-2] - 2 * PAD
    for block, part in enumerate(value):
        ref[(*lead, block, pl.ds(PAD + row, CHUNK))] = part
        if row == 0:
            ref[(*lead, block, pl.ds(PAD + ny, 1))] = part[:1]
        if row + CHUNK == ny:
            ref[(*lead, block, pl.ds(PAD - 1, 1))] = part[CHUNK - 1 :]


def lane():
    return lax.broadcasted_iota(jnp.int32, (CHUNK, LANES), 1)


def after_z(value):
    turned = [pltpu.roll(part, LANES - 1, 1) for part in value]
    turned.append(turned[0])
    edge = lane() == LANES - 1
    return [jnp.where(edge, turned[at + 1], turned[at]) for at in range(len(value))]


def before_z(value):
    turned = [pltpu.roll(part, 1, 1) for part in value]
    edge = lane() == 0
    return [jnp.where(edge, turned[at - 1], turned[at]) for at in range(len(value))]


def side():
    return lax.rem(lax.axis_index("gx"), 2)


def either(first, second):
    return first + side() * (second - first)


class Line:
    def __init__(self, *parts):
        self.parts = parts

    def __call__(self, at, *lead):
        for ref, first, last in self.parts:
            if first <= at <= last:
                return ref, (*lead, at - first)
        raise IndexError(at)


def each(function, *values):
    return [function(*parts) for parts in zip(*values)]


def beside(low, high, up, down, mid):
    return each(
        lambda a, b, c, d, e, f: (a + b) + (c + d) + (e + f),
        low, high, up, down, after_z(mid), before_z(mid),
    )


def potential(low, mid, high, up, down):
    return each(
        lambda c, total: c * (c * c + (6.0 * stiffness - 1.0)) - stiffness * total,
        mid, beside(low, high, up, down, mid),
    )


class Faces:
    def __init__(self, n, refs):
        mx_a, my_a, my_low_a, mz_a, mz_low_a, all_a, *late = refs
        two = lambda ref, first, last, at: ((ref, first, last), *(((late[at], last + 1, n + 1),) if late else ()))
        self.mx = Line(*two(mx_a, -3, n - 2, 0))
        self.my = Line(*two(my_a, -2, n - 1, 1))
        self.my_low = Line(*two(my_low_a, -2, n - 1, 2))
        self.mz = Line(*two(mz_a, -2, n - 1, 3))
        self.mz_low = Line(*two(mz_low_a, -2, n - 1, 4))
        self.all = Line(*two(all_a, -2, n - 2, 5))

    def flow(self, row, at, mid, up, down, low=None, high=None):
        total = each(
            lambda a, b, c, d, e, u, v, w, x, y: (a * u + b * v) + (c * w + d * x) - e * y,
            flat(*self.my(at), row), flat(*self.my_low(at), row), flat(*self.mz(at), row),
            flat(*self.mz_low(at), row), flat(*self.all(at), row), up, down, after_z(mid), before_z(mid), mid,
        )
        if low is not None:
            total = add_product(total, flat(*self.mx(at - 1), row), low)
        if high is not None:
            total = add_product(total, flat(*self.mx(at), row), high)
        return total


def add_product(total, a, b):
    return each(lambda t, x, y: t + x * y, total, a, b)


def sub(a, b):
    return each(lambda x, y: x - y, a, b)


def own_kernel(initial, mobility, conc, mob, to_chip, to_core):
    runs, n, ny, _ = initial.shape
    place = [either(n - 1 - at, at) for at in range(n)]

    def one_run(run, carry):
        for row in chunks(ny):
            for at in range(n):
                put_padded(conc, (run, at), row, plain(initial, (run, place[at]), row))
        return carry

    for run in range(runs):
        one_run(run, 0)
    for row in chunks(ny):
        for at in range(n):
            value = plain(mobility, (place[at],), row)
            put_padded(mob, (at,), row, value)
            if at < 3:
                put_flat(to_core, (at,), row, value)
            if at >= n - 3:
                put_flat(to_chip, (n - 1 - at,), row, value)


def mean(a, b):
    return 0.5 * (a + b)


def put_faces(row, mob, places, faces):
    for at in places:
        mid = padded(*mob(at), row)
        put_flat(*faces.my(at), row, each(mean, mid, padded(*mob(at), row, 1)))
        put_flat(*faces.my_low(at), row, each(mean, mid, padded(*mob(at), row, -1)))
        put_flat(*faces.mz(at), row, each(mean, mid, after_z(mid)))
        put_flat(*faces.mz_low(at), row, each(mean, mid, before_z(mid)))


def put_all(row, faces, places):
    for at in places:
        put_flat(*faces.all(at), row, each(
            lambda a, b, c, d, e, f: (a + b) + (c + d) + (e + f),
            flat(*faces.mx(at - 1), row), flat(*faces.mx(at), row), flat(*faces.my(at), row),
            flat(*faces.my_low(at), row), flat(*faces.mz(at), row), flat(*faces.mz_low(at), row),
        ))


def put_potential(row, field, run, places, target):
    mids = {at: padded(*field(at, run), row) for at in range(places[0] - 1, places[-1] + 2)}
    for at in places:
        value = potential(
            mids[at - 1], mids[at], mids[at + 1],
            padded(*field(at, run), row, 1), padded(*field(at, run), row, -1),
        )
        put_padded(*target(at, run), row, value)


def put_step(row, faces, chem, state, run, places, target):
    mids = {at: padded(*chem(at, run), row) for at in range(places[0] - 1, places[-1] + 2)}
    for at in places:
        flow = faces.flow(
            row, at, mids[at], padded(*chem(at, run), row, 1), padded(*chem(at, run), row, -1),
            mids[at - 1], mids[at + 1],
        )
        value = each(lambda a, b: a + time_step * b, padded(*state(at, run), row), flow)
        target(at, value)


def put_miss(row, runs, observed, place, run, at, value, adjoint2):
    miss = sub(value, plain(observed, (run, place[at]), row))
    adjoint = each(lambda a: a * (1.0 / runs), miss)
    put_padded(*adjoint2(at, run), row, adjoint)
    return adjoint, sum(part * part for part in miss)


def core_kernel(of_core, m_core, conc_own, mob_own, conc_core, chem0, mx, my, my_low, mz, mz_low, m_all, rim):
    runs, n = conc_own.shape[:2]
    ny = of_core.shape[2]
    mob = Line((rim, -3, -1), (mob_own, 0, n - 1))
    faces = Faces(n, (mx, my, my_low, mz, mz_low, m_all))
    for row in chunks(ny):
        for at in range(3):
            put_padded(rim, (2 - at,), row, flat(m_core, (at,), row))
    for row in chunks(ny):
        mids = [padded(*mob(at), row) for at in range(-3, n)]
        for at in range(n + 2):
            put_flat(mx, (at,), row, each(mean, mids[at], mids[at + 1]))
        put_faces(row, mob, range(-2, n), faces)
    for row in chunks(ny):
        put_all(row, faces, range(-2, n - 1))
    place = [either(at, 3 - at) for at in range(4)]
    conc = Line((conc_core, -4, -1), (conc_own, 0, n - 1))

    def one_run(run, carry):
        for row in chunks(ny):
            for at in range(4):
                put_padded(conc_core, (run, 3 - at), row, plain(of_core, (run, place[at]), row))
        for row in chunks(ny):
            put_potential(row, conc, run, range(-3, n - 1), Line((chem0, -3, n - 2)))
        return carry

    for run in range(runs):
        one_run(run, 0)


def chip_kernel(
    of_chip, conc_own, conc_core, chem0_a, observed, mx, my, my_low, mz, mz_low, m_all,
    conc_chip, chem0_b, state1_a, chem1_a, adjoint2_a, squares,
):
    runs, n = conc_own.shape[:2]
    ny = observed.shape[2]
    faces = Faces(n, (mx, my, my_low, mz, mz_low, m_all))
    message = [either(3 - at, at) for at in range(4)]
    place = [either(n - 1 - at, at) for at in range(n)]
    conc = Line((conc_core, -4, -1), (conc_own, 0, n - 1), (conc_chip, n, n + 3))
    chem0 = Line((chem0_a, -3, n - 2), (chem0_b, n - 1, n + 2))
    state1 = Line((state1_a, -2, n - 2))
    chem1 = Line((chem1_a, -1, n - 3))
    adjoint2 = Line((adjoint2_a, 0, n - 4))
    squares[...] = jnp.zeros_like(squares)

    def one_run(run, carry):
        for row in chunks(ny):
            for at in range(4):
                put_padded(conc_chip, (run, at), row, plain(of_chip, (run, message[at]), row))
        for row in chunks(ny):
            put_potential(row, conc, run, range(n - 1, n + 3), chem0)
        for row in chunks(ny):
            put_step(
                row, faces, chem0, conc, run, range(-2, n - 1),
                lambda at, value: put_padded(*state1(at, run), row, value),
            )
        for row in chunks(ny):
            put_potential(row, state1, run, range(-1, n - 2), chem1)
        for row in chunks(ny):

            def target(at, value):
                squares[...] += put_miss(row, runs, observed, place, run, at, value, adjoint2)[1]

            put_step(row, faces, chem1, state1, run, range(0, n - 3), target)
        return carry

    for run in range(runs):
        one_run(run, 0)


def forward_kernel(
    m_chip, mob_own, conc_own, conc_chip, chem0_a, chem0_b, state1_a, chem1_a, adjoint2_a, squares, observed,
    mx_a, my_a, my_low_a, mz_a, mz_low_a, all_a,
    mx_b, my_b, my_low_b, mz_b, mz_low_b, all_b, state1_b, chem1_b, adjoint2_b, to_core, to_chip, share, rim, total,
):
    runs, n = conc_own.shape[:2]
    ny = observed.shape[2]
    faces = Faces(n, (mx_a, my_a, my_low_a, mz_a, mz_low_a, all_a, mx_b, my_b, my_low_b, mz_b, mz_low_b, all_b))
    mob = Line((mob_own, 0, n - 1), (rim, n, n + 2))
    place = [either(n - 1 - at, at) for at in range(n)]
    conc = Line((conc_own, 0, n - 1), (conc_chip, n, n + 3))
    chem0 = Line((chem0_a, -3, n - 2), (chem0_b, n - 1, n + 2))
    state1 = Line((state1_a, -2, n - 2), (state1_b, n - 1, n + 1))
    chem1 = Line((chem1_a, -1, n - 3), (chem1_b, n - 2, n))
    adjoint2 = Line((adjoint2_a, 0, n - 4), (adjoint2_b, n - 3, n - 1))
    for row in chunks(ny):
        for at in range(3):
            put_padded(rim, (at,), row, flat(m_chip, (at,), row))
    for row in chunks(ny):
        mids = [padded(*mob(at), row) for at in range(n - 1, n + 3)]
        for at in range(3):
            put_flat(mx_b, (at,), row, each(mean, mids[at], mids[at + 1]))
        put_faces(row, mob, range(n, n + 2), faces)
    for row in chunks(ny):
        put_all(row, faces, range(n - 1, n + 2))
    total[...] = squares[...]

    def one_run(run, carry):
        for row in chunks(ny):
            put_step(
                row, faces, chem0, conc, run, range(n - 1, n + 2),
                lambda at, value: put_padded(*state1(at, run), row, value),
            )
        for row in chunks(ny):
            put_potential(row, state1, run, range(n - 2, n + 1), chem1)
        for row in chunks(ny):

            def target(at, value):
                adjoint, square = put_miss(row, runs, observed, place, run, at, value, adjoint2)
                total[...] += square
                put_flat(to_chip, (run, n - 1 - at), row, adjoint)
                if at < 3:
                    put_flat(to_core, (run, at), row, adjoint)

            put_step(row, faces, chem1, state1, run, range(n - 3, n), target)
            for at in range(min(3, n - 3)):
                put_flat(to_core, (run, at), row, padded(*adjoint2(at, run), row))
        return carry

    for run in range(runs):
        one_run(run, 0)
    columns = (0.5 / runs) * jnp.sum(total[...], axis=0, keepdims=True)
    mine = jnp.broadcast_to(jnp.sum(columns, axis=1, keepdims=True), share.shape)
    sums = counts(lax.axis_index("gx")) == 1
    share[...] = jnp.where(sums, mine, 0.0)
    to_core[0, 0, 0, ny:] = jnp.where(sums, 0.0, mine)


def put_adjoint1(row, flow, adjoint2, run, places, weight, target):
    mids = {at: padded(*flow(at, run), row) for at in range(places[0] - 1, places[-1] + 2)}
    for at in places:
        total = beside(
            mids[at - 1], mids[at + 1], padded(*flow(at, run), row, 1), padded(*flow(at, run), row, -1), mids[at]
        )
        value = each(
            lambda a, w, f, t: a + w * f - (time_step * stiffness) * t,
            padded(*adjoint2(at, run), row), weight(at), mids[at], total,
        )
        put_padded(*target(at, run), row, value)


def slope(state):
    return each(lambda c: time_step * (3.0 * c * c + (6.0 * stiffness - 1.0)), state)


def step_x(field, run, at, row):
    return sub(padded(*field(at + 1, run), row), padded(*field(at, run), row))


def step_y(field, run, at, row):
    return sub(padded(*field(at, run), row, 1), padded(*field(at, run), row))


def step_z(field, run, at, row):
    mid = padded(*field(at, run), row)
    return sub(after_z(mid), mid)


def early_kernel(
    of_core, mx_a, my_a, my_low_a, mz_a, mz_low_a, all_a, mx_b, my_b, my_low_b, mz_b, mz_low_b, all_b,
    chem0_a, chem0_b, state1_a, state1_b, chem1_a, chem1_b, adjoint2_a, adjoint2_b,
    share_in, flow_a, flow_part, adjoint1_a, weight_b, step_z_b, part, sum_x_b, sum_y_b, sum_z_b, share,
    rim, sum_x, sum_y, sum_z,
):
    share[...] = share_in[...]
    runs = of_core.shape[0]
    n = part.shape[0] + 2
    ny = part.shape[-2]
    faces = Faces(n, (mx_a, my_a, my_low_a, mz_a, mz_low_a, all_a, mx_b, my_b, my_low_b, mz_b, mz_low_b, all_b))
    chem0 = Line((chem0_a, -3, n - 2), (chem0_b, n - 1, n + 2))
    state1 = Line((state1_a, -2, n - 2), (state1_b, n - 1, n + 1))
    chem1 = Line((chem1_a, -1, n - 3), (chem1_b, n - 2, n))
    adjoint2 = Line((rim, -3, -1), (adjoint2_a, 0, n - 4), (adjoint2_b, n - 3, n - 1))
    flow = Line((flow_a, -2, n - 2), (flow_part, n - 1, n - 1))
    adjoint1 = Line((adjoint1_a, -1, n - 3))
    for sums in (sum_x, sum_y, sum_z):
        sums[...] = jnp.zeros_like(sums)

    def one_run(run, carry):
        for row in chunks(ny):
            for at in range(3):
                put_padded(rim, (run, 2 - at), row, flat(of_core, (run, at), row))
        for row in chunks(ny):
            mids = {at: padded(*adjoint2(at, run), row) for at in range(-3, n)}
            for at in range(-2, n):
                value = faces.flow(
                    row, at, mids[at], padded(*adjoint2(at, run), row, 1), padded(*adjoint2(at, run), row, -1),
                    mids[at - 1], mids.get(at + 1),
                )
                put_padded(*flow(at, run), row, value)
        for row in chunks(ny):
            put_adjoint1(
                row, flow, adjoint2, run, range(-1, n - 2),
                lambda at: slope(padded(*state1(at, run), row)), adjoint1,
            )
            for at in range(n - 2, n + 1):
                put_flat(weight_b, (run, at - (n - 2)), row, slope(padded(*state1(at, run), row)))
        for row in chunks(ny):
            for at in range(-1, n - 1):
                total = add_product(
                    flat(sum_x, (at + 1,), row), step_x(adjoint2, run, at, row), step_x(chem1, run, at, row)
                )
                if at < n - 3:
                    total = add_product(total, step_x(adjoint1, run, at, row), step_x(chem0, run, at, row))
                put_flat(sum_x, (at + 1,), row, total)
            for at in range(n):
                total_y = add_product(
                    padded(sum_y, (at,), row), step_y(adjoint2, run, at, row), step_y(chem1, run, at, row)
                )
                total_z = add_product(
                    flat(sum_z, (at,), row), step_z(adjoint2, run, at, row), step_z(chem1, run, at, row)
                )
                slant = step_z(chem0, run, at, row)
                if at < n - 2:
                    total_y = add_product(total_y, step_y(adjoint1, run, at, row), step_y(chem0, run, at, row))
                    total_z = add_product(total_z, step_z(adjoint1, run, at, row), slant)
                else:
                    put_flat(step_z_b, (run, at - (n - 2)), row, slant)
                put_padded(sum_y, (at,), row, total_y)
                put_flat(sum_z, (at,), row, total_z)
        return carry

    for run in range(runs):
        one_run(run, 0)
    for row in chunks(ny):
        for at in range(n - 2):
            sides = flat(sum_z, (at,), row)
            value = each(
                lambda a, b, c, d, e: -0.5 * ((a + b) + (c + d) + e),
                padded(sum_y, (at,), row), padded(sum_y, (at,), row, -1), sides, before_z(sides),
                flat(sum_x, (at,), row),
            )
            if at < n - 3:
                value = each(lambda a, b: a - 0.5 * b, value, flat(sum_x, (at + 1,), row))
            put_flat(part, (at,), row, value)
        for at in range(2):
            put_flat(sum_x_b, (at,), row, flat(sum_x, (n - 2 + at,), row))
            put_flat(sum_y_b, (at,), row, padded(sum_y, (n - 2 + at,), row))
            put_flat(sum_z_b, (at,), row, flat(sum_z, (n - 2 + at,), row))


def late_kernel(
    of_chip, mx_a, my_a, my_low_a, mz_a, mz_low_a, all_a, mx_b, my_b, my_low_b, mz_b, mz_low_b, all_b,
    chem0_a, chem0_b, chem1_b, adjoint2_b, flow_a, flow_part, adjoint1_a, weight_b, step_z_b,
    part, sum_x_b, sum_y_b, sum_z_b, share_in, result, share, rim, flow_b, adjoint1_b, sum_x, sum_y, sum_z,
):
    share[...] = share_in[...]
    runs = of_chip.shape[0]
    n, ny, _ = result.shape
    faces = Faces(n, (mx_a, my_a, my_low_a, mz_a, mz_low_a, all_a, mx_b, my_b, my_low_b, mz_b, mz_low_b, all_b))
    place = [either(n - 1 - at, at) for at in range(n)]
    chem0 = Line((chem0_a, -3, n - 2), (chem0_b, n - 1, n + 2))
    chem1 = Line((chem1_b, n - 2, n))
    adjoint2 = Line((adjoint2_b, n - 3, n - 1), (rim, n, n + 2))
    flow = Line((flow_a, -2, n - 2), (flow_b, n - 1, n + 1))
    adjoint1 = Line((adjoint1_a, -1, n - 3), (adjoint1_b, n - 2, n))
    for row in chunks(ny):
        for at in range(2):
            put_flat(sum_x, (at,), row, flat(sum_x_b, (at,), row))
            put_padded(sum_y, (at,), row, flat(sum_y_b, (at,), row))
            put_flat(sum_z, (at,), row, flat(sum_z_b, (at,), row))
    sum_x[2] = jnp.zeros_like(sum_x[2])

    def one_run(run, carry):
        for row in chunks(ny):
            for at in range(3):
                put_padded(rim, (run, at), row, flat(of_chip, (run, at), row))
        for row in chunks(ny):
            mids = {at: padded(*adjoint2(at, run), row) for at in range(n - 1, n + 3)}
            value = add_product(padded(flow_part, (run, 0), row), flat(*faces.mx(n - 1), row), mids[n])
            put_padded(*flow(n - 1, run), row, value)
            for at in range(n, n + 2):
                value = faces.flow(
                    row, at, mids[at], padded(*adjoint2(at, run), row, 1), padded(*adjoint2(at, run), row, -1),
                    mids[at - 1], mids[at + 1],
                )
                put_padded(*flow(at, run), row, value)
        for row in chunks(ny):
            put_adjoint1(
                row, flow, adjoint2, run, range(n - 2, n + 1),
                lambda at: flat(weight_b, (run, at - (n - 2)), row), adjoint1,
            )
        for row in chunks(ny):
            for at in range(n - 3, n):
                total = add_product(
                    flat(sum_x, (at - (n - 3),), row), step_x(adjoint1, run, at, row), step_x(chem0, run, at, row)
                )
                if at == n - 1:
                    total = add_product(total, step_x(adjoint2, run, at, row), step_x(chem1, run, at, row))
                put_flat(sum_x, (at - (n - 3),), row, total)
            for at in range(n - 2, n):
                to = (at - (n - 2),)
                put_padded(sum_y, to, row, add_product(
                    padded(sum_y, to, row), step_y(adjoint1, run, at, row), step_y(chem0, run, at, row)
                ))
                put_flat(sum_z, to, row, add_product(
                    flat(sum_z, to, row), step_z(adjoint1, run, at, row), flat(step_z_b, (run, *to), row)
                ))
        return carry

    for run in range(runs):
        one_run(run, 0)
    for row in chunks(ny):
        for at in range(n - 2):
            value = flat(part, (at,), row)
            if at == n - 3:
                value = each(lambda a, b: a - 0.5 * b, value, flat(sum_x, (0,), row))
            put_plain(result, (place[at],), row, value)
        for at in range(2):
            sides = flat(sum_z, (at,), row)
            value = each(
                lambda a, b, c, d, e, f: -0.5 * ((a + b) + (c + d) + (e + f)),
                flat(sum_x, (at,), row), flat(sum_x, (at + 1,), row),
                padded(sum_y, (at,), row), padded(sum_y, (at,), row, -1), sides, before_z(sides),
            )
            put_plain(result, (place[n - 2 + at],), row, value)


def counts(at):
    return (at ^ (at >> 1)) & 1


def misfit_kernel(core, other_core, across, other_across, misfit):
    misfit[0] = ((core[...] + other_core[...]) + (across[...] + other_across[...]))[0, 0]


def call(kernel, outs, scratch, args, flops, scalar=None):
    moved = 4 * (sum(a.size for a in args) + sum(math.prod(o) for o in outs))
    return pl.pallas_call(
        kernel,
        out_shape=tuple(jax.ShapeDtypeStruct(o, jnp.float32) for o in outs),
        in_specs=[VMEM] * len(args),
        out_specs=tuple(SMEM if at == scalar else VMEM for at in range(len(outs))),
        scratch_shapes=[pltpu.VMEM(s, jnp.float32) for s in scratch],
        compiler_params=pltpu.CompilerParams(vmem_limit_bytes=16 * 1024 * 1024),
        cost_estimate=pl.CostEstimate(flops=flops, bytes_accessed=moved, transcendentals=0),
    )(*args)


def on_device(initial, observed, mobility):
    runs, n, ny, nz = initial.shape
    blocks = nz // LANES
    count = lax.axis_size("gx")
    over_chips = [(i, (i - 1 + 2 * (i % 2)) % count) for i in range(count)]
    over_cores = [(i, i ^ 1) for i in range(count)]
    cell = ny * nz

    def neighbours(to_chip, to_core):
        of_core = lax.ppermute(to_core, "gx", over_cores)
        return lax.ppermute(to_chip, "gx", over_chips), of_core

    def lies(*lead):
        return (*lead, blocks, ny, LANES)

    def lies_padded(*lead):
        return (*lead, blocks, ny + 2 * PAD, LANES)

    if n == 4:
        near = (initial, initial)
    else:
        near = [lax.dynamic_slice_in_dim(initial, at, 4, 1) for at in (either(0, n - 4), either(n - 4, 0))]
    of_chip, of_core = neighbours(*near)
    conc, mob, to_chip, to_core = call(
        own_kernel, (lies_padded(runs, n), lies_padded(n), lies(3), lies(3)), (), (initial, mobility),
        runs * n * cell,
    )
    m_chip, m_core = neighbours(to_chip, to_core)
    conc_core, chem0_a, *faces_a = call(
        core_kernel,
        (
            lies_padded(runs, 4), lies_padded(runs, n + 2),
            lies(n + 2), lies(n + 2), lies(n + 2), lies(n + 2), lies(n + 2), lies(n + 1),
        ),
        (lies_padded(3),),
        (of_core, m_core, conc, mob),
        20 * runs * (n + 2) * cell,
    )
    conc_chip, chem0_b, state1_a, chem1_a, adjoint2_a, squares = call(
        chip_kernel,
        (
            lies_padded(runs, 4), lies_padded(runs, 4), lies_padded(runs, n + 1),
            lies_padded(runs, n - 1), lies_padded(runs, n - 3), (CHUNK, LANES),
        ),
        (),
        (of_chip, conc, conc_core, chem0_a, observed, *faces_a),
        60 * runs * (n - 1) * cell,
    )
    *faces_b, state1_b, chem1_b, adjoint2_b, to_core, to_chip, share = call(
        forward_kernel,
        (
            lies(3), lies(2), lies(2), lies(2), lies(2), lies(3),
            lies_padded(runs, 3), lies_padded(runs, 3), lies_padded(runs, 3),
            (runs, 3, blocks, ny + ROWS, LANES), lies(runs, 3), (ROWS, LANES),
        ),
        (lies_padded(3), (CHUNK, LANES)),
        (m_chip, mob, conc, conc_chip, chem0_a, chem0_b, state1_a, chem1_a, adjoint2_a, squares, observed, *faces_a),
        60 * runs * 3 * cell,
    )
    faces = (*faces_a, *faces_b)
    of_chip, of_core = neighbours(to_chip, to_core)
    groups = lax.axis_size("group")

    def target(group, at, apart):
        if counts(at):
            return group * count + (at ^ apart)
        return min(group ^ 1, groups - 1) * count + at

    def hop(value, apart):
        pairs = [
            (group * count + at, target(group, at, apart)) for group in range(groups) for at in range(count)
        ]
        return lax.ppermute(value, ("group", "gx"), pairs)

    def hops(value, bits):
        aparts = [sum(2 << bit for at, bit in enumerate(bits) if which >> at & 1) for which in range(1, 1 << len(bits))]
        return [hop(value, apart) for apart in aparts]

    share = share + of_core[0, 0, 0, ny:]
    upper = range(count.bit_length() - 3, 0, -1)
    steps = [upper[at : at + 2] for at in range(0, len(upper), 2)]
    fars = hops(share, steps[0])
    flow_a, flow_part, adjoint1_a, weight_b, step_z_b, part, *sums_b, share = call(
        early_kernel,
        (
            lies_padded(runs, n + 1), lies_padded(runs, 1), lies_padded(runs, n - 1), lies(runs, 3), lies(runs, 2),
            lies(n - 2), lies(2), lies(2), lies(2), (ROWS, LANES),
        ),
        (lies_padded(runs, 3), lies(n), lies_padded(n), lies(n)),
        (of_core, *faces, chem0_a, chem0_b, state1_a, state1_b, chem1_a, chem1_b, adjoint2_a, adjoint2_b, share),
        60 * runs * n * cell,
    )
    for bits in steps[1:]:
        share = share + sum(fars)
        fars = hops(share, bits)
    share = share + sum(fars)
    fars = [lax.ppermute(share, "gx", [(at, at ^ apart) for at in range(count)]) for apart in (1, 2, 3)]
    result, share = call(
        late_kernel,
        ((n, ny, nz), (ROWS, LANES)),
        (
            lies_padded(runs, 3), lies_padded(runs, 3), lies_padded(runs, 3),
            lies(3), lies_padded(2), lies(2),
        ),
        (
            of_chip, *faces, chem0_a, chem0_b, chem1_b, adjoint2_b, flow_a, flow_part, adjoint1_a,
            weight_b, step_z_b, part, *sums_b, share,
        ),
        60 * runs * 3 * cell,
    )
    (misfit,) = call(misfit_kernel, ((1,),), (), (share, *fars), 1, scalar=0)
    return (result, misfit)


def solution(mesh):
    placed = (
        P("group", "gx", None, None),
        P("group", "gx", None, None),
        P(("group", "gx"), None, None),
    )
    return jax.shard_map(
        on_device,
        mesh=mesh,
        in_specs=placed,
        out_specs=(P(("group", "gx"), None, None), P("group")),
        check_vma=False,
    )
```

```python
import functools
import math

import jax
import jax.numpy as jnp
from jax import lax
from jax.experimental import pallas as pl
from jax.experimental.pallas import tpu as pltpu
from jax.sharding import PartitionSpec as P

stiffness = 0.5
time_step = 0.005
VMEM = pl.BlockSpec(memory_space=pltpu.VMEM)
SMEM = pl.BlockSpec(memory_space=pltpu.SMEM)
LANES = 128
ROWS = 8
PAD = ROWS
CHUNK = 8


def chunks(ny):
    return range(0, ny, CHUNK)


def plain(ref, lead, row):
    return [
        ref[(*lead, pl.ds(row, CHUNK), pl.ds(at, LANES))] for at in range(0, ref.shape[-1], LANES)
    ]


def put_plain(ref, lead, row, value):
    for block, part in enumerate(value):
        ref[(*lead, pl.ds(row, CHUNK), pl.ds(block * LANES, LANES))] = part


def flat(ref, lead, row):
    return [ref[(*lead, block, pl.ds(row, CHUNK))] for block in range(ref.shape[-3])]


def put_flat(ref, lead, row, value):
    for block, part in enumerate(value):
        ref[(*lead, block, pl.ds(row, CHUNK))] = part


def padded(ref, lead, row, shift=0):
    return [ref[(*lead, block, pl.ds(PAD + row + shift, CHUNK))] for block in range(ref.shape[-3])]


def put_padded(ref, lead, row, value):
    ny = ref.shape[-2] - 2 * PAD
    for block, part in enumerate(value):
        ref[(*lead, block, pl.ds(PAD + row, CHUNK))] = part
        if row == 0:
            ref[(*lead, block, pl.ds(PAD + ny, 1))] = part[:1]
        if row + CHUNK == ny:
            ref[(*lead, block, pl.ds(PAD - 1, 1))] = part[CHUNK - 1 :]


def lane():
    return lax.broadcasted_iota(jnp.int32, (CHUNK, LANES), 1)


def after_z(value):
    turned = [pltpu.roll(part, LANES - 1, 1) for part in value]
    turned.append(turned[0])
    edge = lane() == LANES - 1
    return [jnp.where(edge, turned[at + 1], turned[at]) for at in range(len(value))]


def before_z(value):
    turned = [pltpu.roll(part, 1, 1) for part in value]
    edge = lane() == 0
    return [jnp.where(edge, turned[at - 1], turned[at]) for at in range(len(value))]


def side():
    return lax.rem(lax.axis_index("gx"), 2)


def either(first, second):
    return first + side() * (second - first)


class Line:
    def __init__(self, *parts):
        self.parts = parts

    def __call__(self, at, *lead):
        for ref, first, last in self.parts:
            if first <= at <= last:
                return ref, (*lead, at - first)
        raise IndexError(at)


def each(function, *values):
    return [function(*parts) for parts in zip(*values)]


def beside(low, high, up, down, mid):
    return each(
        lambda a, b, c, d, e, f: (a + b) + (c + d) + (e + f),
        low, high, up, down, after_z(mid), before_z(mid),
    )


def potential(low, mid, high, up, down):
    return each(
        lambda c, total: c * (c * c + (6.0 * stiffness - 1.0)) - stiffness * total,
        mid, beside(low, high, up, down, mid),
    )


class Faces:
    def __init__(self, n, refs):
        mx_a, my_a, my_low_a, mz_a, mz_low_a, all_a, *late = refs
        two = lambda ref, first, last, at: ((ref, first, last), *(((late[at], last + 1, n + 1),) if late else ()))
        self.mx = Line(*two(mx_a, -3, n - 2, 0))
        self.my = Line(*two(my_a, -2, n - 1, 1))
        self.my_low = Line(*two(my_low_a, -2, n - 1, 2))
        self.mz = Line(*two(mz_a, -2, n - 1, 3))
        self.mz_low = Line(*two(mz_low_a, -2, n - 1, 4))
        self.all = Line(*two(all_a, -2, n - 2, 5))

    def flow(self, row, at, mid, up, down, low=None, high=None):
        total = each(
            lambda a, b, c, d, e, u, v, w, x, y: (a * u + b * v) + (c * w + d * x) - e * y,
            flat(*self.my(at), row), flat(*self.my_low(at), row), flat(*self.mz(at), row),
            flat(*self.mz_low(at), row), flat(*self.all(at), row), up, down, after_z(mid), before_z(mid), mid,
        )
        if low is not None:
            total = add_product(total, flat(*self.mx(at - 1), row), low)
        if high is not None:
            total = add_product(total, flat(*self.mx(at), row), high)
        return total


def add_product(total, a, b):
    return each(lambda t, x, y: t + x * y, total, a, b)


def sub(a, b):
    return each(lambda x, y: x - y, a, b)


def own_kernel(initial, mobility, conc, mob, to_chip, to_core, same):
    runs, n, ny, _ = initial.shape
    same[...] = initial[...]
    place = [either(n - 1 - at, at) for at in range(n)]

    def one_run(run, carry):
        for row in chunks(ny):
            for at in range(n):
                put_padded(conc, (run, at), row, plain(initial, (run, place[at]), row))
        return carry

    for run in range(runs):
        one_run(run, 0)
    for row in chunks(ny):
        for at in range(n):
            value = plain(mobility, (place[at],), row)
            put_padded(mob, (at,), row, value)
            if at < 3:
                put_flat(to_core, (at,), row, value)
            if at >= n - 3:
                put_flat(to_chip, (n - 1 - at,), row, value)


def mean(a, b):
    return 0.5 * (a + b)


def put_faces(row, mob, places, faces):
    for at in places:
        mid = padded(*mob(at), row)
        put_flat(*faces.my(at), row, each(mean, mid, padded(*mob(at), row, 1)))
        put_flat(*faces.my_low(at), row, each(mean, mid, padded(*mob(at), row, -1)))
        put_flat(*faces.mz(at), row, each(mean, mid, after_z(mid)))
        put_flat(*faces.mz_low(at), row, each(mean, mid, before_z(mid)))


def put_all(row, faces, places):
    for at in places:
        put_flat(*faces.all(at), row, each(
            lambda a, b, c, d, e, f: (a + b) + (c + d) + (e + f),
            flat(*faces.mx(at - 1), row), flat(*faces.mx(at), row), flat(*faces.my(at), row),
            flat(*faces.my_low(at), row), flat(*faces.mz(at), row), flat(*faces.mz_low(at), row),
        ))


def put_potential(row, field, run, places, target):
    mids = {at: padded(*field(at, run), row) for at in range(places[0] - 1, places[-1] + 2)}
    for at in places:
        value = potential(
            mids[at - 1], mids[at], mids[at + 1],
            padded(*field(at, run), row, 1), padded(*field(at, run), row, -1),
        )
        put_padded(*target(at, run), row, value)


def put_step(row, faces, chem, state, run, places, target):
    mids = {at: padded(*chem(at, run), row) for at in range(places[0] - 1, places[-1] + 2)}
    for at in places:
        flow = faces.flow(
            row, at, mids[at], padded(*chem(at, run), row, 1), padded(*chem(at, run), row, -1),
            mids[at - 1], mids[at + 1],
        )
        value = each(lambda a, b: a + time_step * b, padded(*state(at, run), row), flow)
        target(at, value)


def put_miss(row, runs, observed, place, run, at, value, adjoint2):
    miss = sub(value, plain(observed, (run, place[at]), row))
    adjoint = each(lambda a: a * (1.0 / runs), miss)
    put_padded(*adjoint2(at, run), row, adjoint)
    return adjoint, sum(part * part for part in miss)


def core_kernel(of_core, m_core, conc_own, mob_own, conc_core, chem0, mx, my, my_low, mz, mz_low, m_all, rim):
    runs, n = conc_own.shape[:2]
    ny = of_core.shape[2]
    mob = Line((rim, -3, -1), (mob_own, 0, n - 1))
    faces = Faces(n, (mx, my, my_low, mz, mz_low, m_all))
    for row in chunks(ny):
        for at in range(3):
            put_padded(rim, (2 - at,), row, flat(m_core, (at,), row))
    for row in chunks(ny):
        mids = [padded(*mob(at), row) for at in range(-3, n)]
        for at in range(n + 2):
            put_flat(mx, (at,), row, each(mean, mids[at], mids[at + 1]))
        put_faces(row, mob, range(-2, n), faces)
    for row in chunks(ny):
        put_all(row, faces, range(-2, n - 1))
    place = [either(at, 3 - at) for at in range(4)]
    conc = Line((conc_core, -4, -1), (conc_own, 0, n - 1))

    def one_run(run, carry):
        for row in chunks(ny):
            for at in range(4):
                put_padded(conc_core, (run, 3 - at), row, plain(of_core, (run, place[at]), row))
        for row in chunks(ny):
            put_potential(row, conc, run, range(-3, n - 1), Line((chem0, -3, n - 2)))
        return carry

    for run in range(runs):
        one_run(run, 0)


def chip_kernel(
    of_chip, conc_own, conc_core, chem0_a, observed, mx, my, my_low, mz, mz_low, m_all,
    conc_chip, chem0_b, state1_a, chem1_a, adjoint2_a, squares,
):
    runs, n = conc_own.shape[:2]
    ny = observed.shape[2]
    faces = Faces(n, (mx, my, my_low, mz, mz_low, m_all))
    message = [either(3 - at, at) for at in range(4)]
    place = [either(n - 1 - at, at) for at in range(n)]
    conc = Line((conc_core, -4, -1), (conc_own, 0, n - 1), (conc_chip, n, n + 3))
    chem0 = Line((chem0_a, -3, n - 2), (chem0_b, n - 1, n + 2))
    state1 = Line((state1_a, -2, n - 2))
    chem1 = Line((chem1_a, -1, n - 3))
    adjoint2 = Line((adjoint2_a, 0, n - 4))
    squares[...] = jnp.zeros_like(squares)

    def one_run(run, carry):
        for row in chunks(ny):
            for at in range(4):
                put_padded(conc_chip, (run, at), row, plain(of_chip, (run, message[at]), row))
        for row in chunks(ny):
            put_potential(row, conc, run, range(n - 1, n + 3), chem0)
        for row in chunks(ny):
            put_step(
                row, faces, chem0, conc, run, range(-2, n - 1),
                lambda at, value: put_padded(*state1(at, run), row, value),
            )
        for row in chunks(ny):
            put_potential(row, state1, run, range(-1, n - 2), chem1)
        for row in chunks(ny):

            def target(at, value):
                squares[...] += put_miss(row, runs, observed, place, run, at, value, adjoint2)[1]

            put_step(row, faces, chem1, state1, run, range(0, n - 3), target)
        return carry

    for run in range(runs):
        one_run(run, 0)


def forward_kernel(
    m_chip, mob_own, conc_own, conc_chip, chem0_a, chem0_b, state1_a, chem1_a, adjoint2_a, squares, observed,
    mx_a, my_a, my_low_a, mz_a, mz_low_a, all_a,
    mx_b, my_b, my_low_b, mz_b, mz_low_b, all_b, state1_b, chem1_b, adjoint2_b, to_core, to_chip, share, rim, total,
):
    runs, n = conc_own.shape[:2]
    ny = observed.shape[2]
    faces = Faces(n, (mx_a, my_a, my_low_a, mz_a, mz_low_a, all_a, mx_b, my_b, my_low_b, mz_b, mz_low_b, all_b))
    mob = Line((mob_own, 0, n - 1), (rim, n, n + 2))
    place = [either(n - 1 - at, at) for at in range(n)]
    conc = Line((conc_own, 0, n - 1), (conc_chip, n, n + 3))
    chem0 = Line((chem0_a, -3, n - 2), (chem0_b, n - 1, n + 2))
    state1 = Line((state1_a, -2, n - 2), (state1_b, n - 1, n + 1))
    chem1 = Line((chem1_a, -1, n - 3), (chem1_b, n - 2, n))
    adjoint2 = Line((adjoint2_a, 0, n - 4), (adjoint2_b, n - 3, n - 1))
    for row in chunks(ny):
        for at in range(3):
            put_padded(rim, (at,), row, flat(m_chip, (at,), row))
    for row in chunks(ny):
        mids = [padded(*mob(at), row) for at in range(n - 1, n + 3)]
        for at in range(3):
            put_flat(mx_b, (at,), row, each(mean, mids[at], mids[at + 1]))
        put_faces(row, mob, range(n, n + 2), faces)
    for row in chunks(ny):
        put_all(row, faces, range(n - 1, n + 2))
    total[...] = squares[...]

    def one_run(run, carry):
        for row in chunks(ny):
            put_step(
                row, faces, chem0, conc, run, range(n - 1, n + 2),
                lambda at, value: put_padded(*state1(at, run), row, value),
            )
        for row in chunks(ny):
            put_potential(row, state1, run, range(n - 2, n + 1), chem1)
        for row in chunks(ny):

            def target(at, value):
                adjoint, square = put_miss(row, runs, observed, place, run, at, value, adjoint2)
                total[...] += square
                put_flat(to_chip, (run, n - 1 - at), row, adjoint)
                if at < 3:
                    put_flat(to_core, (run, at), row, adjoint)

            put_step(row, faces, chem1, state1, run, range(n - 3, n), target)
            for at in range(min(3, n - 3)):
                put_flat(to_core, (run, at), row, padded(*adjoint2(at, run), row))
        return carry

    for run in range(runs):
        one_run(run, 0)
    columns = (0.5 / runs) * jnp.sum(total[...], axis=0, keepdims=True)
    mine = jnp.broadcast_to(jnp.sum(columns, axis=1, keepdims=True), share.shape)
    sums = counts(lax.axis_index("gx")) == 1
    share[...] = jnp.where(sums, mine, 0.0)
    to_core[0, 0, 0, ny:] = jnp.where(sums, 0.0, mine)


def put_adjoint1(row, flow, adjoint2, run, places, weight, target):
    mids = {at: padded(*flow(at, run), row) for at in range(places[0] - 1, places[-1] + 2)}
    for at in places:
        total = beside(
            mids[at - 1], mids[at + 1], padded(*flow(at, run), row, 1), padded(*flow(at, run), row, -1), mids[at]
        )
        value = each(
            lambda a, w, f, t: a + w * f - (time_step * stiffness) * t,
            padded(*adjoint2(at, run), row), weight(at), mids[at], total,
        )
        put_padded(*target(at, run), row, value)


def slope(state):
    return each(lambda c: time_step * (3.0 * c * c + (6.0 * stiffness - 1.0)), state)


def step_x(field, run, at, row):
    return sub(padded(*field(at + 1, run), row), padded(*field(at, run), row))


def step_y(field, run, at, row):
    return sub(padded(*field(at, run), row, 1), padded(*field(at, run), row))


def step_z(field, run, at, row):
    mid = padded(*field(at, run), row)
    return sub(after_z(mid), mid)


def early_kernel(
    of_core, mx_a, my_a, my_low_a, mz_a, mz_low_a, all_a, mx_b, my_b, my_low_b, mz_b, mz_low_b, all_b,
    chem0_a, chem0_b, state1_a, state1_b, chem1_a, chem1_b, adjoint2_a, adjoint2_b,
    share_in, flow_a, flow_part, adjoint1_a, weight_b, step_z_b, part, sum_x_b, sum_y_b, sum_z_b, share,
    rim, sum_x, sum_y, sum_z,
):
    share[...] = share_in[...]
    runs = of_core.shape[0]
    n = part.shape[0] + 2
    ny = part.shape[-2]
    faces = Faces(n, (mx_a, my_a, my_low_a, mz_a, mz_low_a, all_a, mx_b, my_b, my_low_b, mz_b, mz_low_b, all_b))
    chem0 = Line((chem0_a, -3, n - 2), (chem0_b, n - 1, n + 2))
    state1 = Line((state1_a, -2, n - 2), (state1_b, n - 1, n + 1))
    chem1 = Line((chem1_a, -1, n - 3), (chem1_b, n - 2, n))
    adjoint2 = Line((rim, -3, -1), (adjoint2_a, 0, n - 4), (adjoint2_b, n - 3, n - 1))
    flow = Line((flow_a, -2, n - 2), (flow_part, n - 1, n - 1))
    adjoint1 = Line((adjoint1_a, -1, n - 3))
    for sums in (sum_x, sum_y, sum_z):
        sums[...] = jnp.zeros_like(sums)

    def one_run(run, carry):
        for row in chunks(ny):
            for at in range(3):
                put_padded(rim, (run, 2 - at), row, flat(of_core, (run, at), row))
        for row in chunks(ny):
            mids = {at: padded(*adjoint2(at, run), row) for at in range(-3, n)}
            for at in range(-2, n):
                value = faces.flow(
                    row, at, mids[at], padded(*adjoint2(at, run), row, 1), padded(*adjoint2(at, run), row, -1),
                    mids[at - 1], mids.get(at + 1),
                )
                put_padded(*flow(at, run), row, value)
        for row in chunks(ny):
            put_adjoint1(
                row, flow, adjoint2, run, range(-1, n - 2),
                lambda at: slope(padded(*state1(at, run), row)), adjoint1,
            )
            for at in range(n - 2, n + 1):
                put_flat(weight_b, (run, at - (n - 2)), row, slope(padded(*state1(at, run), row)))
        for row in chunks(ny):
            for at in range(-1, n - 1):
                total = add_product(
                    flat(sum_x, (at + 1,), row), step_x(adjoint2, run, at, row), step_x(chem1, run, at, row)
                )
                if at < n - 3:
                    total = add_product(total, step_x(adjoint1, run, at, row), step_x(chem0, run, at, row))
                put_flat(sum_x, (at + 1,), row, total)
            for at in range(n):
                total_y = add_product(
                    padded(sum_y, (at,), row), step_y(adjoint2, run, at, row), step_y(chem1, run, at, row)
                )
                total_z = add_product(
                    flat(sum_z, (at,), row), step_z(adjoint2, run, at, row), step_z(chem1, run, at, row)
                )
                slant = step_z(chem0, run, at, row)
                if at < n - 2:
                    total_y = add_product(total_y, step_y(adjoint1, run, at, row), step_y(chem0, run, at, row))
                    total_z = add_product(total_z, step_z(adjoint1, run, at, row), slant)
                else:
                    put_flat(step_z_b, (run, at - (n - 2)), row, slant)
                put_padded(sum_y, (at,), row, total_y)
                put_flat(sum_z, (at,), row, total_z)
        return carry

    for run in range(runs):
        one_run(run, 0)
    for row in chunks(ny):
        for at in range(n - 2):
            sides = flat(sum_z, (at,), row)
            value = each(
                lambda a, b, c, d, e: -0.5 * ((a + b) + (c + d) + e),
                padded(sum_y, (at,), row), padded(sum_y, (at,), row, -1), sides, before_z(sides),
                flat(sum_x, (at,), row),
            )
            if at < n - 3:
                value = each(lambda a, b: a - 0.5 * b, value, flat(sum_x, (at + 1,), row))
            put_flat(part, (at,), row, value)
        for at in range(2):
            put_flat(sum_x_b, (at,), row, flat(sum_x, (n - 2 + at,), row))
            put_flat(sum_y_b, (at,), row, padded(sum_y, (n - 2 + at,), row))
            put_flat(sum_z_b, (at,), row, flat(sum_z, (n - 2 + at,), row))


def late_kernel(
    of_chip, mx_a, my_a, my_low_a, mz_a, mz_low_a, all_a, mx_b, my_b, my_low_b, mz_b, mz_low_b, all_b,
    chem0_a, chem0_b, chem1_b, adjoint2_b, flow_a, flow_part, adjoint1_a, weight_b, step_z_b,
    part, sum_x_b, sum_y_b, sum_z_b, share_in, result, share, rim, flow_b, adjoint1_b, sum_x, sum_y, sum_z,
):
    share[...] = share_in[...]
    runs = of_chip.shape[0]
    n, ny, _ = result.shape
    faces = Faces(n, (mx_a, my_a, my_low_a, mz_a, mz_low_a, all_a, mx_b, my_b, my_low_b, mz_b, mz_low_b, all_b))
    place = [either(n - 1 - at, at) for at in range(n)]
    chem0 = Line((chem0_a, -3, n - 2), (chem0_b, n - 1, n + 2))
    chem1 = Line((chem1_b, n - 2, n))
    adjoint2 = Line((adjoint2_b, n - 3, n - 1), (rim, n, n + 2))
    flow = Line((flow_a, -2, n - 2), (flow_b, n - 1, n + 1))
    adjoint1 = Line((adjoint1_a, -1, n - 3), (adjoint1_b, n - 2, n))
    for row in chunks(ny):
        for at in range(2):
            put_flat(sum_x, (at,), row, flat(sum_x_b, (at,), row))
            put_padded(sum_y, (at,), row, flat(sum_y_b, (at,), row))
            put_flat(sum_z, (at,), row, flat(sum_z_b, (at,), row))
    sum_x[2] = jnp.zeros_like(sum_x[2])

    def one_run(run, carry):
        for row in chunks(ny):
            for at in range(3):
                put_padded(rim, (run, at), row, flat(of_chip, (run, at), row))
        for row in chunks(ny):
            mids = {at: padded(*adjoint2(at, run), row) for at in range(n - 1, n + 3)}
            value = add_product(padded(flow_part, (run, 0), row), flat(*faces.mx(n - 1), row), mids[n])
            put_padded(*flow(n - 1, run), row, value)
            for at in range(n, n + 2):
                value = faces.flow(
                    row, at, mids[at], padded(*adjoint2(at, run), row, 1), padded(*adjoint2(at, run), row, -1),
                    mids[at - 1], mids[at + 1],
                )
                put_padded(*flow(at, run), row, value)
        for row in chunks(ny):
            put_adjoint1(
                row, flow, adjoint2, run, range(n - 2, n + 1),
                lambda at: flat(weight_b, (run, at - (n - 2)), row), adjoint1,
            )
        for row in chunks(ny):
            for at in range(n - 3, n):
                total = add_product(
                    flat(sum_x, (at - (n - 3),), row), step_x(adjoint1, run, at, row), step_x(chem0, run, at, row)
                )
                if at == n - 1:
                    total = add_product(total, step_x(adjoint2, run, at, row), step_x(chem1, run, at, row))
                put_flat(sum_x, (at - (n - 3),), row, total)
            for at in range(n - 2, n):
                to = (at - (n - 2),)
                put_padded(sum_y, to, row, add_product(
                    padded(sum_y, to, row), step_y(adjoint1, run, at, row), step_y(chem0, run, at, row)
                ))
                put_flat(sum_z, to, row, add_product(
                    flat(sum_z, to, row), step_z(adjoint1, run, at, row), flat(step_z_b, (run, *to), row)
                ))
        return carry

    for run in range(runs):
        one_run(run, 0)
    for row in chunks(ny):
        for at in range(n - 2):
            value = flat(part, (at,), row)
            if at == n - 3:
                value = each(lambda a, b: a - 0.5 * b, value, flat(sum_x, (0,), row))
            put_plain(result, (place[at],), row, value)
        for at in range(2):
            sides = flat(sum_z, (at,), row)
            value = each(
                lambda a, b, c, d, e, f: -0.5 * ((a + b) + (c + d) + (e + f)),
                flat(sum_x, (at,), row), flat(sum_x, (at + 1,), row),
                padded(sum_y, (at,), row), padded(sum_y, (at,), row, -1), sides, before_z(sides),
            )
            put_plain(result, (place[n - 2 + at],), row, value)


def counts(at):
    return (at ^ (at >> 1)) & 1


def misfit_kernel(core, other_core, across, other_across, misfit):
    misfit[0] = ((core[...] + other_core[...]) + (across[...] + other_across[...]))[0, 0]


def call(kernel, outs, scratch, args, flops, scalar=None):
    moved = 4 * (sum(a.size for a in args) + sum(math.prod(o) for o in outs))
    return pl.pallas_call(
        kernel,
        out_shape=tuple(jax.ShapeDtypeStruct(o, jnp.float32) for o in outs),
        in_specs=[VMEM] * len(args),
        out_specs=tuple(SMEM if at == scalar else VMEM for at in range(len(outs))),
        scratch_shapes=[pltpu.VMEM(s, jnp.float32) for s in scratch],
        compiler_params=pltpu.CompilerParams(vmem_limit_bytes=16 * 1024 * 1024),
        cost_estimate=pl.CostEstimate(flops=flops, bytes_accessed=moved, transcendentals=0),
    )(*args)


def on_device(initial, observed, mobility):
    runs, n, ny, nz = initial.shape
    blocks = nz // LANES
    count = lax.axis_size("gx")
    over_chips = [(i, (i - 1 + 2 * (i % 2)) % count) for i in range(count)]
    over_cores = [(i, i ^ 1) for i in range(count)]
    cell = ny * nz

    def neighbours(to_chip, to_core):
        of_core = lax.ppermute(to_core, "gx", over_cores)
        return lax.ppermute(to_chip, "gx", over_chips), of_core

    def lies(*lead):
        return (*lead, blocks, ny, LANES)

    def lies_padded(*lead):
        return (*lead, blocks, ny + 2 * PAD, LANES)

    def nearest(field, first, second):
        return field if n == 4 else lax.dynamic_slice_in_dim(field, either(first, second), 4, 1)

    of_chip = lax.ppermute(nearest(initial, 0, n - 4), "gx", over_chips)
    conc, mob, to_chip, to_core, same = call(
        own_kernel, (lies_padded(runs, n), lies_padded(n), lies(3), lies(3), initial.shape), (), (initial, mobility),
        runs * n * cell,
    )
    of_core = lax.ppermute(nearest(same, n - 4, 0), "gx", over_cores)
    m_chip, m_core = neighbours(to_chip, to_core)
    conc_core, chem0_a, *faces_a = call(
        core_kernel,
        (
            lies_padded(runs, 4), lies_padded(runs, n + 2),
            lies(n + 2), lies(n + 2), lies(n + 2), lies(n + 2), lies(n + 2), lies(n + 1),
        ),
        (lies_padded(3),),
        (of_core, m_core, conc, mob),
        20 * runs * (n + 2) * cell,
    )
    conc_chip, chem0_b, state1_a, chem1_a, adjoint2_a, squares = call(
        chip_kernel,
        (
            lies_padded(runs, 4), lies_padded(runs, 4), lies_padded(runs, n + 1),
            lies_padded(runs, n - 1), lies_padded(runs, n - 3), (CHUNK, LANES),
        ),
        (),
        (of_chip, conc, conc_core, chem0_a, observed, *faces_a),
        60 * runs * (n - 1) * cell,
    )
    *faces_b, state1_b, chem1_b, adjoint2_b, to_core, to_chip, share = call(
        forward_kernel,
        (
            lies(3), lies(2), lies(2), lies(2), lies(2), lies(3),
            lies_padded(runs, 3), lies_padded(runs, 3), lies_padded(runs, 3),
            (runs, 3, blocks, ny + ROWS, LANES), lies(runs, 3), (ROWS, LANES),
        ),
        (lies_padded(3), (CHUNK, LANES)),
        (m_chip, mob, conc, conc_chip, chem0_a, chem0_b, state1_a, chem1_a, adjoint2_a, squares, observed, *faces_a),
        60 * runs * 3 * cell,
    )
    faces = (*faces_a, *faces_b)
    of_chip, of_core = neighbours(to_chip, to_core)
    groups = lax.axis_size("group")

    def target(group, at, apart):
        if counts(at):
            return group * count + (at ^ apart)
        return min(group ^ 1, groups - 1) * count + at

    def hop(value, apart):
        pairs = [
            (group * count + at, target(group, at, apart)) for group in range(groups) for at in range(count)
        ]
        return lax.ppermute(value, ("group", "gx"), pairs)

    def hops(value, bits):
        aparts = [sum(2 << bit for at, bit in enumerate(bits) if which >> at & 1) for which in range(1, 1 << len(bits))]
        return [hop(value, apart) for apart in aparts]

    share = share + of_core[0, 0, 0, ny:]
    upper = range(count.bit_length() - 3, 0, -1)
    steps = [upper[at : at + 2] for at in range(0, len(upper), 2)]
    fars = hops(share, steps[0])
    flow_a, flow_part, adjoint1_a, weight_b, step_z_b, part, *sums_b, share = call(
        early_kernel,
        (
            lies_padded(runs, n + 1), lies_padded(runs, 1), lies_padded(runs, n - 1), lies(runs, 3), lies(runs, 2),
            lies(n - 2), lies(2), lies(2), lies(2), (ROWS, LANES),
        ),
        (lies_padded(runs, 3), lies(n), lies_padded(n), lies(n)),
        (of_core, *faces, chem0_a, chem0_b, state1_a, state1_b, chem1_a, chem1_b, adjoint2_a, adjoint2_b, share),
        60 * runs * n * cell,
    )
    for bits in steps[1:]:
        share = share + sum(fars)
        fars = hops(share, bits)
    share = share + sum(fars)
    fars = [lax.ppermute(share, "gx", [(at, at ^ apart) for at in range(count)]) for apart in (1, 2, 3)]
    result, share = call(
        late_kernel,
        ((n, ny, nz), (ROWS, LANES)),
        (
            lies_padded(runs, 3), lies_padded(runs, 3), lies_padded(runs, 3),
            lies(3), lies_padded(2), lies(2),
        ),
        (
            of_chip, *faces, chem0_a, chem0_b, chem1_b, adjoint2_b, flow_a, flow_part, adjoint1_a,
            weight_b, step_z_b, part, *sums_b, share,
        ),
        60 * runs * 3 * cell,
    )
    (misfit,) = call(misfit_kernel, ((1,),), (), (share, *fars), 1, scalar=0)
    return (result, misfit)


def solution(mesh):
    placed = (
        P("group", "gx", None, None),
        P("group", "gx", None, None),
        P(("group", "gx"), None, None),
    )
    return jax.shard_map(
        on_device,
        mesh=mesh,
        in_specs=placed,
        out_specs=(P(("group", "gx"), None, None), P("group")),
        check_vma=False,
    )
```

```python
import functools
import math

import jax
import jax.numpy as jnp
from jax import lax
from jax.experimental import pallas as pl
from jax.experimental.pallas import tpu as pltpu
from jax.sharding import PartitionSpec as P

stiffness = 0.5
time_step = 0.005
VMEM = pl.BlockSpec(memory_space=pltpu.VMEM)
SMEM = pl.BlockSpec(memory_space=pltpu.SMEM)
LANES = 128
ROWS = 8
PAD = ROWS
CHUNK = 32


def chunks(ny):
    return range(0, ny, CHUNK)


def plain(ref, lead, row):
    return [
        ref[(*lead, pl.ds(row, CHUNK), pl.ds(at, LANES))] for at in range(0, ref.shape[-1], LANES)
    ]


def put_plain(ref, lead, row, value):
    for block, part in enumerate(value):
        ref[(*lead, pl.ds(row, CHUNK), pl.ds(block * LANES, LANES))] = part


def flat(ref, lead, row):
    return [ref[(*lead, block, pl.ds(row, CHUNK))] for block in range(ref.shape[-3])]


def put_flat(ref, lead, row, value):
    for block, part in enumerate(value):
        ref[(*lead, block, pl.ds(row, CHUNK))] = part


def padded(ref, lead, row, shift=0):
    return [ref[(*lead, block, pl.ds(PAD + row + shift, CHUNK))] for block in range(ref.shape[-3])]


def put_padded(ref, lead, row, value):
    ny = ref.shape[-2] - 2 * PAD
    for block, part in enumerate(value):
        ref[(*lead, block, pl.ds(PAD + row, CHUNK))] = part
        if row == 0:
            ref[(*lead, block, pl.ds(PAD + ny, 1))] = part[:1]
        if row + CHUNK == ny:
            ref[(*lead, block, pl.ds(PAD - 1, 1))] = part[CHUNK - 1 :]


def lane():
    return lax.broadcasted_iota(jnp.int32, (CHUNK, LANES), 1)


def after_z(value):
    turned = [pltpu.roll(part, LANES - 1, 1) for part in value]
    turned.append(turned[0])
    edge = lane() == LANES - 1
    return [jnp.where(edge, turned[at + 1], turned[at]) for at in range(len(value))]


def before_z(value):
    turned = [pltpu.roll(part, 1, 1) for part in value]
    edge = lane() == 0
    return [jnp.where(edge, turned[at - 1], turned[at]) for at in range(len(value))]


def side():
    return lax.rem(lax.axis_index("gx"), 2)


def either(first, second):
    return first + side() * (second - first)


class Line:
    def __init__(self, *parts):
        self.parts = parts

    def __call__(self, at, *lead):
        for ref, first, last in self.parts:
            if first <= at <= last:
                return ref, (*lead, at - first)
        raise IndexError(at)


def each(function, *values):
    return [function(*parts) for parts in zip(*values)]


def beside(low, high, up, down, mid):
    return each(
        lambda a, b, c, d, e, f: (a + b) + (c + d) + (e + f),
        low, high, up, down, after_z(mid), before_z(mid),
    )


def potential(low, mid, high, up, down):
    return each(
        lambda c, total: c * (c * c + (6.0 * stiffness - 1.0)) - stiffness * total,
        mid, beside(low, high, up, down, mid),
    )


class Faces:
    def __init__(self, n, refs):
        mx_a, my_a, my_low_a, mz_a, mz_low_a, all_a, *late = refs
        two = lambda ref, first, last, at: ((ref, first, last), *(((late[at], last + 1, n + 1),) if late else ()))
        self.mx = Line(*two(mx_a, -3, n - 2, 0))
        self.my = Line(*two(my_a, -2, n - 1, 1))
        self.my_low = Line(*two(my_low_a, -2, n - 1, 2))
        self.mz = Line(*two(mz_a, -2, n - 1, 3))
        self.mz_low = Line(*two(mz_low_a, -2, n - 1, 4))
        self.all = Line(*two(all_a, -2, n - 2, 5))

    def flow(self, row, at, mid, up, down, low=None, high=None):
        total = each(
            lambda a, b, c, d, e, u, v, w, x, y: (a * u + b * v) + (c * w + d * x) - e * y,
            flat(*self.my(at), row), flat(*self.my_low(at), row), flat(*self.mz(at), row),
            flat(*self.mz_low(at), row), flat(*self.all(at), row), up, down, after_z(mid), before_z(mid), mid,
        )
        if low is not None:
            total = add_product(total, flat(*self.mx(at - 1), row), low)
        if high is not None:
            total = add_product(total, flat(*self.mx(at), row), high)
        return total


def add_product(total, a, b):
    return each(lambda t, x, y: t + x * y, total, a, b)


def sub(a, b):
    return each(lambda x, y: x - y, a, b)


def own_kernel(initial, mobility, conc, mob, to_chip, to_core):
    runs, n, ny, _ = initial.shape
    place = [either(n - 1 - at, at) for at in range(n)]

    def one_run(run, carry):
        for row in chunks(ny):
            for at in range(n):
                put_padded(conc, (run, at), row, plain(initial, (run, place[at]), row))
        return carry

    for run in range(runs):
        one_run(run, 0)
    for row in chunks(ny):
        for at in range(n):
            value = plain(mobility, (place[at],), row)
            put_padded(mob, (at,), row, value)
            if at < 3:
                put_flat(to_core, (at,), row, value)
            if at >= n - 3:
                put_flat(to_chip, (n - 1 - at,), row, value)


def mean(a, b):
    return 0.5 * (a + b)


def put_faces(row, mob, places, faces):
    for at in places:
        mid = padded(*mob(at), row)
        put_flat(*faces.my(at), row, each(mean, mid, padded(*mob(at), row, 1)))
        put_flat(*faces.my_low(at), row, each(mean, mid, padded(*mob(at), row, -1)))
        put_flat(*faces.mz(at), row, each(mean, mid, after_z(mid)))
        put_flat(*faces.mz_low(at), row, each(mean, mid, before_z(mid)))


def put_all(row, faces, places):
    for at in places:
        put_flat(*faces.all(at), row, each(
            lambda a, b, c, d, e, f: (a + b) + (c + d) + (e + f),
            flat(*faces.mx(at - 1), row), flat(*faces.mx(at), row), flat(*faces.my(at), row),
            flat(*faces.my_low(at), row), flat(*faces.mz(at), row), flat(*faces.mz_low(at), row),
        ))


def put_potential(row, field, run, places, target):
    mids = {at: padded(*field(at, run), row) for at in range(places[0] - 1, places[-1] + 2)}
    for at in places:
        value = potential(
            mids[at - 1], mids[at], mids[at + 1],
            padded(*field(at, run), row, 1), padded(*field(at, run), row, -1),
        )
        put_padded(*target(at, run), row, value)


def put_step(row, faces, chem, state, run, places, target):
    mids = {at: padded(*chem(at, run), row) for at in range(places[0] - 1, places[-1] + 2)}
    for at in places:
        flow = faces.flow(
            row, at, mids[at], padded(*chem(at, run), row, 1), padded(*chem(at, run), row, -1),
            mids[at - 1], mids[at + 1],
        )
        value = each(lambda a, b: a + time_step * b, padded(*state(at, run), row), flow)
        target(at, value)


def put_miss(row, runs, observed, place, run, at, value, adjoint2):
    miss = sub(value, plain(observed, (run, place[at]), row))
    adjoint = each(lambda a: a * (1.0 / runs), miss)
    put_padded(*adjoint2(at, run), row, adjoint)
    return adjoint, sum(part * part for part in miss)


def core_kernel(of_core, m_core, conc_own, mob_own, conc_core, chem0, mx, my, my_low, mz, mz_low, m_all, rim):
    runs, n = conc_own.shape[:2]
    ny = of_core.shape[2]
    mob = Line((rim, -3, -1), (mob_own, 0, n - 1))
    faces = Faces(n, (mx, my, my_low, mz, mz_low, m_all))
    for row in chunks(ny):
        for at in range(3):
            put_padded(rim, (2 - at,), row, flat(m_core, (at,), row))
    for row in chunks(ny):
        mids = [padded(*mob(at), row) for at in range(-3, n)]
        for at in range(n + 2):
            put_flat(mx, (at,), row, each(mean, mids[at], mids[at + 1]))
        put_faces(row, mob, range(-2, n), faces)
    for row in chunks(ny):
        put_all(row, faces, range(-2, n - 1))
    place = [either(at, 3 - at) for at in range(4)]
    conc = Line((conc_core, -4, -1), (conc_own, 0, n - 1))

    def one_run(run, carry):
        for row in chunks(ny):
            for at in range(4):
                put_padded(conc_core, (run, 3 - at), row, plain(of_core, (run, place[at]), row))
        for row in chunks(ny):
            put_potential(row, conc, run, range(-3, n - 1), Line((chem0, -3, n - 2)))
        return carry

    for run in range(runs):
        one_run(run, 0)


def chip_kernel(
    of_chip, conc_own, conc_core, chem0_a, observed, mx, my, my_low, mz, mz_low, m_all,
    conc_chip, chem0_b, state1_a, chem1_a, adjoint2_a, squares,
):
    runs, n = conc_own.shape[:2]
    ny = observed.shape[2]
    faces = Faces(n, (mx, my, my_low, mz, mz_low, m_all))
    message = [either(3 - at, at) for at in range(4)]
    place = [either(n - 1 - at, at) for at in range(n)]
    conc = Line((conc_core, -4, -1), (conc_own, 0, n - 1), (conc_chip, n, n + 3))
    chem0 = Line((chem0_a, -3, n - 2), (chem0_b, n - 1, n + 2))
    state1 = Line((state1_a, -2, n - 2))
    chem1 = Line((chem1_a, -1, n - 3))
    adjoint2 = Line((adjoint2_a, 0, n - 4))
    squares[...] = jnp.zeros_like(squares)

    def one_run(run, carry):
        for row in chunks(ny):
            for at in range(4):
                put_padded(conc_chip, (run, at), row, plain(of_chip, (run, message[at]), row))
        for row in chunks(ny):
            put_potential(row, conc, run, range(n - 1, n + 3), chem0)
        for row in chunks(ny):
            put_step(
                row, faces, chem0, conc, run, range(-2, n - 1),
                lambda at, value: put_padded(*state1(at, run), row, value),
            )
        for row in chunks(ny):
            put_potential(row, state1, run, range(-1, n - 2), chem1)
        for row in chunks(ny):

            def target(at, value):
                squares[...] += put_miss(row, runs, observed, place, run, at, value, adjoint2)[1]

            put_step(row, faces, chem1, state1, run, range(0, n - 3), target)
        return carry

    for run in range(runs):
        one_run(run, 0)


def forward_kernel(
    m_chip, mob_own, conc_own, conc_chip, chem0_a, chem0_b, state1_a, chem1_a, adjoint2_a, squares, observed,
    mx_a, my_a, my_low_a, mz_a, mz_low_a, all_a,
    mx_b, my_b, my_low_b, mz_b, mz_low_b, all_b, state1_b, chem1_b, adjoint2_b, to_core, to_chip, share, rim, total,
):
    runs, n = conc_own.shape[:2]
    ny = observed.shape[2]
    faces = Faces(n, (mx_a, my_a, my_low_a, mz_a, mz_low_a, all_a, mx_b, my_b, my_low_b, mz_b, mz_low_b, all_b))
    mob = Line((mob_own, 0, n - 1), (rim, n, n + 2))
    place = [either(n - 1 - at, at) for at in range(n)]
    conc = Line((conc_own, 0, n - 1), (conc_chip, n, n + 3))
    chem0 = Line((chem0_a, -3, n - 2), (chem0_b, n - 1, n + 2))
    state1 = Line((state1_a, -2, n - 2), (state1_b, n - 1, n + 1))
    chem1 = Line((chem1_a, -1, n - 3), (chem1_b, n - 2, n))
    adjoint2 = Line((adjoint2_a, 0, n - 4), (adjoint2_b, n - 3, n - 1))
    for row in chunks(ny):
        for at in range(3):
            put_padded(rim, (at,), row, flat(m_chip, (at,), row))
    for row in chunks(ny):
        mids = [padded(*mob(at), row) for at in range(n - 1, n + 3)]
        for at in range(3):
            put_flat(mx_b, (at,), row, each(mean, mids[at], mids[at + 1]))
        put_faces(row, mob, range(n, n + 2), faces)
    for row in chunks(ny):
        put_all(row, faces, range(n - 1, n + 2))
    total[...] = squares[...]

    def one_run(run, carry):
        for row in chunks(ny):
            put_step(
                row, faces, chem0, conc, run, range(n - 1, n + 2),
                lambda at, value: put_padded(*state1(at, run), row, value),
            )
        for row in chunks(ny):
            put_potential(row, state1, run, range(n - 2, n + 1), chem1)
        for row in chunks(ny):

            def target(at, value):
                adjoint, square = put_miss(row, runs, observed, place, run, at, value, adjoint2)
                total[...] += square
                put_flat(to_chip, (run, n - 1 - at), row, adjoint)
                if at < 3:
                    put_flat(to_core, (run, at), row, adjoint)

            put_step(row, faces, chem1, state1, run, range(n - 3, n), target)
            for at in range(min(3, n - 3)):
                put_flat(to_core, (run, at), row, padded(*adjoint2(at, run), row))
        return carry

    for run in range(runs):
        one_run(run, 0)
    columns = (0.5 / runs) * jnp.sum(total[...], axis=0, keepdims=True)
    mine = jnp.broadcast_to(jnp.sum(columns, axis=1, keepdims=True), share.shape)
    sums = counts(lax.axis_index("gx")) == 1
    share[...] = jnp.where(sums, mine, 0.0)
    to_core[0, 0, 0, ny:] = jnp.where(sums, 0.0, mine)


def put_adjoint1(row, flow, adjoint2, run, places, weight, target):
    mids = {at: padded(*flow(at, run), row) for at in range(places[0] - 1, places[-1] + 2)}
    for at in places:
        total = beside(
            mids[at - 1], mids[at + 1], padded(*flow(at, run), row, 1), padded(*flow(at, run), row, -1), mids[at]
        )
        value = each(
            lambda a, w, f, t: a + w * f - (time_step * stiffness) * t,
            padded(*adjoint2(at, run), row), weight(at), mids[at], total,
        )
        put_padded(*target(at, run), row, value)


def slope(state):
    return each(lambda c: time_step * (3.0 * c * c + (6.0 * stiffness - 1.0)), state)


def step_x(field, run, at, row):
    return sub(padded(*field(at + 1, run), row), padded(*field(at, run), row))


def step_y(field, run, at, row):
    return sub(padded(*field(at, run), row, 1), padded(*field(at, run), row))


def step_z(field, run, at, row):
    mid = padded(*field(at, run), row)
    return sub(after_z(mid), mid)


def early_kernel(
    of_core, mx_a, my_a, my_low_a, mz_a, mz_low_a, all_a, mx_b, my_b, my_low_b, mz_b, mz_low_b, all_b,
    chem0_a, chem0_b, state1_a, state1_b, chem1_a, chem1_b, adjoint2_a, adjoint2_b,
    share_in, flow_a, flow_part, adjoint1_a, weight_b, step_z_b, part, sum_x_b, sum_y_b, sum_z_b, share,
    rim, sum_x, sum_y, sum_z,
):
    share[...] = share_in[...]
    runs = of_core.shape[0]
    n = part.shape[0] + 2
    ny = part.shape[-2]
    faces = Faces(n, (mx_a, my_a, my_low_a, mz_a, mz_low_a, all_a, mx_b, my_b, my_low_b, mz_b, mz_low_b, all_b))
    chem0 = Line((chem0_a, -3, n - 2), (chem0_b, n - 1, n + 2))
    state1 = Line((state1_a, -2, n - 2), (state1_b, n - 1, n + 1))
    chem1 = Line((chem1_a, -1, n - 3), (chem1_b, n - 2, n))
    adjoint2 = Line((rim, -3, -1), (adjoint2_a, 0, n - 4), (adjoint2_b, n - 3, n - 1))
    flow = Line((flow_a, -2, n - 2), (flow_part, n - 1, n - 1))
    adjoint1 = Line((adjoint1_a, -1, n - 3))
    for sums in (sum_x, sum_y, sum_z):
        sums[...] = jnp.zeros_like(sums)

    def one_run(run, carry):
        for row in chunks(ny):
            for at in range(3):
                put_padded(rim, (run, 2 - at), row, flat(of_core, (run, at), row))
        for row in chunks(ny):
            mids = {at: padded(*adjoint2(at, run), row) for at in range(-3, n)}
            for at in range(-2, n):
                value = faces.flow(
                    row, at, mids[at], padded(*adjoint2(at, run), row, 1), padded(*adjoint2(at, run), row, -1),
                    mids[at - 1], mids.get(at + 1),
                )
                put_padded(*flow(at, run), row, value)
        for row in chunks(ny):
            put_adjoint1(
                row, flow, adjoint2, run, range(-1, n - 2),
                lambda at: slope(padded(*state1(at, run), row)), adjoint1,
            )
            for at in range(n - 2, n + 1):
                put_flat(weight_b, (run, at - (n - 2)), row, slope(padded(*state1(at, run), row)))
        for row in chunks(ny):
            for at in range(-1, n - 1):
                total = add_product(
                    flat(sum_x, (at + 1,), row), step_x(adjoint2, run, at, row), step_x(chem1, run, at, row)
                )
                if at < n - 3:
                    total = add_product(total, step_x(adjoint1, run, at, row), step_x(chem0, run, at, row))
                put_flat(sum_x, (at + 1,), row, total)
            for at in range(n):
                total_y = add_product(
                    padded(sum_y, (at,), row), step_y(adjoint2, run, at, row), step_y(chem1, run, at, row)
                )
                total_z = add_product(
                    flat(sum_z, (at,), row), step_z(adjoint2, run, at, row), step_z(chem1, run, at, row)
                )
                slant = step_z(chem0, run, at, row)
                if at < n - 2:
                    total_y = add_product(total_y, step_y(adjoint1, run, at, row), step_y(chem0, run, at, row))
                    total_z = add_product(total_z, step_z(adjoint1, run, at, row), slant)
                else:
                    put_flat(step_z_b, (run, at - (n - 2)), row, slant)
                put_padded(sum_y, (at,), row, total_y)
                put_flat(sum_z, (at,), row, total_z)
        return carry

    for run in range(runs):
        one_run(run, 0)
    for row in chunks(ny):
        for at in range(n - 2):
            sides = flat(sum_z, (at,), row)
            value = each(
                lambda a, b, c, d, e: -0.5 * ((a + b) + (c + d) + e),
                padded(sum_y, (at,), row), padded(sum_y, (at,), row, -1), sides, before_z(sides),
                flat(sum_x, (at,), row),
            )
            if at < n - 3:
                value = each(lambda a, b: a - 0.5 * b, value, flat(sum_x, (at + 1,), row))
            put_flat(part, (at,), row, value)
        for at in range(2):
            put_flat(sum_x_b, (at,), row, flat(sum_x, (n - 2 + at,), row))
            put_flat(sum_y_b, (at,), row, padded(sum_y, (n - 2 + at,), row))
            put_flat(sum_z_b, (at,), row, flat(sum_z, (n - 2 + at,), row))


def late_kernel(
    of_chip, mx_a, my_a, my_low_a, mz_a, mz_low_a, all_a, mx_b, my_b, my_low_b, mz_b, mz_low_b, all_b,
    chem0_a, chem0_b, chem1_b, adjoint2_b, flow_a, flow_part, adjoint1_a, weight_b, step_z_b,
    part, sum_x_b, sum_y_b, sum_z_b, share_in, result, share, rim, flow_b, adjoint1_b, sum_x, sum_y, sum_z,
):
    share[...] = share_in[...]
    runs = of_chip.shape[0]
    n, ny, _ = result.shape
    faces = Faces(n, (mx_a, my_a, my_low_a, mz_a, mz_low_a, all_a, mx_b, my_b, my_low_b, mz_b, mz_low_b, all_b))
    place = [either(n - 1 - at, at) for at in range(n)]
    chem0 = Line((chem0_a, -3, n - 2), (chem0_b, n - 1, n + 2))
    chem1 = Line((chem1_b, n - 2, n))
    adjoint2 = Line((adjoint2_b, n - 3, n - 1), (rim, n, n + 2))
    flow = Line((flow_a, -2, n - 2), (flow_b, n - 1, n + 1))
    adjoint1 = Line((adjoint1_a, -1, n - 3), (adjoint1_b, n - 2, n))
    for row in chunks(ny):
        for at in range(2):
            put_flat(sum_x, (at,), row, flat(sum_x_b, (at,), row))
            put_padded(sum_y, (at,), row, flat(sum_y_b, (at,), row))
            put_flat(sum_z, (at,), row, flat(sum_z_b, (at,), row))
    sum_x[2] = jnp.zeros_like(sum_x[2])

    def one_run(run, carry):
        for row in chunks(ny):
            for at in range(3):
                put_padded(rim, (run, at), row, flat(of_chip, (run, at), row))
        for row in chunks(ny):
            mids = {at: padded(*adjoint2(at, run), row) for at in range(n - 1, n + 3)}
            value = add_product(padded(flow_part, (run, 0), row), flat(*faces.mx(n - 1), row), mids[n])
            put_padded(*flow(n - 1, run), row, value)
            for at in range(n, n + 2):
                value = faces.flow(
                    row, at, mids[at], padded(*adjoint2(at, run), row, 1), padded(*adjoint2(at, run), row, -1),
                    mids[at - 1], mids[at + 1],
                )
                put_padded(*flow(at, run), row, value)
        for row in chunks(ny):
            put_adjoint1(
                row, flow, adjoint2, run, range(n - 2, n + 1),
                lambda at: flat(weight_b, (run, at - (n - 2)), row), adjoint1,
            )
        for row in chunks(ny):
            for at in range(n - 3, n):
                total = add_product(
                    flat(sum_x, (at - (n - 3),), row), step_x(adjoint1, run, at, row), step_x(chem0, run, at, row)
                )
                if at == n - 1:
                    total = add_product(total, step_x(adjoint2, run, at, row), step_x(chem1, run, at, row))
                put_flat(sum_x, (at - (n - 3),), row, total)
            for at in range(n - 2, n):
                to = (at - (n - 2),)
                put_padded(sum_y, to, row, add_product(
                    padded(sum_y, to, row), step_y(adjoint1, run, at, row), step_y(chem0, run, at, row)
                ))
                put_flat(sum_z, to, row, add_product(
                    flat(sum_z, to, row), step_z(adjoint1, run, at, row), flat(step_z_b, (run, *to), row)
                ))
        return carry

    for run in range(runs):
        one_run(run, 0)
    for row in chunks(ny):
        for at in range(n - 2):
            value = flat(part, (at,), row)
            if at == n - 3:
                value = each(lambda a, b: a - 0.5 * b, value, flat(sum_x, (0,), row))
            put_plain(result, (place[at],), row, value)
        for at in range(2):
            sides = flat(sum_z, (at,), row)
            value = each(
                lambda a, b, c, d, e, f: -0.5 * ((a + b) + (c + d) + (e + f)),
                flat(sum_x, (at,), row), flat(sum_x, (at + 1,), row),
                padded(sum_y, (at,), row), padded(sum_y, (at,), row, -1), sides, before_z(sides),
            )
            put_plain(result, (place[n - 2 + at],), row, value)


def counts(at):
    return (at ^ (at >> 1)) & 1


def misfit_kernel(core, other_core, across, other_across, misfit):
    misfit[0] = ((core[...] + other_core[...]) + (across[...] + other_across[...]))[0, 0]


def call(kernel, outs, scratch, args, flops, scalar=None):
    moved = 4 * (sum(a.size for a in args) + sum(math.prod(o) for o in outs))
    return pl.pallas_call(
        kernel,
        out_shape=tuple(jax.ShapeDtypeStruct(o, jnp.float32) for o in outs),
        in_specs=[VMEM] * len(args),
        out_specs=tuple(SMEM if at == scalar else VMEM for at in range(len(outs))),
        scratch_shapes=[pltpu.VMEM(s, jnp.float32) for s in scratch],
        compiler_params=pltpu.CompilerParams(vmem_limit_bytes=16 * 1024 * 1024),
        cost_estimate=pl.CostEstimate(flops=flops, bytes_accessed=moved, transcendentals=0),
    )(*args)


def on_device(initial, observed, mobility):
    runs, n, ny, nz = initial.shape
    blocks = nz // LANES
    count = lax.axis_size("gx")
    over_chips = [(i, (i - 1 + 2 * (i % 2)) % count) for i in range(count)]
    over_cores = [(i, i ^ 1) for i in range(count)]
    cell = ny * nz

    def neighbours(to_chip, to_core):
        of_core = lax.ppermute(to_core, "gx", over_cores)
        return lax.ppermute(to_chip, "gx", over_chips), of_core

    def lies(*lead):
        return (*lead, blocks, ny, LANES)

    def lies_padded(*lead):
        return (*lead, blocks, ny + 2 * PAD, LANES)

    if n == 4:
        near = (initial, initial)
    else:
        near = [lax.dynamic_slice_in_dim(initial, at, 4, 1) for at in (either(0, n - 4), either(n - 4, 0))]
    of_chip, of_core = neighbours(*near)
    conc, mob, to_chip, to_core = call(
        own_kernel, (lies_padded(runs, n), lies_padded(n), lies(3), lies(3)), (), (initial, mobility),
        runs * n * cell,
    )
    m_chip, m_core = neighbours(to_chip, to_core)
    conc_core, chem0_a, *faces_a = call(
        core_kernel,
        (
            lies_padded(runs, 4), lies_padded(runs, n + 2),
            lies(n + 2), lies(n + 2), lies(n + 2), lies(n + 2), lies(n + 2), lies(n + 1),
        ),
        (lies_padded(3),),
        (of_core, m_core, conc, mob),
        20 * runs * (n + 2) * cell,
    )
    conc_chip, chem0_b, state1_a, chem1_a, adjoint2_a, squares = call(
        chip_kernel,
        (
            lies_padded(runs, 4), lies_padded(runs, 4), lies_padded(runs, n + 1),
            lies_padded(runs, n - 1), lies_padded(runs, n - 3), (CHUNK, LANES),
        ),
        (),
        (of_chip, conc, conc_core, chem0_a, observed, *faces_a),
        60 * runs * (n - 1) * cell,
    )
    *faces_b, state1_b, chem1_b, adjoint2_b, to_core, to_chip, share = call(
        forward_kernel,
        (
            lies(3), lies(2), lies(2), lies(2), lies(2), lies(3),
            lies_padded(runs, 3), lies_padded(runs, 3), lies_padded(runs, 3),
            (runs, 3, blocks, ny + ROWS, LANES), lies(runs, 3), (ROWS, LANES),
        ),
        (lies_padded(3), (CHUNK, LANES)),
        (m_chip, mob, conc, conc_chip, chem0_a, chem0_b, state1_a, chem1_a, adjoint2_a, squares, observed, *faces_a),
        60 * runs * 3 * cell,
    )
    faces = (*faces_a, *faces_b)
    of_chip, of_core = neighbours(to_chip, to_core)
    groups = lax.axis_size("group")

    def target(group, at, apart):
        if counts(at):
            return group * count + (at ^ apart)
        return min(group ^ 1, groups - 1) * count + at

    def hop(value, apart):
        pairs = [
            (group * count + at, target(group, at, apart)) for group in range(groups) for at in range(count)
        ]
        return lax.ppermute(value, ("group", "gx"), pairs)

    def hops(value, bits):
        aparts = [sum(2 << bit for at, bit in enumerate(bits) if which >> at & 1) for which in range(1, 1 << len(bits))]
        return [hop(value, apart) for apart in aparts]

    share = share + of_core[0, 0, 0, ny:]
    upper = range(count.bit_length() - 3, 0, -1)
    steps = [upper[at : at + 2] for at in range(0, len(upper), 2)]
    fars = hops(share, steps[0])
    flow_a, flow_part, adjoint1_a, weight_b, step_z_b, part, *sums_b, share = call(
        early_kernel,
        (
            lies_padded(runs, n + 1), lies_padded(runs, 1), lies_padded(runs, n - 1), lies(runs, 3), lies(runs, 2),
            lies(n - 2), lies(2), lies(2), lies(2), (ROWS, LANES),
        ),
        (lies_padded(runs, 3), lies(n), lies_padded(n), lies(n)),
        (of_core, *faces, chem0_a, chem0_b, state1_a, state1_b, chem1_a, chem1_b, adjoint2_a, adjoint2_b, share),
        60 * runs * n * cell,
    )
    for bits in steps[1:]:
        share = share + sum(fars)
        fars = hops(share, bits)
    share = share + sum(fars)
    fars = [lax.ppermute(share, "gx", [(at, at ^ apart) for at in range(count)]) for apart in (1, 2, 3)]
    result, share = call(
        late_kernel,
        ((n, ny, nz), (ROWS, LANES)),
        (
            lies_padded(runs, 3), lies_padded(runs, 3), lies_padded(runs, 3),
            lies(3), lies_padded(2), lies(2),
        ),
        (
            of_chip, *faces, chem0_a, chem0_b, chem1_b, adjoint2_b, flow_a, flow_part, adjoint1_a,
            weight_b, step_z_b, part, *sums_b, share,
        ),
        60 * runs * 3 * cell,
    )
    (misfit,) = call(misfit_kernel, ((1,),), (), (share, *fars), 1, scalar=0)
    return (result, misfit)


def solution(mesh):
    placed = (
        P("group", "gx", None, None),
        P("group", "gx", None, None),
        P(("group", "gx"), None, None),
    )
    return jax.shard_map(
        on_device,
        mesh=mesh,
        in_specs=placed,
        out_specs=(P(("group", "gx"), None, None), P("group")),
        check_vma=False,
    )
```

```python
import functools
import math

import jax
import jax.numpy as jnp
from jax import lax
from jax.experimental import pallas as pl
from jax.experimental.pallas import tpu as pltpu
from jax.sharding import PartitionSpec as P

stiffness = 0.5
time_step = 0.005
VMEM = pl.BlockSpec(memory_space=pltpu.VMEM)
SMEM = pl.BlockSpec(memory_space=pltpu.SMEM)
LANES = 128
ROWS = 8
PAD = ROWS
CHUNK = 8


def chunks(ny):
    return range(0, ny, CHUNK)


def plain(ref, lead, row):
    return [
        ref[(*lead, pl.ds(row, CHUNK), pl.ds(at, LANES))] for at in range(0, ref.shape[-1], LANES)
    ]


def put_plain(ref, lead, row, value):
    for block, part in enumerate(value):
        ref[(*lead, pl.ds(row, CHUNK), pl.ds(block * LANES, LANES))] = part


def flat(ref, lead, row):
    return [ref[(*lead, block, pl.ds(row, CHUNK))] for block in range(ref.shape[-3])]


def put_flat(ref, lead, row, value):
    for block, part in enumerate(value):
        ref[(*lead, block, pl.ds(row, CHUNK))] = part


def padded(ref, lead, row, shift=0):
    return [ref[(*lead, block, pl.ds(PAD + row + shift, CHUNK))] for block in range(ref.shape[-3])]


def put_padded(ref, lead, row, value):
    ny = ref.shape[-2] - 2 * PAD
    for block, part in enumerate(value):
        ref[(*lead, block, pl.ds(PAD + row, CHUNK))] = part
        if row == 0:
            ref[(*lead, block, pl.ds(PAD + ny, 1))] = part[:1]
        if row + CHUNK == ny:
            ref[(*lead, block, pl.ds(PAD - 1, 1))] = part[CHUNK - 1 :]


def lane():
    return lax.broadcasted_iota(jnp.int32, (CHUNK, LANES), 1)


def after_z(value):
    turned = [pltpu.roll(part, LANES - 1, 1) for part in value]
    turned.append(turned[0])
    edge = lane() == LANES - 1
    return [jnp.where(edge, turned[at + 1], turned[at]) for at in range(len(value))]


def before_z(value):
    turned = [pltpu.roll(part, 1, 1) for part in value]
    edge = lane() == 0
    return [jnp.where(edge, turned[at - 1], turned[at]) for at in range(len(value))]


def side():
    return lax.rem(lax.axis_index("gx"), 2)


def either(first, second):
    return first + side() * (second - first)


class Line:
    def __init__(self, *parts):
        self.parts = parts

    def __call__(self, at, *lead):
        for ref, first, last in self.parts:
            if first <= at <= last:
                return ref, (*lead, at - first)
        raise IndexError(at)


def each(function, *values):
    return [function(*parts) for parts in zip(*values)]


def beside(low, high, up, down, mid):
    return each(
        lambda a, b, c, d, e, f: (a + b) + (c + d) + (e + f),
        low, high, up, down, after_z(mid), before_z(mid),
    )


def potential(low, mid, high, up, down):
    return each(
        lambda c, total: c * (c * c + (6.0 * stiffness - 1.0)) - stiffness * total,
        mid, beside(low, high, up, down, mid),
    )


class Faces:
    def __init__(self, n, refs):
        mx_a, my_a, my_low_a, mz_a, mz_low_a, all_a, *late = refs
        two = lambda ref, first, last, at: ((ref, first, last), *(((late[at], last + 1, n + 1),) if late else ()))
        self.mx = Line(*two(mx_a, -3, n - 2, 0))
        self.my = Line(*two(my_a, -2, n - 1, 1))
        self.my_low = Line(*two(my_low_a, -2, n - 1, 2))
        self.mz = Line(*two(mz_a, -2, n - 1, 3))
        self.mz_low = Line(*two(mz_low_a, -2, n - 1, 4))
        self.all = Line(*two(all_a, -2, n - 2, 5))

    def flow(self, row, at, mid, up, down, low=None, high=None):
        total = each(
            lambda a, b, c, d, e, u, v, w, x, y: (a * u + b * v) + (c * w + d * x) - e * y,
            flat(*self.my(at), row), flat(*self.my_low(at), row), flat(*self.mz(at), row),
            flat(*self.mz_low(at), row), flat(*self.all(at), row), up, down, after_z(mid), before_z(mid), mid,
        )
        if low is not None:
            total = add_product(total, flat(*self.mx(at - 1), row), low)
        if high is not None:
            total = add_product(total, flat(*self.mx(at), row), high)
        return total


def add_product(total, a, b):
    return each(lambda t, x, y: t + x * y, total, a, b)


def sub(a, b):
    return each(lambda x, y: x - y, a, b)


def own_kernel(initial, mobility, conc, mob, to_chip, to_core):
    runs, n, ny, _ = initial.shape
    place = [either(n - 1 - at, at) for at in range(n)]

    def one_run(run, carry):
        for row in chunks(ny):
            for at in range(n):
                put_padded(conc, (run, at), row, plain(initial, (run, place[at]), row))
        return carry

    for run in range(runs):
        one_run(run, 0)
    for row in chunks(ny):
        for at in range(n):
            value = plain(mobility, (place[at],), row)
            put_padded(mob, (at,), row, value)
            if at < 3:
                put_flat(to_core, (at,), row, value)
            if at >= n - 3:
                put_flat(to_chip, (n - 1 - at,), row, value)


def mean(a, b):
    return 0.5 * (a + b)


def put_faces(row, mob, places, faces):
    for at in places:
        mid = padded(*mob(at), row)
        put_flat(*faces.my(at), row, each(mean, mid, padded(*mob(at), row, 1)))
        put_flat(*faces.my_low(at), row, each(mean, mid, padded(*mob(at), row, -1)))
        put_flat(*faces.mz(at), row, each(mean, mid, after_z(mid)))
        put_flat(*faces.mz_low(at), row, each(mean, mid, before_z(mid)))


def put_all(row, faces, places):
    for at in places:
        put_flat(*faces.all(at), row, each(
            lambda a, b, c, d, e, f: (a + b) + (c + d) + (e + f),
            flat(*faces.mx(at - 1), row), flat(*faces.mx(at), row), flat(*faces.my(at), row),
            flat(*faces.my_low(at), row), flat(*faces.mz(at), row), flat(*faces.mz_low(at), row),
        ))


def put_potential(row, field, run, places, target):
    mids = {at: padded(*field(at, run), row) for at in range(places[0] - 1, places[-1] + 2)}
    for at in places:
        value = potential(
            mids[at - 1], mids[at], mids[at + 1],
            padded(*field(at, run), row, 1), padded(*field(at, run), row, -1),
        )
        put_padded(*target(at, run), row, value)


def put_step(row, faces, chem, state, run, places, target):
    mids = {at: padded(*chem(at, run), row) for at in range(places[0] - 1, places[-1] + 2)}
    for at in places:
        flow = faces.flow(
            row, at, mids[at], padded(*chem(at, run), row, 1), padded(*chem(at, run), row, -1),
            mids[at - 1], mids[at + 1],
        )
        value = each(lambda a, b: a + time_step * b, padded(*state(at, run), row), flow)
        target(at, value)


def put_miss(row, runs, observed, place, run, at, value, adjoint2):
    miss = sub(value, plain(observed, (run, place[at]), row))
    adjoint = each(lambda a: a * (1.0 / runs), miss)
    put_padded(*adjoint2(at, run), row, adjoint)
    return adjoint, sum(part * part for part in miss)


def core_kernel(of_core, m_core, conc_own, mob_own, conc_core, chem0, mx, my, my_low, mz, mz_low, m_all, rim):
    runs, n = conc_own.shape[:2]
    ny = of_core.shape[2]
    mob = Line((rim, -3, -1), (mob_own, 0, n - 1))
    faces = Faces(n, (mx, my, my_low, mz, mz_low, m_all))
    for row in chunks(ny):
        for at in range(3):
            put_padded(rim, (2 - at,), row, flat(m_core, (at,), row))
    for row in chunks(ny):
        mids = [padded(*mob(at), row) for at in range(-3, n)]
        for at in range(n + 2):
            put_flat(mx, (at,), row, each(mean, mids[at], mids[at + 1]))
        put_faces(row, mob, range(-2, n), faces)
    for row in chunks(ny):
        put_all(row, faces, range(-2, n - 1))
    place = [either(at, 3 - at) for at in range(4)]
    conc = Line((conc_core, -4, -1), (conc_own, 0, n - 1))

    def one_run(run, carry):
        for row in chunks(ny):
            for at in range(4):
                put_padded(conc_core, (run, 3 - at), row, plain(of_core, (run, place[at]), row))
        for row in chunks(ny):
            put_potential(row, conc, run, range(-3, n - 1), Line((chem0, -3, n - 2)))
        return carry

    for run in range(runs):
        one_run(run, 0)


def chip_kernel(
    of_chip, conc_own, conc_core, chem0_a, observed, mx, my, my_low, mz, mz_low, m_all,
    conc_chip, chem0_b, state1_a, chem1_a, adjoint2_a, squares,
):
    runs, n = conc_own.shape[:2]
    ny = observed.shape[2]
    faces = Faces(n, (mx, my, my_low, mz, mz_low, m_all))
    message = [either(3 - at, at) for at in range(4)]
    place = [either(n - 1 - at, at) for at in range(n)]
    conc = Line((conc_core, -4, -1), (conc_own, 0, n - 1), (conc_chip, n, n + 3))
    chem0 = Line((chem0_a, -3, n - 2), (chem0_b, n - 1, n + 2))
    state1 = Line((state1_a, -2, n - 2))
    chem1 = Line((chem1_a, -1, n - 3))
    adjoint2 = Line((adjoint2_a, 0, n - 4))
    squares[...] = jnp.zeros_like(squares)

    def one_run(run, carry):
        for row in chunks(ny):
            for at in range(4):
                put_padded(conc_chip, (run, at), row, plain(of_chip, (run, message[at]), row))
        for row in chunks(ny):
            put_potential(row, conc, run, range(n - 1, n + 3), chem0)
        for row in chunks(ny):
            put_step(
                row, faces, chem0, conc, run, range(-2, n - 1),
                lambda at, value: put_padded(*state1(at, run), row, value),
            )
        for row in chunks(ny):
            put_potential(row, state1, run, range(-1, n - 2), chem1)
        for row in chunks(ny):

            def target(at, value):
                squares[...] += put_miss(row, runs, observed, place, run, at, value, adjoint2)[1]

            put_step(row, faces, chem1, state1, run, range(0, n - 3), target)
        return carry

    for run in range(runs):
        one_run(run, 0)


def forward_kernel(
    m_chip, mob_own, conc_own, conc_chip, chem0_a, chem0_b, state1_a, chem1_a, adjoint2_a, squares, observed,
    mx_a, my_a, my_low_a, mz_a, mz_low_a, all_a,
    mx_b, my_b, my_low_b, mz_b, mz_low_b, all_b, state1_b, chem1_b, adjoint2_b, to_core, to_chip, share, rim, total,
):
    runs, n = conc_own.shape[:2]
    ny = observed.shape[2]
    faces = Faces(n, (mx_a, my_a, my_low_a, mz_a, mz_low_a, all_a, mx_b, my_b, my_low_b, mz_b, mz_low_b, all_b))
    mob = Line((mob_own, 0, n - 1), (rim, n, n + 2))
    place = [either(n - 1 - at, at) for at in range(n)]
    conc = Line((conc_own, 0, n - 1), (conc_chip, n, n + 3))
    chem0 = Line((chem0_a, -3, n - 2), (chem0_b, n - 1, n + 2))
    state1 = Line((state1_a, -2, n - 2), (state1_b, n - 1, n + 1))
    chem1 = Line((chem1_a, -1, n - 3), (chem1_b, n - 2, n))
    adjoint2 = Line((adjoint2_a, 0, n - 4), (adjoint2_b, n - 3, n - 1))
    for row in chunks(ny):
        for at in range(3):
            put_padded(rim, (at,), row, flat(m_chip, (at,), row))
    for row in chunks(ny):
        mids = [padded(*mob(at), row) for at in range(n - 1, n + 3)]
        for at in range(3):
            put_flat(mx_b, (at,), row, each(mean, mids[at], mids[at + 1]))
        put_faces(row, mob, range(n, n + 2), faces)
    for row in chunks(ny):
        put_all(row, faces, range(n - 1, n + 2))
    total[...] = squares[...]

    def one_run(run, carry):
        for row in chunks(ny):
            put_step(
                row, faces, chem0, conc, run, range(n - 1, n + 2),
                lambda at, value: put_padded(*state1(at, run), row, value),
            )
        for row in chunks(ny):
            put_potential(row, state1, run, range(n - 2, n + 1), chem1)
        for row in chunks(ny):

            def target(at, value):
                adjoint, square = put_miss(row, runs, observed, place, run, at, value, adjoint2)
                total[...] += square
                put_flat(to_chip, (run, n - 1 - at), row, adjoint)
                if at < 3:
                    put_flat(to_core, (run, at), row, adjoint)

            put_step(row, faces, chem1, state1, run, range(n - 3, n), target)
            for at in range(min(3, n - 3)):
                put_flat(to_core, (run, at), row, padded(*adjoint2(at, run), row))
        return carry

    for run in range(runs):
        one_run(run, 0)
    columns = (0.5 / runs) * jnp.sum(total[...], axis=0, keepdims=True)
    mine = jnp.broadcast_to(jnp.sum(columns, axis=1, keepdims=True), share.shape)
    sums = counts(lax.axis_index("gx")) == 1
    share[...] = jnp.where(sums, mine, 0.0)
    to_core[0, 0, 0, ny:] = jnp.where(sums, 0.0, mine)


def put_adjoint1(row, flow, adjoint2, run, places, weight, target):
    mids = {at: padded(*flow(at, run), row) for at in range(places[0] - 1, places[-1] + 2)}
    for at in places:
        total = beside(
            mids[at - 1], mids[at + 1], padded(*flow(at, run), row, 1), padded(*flow(at, run), row, -1), mids[at]
        )
        value = each(
            lambda a, w, f, t: a + w * f - (time_step * stiffness) * t,
            padded(*adjoint2(at, run), row), weight(at), mids[at], total,
        )
        put_padded(*target(at, run), row, value)


def slope(state):
    return each(lambda c: time_step * (3.0 * c * c + (6.0 * stiffness - 1.0)), state)


def step_x(field, run, at, row):
    return sub(padded(*field(at + 1, run), row), padded(*field(at, run), row))


def step_y(field, run, at, row):
    return sub(padded(*field(at, run), row, 1), padded(*field(at, run), row))


def step_z(field, run, at, row):
    mid = padded(*field(at, run), row)
    return sub(after_z(mid), mid)


def early_kernel(
    of_core, mx_a, my_a, my_low_a, mz_a, mz_low_a, all_a, mx_b, my_b, my_low_b, mz_b, mz_low_b, all_b,
    chem0_a, chem0_b, state1_a, state1_b, chem1_a, chem1_b, adjoint2_a, adjoint2_b,
    share_in, flow_a, flow_part, adjoint1_a, weight_b, step_z_b, part, sum_x_b, sum_y_b, sum_z_b, share,
    rim, sum_x, sum_y, sum_z,
):
    share[...] = share_in[...]
    runs = of_core.shape[0]
    n = part.shape[0] + 2
    ny = part.shape[-2]
    faces = Faces(n, (mx_a, my_a, my_low_a, mz_a, mz_low_a, all_a, mx_b, my_b, my_low_b, mz_b, mz_low_b, all_b))
    chem0 = Line((chem0_a, -3, n - 2), (chem0_b, n - 1, n + 2))
    state1 = Line((state1_a, -2, n - 2), (state1_b, n - 1, n + 1))
    chem1 = Line((chem1_a, -1, n - 3), (chem1_b, n - 2, n))
    adjoint2 = Line((rim, -3, -1), (adjoint2_a, 0, n - 4), (adjoint2_b, n - 3, n - 1))
    flow = Line((flow_a, -2, n - 2), (flow_part, n - 1, n - 1))
    adjoint1 = Line((adjoint1_a, -1, n - 3))
    for sums in (sum_x, sum_y, sum_z):
        sums[...] = jnp.zeros_like(sums)

    def one_run(run, carry):
        for row in chunks(ny):
            for at in range(3):
                put_padded(rim, (run, 2 - at), row, flat(of_core, (run, at), row))
        for row in chunks(ny):
            mids = {at: padded(*adjoint2(at, run), row) for at in range(-3, n)}
            for at in range(-2, n):
                value = faces.flow(
                    row, at, mids[at], padded(*adjoint2(at, run), row, 1), padded(*adjoint2(at, run), row, -1),
                    mids[at - 1], mids.get(at + 1),
                )
                put_padded(*flow(at, run), row, value)
        for row in chunks(ny):
            put_adjoint1(
                row, flow, adjoint2, run, range(-1, n - 2),
                lambda at: slope(padded(*state1(at, run), row)), adjoint1,
            )
            for at in range(n - 2, n + 1):
                put_flat(weight_b, (run, at - (n - 2)), row, slope(padded(*state1(at, run), row)))
        for row in chunks(ny):
            for at in range(-1, n - 1):
                total = add_product(
                    flat(sum_x, (at + 1,), row), step_x(adjoint2, run, at, row), step_x(chem1, run, at, row)
                )
                if at < n - 3:
                    total = add_product(total, step_x(adjoint1, run, at, row), step_x(chem0, run, at, row))
                put_flat(sum_x, (at + 1,), row, total)
            for at in range(n):
                total_y = add_product(
                    padded(sum_y, (at,), row), step_y(adjoint2, run, at, row), step_y(chem1, run, at, row)
                )
                total_z = add_product(
                    flat(sum_z, (at,), row), step_z(adjoint2, run, at, row), step_z(chem1, run, at, row)
                )
                slant = step_z(chem0, run, at, row)
                if at < n - 2:
                    total_y = add_product(total_y, step_y(adjoint1, run, at, row), step_y(chem0, run, at, row))
                    total_z = add_product(total_z, step_z(adjoint1, run, at, row), slant)
                else:
                    put_flat(step_z_b, (run, at - (n - 2)), row, slant)
                put_padded(sum_y, (at,), row, total_y)
                put_flat(sum_z, (at,), row, total_z)
        return carry

    for run in range(runs):
        one_run(run, 0)
    for row in chunks(ny):
        for at in range(n - 2):
            sides = flat(sum_z, (at,), row)
            value = each(
                lambda a, b, c, d, e: -0.5 * ((a + b) + (c + d) + e),
                padded(sum_y, (at,), row), padded(sum_y, (at,), row, -1), sides, before_z(sides),
                flat(sum_x, (at,), row),
            )
            if at < n - 3:
                value = each(lambda a, b: a - 0.5 * b, value, flat(sum_x, (at + 1,), row))
            put_flat(part, (at,), row, value)
        for at in range(2):
            put_flat(sum_x_b, (at,), row, flat(sum_x, (n - 2 + at,), row))
            put_flat(sum_y_b, (at,), row, padded(sum_y, (n - 2 + at,), row))
            put_flat(sum_z_b, (at,), row, flat(sum_z, (n - 2 + at,), row))


def late_kernel(
    of_chip, mx_a, my_a, my_low_a, mz_a, mz_low_a, all_a, mx_b, my_b, my_low_b, mz_b, mz_low_b, all_b,
    chem0_a, chem0_b, chem1_b, adjoint2_b, flow_a, flow_part, adjoint1_a, weight_b, step_z_b,
    part, sum_x_b, sum_y_b, sum_z_b, share_in, result, share, rim, flow_b, adjoint1_b, sum_x, sum_y, sum_z,
):
    share[...] = share_in[...]
    runs = of_chip.shape[0]
    n, ny, _ = result.shape
    faces = Faces(n, (mx_a, my_a, my_low_a, mz_a, mz_low_a, all_a, mx_b, my_b, my_low_b, mz_b, mz_low_b, all_b))
    place = [either(n - 1 - at, at) for at in range(n)]
    chem0 = Line((chem0_a, -3, n - 2), (chem0_b, n - 1, n + 2))
    chem1 = Line((chem1_b, n - 2, n))
    adjoint2 = Line((adjoint2_b, n - 3, n - 1), (rim, n, n + 2))
    flow = Line((flow_a, -2, n - 2), (flow_b, n - 1, n + 1))
    adjoint1 = Line((adjoint1_a, -1, n - 3), (adjoint1_b, n - 2, n))
    for row in chunks(ny):
        for at in range(2):
            put_flat(sum_x, (at,), row, flat(sum_x_b, (at,), row))
            put_padded(sum_y, (at,), row, flat(sum_y_b, (at,), row))
            put_flat(sum_z, (at,), row, flat(sum_z_b, (at,), row))
    sum_x[2] = jnp.zeros_like(sum_x[2])

    def one_run(run, carry):
        for row in chunks(ny):
            for at in range(3):
                put_padded(rim, (run, at), row, flat(of_chip, (run, at), row))
        for row in chunks(ny):
            mids = {at: padded(*adjoint2(at, run), row) for at in range(n - 1, n + 3)}
            value = add_product(padded(flow_part, (run, 0), row), flat(*faces.mx(n - 1), row), mids[n])
            put_padded(*flow(n - 1, run), row, value)
            for at in range(n, n + 2):
                value = faces.flow(
                    row, at, mids[at], padded(*adjoint2(at, run), row, 1), padded(*adjoint2(at, run), row, -1),
                    mids[at - 1], mids[at + 1],
                )
                put_padded(*flow(at, run), row, value)
        for row in chunks(ny):
            put_adjoint1(
                row, flow, adjoint2, run, range(n - 2, n + 1),
                lambda at: flat(weight_b, (run, at - (n - 2)), row), adjoint1,
            )
        for row in chunks(ny):
            for at in range(n - 3, n):
                total = add_product(
                    flat(sum_x, (at - (n - 3),), row), step_x(adjoint1, run, at, row), step_x(chem0, run, at, row)
                )
                if at == n - 1:
                    total = add_product(total, step_x(adjoint2, run, at, row), step_x(chem1, run, at, row))
                put_flat(sum_x, (at - (n - 3),), row, total)
            for at in range(n - 2, n):
                to = (at - (n - 2),)
                put_padded(sum_y, to, row, add_product(
                    padded(sum_y, to, row), step_y(adjoint1, run, at, row), step_y(chem0, run, at, row)
                ))
                put_flat(sum_z, to, row, add_product(
                    flat(sum_z, to, row), step_z(adjoint1, run, at, row), flat(step_z_b, (run, *to), row)
                ))
        return carry

    for run in range(runs):
        one_run(run, 0)
    for row in chunks(ny):
        for at in range(n - 2):
            value = flat(part, (at,), row)
            if at == n - 3:
                value = each(lambda a, b: a - 0.5 * b, value, flat(sum_x, (0,), row))
            put_plain(result, (place[at],), row, value)
        for at in range(2):
            sides = flat(sum_z, (at,), row)
            value = each(
                lambda a, b, c, d, e, f: -0.5 * ((a + b) + (c + d) + (e + f)),
                flat(sum_x, (at,), row), flat(sum_x, (at + 1,), row),
                padded(sum_y, (at,), row), padded(sum_y, (at,), row, -1), sides, before_z(sides),
            )
            put_plain(result, (place[n - 2 + at],), row, value)


def counts(at):
    return (at ^ (at >> 1)) & 1


def misfit_kernel(core, other_across, across, other_core, misfit):
    misfit[0] = ((core[...] + other_core[...]) + (across[...] + other_across[...]))[0, 0]


def call(kernel, outs, scratch, args, flops, scalar=None):
    moved = 4 * (sum(a.size for a in args) + sum(math.prod(o) for o in outs))
    return pl.pallas_call(
        kernel,
        out_shape=tuple(jax.ShapeDtypeStruct(o, jnp.float32) for o in outs),
        in_specs=[VMEM] * len(args),
        out_specs=tuple(SMEM if at == scalar else VMEM for at in range(len(outs))),
        scratch_shapes=[pltpu.VMEM(s, jnp.float32) for s in scratch],
        compiler_params=pltpu.CompilerParams(vmem_limit_bytes=16 * 1024 * 1024),
        cost_estimate=pl.CostEstimate(flops=flops, bytes_accessed=moved, transcendentals=0),
    )(*args)


def on_device(initial, observed, mobility):
    runs, n, ny, nz = initial.shape
    blocks = nz // LANES
    count = lax.axis_size("gx")
    over_chips = [(i, (i - 1 + 2 * (i % 2)) % count) for i in range(count)]
    over_cores = [(i, i ^ 1) for i in range(count)]
    cell = ny * nz

    def neighbours(to_chip, to_core):
        of_core = lax.ppermute(to_core, "gx", over_cores)
        return lax.ppermute(to_chip, "gx", over_chips), of_core

    def lies(*lead):
        return (*lead, blocks, ny, LANES)

    def lies_padded(*lead):
        return (*lead, blocks, ny + 2 * PAD, LANES)

    if n == 4:
        near = (initial, initial)
    else:
        near = [lax.dynamic_slice_in_dim(initial, at, 4, 1) for at in (either(0, n - 4), either(n - 4, 0))]
    of_chip, of_core = neighbours(*near)
    conc, mob, to_chip, to_core = call(
        own_kernel, (lies_padded(runs, n), lies_padded(n), lies(3), lies(3)), (), (initial, mobility),
        runs * n * cell,
    )
    m_chip, m_core = neighbours(to_chip, to_core)
    conc_core, chem0_a, *faces_a = call(
        core_kernel,
        (
            lies_padded(runs, 4), lies_padded(runs, n + 2),
            lies(n + 2), lies(n + 2), lies(n + 2), lies(n + 2), lies(n + 2), lies(n + 1),
        ),
        (lies_padded(3),),
        (of_core, m_core, conc, mob),
        20 * runs * (n + 2) * cell,
    )
    conc_chip, chem0_b, state1_a, chem1_a, adjoint2_a, squares = call(
        chip_kernel,
        (
            lies_padded(runs, 4), lies_padded(runs, 4), lies_padded(runs, n + 1),
            lies_padded(runs, n - 1), lies_padded(runs, n - 3), (CHUNK, LANES),
        ),
        (),
        (of_chip, conc, conc_core, chem0_a, observed, *faces_a),
        60 * runs * (n - 1) * cell,
    )
    *faces_b, state1_b, chem1_b, adjoint2_b, to_core, to_chip, share = call(
        forward_kernel,
        (
            lies(3), lies(2), lies(2), lies(2), lies(2), lies(3),
            lies_padded(runs, 3), lies_padded(runs, 3), lies_padded(runs, 3),
            (runs, 3, blocks, ny + ROWS, LANES), lies(runs, 3), (ROWS, LANES),
        ),
        (lies_padded(3), (CHUNK, LANES)),
        (m_chip, mob, conc, conc_chip, chem0_a, chem0_b, state1_a, chem1_a, adjoint2_a, squares, observed, *faces_a),
        60 * runs * 3 * cell,
    )
    faces = (*faces_a, *faces_b)
    of_chip, of_core = neighbours(to_chip, to_core)
    groups = lax.axis_size("group")

    def target(group, at, apart):
        if counts(at):
            return group * count + (at ^ apart)
        return min(group ^ 1, groups - 1) * count + at

    def hop(value, apart):
        pairs = [
            (group * count + at, target(group, at, apart)) for group in range(groups) for at in range(count)
        ]
        return lax.ppermute(value, ("group", "gx"), pairs)

    def hops(value, bits):
        aparts = [sum(2 << bit for at, bit in enumerate(bits) if which >> at & 1) for which in range(1, 1 << len(bits))]
        return [hop(value, apart) for apart in aparts]

    share = share + of_core[0, 0, 0, ny:]
    upper = range(count.bit_length() - 3, 0, -1)
    steps = [upper[at : at + 2] for at in range(0, len(upper), 2)]
    fars = hops(share, steps[0])
    flow_a, flow_part, adjoint1_a, weight_b, step_z_b, part, *sums_b, share = call(
        early_kernel,
        (
            lies_padded(runs, n + 1), lies_padded(runs, 1), lies_padded(runs, n - 1), lies(runs, 3), lies(runs, 2),
            lies(n - 2), lies(2), lies(2), lies(2), (ROWS, LANES),
        ),
        (lies_padded(runs, 3), lies(n), lies_padded(n), lies(n)),
        (of_core, *faces, chem0_a, chem0_b, state1_a, state1_b, chem1_a, chem1_b, adjoint2_a, adjoint2_b, share),
        60 * runs * n * cell,
    )
    for bits in steps[1:]:
        share = share + sum(fars)
        fars = hops(share, bits)
    share = share + sum(fars)
    fars = [lax.ppermute(share, "gx", [(at, at ^ apart) for at in range(count)]) for apart in (3, 2, 1)]
    result, share = call(
        late_kernel,
        ((n, ny, nz), (ROWS, LANES)),
        (
            lies_padded(runs, 3), lies_padded(runs, 3), lies_padded(runs, 3),
            lies(3), lies_padded(2), lies(2),
        ),
        (
            of_chip, *faces, chem0_a, chem0_b, chem1_b, adjoint2_b, flow_a, flow_part, adjoint1_a,
            weight_b, step_z_b, part, *sums_b, share,
        ),
        60 * runs * 3 * cell,
    )
    (misfit,) = call(misfit_kernel, ((1,),), (), (share, *fars), 1, scalar=0)
    return (result, misfit)


def solution(mesh):
    placed = (
        P("group", "gx", None, None),
        P("group", "gx", None, None),
        P(("group", "gx"), None, None),
    )
    return jax.shard_map(
        on_device,
        mesh=mesh,
        in_specs=placed,
        out_specs=(P(("group", "gx"), None, None), P("group")),
        check_vma=False,
    )
```
